32 devices in a mesh: tu: 8 (over z, x), tv: 4 (over y, core).
Axes of the slice: x: 2, y: 2, z: 4, core: 2. Of those that a mesh axis runs over, the one named last changes fastest.
Arguments:
- aperture_amp: bfloat16 [128, 512, 512], P(('tu', 'tv')), may hold values from 0.19921875 to 1.796875
- aperture_phase: bfloat16 [128, 512, 512], P(('tu', 'tv')), may hold values from -3.140625 to 3.140625
- plane_depths: float32 [4], replicated, may hold values from 8 to 344
- send_list: int32 [32, 32, 2], P(('tu', 'tv')), may hold values from 0 to 15, as said below
- send_count: int32 [32, 32], P(('tu', 'tv')), may hold values from 0 to 2, as said below
- vis_left: bfloat16 [12288, 128, 128], P(('tu', 'tv')), may hold values from -0.078125 to 0.078125
- vis_right: bfloat16 [12288, 64, 128], P(('tu', 'tv')), may hold values from -0.75 to 0.75
- block_slot: int32 [12288], P(('tu', 'tv')), may hold values from 0 to 63, as said below
- block_pos: int32 [12288], P(('tu', 'tv')), may hold values from 0 to 31
- block_count: int32 [32], P(('tu', 'tv')), may hold values from 96 to 384, as said below
Outputs:
- uv_grid: float32 [2, 2048, 2048], P(None, 'tu', 'tv')
The draws below stay inside these ranges and needn't reach their ends.
Inputs may be any that keep to these rules, and one draw needn't show every extreme that they name: `send_list`: each owner sends every one of its kernels to 2 slots, 32 in all; the used slots of an owner and tile are the first send_count of them; entries of unused slots are arbitrary kernel numbers in range. One tile, drawn afresh, receives 2 slots from every owner; a row of send_count sums to 32. `block_slot`: names a slot r = d * 2 + c that the block's tile receives, with c < send_count[d, tile]. `block_count`: some tile uses all 384 slots.
All inputs are finite; a program needn't handle non-finite values.
Results may differ from the reference program's by a relative error of at most 0.0065.
Values may be sent and summed in bfloat16 or wider, within the bound.
No kernel may reach another device: no remote copies, remote signals or barrier semaphores. Data moves between devices by JAX's collectives and lax.ppermute only.
A program may use at most 192 MiB of HBM per device.

```python
import math
import jax
import jax.numpy as jnp
from jax import lax

SCREEN = 512
KSIZE = 64
PATCH = 128
W_PLANES = 4
K_DEV = 16
CAP = 2
FAN = 2
B_DEV = 384
TILE_U = 256
TILE_V = 512
SCREENS = 128
BLOCKS = 12288
NU = 2048
NV = 2048
N_TU = 8
N_TV = 4
DEVICES = 32


def draw_plane_depths(key, part):
    planes = jnp.arange(W_PLANES, dtype=jnp.int32).astype(jnp.float32)
    jitter = jax.random.uniform(jax.random.fold_in(key, 53), (W_PLANES,), jnp.float32)
    units = 12.0 * planes + 1.0 + 6.0 * jitter
    return (units * (SCREEN / 64.0)).astype(jnp.float32)


def routing(key):
    slot_total = DEVICES * CAP
    sends = K_DEV * FAN
    favored = jax.random.randint(jax.random.fold_in(key, 7), (), 0, DEVICES)

    def per_source(source):
        source_key = jax.random.fold_in(jax.random.fold_in(key, 11), source)
        permuted = jax.random.permutation(source_key, slot_total).astype(jnp.int32)
        scores = jnp.where(permuted // CAP == favored, -1, jnp.arange(slot_total, dtype=jnp.int32))
        ordering = jnp.argsort(scores, stable=True)
        dest_seq = permuted[ordering][:sends] // CAP
        onehot = (dest_seq[:, None] == jnp.arange(DEVICES, dtype=jnp.int32)[None, :]).astype(jnp.int32)
        before = jnp.cumsum(onehot, axis=0) - onehot
        slot_ids = jnp.sum(before * onehot, axis=1)
        counts = jnp.sum(onehot, axis=0)
        kernel_ids = jnp.arange(sends, dtype=jnp.int32) // FAN
        filler = jax.random.randint(jax.random.fold_in(source_key, 3), (DEVICES, CAP), 0, K_DEV)
        lists = filler.at[dest_seq, slot_ids].set(kernel_ids)
        return (lists.astype(jnp.int32), counts.astype(jnp.int32))
    return jax.vmap(per_source)(jnp.arange(DEVICES, dtype=jnp.int32))


def draw_send_list(key, part):
    return routing(key)[0]


def draw_send_count(key, part):
    return routing(key)[1]


def draw_block_slot(key, part):
    lists, counts = routing(key)
    is_live = (jnp.arange(CAP, dtype=jnp.int32)[None, None, :] < counts.T[:, :, None]).reshape(DEVICES, DEVICES * CAP).astype(jnp.int32)
    live_total = jnp.sum(is_live, axis=1)
    running = jnp.cumsum(is_live, axis=1)
    random_bits = jax.random.randint(jax.random.fold_in(key, 29), (DEVICES, B_DEV), 0, 2 ** 30)
    chosen = random_bits % jnp.maximum(live_total, 1)[:, None]
    picked = jnp.argmax(running[:, None, :] > chosen[:, :, None], axis=2).astype(jnp.int32)
    return picked.reshape(-1)


def draw_block_count(key, part):
    counts = jax.random.randint(jax.random.fold_in(key, 41), (DEVICES,), B_DEV // 4, B_DEV + 1)
    fullest = jax.random.randint(jax.random.fold_in(key, 43), (), 0, DEVICES)
    return jnp.where(jnp.arange(DEVICES, dtype=jnp.int32) == fullest, B_DEV, counts).astype(jnp.int32)


def touch_ends(drawn, key, smallest, largest):
    dims = drawn.shape
    place = [jax.random.randint(jax.random.fold_in(key, axis), (), 0, dims[axis]) for axis in range(len(dims))]
    drawn = drawn.at[tuple(place)].set(smallest)
    longest = dims.index(max(dims))
    place[longest] = (place[longest] + 1) % dims[longest]
    return drawn.at[tuple(place)].set(largest)


def levels(stream_key, dims, cuts, least, largest):
    factor_of, own = 1.0, jax.random.fold_in(stream_key, 6)
    for axis_at, shards_of in cuts:
        draws = jnp.exp(jax.random.uniform(jax.random.fold_in(own, axis_at), (shards_of,), jnp.float32, least / len(cuts), largest / len(cuts)))
        factor_of = factor_of * jnp.repeat(draws, dims[axis_at] // shards_of).reshape([-1 if axis == axis_at else 1 for axis in range(len(dims))])
    return factor_of


def normal_values(rng, dims, spread, most, pieces=(), kind=jnp.bfloat16):
    values = spread * jax.random.normal(rng, dims, jnp.float32)
    if pieces:
        values = values * levels(rng, dims, pieces, -0.22, 0.18)
    return jnp.clip(values, -most, most).astype(kind)


def setup_inputs(seed: int = 0) -> dict:
    keys = jax.random.split(jax.random.key(seed), 11)
    return {
        "aperture_amp": jnp.clip(0.19921875 + 1.5976562 * jax.random.uniform(keys[0], (SCREENS, SCREEN, SCREEN), jnp.float32) ** levels(keys[0], (SCREENS, SCREEN, SCREEN), ((0, 32),), -0.2, 0.2), 0.19921875, 1.796875).astype(jnp.bfloat16),
        "aperture_phase": jnp.clip(jax.random.uniform(keys[1], (SCREENS, SCREEN, SCREEN), jnp.float32, -3.140625, 3.140625), -3.140625, 3.140625).astype(jnp.bfloat16),
        "plane_depths": draw_plane_depths(jax.random.fold_in(keys[10], 71), 0),
        "send_list": draw_send_list(jax.random.fold_in(keys[10], 71), 0),
        "send_count": draw_send_count(jax.random.fold_in(keys[10], 71), 0),
        "vis_left": normal_values(keys[5], (BLOCKS, PATCH, 2 * KSIZE), (8 * KSIZE * B_DEV * KSIZE * KSIZE // (TILE_U * TILE_V)) ** -0.5, 0.078125, ((0, 32),)),
        "vis_right": normal_values(keys[6], (BLOCKS, KSIZE, PATCH), KSIZE ** -0.5, 0.75, ((0, 32),)),
        "block_slot": draw_block_slot(jax.random.fold_in(keys[10], 71), 0),
        "block_pos": touch_ends(jax.random.randint(keys[8], (BLOCKS,), 0, (TILE_U // KSIZE) * (TILE_V // KSIZE)), jax.random.fold_in(keys[8], 1), 0, ((TILE_U // KSIZE) * (TILE_V // KSIZE)) - 1).astype(jnp.int32),
        "block_count": draw_block_count(jax.random.fold_in(keys[10], 71), 0),
    }


def dft_table(kernel_size, screen_size):
    frequency = jnp.arange(kernel_size, dtype=jnp.int32) - kernel_size // 2
    cell_ids = jnp.arange(screen_size, dtype=jnp.int32)
    turns = jnp.mod(frequency[:, None] * cell_ids[None, :], screen_size).astype(jnp.float32)
    angles = (2.0 * math.pi / screen_size) * turns
    return jnp.concatenate([jnp.cos(angles), -jnp.sin(angles)], axis=0).astype(jnp.bfloat16)


def aperture_screens(amplitude, phase_rows, plane_depths):
    screen_size = amplitude.shape[-1]
    coords = (jnp.arange(screen_size, dtype=jnp.int32).astype(jnp.float32) - screen_size // 2) / screen_size
    radius = coords[:, None] ** 2 + coords[None, :] ** 2
    angles = phase_rows.astype(jnp.float32)[:, None] + (2.0 * math.pi) * plane_depths[None, :, None, None] * radius
    magnitude = amplitude.astype(jnp.float32)[:, None]
    real_part = (magnitude * jnp.cos(angles)).astype(jnp.bfloat16)
    imag_part = (magnitude * jnp.sin(angles)).astype(jnp.bfloat16)
    stacked = jnp.concatenate([real_part, imag_part], axis=-1)
    return stacked.reshape(-1, screen_size, 2 * screen_size)


def kernels_from(stacked, kernel_size):
    screen_size = stacked.shape[1]
    dft = dft_table(kernel_size, screen_size).astype(jnp.float32)
    product = jnp.einsum("as,ksn->kan", dft, stacked.astype(jnp.float32), precision=lax.Precision.HIGHEST)
    half_real = product[:, :kernel_size, :screen_size] - product[:, kernel_size:, screen_size:]
    half_imag = product[:, :kernel_size, screen_size:] + product[:, kernel_size:, :screen_size]
    halves = jnp.concatenate([half_real, half_imag], axis=1).astype(jnp.bfloat16)
    second = jnp.einsum("kas,bs->kab", halves.astype(jnp.float32), dft, precision=lax.Precision.HIGHEST)
    out_real = second[:, :kernel_size, :kernel_size] - second[:, kernel_size:, kernel_size:]
    out_imag = second[:, :kernel_size, kernel_size:] + second[:, kernel_size:, :kernel_size]
    return (jnp.concatenate([out_real, out_imag], axis=-1) / screen_size).astype(jnp.bfloat16)


def grid_patches(block_kernels, left_rows, right_rows):
    kernel_size = block_kernels.shape[1]
    real_k = block_kernels[:, :, :kernel_size]
    imag_k = block_kernels[:, :, kernel_size:]
    operator_rows = jnp.concatenate([block_kernels, jnp.concatenate([-imag_k, real_k], axis=2)], axis=1)
    mixed = jnp.einsum("gpc,gcd->gpd", left_rows.astype(jnp.float32), operator_rows.astype(jnp.float32), precision=lax.Precision.HIGHEST).astype(jnp.bfloat16)
    mixed = mixed.reshape(mixed.shape[0], mixed.shape[1], 2, kernel_size)
    return jnp.einsum("gpck,gkq->gcpq", mixed.astype(jnp.float32), right_rows.astype(jnp.float32), precision=lax.Precision.HIGHEST)


def spread_patches(placed, row_slots, col_slots, kernel_size):
    placed = placed.reshape(row_slots, col_slots, 2, 2, kernel_size, 2, kernel_size)
    extended = jnp.zeros((row_slots + 1, col_slots + 1, 2, kernel_size, kernel_size), jnp.float32)
    for row_shift in range(2):
        for col_shift in range(2):
            extended = extended.at[row_shift:row_shift + row_slots, col_shift:col_shift + col_slots].add(placed[:, :, :, row_shift, :, col_shift, :])
    extended = extended.transpose(2, 0, 3, 1, 4)
    return extended.reshape(2, (row_slots + 1) * kernel_size, (col_slots + 1) * kernel_size)


def reference(aperture_amp, aperture_phase, plane_depths, send_list, send_count, vis_left, vis_right, block_slot, block_pos, block_count):
    devices_total = N_TU * N_TV
    row_slots = TILE_U // KSIZE
    col_slots = TILE_V // KSIZE

    def per_screen(screen_pair):
        return kernels_from(aperture_screens(screen_pair[0][None], screen_pair[1][None], plane_depths), KSIZE)

    kernels = lax.map(per_screen, (aperture_amp, aperture_phase)).reshape(-1, KSIZE, 2 * KSIZE)
    sources = jnp.arange(devices_total, dtype=jnp.int32)

    def per_tile(tile_in):
        tile_id, left_rows, right_rows, slot_ids, positions, tile_count = tile_in
        chosen = sources[:, None] * K_DEV + send_list[:, tile_id, :]
        is_live = jnp.arange(CAP, dtype=jnp.int32)[None, :] < send_count[:, tile_id][:, None]
        received = jnp.where(is_live[:, :, None, None], kernels[chosen], jnp.zeros((), jnp.bfloat16))
        received = received.reshape(devices_total * CAP, KSIZE, 2 * KSIZE)
        patches = grid_patches(received[slot_ids], left_rows, right_rows)
        block_live = (jnp.arange(B_DEV, dtype=jnp.int32) < tile_count).astype(jnp.float32)
        patches = patches * block_live[:, None, None, None]
        placed = jax.ops.segment_sum(patches, positions, num_segments=row_slots * col_slots)
        return spread_patches(placed, row_slots, col_slots, KSIZE)

    tiles_in = (sources,
                vis_left.reshape(devices_total, B_DEV, PATCH, 2 * KSIZE),
                vis_right.reshape(devices_total, B_DEV, KSIZE, PATCH),
                block_slot.reshape(devices_total, B_DEV),
                block_pos.reshape(devices_total, B_DEV),
                block_count)
    extended = lax.map(per_tile, tiles_in).reshape(N_TU, N_TV, 2, TILE_U + KSIZE, TILE_V + KSIZE)
    bottom = extended[:, :, :, TILE_U:, :]
    moved = jnp.concatenate([jnp.zeros_like(bottom[:1]), bottom[:-1]], axis=0)
    extended = extended.at[:, :, :, :KSIZE, :].add(moved)
    side = extended[:, :, :, :TILE_U, TILE_V:]
    moved = jnp.concatenate([jnp.zeros_like(side[:, :1]), side[:, :-1]], axis=1)
    tiles = extended[:, :, :, :TILE_U, :TILE_V].at[:, :, :, :, :KSIZE].add(moved)
    return tiles.transpose(2, 0, 3, 1, 4).reshape(2, NU, NV)
```

```python
import functools
import math

import jax
import jax.numpy as jnp
import numpy as np
from jax import lax
from jax.experimental import pallas as pl
from jax.experimental.pallas import tpu as pltpu
from jax.sharding import PartitionSpec as P

TILE_U = 256
TILE_V = 512
QUAD = 4

def _fit(fn, degree):
    span = math.pi ** 2
    nodes = 0.5 * span * (1.0 - np.cos(np.pi * (np.arange(400) + 0.5) / 400))
    cheb = np.polynomial.chebyshev.Chebyshev.fit(nodes, fn(np.sqrt(nodes)), degree, domain=[0, span])
    return [float(c) for c in cheb.convert(kind=np.polynomial.Polynomial).coef]


COS_POLY = _fit(np.cos, 6)
SIN_POLY = _fit(lambda x: np.sin(x) / x, 5)


def horner(coefs, u):
    total = jnp.full_like(u, coefs[-1])
    for coef in coefs[-2::-1]:
        total = total * u + coef
    return total


def cos_sin(x):
    u = x * x
    return horner(COS_POLY, u), x * horner(SIN_POLY, u)


def from_behind(block, axis, distance):
    devices = range(lax.axis_size(axis))
    route = [(i - distance, i) for i in devices if i - distance in devices]
    return lax.ppermute(block, axis, route)


def dft_table(kernel_size, screen_size):
    frequency = np.arange(kernel_size) - kernel_size // 2
    turns = np.mod(frequency[:, None] * np.arange(screen_size)[None, :], screen_size)
    angles = (2.0 * math.pi / screen_size) * turns
    return np.concatenate([np.cos(angles), -np.sin(angles)], axis=0).astype(jnp.bfloat16)


def kernels_body(
    send_ref, count_ref, depth_ref, amp_ref, phase_ref, dft_ref, out_ref, table, screen, halves, made
):
    step = pl.program_id(0)
    size = amp_ref.shape[-1]
    planes = depth_ref.shape[0]
    kernel_size = dft_ref.shape[0] // 2

    @pl.when(step == 0)
    def _():
        cells = lax.broadcasted_iota(jnp.int32, (1, size), 1).astype(jnp.float32)
        place = (cells - size // 2) / size
        square = place * place
        real_f = dft_ref[:kernel_size, :].astype(jnp.float32)
        imag_f = dft_ref[kernel_size:, :].astype(jnp.float32)
        for p in range(planes):
            turns = depth_ref[p] * square
            turns = turns - jnp.round(turns)
            real_e, imag_e = cos_sin((2.0 * math.pi) * turns)
            real_g = real_f * real_e - imag_f * imag_e
            imag_g = real_f * imag_e + imag_f * real_e
            base = p * 2 * kernel_size
            table[base : base + kernel_size, :size] = real_g.astype(jnp.bfloat16)
            table[base : base + kernel_size, size:] = (-imag_g).astype(jnp.bfloat16)
            table[base + kernel_size : base + 2 * kernel_size, :size] = imag_g.astype(jnp.bfloat16)
            table[base + kernel_size : base + 2 * kernel_size, size:] = real_g.astype(jnp.bfloat16)

    width = 256
    for start in range(0, size, width):
        cols = slice(start, start + width)
        magnitude = amp_ref[0, :, cols].astype(jnp.float32)
        real_e, imag_e = cos_sin(phase_ref[0, :, cols].astype(jnp.float32))
        screen[:size, cols] = (magnitude * real_e).astype(jnp.bfloat16)
        screen[size:, cols] = (magnitude * imag_e).astype(jnp.bfloat16)
        product = jnp.dot(table[...], screen[:, cols], preferred_element_type=jnp.float32)
        for p in range(planes):
            base = p * 2 * kernel_size
            halves[p, :, start : start + width] = product[base : base + kernel_size].astype(jnp.bfloat16)
            halves[p, :, size + start : size + start + width] = product[
                base + kernel_size : base + 2 * kernel_size
            ].astype(jnp.bfloat16)
    for p in range(planes):
        base = p * 2 * kernel_size
        second = lax.dot_general(
            halves[p],
            table[base : base + 2 * kernel_size, :],
            (((1,), (1,)), ((), ())),
            preferred_element_type=jnp.float32,
        )
        made[step * planes + p] = (second * (1.0 / size)).astype(jnp.bfloat16)

    @pl.when(step == pl.num_programs(0) - 1)
    def _():
        tiles, capacity = send_ref.shape

        @pl.loop(0, tiles)
        def _(t):
            for c in range(capacity):
                chosen = made[send_ref[t, c]]
                live = c < count_ref[t]
                out_ref[t * capacity + c] = jnp.where(live, chosen, jnp.zeros_like(chosen))


def make_kernels(aperture_amp, aperture_phase, plane_depths, send_rows, counts, kernel_size):
    screens, size, _ = aperture_amp.shape
    planes = plane_depths.shape[0]
    tiles, capacity = send_rows.shape
    dft = jnp.asarray(dft_table(kernel_size, size))
    return pl.pallas_call(
        kernels_body,
        grid_spec=pltpu.PrefetchScalarGridSpec(
            num_scalar_prefetch=3,
            grid=(screens,),
            in_specs=[
                pl.BlockSpec((1, size, size), lambda s, *_: (s, 0, 0)),
                pl.BlockSpec((1, size, size), lambda s, *_: (s, 0, 0)),
                pl.BlockSpec((2 * kernel_size, size), lambda s, *_: (0, 0)),
            ],
            out_specs=pl.BlockSpec((tiles * capacity, kernel_size, 2 * kernel_size), lambda s, *_: (0, 0, 0)),
            scratch_shapes=[
                pltpu.VMEM((planes * 2 * kernel_size, 2 * size), jnp.bfloat16),
                pltpu.VMEM((2 * size, size), jnp.bfloat16),
                pltpu.VMEM((planes, kernel_size, 2 * size), jnp.bfloat16),
                pltpu.VMEM((screens * planes, kernel_size, 2 * kernel_size), jnp.bfloat16),
            ],
        ),
        out_shape=jax.ShapeDtypeStruct((tiles * capacity, kernel_size, 2 * kernel_size), jnp.bfloat16),
        compiler_params=pltpu.CompilerParams(vmem_limit_bytes=40 * 2**20),
        name="make_kernels",
    )(send_rows, counts, plane_depths, aperture_amp, aperture_phase, dft)


def plan_body(pos_ref, slot_ref, count_ref, block_out, slot_out, anchor_out, total_out, tally, cursor):
    anchors = tally.shape[0]

    @pl.loop(0, anchors)
    def _(q):
        tally[q] = 0

    live = count_ref[0]

    @pl.loop(0, live)
    def _(j):
        q = pos_ref[j]
        tally[q] = tally[q] + 1

    def lay(q, quad):
        number = tally[q]
        quads = (number + QUAD - 1) // QUAD
        cursor[q] = quad * QUAD

        @pl.loop(0, quads)
        def _(i):
            anchor_out[quad + i] = q

        @pl.loop(number, quads * QUAD)
        def _(i):
            block_out[quad * QUAD + i] = 0
            slot_out[quad * QUAD + i] = -1

        return quad + quads

    quad_total = lax.fori_loop(0, anchors, lay, 0)
    total_out[0] = quad_total

    @pl.loop(0, live)
    def _(j):
        q = pos_ref[j]
        at = cursor[q]
        cursor[q] = at + 1
        block_out[at] = j
        slot_out[at] = slot_ref[j]


def quad_capacity(blocks, anchors):
    quads = (blocks + (QUAD - 1) * anchors) // QUAD
    return quads + 4


def plan_blocks(block_pos, block_slot, block_count, anchors):
    blocks = block_pos.shape[0]
    quads = quad_capacity(blocks, anchors)
    smem = pl.BlockSpec(memory_space=pltpu.SMEM)
    return pl.pallas_call(
        plan_body,
        in_specs=[smem] * 3,
        out_specs=[smem] * 4,
        out_shape=[
            jax.ShapeDtypeStruct((quads * QUAD,), jnp.int32),
            jax.ShapeDtypeStruct((quads * QUAD,), jnp.int32),
            jax.ShapeDtypeStruct((quads,), jnp.int32),
            jax.ShapeDtypeStruct((1,), jnp.int32),
        ],
        scratch_shapes=[pltpu.SMEM((anchors,), jnp.int32), pltpu.SMEM((anchors,), jnp.int32)],
        name="plan_blocks",
    )(block_pos, block_slot, block_count)


def grid_body(
    block_ref, slot_ref, anchor_ref, total_ref, kern_ref, left_ref, right_ref,
    tile_ref, row_ref, col_ref, corner_ref, mixed, sums,
):
    slots, kernel_size, _ = kern_ref.shape
    patch = left_ref.shape[1]
    anchors = sums.shape[0]
    row_slots = tile_ref.shape[1] // kernel_size
    col_slots = tile_ref.shape[2] // kernel_size
    total = total_ref[0]

    @pl.loop(0, anchors)
    def _(q):
        sums[q] = jnp.zeros(sums.shape[1:], sums.dtype)

    zero = jnp.zeros((kernel_size, patch), jnp.bfloat16)

    def first(quad, place):
        for e in range(QUAD):
            at = quad * QUAD + e
            slot = slot_ref[at]
            right = right_ref[block_ref[at]]
            kern = kern_ref[jnp.maximum(slot, 0)]
            kern = jnp.where(slot >= 0, kern, jnp.zeros_like(kern))
            spread = jnp.concatenate(
                [jnp.concatenate([right, zero], axis=1), jnp.concatenate([zero, right], axis=1)], axis=0
            )
            out = jnp.dot(kern, spread, preferred_element_type=jnp.float32)
            real, imag = out[:, :patch], out[:, patch:]
            base = e * 2 * kernel_size
            mixed[place, base : base + kernel_size, :patch] = real.astype(jnp.bfloat16)
            mixed[place, base : base + kernel_size, patch:] = imag.astype(jnp.bfloat16)
            mixed[place, base + kernel_size : base + 2 * kernel_size, :patch] = (-imag).astype(jnp.bfloat16)
            mixed[place, base + kernel_size : base + 2 * kernel_size, patch:] = real.astype(jnp.bfloat16)

    def second(quad, place):
        left = jnp.concatenate([left_ref[block_ref[quad * QUAD + e]] for e in range(QUAD)], axis=1)
        q = anchor_ref[quad]
        sums[q] += jnp.dot(left, mixed[place], preferred_element_type=jnp.float32)

    first(0, 0)

    @pl.loop(0, total)
    def _(quad):
        place = quad % 2
        first(jnp.minimum(quad + 1, total - 1), 1 - place)
        second(quad, place)

    lane = lax.broadcasted_iota(jnp.int32, (kernel_size, patch), 1)
    low = lane < kernel_size
    col_tiles = tile_ref.shape[2] // patch
    for c in range(2):
        for a in range(row_slots + 1):
            def strip(col):
                parts = []
                if a < row_slots:
                    parts.append(sums[a * col_slots + col, :kernel_size, c * patch : (c + 1) * patch])
                if a > 0:
                    parts.append(sums[(a - 1) * col_slots + col, kernel_size:, c * patch : (c + 1) * patch])
                return parts[0] if len(parts) == 1 else parts[0] + parts[1]

            behind = None
            for tile in range(col_tiles):
                even = strip(2 * tile)
                odd = pltpu.roll(strip(2 * tile + 1), kernel_size, 1)
                if behind is None:
                    value = even + jnp.where(low, 0.0, odd)
                else:
                    value = even + jnp.where(low, behind, odd)
                behind = odd
                lanes = slice(tile * patch, (tile + 1) * patch)
                if a < row_slots:
                    tile_ref[c, a * kernel_size : (a + 1) * kernel_size, lanes] = value
                else:
                    row_ref[c, :, lanes] = value.astype(row_ref.dtype)
            edge = jnp.where(low, behind, 0.0)
            if c == 0:
                kept = edge
            else:
                kept = pltpu.roll(edge, kernel_size, 1)
            if a < row_slots:
                rows = slice(a * kernel_size, (a + 1) * kernel_size)
                if c == 0:
                    col_ref[rows, :] = kept.astype(col_ref.dtype)
                else:
                    col_ref[rows, :] = (col_ref[rows, :].astype(jnp.float32) + kept).astype(col_ref.dtype)
            else:
                if c == 0:
                    corner_ref[...] = kept.astype(corner_ref.dtype)
                else:
                    corner_ref[...] = (corner_ref[...].astype(jnp.float32) + kept).astype(corner_ref.dtype)


def grid_tile(plan, kernels, vis_left, vis_right):
    block_plan, slot_plan, anchor_plan, quad_total = plan
    kernel_size = kernels.shape[1]
    patch = vis_left.shape[1]
    anchors = (TILE_U // kernel_size) * (TILE_V // kernel_size)
    smem = pl.BlockSpec(memory_space=pltpu.SMEM)
    vmem = pl.BlockSpec(memory_space=pltpu.VMEM)
    left = pltpu.with_memory_space_constraint(vis_left, pltpu.VMEM)
    right = pltpu.with_memory_space_constraint(vis_right, pltpu.VMEM)
    return pl.pallas_call(
        grid_body,
        in_specs=[smem] * 4 + [vmem] * 3,
        out_specs=[vmem] * 4,
        out_shape=[
            jax.ShapeDtypeStruct((2, TILE_U, TILE_V), jnp.float32),
            jax.ShapeDtypeStruct((2, kernel_size, TILE_V), jnp.bfloat16),
            jax.ShapeDtypeStruct((TILE_U, 2 * kernel_size), jnp.bfloat16),
            jax.ShapeDtypeStruct((kernel_size, 2 * kernel_size), jnp.bfloat16),
        ],
        scratch_shapes=[
            pltpu.VMEM((2, QUAD * 2 * kernel_size, 2 * patch), jnp.bfloat16),
            pltpu.VMEM((anchors, patch, 2 * patch), jnp.float32),
        ],
        compiler_params=pltpu.CompilerParams(vmem_limit_bytes=24 * 2**20),
        name="grid_tile",
    )(block_plan, slot_plan, anchor_plan, quad_total, kernels, left, right)


def shards(
    aperture_amp,
    aperture_phase,
    plane_depths,
    send_list,
    send_count,
    vis_left,
    vis_right,
    block_slot,
    block_pos,
    block_count,
):
    kernel_size = vis_right.shape[1]
    anchors = (TILE_U // kernel_size) * (TILE_V // kernel_size)
    outgoing = make_kernels(
        aperture_amp, aperture_phase, plane_depths, send_list[0], send_count[0], kernel_size
    )
    tiles, capacity = send_list.shape[1:]
    outgoing = outgoing.reshape((tiles, capacity) + outgoing.shape[1:])
    arrived = lax.all_to_all(outgoing, ("tu", "tv"), split_axis=0, concat_axis=0, tiled=True)
    plan = plan_blocks(block_pos, block_slot, block_count, anchors)
    received = arrived.reshape((-1,) + arrived.shape[2:])
    tile, row, col, corner = grid_tile(plan, received, vis_left, vis_right)
    col = jnp.concatenate([corner, col], axis=0)
    row = from_behind(row, "tu", 1)
    col = from_behind(col, "tv", 1)
    corner = from_behind(col[:kernel_size], "tu", 1)
    col = col[kernel_size:].astype(jnp.float32)
    corner = corner.astype(jnp.float32)
    tile = tile.at[:, :kernel_size, :].add(row.astype(jnp.float32))
    col = col.at[:kernel_size].add(corner)
    col = jnp.stack([col[:, :kernel_size], col[:, kernel_size:]])
    return tile.at[:, :, :kernel_size].add(col)


def solution(mesh):
    placed = (
        P(("tu", "tv"), None, None),
        P(("tu", "tv"), None, None),
        P(),
        P(("tu", "tv"), None, None),
        P(("tu", "tv"), None),
        P(("tu", "tv"), None, None),
        P(("tu", "tv"), None, None),
        P(("tu", "tv")),
        P(("tu", "tv")),
        P(("tu", "tv")),
    )
    return jax.shard_map(
        shards, mesh=mesh, in_specs=placed, out_specs=P(None, "tu", "tv"), check_vma=False
    )
```

```python
import functools
import math

import jax
import jax.numpy as jnp
import numpy as np
from jax import lax
from jax.experimental import pallas as pl
from jax.experimental.pallas import tpu as pltpu
from jax.sharding import PartitionSpec as P

TILE_U = 256
TILE_V = 512
QUAD = 4
UNROLL = 4
SPLIT = 1

def _fit(fn, degree):
    span = math.pi ** 2
    nodes = 0.5 * span * (1.0 - np.cos(np.pi * (np.arange(400) + 0.5) / 400))
    cheb = np.polynomial.chebyshev.Chebyshev.fit(nodes, fn(np.sqrt(nodes)), degree, domain=[0, span])
    return [float(c) for c in cheb.convert(kind=np.polynomial.Polynomial).coef]


COS_POLY = _fit(np.cos, 6)
SIN_POLY = _fit(lambda x: np.sin(x) / x, 5)


def horner(coefs, u):
    total = jnp.full_like(u, coefs[-1])
    for coef in coefs[-2::-1]:
        total = total * u + coef
    return total


def cos_sin(x):
    u = x * x
    return horner(COS_POLY, u), x * horner(SIN_POLY, u)


def from_behind(block, axis, distance):
    devices = range(lax.axis_size(axis))
    route = [(i - distance, i) for i in devices if i - distance in devices]
    return lax.ppermute(block, axis, route)


def in_hbm(array):
    return pltpu.with_memory_space_constraint(array, pltpu.HBM)


def in_vmem(array):
    return pltpu.with_memory_space_constraint(array, pltpu.VMEM)


def kernels_body(
    list_hbm, depth_hbm, amp_hbm, phase_hbm, out_ref,
    chosen_list, depth, amp, phase, table, screen, halves, made, small_sems, bulk_sems,
):
    screens, size, _ = amp.shape
    planes = depth.shape[0]
    kernel_size = out_ref.shape[1]
    small = [
        pltpu.make_async_copy(depth_hbm, depth, small_sems.at[0]),
        pltpu.make_async_copy(list_hbm, chosen_list, small_sems.at[1]),
    ]
    for copy in small:
        copy.start()

    def bulk(s):
        return [
            pltpu.make_async_copy(amp_hbm.at[s], amp.at[s], bulk_sems.at[0, s]),
            pltpu.make_async_copy(phase_hbm.at[s], phase.at[s], bulk_sems.at[1, s]),
        ]

    for s in range(screens):
        for copy in bulk(s):
            copy.start()

    frequency = lax.broadcasted_iota(jnp.int32, (kernel_size, size), 0) - kernel_size // 2
    cells = lax.broadcasted_iota(jnp.int32, (kernel_size, size), 1)
    turns = frequency.astype(jnp.float32) * cells.astype(jnp.float32) / size
    real_f, imag_f = cos_sin((2.0 * math.pi) * (turns - jnp.round(turns)))
    real_f = real_f.astype(jnp.bfloat16).astype(jnp.float32)
    imag_f = (-imag_f).astype(jnp.bfloat16).astype(jnp.float32)
    place = (lax.broadcasted_iota(jnp.int32, (1, size), 1).astype(jnp.float32) - size // 2) / size
    square = place * place
    for copy in small:
        copy.wait()
    for p in range(planes):
        turns = depth[p] * square
        real_e, imag_e = cos_sin((2.0 * math.pi) * (turns - jnp.round(turns)))
        real_g = (real_f * real_e - imag_f * imag_e).astype(jnp.bfloat16)
        imag_g = (real_f * imag_e + imag_f * real_e).astype(jnp.bfloat16)
        top = slice(p * 2 * kernel_size, (p * 2 + 1) * kernel_size)
        low = slice((p * 2 + 1) * kernel_size, (p * 2 + 2) * kernel_size)
        table[top, :size] = real_g
        table[top, size:] = -imag_g
        table[low, :size] = imag_g
        table[low, size:] = real_g

    width = 256

    @pl.loop(0, screens)
    def _(s):
        for copy in bulk(s):
            copy.wait()
        for start in range(0, size, width):
            cols = slice(start, start + width)
            magnitude = amp[s, :, cols].astype(jnp.float32)
            real_e, imag_e = cos_sin(phase[s, :, cols].astype(jnp.float32))
            screen[:size, cols] = (magnitude * real_e).astype(jnp.bfloat16)
            screen[size:, cols] = (magnitude * imag_e).astype(jnp.bfloat16)
            product = jnp.dot(table[...], screen[:, cols], preferred_element_type=jnp.float32)
            for p in range(planes):
                base = p * 2 * kernel_size
                halves[p, :, start : start + width] = product[base : base + kernel_size].astype(jnp.bfloat16)
                halves[p, :, size + start : size + start + width] = product[
                    base + kernel_size : base + 2 * kernel_size
                ].astype(jnp.bfloat16)
        for p in range(planes):
            second = lax.dot_general(
                halves[p],
                table[p * 2 * kernel_size : (p + 1) * 2 * kernel_size, :],
                (((1,), (1,)), ((), ())),
                preferred_element_type=jnp.float32,
            )
            made[s * planes + p] = (second * (1.0 / size)).astype(jnp.bfloat16)

    capacity, tiles = chosen_list.shape

    @pl.loop(0, tiles)
    def _(t):
        for c in range(capacity):
            which = chosen_list[c, t]
            chosen = made[jnp.maximum(which, 0)]
            out_ref[t * capacity + c] = jnp.where(which >= 0, chosen, jnp.zeros_like(chosen))


def make_kernels(aperture_amp, aperture_phase, plane_depths, chosen_list, kernel_size):
    screens, size, _ = aperture_amp.shape
    planes = plane_depths.shape[0]
    capacity, tiles = chosen_list.shape
    hbm = pl.BlockSpec(memory_space=pl.ANY)
    return pl.pallas_call(
        kernels_body,
        in_specs=[hbm] * 4,
        out_specs=pl.BlockSpec(memory_space=pltpu.VMEM),
        out_shape=jax.ShapeDtypeStruct((tiles * capacity, kernel_size, 2 * kernel_size), jnp.bfloat16),
        scratch_shapes=[
            pltpu.SMEM((capacity, tiles), jnp.int32),
            pltpu.SMEM((planes,), jnp.float32),
            pltpu.VMEM((screens, size, size), jnp.bfloat16),
            pltpu.VMEM((screens, size, size), jnp.bfloat16),
            pltpu.VMEM((planes * 2 * kernel_size, 2 * size), jnp.bfloat16),
            pltpu.VMEM((2 * size, size), jnp.bfloat16),
            pltpu.VMEM((planes, kernel_size, 2 * size), jnp.bfloat16),
            pltpu.VMEM((screens * planes, kernel_size, 2 * kernel_size), jnp.bfloat16),
            pltpu.SemaphoreType.DMA((2,)),
            pltpu.SemaphoreType.DMA((2, screens)),
        ],
        compiler_params=pltpu.CompilerParams(vmem_limit_bytes=32 * 2**20),
        name="make_kernels",
    )(in_hbm(chosen_list), in_hbm(plane_depths), in_hbm(aperture_amp), in_hbm(aperture_phase))


class Layout:
    def __init__(self, blocks, anchors):
        step = 2 * UNROLL
        self.parts = SPLIT + 1
        buckets = SPLIT * anchors
        self.quads = (blocks + (QUAD - 1) * buckets) // QUAD + 1 + self.parts * (step - 1) + UNROLL
        self.anchor = self.parts + 1
        self.block = self.anchor + self.quads
        self.slot = self.block + self.quads * QUAD
        self.total = self.slot + self.quads * QUAD


def plan_body(
    pos_ref, slot_ref, count_ref, half_ref, left_hbm, right_hbm, plan_ref, left_ref, right_ref,
    tally, cursor, sems, *, row_slots, col_slots, half_slots,
):
    copies = [
        pltpu.make_async_copy(left_hbm, left_ref, sems.at[0]),
        pltpu.make_async_copy(right_hbm, right_ref, sems.at[1]),
    ]
    for copy in copies:
        copy.start()
    anchors = row_slots * col_slots
    border = row_slots + col_slots - 1
    layout = Layout(pos_ref.shape[0], anchors)
    step = 2 * UNROLL

    @pl.loop(0, SPLIT * anchors)
    def _(b):
        tally[b] = 0

    live = count_ref[0]

    def bucket_of(j):
        q = pos_ref[j]
        row = q // col_slots
        col = q % col_slots
        rank = jnp.where(
            row == row_slots - 1,
            col,
            jnp.where(
                col == col_slots - 1, col_slots + row, border + row * (col_slots - 1) + col
            ),
        )
        if SPLIT == 1:
            return rank
        other = (slot_ref[j] // half_slots) != half_ref[0]
        return rank + jnp.where(other, anchors, 0)

    @pl.loop(0, live)
    def _(j):
        b = bucket_of(j)
        tally[b] = tally[b] + 1

    def dead(quad):
        plan_ref[layout.anchor + quad] = 0
        for e in range(QUAD):
            plan_ref[layout.block + quad * QUAD + e] = 0
            plan_ref[layout.slot + quad * QUAD + e] = -1

    def lay(b, quad):
        rank = lax.rem(b, anchors)
        inner = rank - border
        q = jnp.where(
            rank < col_slots,
            (row_slots - 1) * col_slots + rank,
            jnp.where(
                rank < border,
                (rank - col_slots) * col_slots + col_slots - 1,
                (inner // (col_slots - 1)) * col_slots + lax.rem(inner, col_slots - 1),
            ),
        )
        number = tally[b]
        quads = (number + QUAD - 1) // QUAD
        cursor[b] = quad * QUAD

        @pl.loop(0, quads)
        def _(i):
            plan_ref[layout.anchor + quad + i] = q

        @pl.loop(quad * QUAD + number, (quad + quads) * QUAD)
        def _(i):
            plan_ref[layout.block + i] = 0
            plan_ref[layout.slot + i] = -1

        return quad + quads

    ends = [border, anchors] if SPLIT == 1 else [anchors, anchors + border, 2 * anchors]
    quad = 0
    begin = 0
    plan_ref[0] = 0
    for part, end in enumerate(ends):
        quad = lax.fori_loop(begin, end, lay, quad)
        begin = end
        full = ((quad + step - 1) // step) * step
        pl.loop(quad, full)(dead)
        quad = full
        plan_ref[part + 1] = quad
    pl.loop(quad, quad + UNROLL)(dead)

    @pl.loop(0, live)
    def _(j):
        b = bucket_of(j)
        at = cursor[b]
        cursor[b] = at + 1
        plan_ref[layout.block + at] = j
        slot = slot_ref[j]
        plan_ref[layout.slot + at] = slot if SPLIT == 1 else lax.rem(slot, half_slots)

    for copy in copies:
        copy.wait()


def plan_blocks(block_pos, block_slot, block_count, half, vis_left, vis_right, half_slots):
    kernel_size = vis_right.shape[1]
    row_slots, col_slots = TILE_U // kernel_size, TILE_V // kernel_size
    layout = Layout(block_pos.shape[0], row_slots * col_slots)
    smem = pl.BlockSpec(memory_space=pltpu.SMEM)
    hbm = pl.BlockSpec(memory_space=pl.ANY)
    vmem = pl.BlockSpec(memory_space=pltpu.VMEM)
    return pl.pallas_call(
        functools.partial(
            plan_body, row_slots=row_slots, col_slots=col_slots, half_slots=half_slots
        ),
        in_specs=[smem] * 4 + [hbm] * 2,
        out_specs=[smem, vmem, vmem],
        out_shape=[
            jax.ShapeDtypeStruct((layout.total,), jnp.int32),
            pltpu.VMEM(vis_left.shape, vis_left.dtype),
            pltpu.VMEM(vis_right.shape, vis_right.dtype),
        ],
        scratch_shapes=[
            pltpu.SMEM((SPLIT * row_slots * col_slots,), jnp.int32),
            pltpu.SMEM((SPLIT * row_slots * col_slots,), jnp.int32),
            pltpu.SemaphoreType.DMA((2,)),
        ],
        compiler_params=pltpu.CompilerParams(vmem_limit_bytes=2**20),
        name="plan_blocks",
    )(block_pos, block_slot, block_count, half, in_hbm(vis_left), in_hbm(vis_right))


def strip(sums, row_slots, col_slots, kernel_size, plane, a, col):
    patch = sums.shape[1]
    lanes = slice(plane * patch, (plane + 1) * patch)
    total = None
    if a < row_slots:
        total = sums[a * col_slots + col, :kernel_size, lanes]
    if a > 0:
        above = sums[(a - 1) * col_slots + col, kernel_size:, lanes]
        total = above if total is None else total + above
    return total


def grid_body(
    plan_ref, kern_ref, left_ref, right_ref, *rest, part, first_part, halo, row_slots, col_slots
):
    if first_part:
        sums, *rest = rest
    else:
        before, sums, *rest = rest
    if halo:
        row_ref, col_ref, corner_ref, *rest = rest
    mixed = rest
    slots, kernel_size, _ = kern_ref.shape
    blocks, patch, _ = left_ref.shape
    anchors = sums.shape[0]
    layout = Layout(blocks, anchors)
    if first_part:

        @pl.loop(0, anchors)
        def _(q):
            sums[q] = jnp.zeros(sums.shape[1:], sums.dtype)

    zero = jnp.zeros((kernel_size, patch), jnp.bfloat16)

    def first(quad, ref, u):
        for e in range(QUAD):
            at = quad * QUAD + e
            slot = plan_ref[layout.slot + at]
            right = right_ref[plan_ref[layout.block + at]]
            kern = kern_ref[jnp.maximum(slot, 0)]
            kern = jnp.where(slot >= 0, kern, jnp.zeros_like(kern))
            spread = jnp.concatenate(
                [jnp.concatenate([right, zero], axis=1), jnp.concatenate([zero, right], axis=1)], axis=0
            )
            out = jnp.dot(kern, spread, preferred_element_type=jnp.float32).astype(jnp.bfloat16)
            top = slice(e * 2 * kernel_size, (e * 2 + 1) * kernel_size)
            low = slice((e * 2 + 1) * kernel_size, (e * 2 + 2) * kernel_size)
            ref[u, top, :] = out
            ref[u, low, :patch] = -out[:, patch:]
            ref[u, low, patch:] = out[:, :patch]

    def second(quad, ref, u):
        left = jnp.concatenate(
            [left_ref[plan_ref[layout.block + quad * QUAD + e]] for e in range(QUAD)], axis=1
        )
        sums[plan_ref[layout.anchor + quad]] += jnp.dot(left, ref[u], preferred_element_type=jnp.float32)

    begin = plan_ref[part]
    end = plan_ref[part + 1]
    for u in range(UNROLL):
        first(begin + u, mixed[0], u)

    @pl.loop(0, (end - begin) // (2 * UNROLL))
    def _(i):
        for h in range(2):
            quad = begin + (2 * i + h) * UNROLL
            for u in range(UNROLL):
                first(quad + UNROLL + u, mixed[1 - h], u)
                second(quad + u, mixed[h], u)

    if not halo:
        return
    low = lax.broadcasted_iota(jnp.int32, (kernel_size, patch), 1) < kernel_size
    take = functools.partial(strip, sums, row_slots, col_slots, kernel_size)
    for plane in range(2):
        behind = 0.0
        for tile in range(col_slots // 2):
            even = take(plane, row_slots, 2 * tile)
            odd = pltpu.roll(take(plane, row_slots, 2 * tile + 1), kernel_size, 1)
            row_ref[plane, :, tile * patch : (tile + 1) * patch] = (
                even + jnp.where(low, behind, odd)
            ).astype(row_ref.dtype)
            behind = odd
    for a in range(row_slots + 1):
        real = pltpu.roll(take(0, a, col_slots - 1), kernel_size, 1)
        imag = take(1, a, col_slots - 1)
        edge = jnp.where(low, real, imag)
        if a < row_slots:
            col_ref[a * kernel_size : (a + 1) * kernel_size, :] = edge.astype(col_ref.dtype)
        else:
            corner_ref[...] = edge.astype(corner_ref.dtype)


def grid_part(plan, part, kernels, left, right, sums, halo):
    kernel_size = kernels.shape[1]
    patch = left.shape[1]
    row_slots, col_slots = TILE_U // kernel_size, TILE_V // kernel_size
    smem = pl.BlockSpec(memory_space=pltpu.SMEM)
    vmem = pl.BlockSpec(memory_space=pltpu.VMEM)
    first_part = sums is None
    operands = [plan, in_vmem(kernels), in_vmem(left), in_vmem(right)]
    if not first_part:
        operands.append(in_vmem(sums))
    out_shape = [pltpu.VMEM((row_slots * col_slots, patch, 2 * patch), jnp.float32)]
    if halo:
        out_shape += [
            jax.ShapeDtypeStruct((2, kernel_size, TILE_V), jnp.bfloat16),
            jax.ShapeDtypeStruct((TILE_U, 2 * kernel_size), jnp.bfloat16),
            jax.ShapeDtypeStruct((kernel_size, 2 * kernel_size), jnp.bfloat16),
        ]
    return pl.pallas_call(
        functools.partial(
            grid_body, part=part, first_part=first_part, halo=halo, row_slots=row_slots, col_slots=col_slots
        ),
        in_specs=[smem] + [vmem] * (len(operands) - 1),
        out_specs=[vmem] * len(out_shape),
        out_shape=out_shape,
        input_output_aliases={} if first_part else {4: 0},
        scratch_shapes=[pltpu.VMEM((UNROLL, QUAD * 2 * kernel_size, 2 * patch), jnp.bfloat16)] * 2,
        compiler_params=pltpu.CompilerParams(vmem_limit_bytes=12 * 2**20),
        name="grid_part",
    )(*operands)


def merge_body(sums, row_ref, col_ref, corner_ref, out_ref):
    kernel_size = row_ref.shape[1]
    patch = sums.shape[1]
    row_slots = out_ref.shape[1] // kernel_size
    col_slots = out_ref.shape[2] // kernel_size
    low = lax.broadcasted_iota(jnp.int32, (kernel_size, patch), 1) < kernel_size
    take = functools.partial(strip, sums, row_slots, col_slots, kernel_size)
    for a in range(row_slots):
        rows = slice(a * kernel_size, (a + 1) * kernel_size)
        edge = col_ref[rows, :].astype(jnp.float32)
        if a == 0:
            edge = edge + corner_ref[...].astype(jnp.float32)
        for plane in range(2):
            behind = edge if plane == 0 else pltpu.roll(edge, kernel_size, 1)
            for tile in range(col_slots // 2):
                lanes = slice(tile * patch, (tile + 1) * patch)
                odd = pltpu.roll(take(plane, a, 2 * tile + 1), kernel_size, 1)
                value = take(plane, a, 2 * tile) + jnp.where(low, behind, odd)
                if a == 0:
                    value = value + row_ref[plane, :, lanes].astype(jnp.float32)
                out_ref[plane, rows, lanes] = value
                behind = odd


def merge_tile(sums, row, col, corner):
    vmem = pl.BlockSpec(memory_space=pltpu.VMEM)
    return pl.pallas_call(
        merge_body,
        in_specs=[vmem] * 4,
        out_specs=vmem,
        out_shape=jax.ShapeDtypeStruct((2, TILE_U, TILE_V), jnp.float32),
        compiler_params=pltpu.CompilerParams(vmem_limit_bytes=8 * 2**20),
        name="merge_tile",
    )(in_vmem(sums), row, col, corner)


def shards(
    aperture_amp,
    aperture_phase,
    plane_depths,
    send_list,
    send_count,
    vis_left,
    vis_right,
    block_slot,
    block_pos,
    block_count,
):
    kernel_size = vis_right.shape[1]
    tiles, capacity = send_list.shape[1:]
    both = ("tu", "tv")
    used = jnp.arange(capacity, dtype=jnp.int32)[:, None] < send_count
    chosen_list = jnp.where(used, send_list[0].T, -1)
    outgoing = make_kernels(aperture_amp, aperture_phase, plane_depths, chosen_list, kernel_size)
    outgoing = outgoing.reshape((tiles, capacity) + outgoing.shape[1:])
    arrived = lax.all_to_all(outgoing, both, split_axis=0, concat_axis=0, tiled=True)
    received = arrived.reshape((-1,) + arrived.shape[2:])
    half = jnp.zeros((1,), jnp.int32)
    plan, left, right = plan_blocks(
        block_pos, block_slot, block_count, half, vis_left, vis_right, tiles * capacity
    )
    sums, row, col, corner = grid_part(plan, 0, received, left, right, None, True)
    row = from_behind(row, "tu", 1)
    col = from_behind(col, "tv", 1)
    rows, cols = lax.axis_size("tu"), lax.axis_size("tv")
    diagonal = [
        (i * cols + j, (i + 1) * cols + j + 1) for i in range(rows - 1) for j in range(cols - 1)
    ]
    corner = lax.ppermute(corner, both, diagonal)
    (sums,) = grid_part(plan, 1, received, left, right, sums, False)
    return merge_tile(sums, row, col, corner)


def solution(mesh):
    placed = (
        P(("tu", "tv"), None, None),
        P(("tu", "tv"), None, None),
        P(),
        P(("tu", "tv"), None, None),
        P(("tu", "tv"), None),
        P(("tu", "tv"), None, None),
        P(("tu", "tv"), None, None),
        P(("tu", "tv")),
        P(("tu", "tv")),
        P(("tu", "tv")),
    )
    return jax.shard_map(
        shards, mesh=mesh, in_specs=placed, out_specs=P(None, "tu", "tv"), check_vma=False
    )
```

```python
import functools
import math

import jax
import jax.numpy as jnp
import numpy as np
from jax import lax
from jax.experimental import pallas as pl
from jax.experimental.pallas import tpu as pltpu
from jax.sharding import PartitionSpec as P

TILE_U = 256
TILE_V = 512
QUAD = 4
UNROLL = 4
STEP = 2 * UNROLL
RING = 4

def _fit(fn, degree):
    span = math.pi ** 2
    nodes = 0.5 * span * (1.0 - np.cos(np.pi * (np.arange(400) + 0.5) / 400))
    cheb = np.polynomial.chebyshev.Chebyshev.fit(nodes, fn(np.sqrt(nodes)), degree, domain=[0, span])
    return [float(c) for c in cheb.convert(kind=np.polynomial.Polynomial).coef]


COS_POLY = _fit(np.cos, 6)
SIN_POLY = _fit(lambda x: np.sin(x) / x, 5)


def horner(coefs, u):
    total = jnp.full_like(u, coefs[-1])
    for coef in coefs[-2::-1]:
        total = total * u + coef
    return total


def cos_sin(x):
    u = x * x
    return horner(COS_POLY, u), x * horner(SIN_POLY, u)


def from_behind(block, axis, distance):
    devices = range(lax.axis_size(axis))
    route = [(i - distance, i) for i in devices if i - distance in devices]
    return lax.ppermute(block, axis, route)


def in_hbm(array):
    return pltpu.with_memory_space_constraint(array, pltpu.HBM)


def in_vmem(array):
    return pltpu.with_memory_space_constraint(array, pltpu.VMEM)


def kernels_body(
    list_hbm, count_hbm, depth_hbm, amp_hbm, phase_hbm, out_ref,
    chosen_list, count, depth, amp, phase, table, screen, halves, made, small_sems, bulk_sems,
):
    screens, size, _ = amp.shape
    planes = depth.shape[0]
    kernel_size = out_ref.shape[1]
    small = [
        pltpu.make_async_copy(depth_hbm, depth, small_sems.at[0]),
        pltpu.make_async_copy(list_hbm, chosen_list, small_sems.at[1]),
        pltpu.make_async_copy(count_hbm, count, small_sems.at[2]),
    ]
    for copy in small:
        copy.start()

    def bulk(s):
        return [
            pltpu.make_async_copy(amp_hbm.at[s], amp.at[s], bulk_sems.at[0, s]),
            pltpu.make_async_copy(phase_hbm.at[s], phase.at[s], bulk_sems.at[1, s]),
        ]

    for s in range(screens):
        for copy in bulk(s):
            copy.start()

    frequency = lax.broadcasted_iota(jnp.int32, (kernel_size, size), 0) - kernel_size // 2
    cells = lax.broadcasted_iota(jnp.int32, (kernel_size, size), 1)
    turns = frequency.astype(jnp.float32) * cells.astype(jnp.float32) / size
    real_f, imag_f = cos_sin((2.0 * math.pi) * (turns - jnp.round(turns)))
    real_f = real_f.astype(jnp.bfloat16).astype(jnp.float32)
    imag_f = (-imag_f).astype(jnp.bfloat16).astype(jnp.float32)
    place = (lax.broadcasted_iota(jnp.int32, (1, size), 1).astype(jnp.float32) - size // 2) / size
    square = place * place
    for copy in small:
        copy.wait()
    for p in range(planes):
        turns = depth[p] * square
        real_e, imag_e = cos_sin((2.0 * math.pi) * (turns - jnp.round(turns)))
        real_g = (real_f * real_e - imag_f * imag_e).astype(jnp.bfloat16)
        imag_g = (real_f * imag_e + imag_f * real_e).astype(jnp.bfloat16)
        top = slice(p * 2 * kernel_size, (p * 2 + 1) * kernel_size)
        low = slice((p * 2 + 1) * kernel_size, (p * 2 + 2) * kernel_size)
        table[top, :size] = real_g
        table[top, size:] = -imag_g
        table[low, :size] = imag_g
        table[low, size:] = real_g

    width = 256

    @pl.loop(0, screens)
    def _(s):
        for copy in bulk(s):
            copy.wait()
        for start in range(0, size, width):
            cols = slice(start, start + width)
            magnitude = amp[s, :, cols].astype(jnp.float32)
            real_e, imag_e = cos_sin(phase[s, :, cols].astype(jnp.float32))
            screen[:size, cols] = (magnitude * real_e).astype(jnp.bfloat16)
            screen[size:, cols] = (magnitude * imag_e).astype(jnp.bfloat16)
            product = jnp.dot(table[...], screen[:, cols], preferred_element_type=jnp.float32)
            for p in range(planes):
                base = p * 2 * kernel_size
                halves[p, :, start : start + width] = product[base : base + kernel_size].astype(jnp.bfloat16)
                halves[p, :, size + start : size + start + width] = product[
                    base + kernel_size : base + 2 * kernel_size
                ].astype(jnp.bfloat16)
        for p in range(planes):
            second = lax.dot_general(
                halves[p],
                table[p * 2 * kernel_size : (p + 1) * 2 * kernel_size, :],
                (((1,), (1,)), ((), ())),
                preferred_element_type=jnp.float32,
            )
            made[s * planes + p] = (second * (1.0 / size)).astype(jnp.bfloat16)

    capacity, tiles = chosen_list.shape

    @pl.loop(0, tiles)
    def _(t):
        for c in range(capacity):
            chosen = made[chosen_list[c, t]]
            out_ref[t * capacity + c] = jnp.where(c < count[0, t], chosen, jnp.zeros_like(chosen))


def make_kernels(aperture_amp, aperture_phase, plane_depths, chosen_list, counts, kernel_size):
    screens, size, _ = aperture_amp.shape
    planes = plane_depths.shape[0]
    capacity, tiles = chosen_list.shape
    hbm = pl.BlockSpec(memory_space=pl.ANY)
    return pl.pallas_call(
        kernels_body,
        in_specs=[hbm] * 5,
        out_specs=pl.BlockSpec(memory_space=pltpu.VMEM),
        out_shape=jax.ShapeDtypeStruct((tiles * capacity, kernel_size, 2 * kernel_size), jnp.bfloat16),
        scratch_shapes=[
            pltpu.SMEM((capacity, tiles), jnp.int32),
            pltpu.SMEM((1, tiles), jnp.int32),
            pltpu.SMEM((planes,), jnp.float32),
            pltpu.VMEM((screens, size, size), jnp.bfloat16),
            pltpu.VMEM((screens, size, size), jnp.bfloat16),
            pltpu.VMEM((planes * 2 * kernel_size, 2 * size), jnp.bfloat16),
            pltpu.VMEM((2 * size, size), jnp.bfloat16),
            pltpu.VMEM((planes, kernel_size, 2 * size), jnp.bfloat16),
            pltpu.VMEM((screens * planes, kernel_size, 2 * kernel_size), jnp.bfloat16),
            pltpu.SemaphoreType.DMA((3,)),
            pltpu.SemaphoreType.DMA((2, screens)),
        ],
        compiler_params=pltpu.CompilerParams(vmem_limit_bytes=32 * 2**20),
        name="make_kernels",
    )(*map(in_hbm, (chosen_list, counts, plane_depths, aperture_amp, aperture_phase)))


class Layout:
    def __init__(self, blocks, anchors):
        self.parts = 2
        quads = (blocks + (QUAD - 1) * anchors) // QUAD + 1 + self.parts * (STEP - 1)
        self.quads = (quads + STEP - 1) // STEP * STEP
        self.anchor = self.parts + 1
        self.slot = self.anchor + self.quads
        self.total = self.slot + (self.quads + UNROLL) * QUAD


def plan_body(
    pos_ref, slot_ref, count_ref, left_hbm, right_hbm, plan_ref, left_ref, right_ref,
    tally, cursor, sems, *, layout, row_slots, col_slots,
):
    anchors = row_slots * col_slots
    border = row_slots + col_slots - 1
    live = count_ref[0]

    def copies(block, place):
        return [
            pltpu.make_async_copy(left_hbm.at[block], left_ref.at[place], sems.at[0]),
            pltpu.make_async_copy(right_hbm.at[block], right_ref.at[place], sems.at[1]),
        ]

    def put(block, place, slot):
        plan_ref[layout.slot + place] = slot
        for copy in copies(block, place):
            copy.start()

    @pl.loop(0, anchors)
    def _(q):
        tally[q] = 0

    @pl.loop(0, live)
    def _(j):
        q = pos_ref[j]
        tally[q] = tally[q] + 1

    def lay(rank, quad):
        inner = rank - border
        q = jnp.where(
            rank < col_slots,
            (row_slots - 1) * col_slots + rank,
            jnp.where(
                rank < border,
                (rank - col_slots) * col_slots + col_slots - 1,
                (inner // (col_slots - 1)) * col_slots + lax.rem(inner, col_slots - 1),
            ),
        )
        number = tally[q]
        quads = (number + QUAD - 1) // QUAD
        cursor[q] = quad * QUAD

        @pl.loop(0, quads)
        def _(i):
            plan_ref[layout.anchor + quad + i] = q

        @pl.loop(quad * QUAD + number, (quad + quads) * QUAD)
        def _(i):
            put(0, i, -1)

        return quad + quads

    quad = 0
    begin = 0
    plan_ref[0] = 0
    for part, end in enumerate([border, anchors]):
        quad = lax.fori_loop(begin, end, lay, quad)
        begin = end
        full = ((quad + STEP - 1) // STEP) * STEP

        @pl.loop(quad, full)
        def _(i):
            plan_ref[layout.anchor + i] = 0
            for e in range(QUAD):
                put(0, i * QUAD + e, -1)

        quad = full
        plan_ref[part + 1] = quad

    @pl.loop(quad * QUAD, (quad + UNROLL) * QUAD)
    def _(i):
        plan_ref[layout.slot + i] = -1

    @pl.loop(0, live)
    def _(j):
        q = pos_ref[j]
        at = cursor[q]
        cursor[q] = at + 1
        put(j, at, slot_ref[j])

    @pl.loop(0, quad * QUAD)
    def _(i):
        for copy in copies(0, 0):
            copy.wait()


def plan_blocks(block_pos, block_slot, block_count, vis_left, vis_right, layout):
    kernel_size = vis_right.shape[1]
    row_slots, col_slots = TILE_U // kernel_size, TILE_V // kernel_size
    smem = pl.BlockSpec(memory_space=pltpu.SMEM)
    hbm = pl.BlockSpec(memory_space=pl.ANY)
    places = layout.quads * QUAD
    return pl.pallas_call(
        functools.partial(plan_body, layout=layout, row_slots=row_slots, col_slots=col_slots),
        in_specs=[smem] * 3 + [hbm] * 2,
        out_specs=[smem, hbm, hbm],
        out_shape=[
            jax.ShapeDtypeStruct((layout.total,), jnp.int32),
            pltpu.HBM((places,) + vis_left.shape[1:], vis_left.dtype),
            pltpu.HBM((places,) + vis_right.shape[1:], vis_right.dtype),
        ],
        scratch_shapes=[
            pltpu.SMEM((row_slots * col_slots,), jnp.int32),
            pltpu.SMEM((row_slots * col_slots,), jnp.int32),
            pltpu.SemaphoreType.DMA((2,)),
        ],
        name="plan_blocks",
    )(block_pos, block_slot, block_count, in_hbm(vis_left), in_hbm(vis_right))


def strip(sums, row_slots, col_slots, kernel_size, plane, a, col):
    patch = sums.shape[1]
    lanes = slice(plane * patch, (plane + 1) * patch)
    total = None
    if a < row_slots:
        total = sums[a * col_slots + col, :kernel_size, lanes]
    if a > 0:
        above = sums[(a - 1) * col_slots + col, kernel_size:, lanes]
        total = above if total is None else total + above
    return total


def grid_body(
    plan_ref, kern_ref, left_hbm, right_hbm, *rest, part, first_part, halo, layout, row_slots, col_slots
):
    if first_part:
        sums, *rest = rest
    else:
        before, sums, *rest = rest
    if halo:
        row_ref, col_ref, corner_ref, *rest = rest
    left_ring, right_ring, sems, *mixed = rest
    slots, kernel_size, _ = kern_ref.shape
    patch = left_hbm.shape[1]
    chunk = STEP * QUAD
    base = plan_ref[part] // STEP
    number = plan_ref[part + 1] // STEP - base

    def fetch(i):
        source = pl.ds((base + i) * chunk, chunk)
        ring = lax.rem(i, RING)
        return [
            pltpu.make_async_copy(left_hbm.at[source], left_ring.at[ring], sems.at[0, ring]),
            pltpu.make_async_copy(right_hbm.at[source], right_ring.at[ring], sems.at[1, ring]),
        ]

    def start(i):
        @pl.when(i < number)
        def _():
            for copy in fetch(i):
                copy.start()

    def wait(i):
        @pl.when(i < number)
        def _():
            for copy in fetch(i):
                copy.wait()

    for i in range(RING):
        start(i)
    if first_part:

        @pl.loop(0, sums.shape[0])
        def _(q):
            sums[q] = jnp.zeros(sums.shape[1:], sums.dtype)

    zero = jnp.zeros((kernel_size, patch), jnp.bfloat16)

    def first(i, ring, at, ref, u):
        for e in range(QUAD):
            slot = plan_ref[layout.slot + ((base + i) * STEP + at) * QUAD + e]
            right = right_ring[ring, at * QUAD + e]
            kern = kern_ref[jnp.maximum(slot, 0)]
            kern = jnp.where(slot >= 0, kern, jnp.zeros_like(kern))
            spread = jnp.concatenate(
                [jnp.concatenate([right, zero], axis=1), jnp.concatenate([zero, right], axis=1)], axis=0
            )
            out = jnp.dot(kern, spread, preferred_element_type=jnp.float32).astype(jnp.bfloat16)
            top = slice(e * 2 * kernel_size, (e * 2 + 1) * kernel_size)
            low = slice((e * 2 + 1) * kernel_size, (e * 2 + 2) * kernel_size)
            ref[u, top, :] = out
            ref[u, low, :patch] = -out[:, patch:]
            ref[u, low, patch:] = out[:, :patch]

    def second(i, ring, at, ref, u):
        left = jnp.concatenate([left_ring[ring, at * QUAD + e] for e in range(QUAD)], axis=1)
        q = plan_ref[layout.anchor + (base + i) * STEP + at]
        sums[q] += jnp.dot(left, ref[u], preferred_element_type=jnp.float32)

    wait(0)
    for u in range(UNROLL):
        first(0, 0, u, mixed[0], u)

    @pl.loop(0, number)
    def _(i):
        here = lax.rem(i, RING)
        there = lax.rem(i + 1, RING)
        wait(i + 1)
        for u in range(UNROLL):
            first(i, here, UNROLL + u, mixed[1], u)
            second(i, here, u, mixed[0], u)
        for u in range(UNROLL):
            first(i + 1, there, u, mixed[0], u)
            second(i, here, UNROLL + u, mixed[1], u)
        start(i + RING)

    if not halo:
        return
    low = lax.broadcasted_iota(jnp.int32, (kernel_size, patch), 1) < kernel_size
    take = functools.partial(strip, sums, row_slots, col_slots, kernel_size)
    for plane in range(2):
        behind = 0.0
        for tile in range(col_slots // 2):
            even = take(plane, row_slots, 2 * tile)
            odd = pltpu.roll(take(plane, row_slots, 2 * tile + 1), kernel_size, 1)
            row_ref[plane, :, tile * patch : (tile + 1) * patch] = (
                even + jnp.where(low, behind, odd)
            ).astype(row_ref.dtype)
            behind = odd
    for a in range(row_slots + 1):
        real = pltpu.roll(take(0, a, col_slots - 1), kernel_size, 1)
        imag = take(1, a, col_slots - 1)
        edge = jnp.where(low, real, imag)
        if a < row_slots:
            col_ref[a * kernel_size : (a + 1) * kernel_size, :] = edge.astype(col_ref.dtype)
        else:
            corner_ref[...] = edge.astype(corner_ref.dtype)


def grid_part(plan, part, kernels, left, right, sums, halo, layout):
    kernel_size = kernels.shape[1]
    patch = left.shape[1]
    row_slots, col_slots = TILE_U // kernel_size, TILE_V // kernel_size
    smem = pl.BlockSpec(memory_space=pltpu.SMEM)
    vmem = pl.BlockSpec(memory_space=pltpu.VMEM)
    hbm = pl.BlockSpec(memory_space=pl.ANY)
    first_part = sums is None
    operands = [plan, in_vmem(kernels), in_hbm(left), in_hbm(right)]
    in_specs = [smem, vmem, hbm, hbm]
    if not first_part:
        operands.append(in_vmem(sums))
        in_specs.append(vmem)
    out_shape = [pltpu.VMEM((row_slots * col_slots, patch, 2 * patch), jnp.float32)]
    if halo:
        out_shape += [
            jax.ShapeDtypeStruct((2, kernel_size, TILE_V), jnp.bfloat16),
            jax.ShapeDtypeStruct((TILE_U, 2 * kernel_size), jnp.bfloat16),
            jax.ShapeDtypeStruct((kernel_size, 2 * kernel_size), jnp.bfloat16),
        ]
    return pl.pallas_call(
        functools.partial(
            grid_body,
            part=part,
            first_part=first_part,
            halo=halo,
            layout=layout,
            row_slots=row_slots,
            col_slots=col_slots,
        ),
        in_specs=in_specs,
        out_specs=[vmem] * len(out_shape),
        out_shape=out_shape,
        input_output_aliases={} if first_part else {4: 0},
        scratch_shapes=[
            pltpu.VMEM((RING, STEP * QUAD) + left.shape[1:], left.dtype),
            pltpu.VMEM((RING, STEP * QUAD) + right.shape[1:], right.dtype),
            pltpu.SemaphoreType.DMA((2, RING)),
        ]
        + [pltpu.VMEM((UNROLL, QUAD * 2 * kernel_size, 2 * patch), jnp.bfloat16)] * 2,
        compiler_params=pltpu.CompilerParams(vmem_limit_bytes=24 * 2**20),
        name="grid_part",
    )(*operands)


def merge_body(sums, row_ref, col_ref, corner_ref, out_ref):
    kernel_size = row_ref.shape[1]
    patch = sums.shape[1]
    row_slots = out_ref.shape[1] // kernel_size
    col_slots = out_ref.shape[2] // kernel_size
    low = lax.broadcasted_iota(jnp.int32, (kernel_size, patch), 1) < kernel_size
    take = functools.partial(strip, sums, row_slots, col_slots, kernel_size)
    for a in range(row_slots):
        rows = slice(a * kernel_size, (a + 1) * kernel_size)
        edge = col_ref[rows, :].astype(jnp.float32)
        if a == 0:
            edge = edge + corner_ref[...].astype(jnp.float32)
        for plane in range(2):
            behind = edge if plane == 0 else pltpu.roll(edge, kernel_size, 1)
            for tile in range(col_slots // 2):
                lanes = slice(tile * patch, (tile + 1) * patch)
                odd = pltpu.roll(take(plane, a, 2 * tile + 1), kernel_size, 1)
                value = take(plane, a, 2 * tile) + jnp.where(low, behind, odd)
                if a == 0:
                    value = value + row_ref[plane, :, lanes].astype(jnp.float32)
                out_ref[plane, rows, lanes] = value
                behind = odd


def merge_tile(sums, row, col, corner):
    vmem = pl.BlockSpec(memory_space=pltpu.VMEM)
    return pl.pallas_call(
        merge_body,
        in_specs=[vmem] * 4,
        out_specs=vmem,
        out_shape=jax.ShapeDtypeStruct((2, TILE_U, TILE_V), jnp.float32),
        compiler_params=pltpu.CompilerParams(vmem_limit_bytes=8 * 2**20),
        name="merge_tile",
    )(in_vmem(sums), row, col, corner)


def shards(
    aperture_amp,
    aperture_phase,
    plane_depths,
    send_list,
    send_count,
    vis_left,
    vis_right,
    block_slot,
    block_pos,
    block_count,
):
    kernel_size = vis_right.shape[1]
    tiles, capacity = send_list.shape[1:]
    both = ("tu", "tv")
    outgoing = make_kernels(
        aperture_amp, aperture_phase, plane_depths, send_list[0].T, send_count, kernel_size
    )
    outgoing = outgoing.reshape((tiles, capacity) + outgoing.shape[1:])
    arrived = lax.all_to_all(outgoing, both, split_axis=0, concat_axis=0, tiled=True)
    received = arrived.reshape((-1,) + arrived.shape[2:])
    layout = Layout(block_pos.shape[0], (TILE_U // kernel_size) * (TILE_V // kernel_size))
    plan, left, right = plan_blocks(block_pos, block_slot, block_count, vis_left, vis_right, layout)
    sums, row, col, corner = grid_part(plan, 0, received, left, right, None, True, layout)
    row = from_behind(row, "tu", 1)
    col = from_behind(col, "tv", 1)
    rows, cols = lax.axis_size("tu"), lax.axis_size("tv")
    diagonal = [
        (i * cols + j, (i + 1) * cols + j + 1) for i in range(rows - 1) for j in range(cols - 1)
    ]
    corner = lax.ppermute(corner, both, diagonal)
    (sums,) = grid_part(plan, 1, received, left, right, sums, False, layout)
    return merge_tile(sums, row, col, corner)


def solution(mesh):
    placed = (
        P(("tu", "tv"), None, None),
        P(("tu", "tv"), None, None),
        P(),
        P(("tu", "tv"), None, None),
        P(("tu", "tv"), None),
        P(("tu", "tv"), None, None),
        P(("tu", "tv"), None, None),
        P(("tu", "tv")),
        P(("tu", "tv")),
        P(("tu", "tv")),
    )
    return jax.shard_map(
        shards, mesh=mesh, in_specs=placed, out_specs=P(None, "tu", "tv"), check_vma=False
    )
```

```python
import functools
import math

import jax
import jax.numpy as jnp
import numpy as np
from jax import lax
from jax.experimental import pallas as pl
from jax.experimental.pallas import tpu as pltpu
from jax.sharding import PartitionSpec as P

TILE_U = 256
TILE_V = 512
QUAD = 4
UNROLL = 4
STEP = 2 * UNROLL
RING = 3

def _fit(fn, degree):
    span = math.pi ** 2
    nodes = 0.5 * span * (1.0 - np.cos(np.pi * (np.arange(400) + 0.5) / 400))
    cheb = np.polynomial.chebyshev.Chebyshev.fit(nodes, fn(np.sqrt(nodes)), degree, domain=[0, span])
    return [float(c) for c in cheb.convert(kind=np.polynomial.Polynomial).coef]


COS_POLY = _fit(np.cos, 6)
SIN_POLY = _fit(lambda x: np.sin(x) / x, 5)


def horner(coefs, u):
    total = jnp.full_like(u, coefs[-1])
    for coef in coefs[-2::-1]:
        total = total * u + coef
    return total


def cos_sin(x):
    u = x * x
    return horner(COS_POLY, u), x * horner(SIN_POLY, u)


def from_behind(block, axis, distance):
    devices = range(lax.axis_size(axis))
    route = [(i - distance, i) for i in devices if i - distance in devices]
    return lax.ppermute(block, axis, route)


def in_hbm(array):
    return pltpu.with_memory_space_constraint(array, pltpu.HBM)


def in_vmem(array):
    return pltpu.with_memory_space_constraint(array, pltpu.VMEM)


def kernels_body(
    list_hbm, count_hbm, depth_hbm, amp_hbm, phase_hbm, out_ref,
    chosen_list, count, depth, amp, phase, table, screen, halves, made, small_sems, bulk_sems,
):
    screens, size, _ = amp.shape
    planes = depth.shape[0]
    kernel_size = out_ref.shape[1]
    small = [
        pltpu.make_async_copy(depth_hbm, depth, small_sems.at[0]),
        pltpu.make_async_copy(list_hbm, chosen_list, small_sems.at[1]),
        pltpu.make_async_copy(count_hbm, count, small_sems.at[2]),
    ]
    for copy in small:
        copy.start()

    def bulk(s):
        return [
            pltpu.make_async_copy(amp_hbm.at[s], amp.at[s], bulk_sems.at[0, s]),
            pltpu.make_async_copy(phase_hbm.at[s], phase.at[s], bulk_sems.at[1, s]),
        ]

    for s in range(screens):
        for copy in bulk(s):
            copy.start()

    frequency = lax.broadcasted_iota(jnp.int32, (kernel_size, size), 0) - kernel_size // 2
    cells = lax.broadcasted_iota(jnp.int32, (kernel_size, size), 1)
    turns = frequency.astype(jnp.float32) * cells.astype(jnp.float32) / size
    real_f, imag_f = cos_sin((2.0 * math.pi) * (turns - jnp.round(turns)))
    real_f = real_f.astype(jnp.bfloat16).astype(jnp.float32)
    imag_f = (-imag_f).astype(jnp.bfloat16).astype(jnp.float32)
    place = (lax.broadcasted_iota(jnp.int32, (1, size), 1).astype(jnp.float32) - size // 2) / size
    square = place * place
    for copy in small:
        copy.wait()
    for p in range(planes):
        turns = depth[p] * square
        real_e, imag_e = cos_sin((2.0 * math.pi) * (turns - jnp.round(turns)))
        real_g = (real_f * real_e - imag_f * imag_e).astype(jnp.bfloat16)
        imag_g = (real_f * imag_e + imag_f * real_e).astype(jnp.bfloat16)
        top = slice(p * 2 * kernel_size, (p * 2 + 1) * kernel_size)
        low = slice((p * 2 + 1) * kernel_size, (p * 2 + 2) * kernel_size)
        table[top, :size] = real_g
        table[top, size:] = -imag_g
        table[low, :size] = imag_g
        table[low, size:] = real_g

    width = 256

    @pl.loop(0, screens)
    def _(s):
        for copy in bulk(s):
            copy.wait()
        for start in range(0, size, width):
            cols = slice(start, start + width)
            magnitude = amp[s, :, cols].astype(jnp.float32)
            real_e, imag_e = cos_sin(phase[s, :, cols].astype(jnp.float32))
            screen[:size, cols] = (magnitude * real_e).astype(jnp.bfloat16)
            screen[size:, cols] = (magnitude * imag_e).astype(jnp.bfloat16)
            product = jnp.dot(table[...], screen[:, cols], preferred_element_type=jnp.float32)
            for p in range(planes):
                base = p * 2 * kernel_size
                halves[p, :, start : start + width] = product[base : base + kernel_size].astype(jnp.bfloat16)
                halves[p, :, size + start : size + start + width] = product[
                    base + kernel_size : base + 2 * kernel_size
                ].astype(jnp.bfloat16)
        for p in range(planes):
            second = lax.dot_general(
                halves[p],
                table[p * 2 * kernel_size : (p + 1) * 2 * kernel_size, :],
                (((1,), (1,)), ((), ())),
                preferred_element_type=jnp.float32,
            )
            made[s * planes + p] = (second * (1.0 / size)).astype(jnp.bfloat16)

    capacity, tiles = chosen_list.shape

    @pl.loop(0, tiles)
    def _(t):
        for c in range(capacity):
            chosen = made[chosen_list[c, t]]
            out_ref[t * capacity + c] = jnp.where(c < count[0, t], chosen, jnp.zeros_like(chosen))


def make_kernels(aperture_amp, aperture_phase, plane_depths, chosen_list, counts, kernel_size):
    screens, size, _ = aperture_amp.shape
    planes = plane_depths.shape[0]
    capacity, tiles = chosen_list.shape
    hbm = pl.BlockSpec(memory_space=pl.ANY)
    return pl.pallas_call(
        kernels_body,
        in_specs=[hbm] * 5,
        out_specs=pl.BlockSpec(memory_space=pltpu.VMEM),
        out_shape=jax.ShapeDtypeStruct((tiles * capacity, kernel_size, 2 * kernel_size), jnp.bfloat16),
        scratch_shapes=[
            pltpu.SMEM((capacity, tiles), jnp.int32),
            pltpu.SMEM((1, tiles), jnp.int32),
            pltpu.SMEM((planes,), jnp.float32),
            pltpu.VMEM((screens, size, size), jnp.bfloat16),
            pltpu.VMEM((screens, size, size), jnp.bfloat16),
            pltpu.VMEM((planes * 2 * kernel_size, 2 * size), jnp.bfloat16),
            pltpu.VMEM((2 * size, size), jnp.bfloat16),
            pltpu.VMEM((planes, kernel_size, 2 * size), jnp.bfloat16),
            pltpu.VMEM((screens * planes, kernel_size, 2 * kernel_size), jnp.bfloat16),
            pltpu.SemaphoreType.DMA((3,)),
            pltpu.SemaphoreType.DMA((2, screens)),
        ],
        compiler_params=pltpu.CompilerParams(vmem_limit_bytes=32 * 2**20),
        name="make_kernels",
    )(*map(in_hbm, (chosen_list, counts, plane_depths, aperture_amp, aperture_phase)))


class Layout:
    def __init__(self, blocks, anchors):
        self.parts = 2
        quads = (blocks + (QUAD - 1) * anchors) // QUAD + 1 + self.parts * (STEP - 1)
        self.quads = (quads + STEP - 1) // STEP * STEP
        self.anchor = self.parts + 1
        self.slot = self.anchor + self.quads
        self.total = self.slot + (self.quads + UNROLL) * QUAD


def plan_body(
    pos_ref, slot_ref, count_ref, left_hbm, right_hbm, plan_ref, left_out, right_out,
    left_ref, right_ref, tally, cursor, sems, *, layout, row_slots, col_slots,
):
    anchors = row_slots * col_slots
    border = row_slots + col_slots - 1
    live = count_ref[0]

    def copies(block, place):
        return [
            pltpu.make_async_copy(left_hbm.at[block], left_ref.at[place], sems.at[0]),
            pltpu.make_async_copy(right_hbm.at[block], right_ref.at[place], sems.at[1]),
        ]

    def put(block, place, slot):
        plan_ref[layout.slot + place] = slot
        for copy in copies(block, place):
            copy.start()

    @pl.loop(0, anchors)
    def _(q):
        tally[q] = 0

    @pl.loop(0, live)
    def _(j):
        q = pos_ref[j]
        tally[q] = tally[q] + 1

    def lay(rank, quad):
        inner = rank - border
        q = jnp.where(
            rank < col_slots,
            (row_slots - 1) * col_slots + rank,
            jnp.where(
                rank < border,
                (rank - col_slots) * col_slots + col_slots - 1,
                (inner // (col_slots - 1)) * col_slots + lax.rem(inner, col_slots - 1),
            ),
        )
        number = tally[q]
        quads = (number + QUAD - 1) // QUAD
        cursor[q] = quad * QUAD

        @pl.loop(0, quads)
        def _(i):
            plan_ref[layout.anchor + quad + i] = q

        @pl.loop(quad * QUAD + number, (quad + quads) * QUAD)
        def _(i):
            put(0, i, -1)

        return quad + quads

    quad = 0
    begin = 0
    plan_ref[0] = 0
    for part, end in enumerate([border, anchors]):
        quad = lax.fori_loop(begin, end, lay, quad)
        begin = end
        full = ((quad + STEP - 1) // STEP) * STEP

        @pl.loop(quad, full)
        def _(i):
            plan_ref[layout.anchor + i] = 0
            for e in range(QUAD):
                put(0, i * QUAD + e, -1)

        quad = full
        plan_ref[part + 1] = quad

    @pl.loop(quad * QUAD, (quad + UNROLL) * QUAD)
    def _(i):
        plan_ref[layout.slot + i] = -1

    @pl.loop(0, live)
    def _(j):
        q = pos_ref[j]
        at = cursor[q]
        cursor[q] = at + 1
        put(j, at, slot_ref[j])

    @pl.loop(0, quad * QUAD)
    def _(i):
        for copy in copies(0, 0):
            copy.wait()

    chunk = STEP * QUAD

    def writes(i):
        rows = pl.ds(i * chunk, chunk)
        return [
            pltpu.make_async_copy(left_ref.at[rows], left_out.at[rows], sems.at[2]),
            pltpu.make_async_copy(right_ref.at[rows], right_out.at[rows], sems.at[3]),
        ]

    @pl.loop(0, quad // STEP)
    def _(i):
        for copy in writes(i):
            copy.start()

    @pl.loop(0, quad // STEP)
    def _(i):
        for copy in writes(i):
            copy.wait()


def plan_blocks(block_pos, block_slot, block_count, vis_left, vis_right, layout):
    kernel_size = vis_right.shape[1]
    row_slots, col_slots = TILE_U // kernel_size, TILE_V // kernel_size
    smem = pl.BlockSpec(memory_space=pltpu.SMEM)
    hbm = pl.BlockSpec(memory_space=pl.ANY)
    places = layout.quads * QUAD
    return pl.pallas_call(
        functools.partial(plan_body, layout=layout, row_slots=row_slots, col_slots=col_slots),
        in_specs=[smem] * 3 + [hbm] * 2,
        out_specs=[smem, hbm, hbm],
        out_shape=[
            jax.ShapeDtypeStruct((layout.total,), jnp.int32),
            pltpu.HBM((places,) + vis_left.shape[1:], vis_left.dtype),
            pltpu.HBM((places,) + vis_right.shape[1:], vis_right.dtype),
        ],
        scratch_shapes=[
            pltpu.VMEM((places,) + vis_left.shape[1:], vis_left.dtype),
            pltpu.VMEM((places,) + vis_right.shape[1:], vis_right.dtype),
            pltpu.SMEM((row_slots * col_slots,), jnp.int32),
            pltpu.SMEM((row_slots * col_slots,), jnp.int32),
            pltpu.SemaphoreType.DMA((4,)),
        ],
        compiler_params=pltpu.CompilerParams(vmem_limit_bytes=36 * 2**20),
        name="plan_blocks",
    )(block_pos, block_slot, block_count, in_hbm(vis_left), in_hbm(vis_right))


def strip(sums, row_slots, col_slots, kernel_size, plane, a, col):
    patch = sums.shape[1]
    lanes = slice(plane * patch, (plane + 1) * patch)
    total = None
    if a < row_slots:
        total = sums[a * col_slots + col, :kernel_size, lanes]
    if a > 0:
        above = sums[(a - 1) * col_slots + col, kernel_size:, lanes]
        total = above if total is None else total + above
    return total


def grid_body(
    plan_ref, kern_ref, left_hbm, right_hbm, *rest, part, first_part, halo, layout, row_slots, col_slots
):
    if not first_part:
        rest = rest[4:]
    sums, left_ring, right_ring, ahead, *rest = rest
    if halo:
        row_ref, col_ref, corner_ref, *rest = rest
    behind_ref, sems = rest
    mixed = (ahead, behind_ref)
    slots, kernel_size, _ = kern_ref.shape
    patch = left_hbm.shape[1]
    chunk = STEP * QUAD
    begin = plan_ref[part] // STEP
    end = plan_ref[part + 1] // STEP
    total = plan_ref[layout.parts] // STEP

    def fetch(i):
        source = pl.ds(i * chunk, chunk)
        ring = lax.rem(i, RING)
        return [
            pltpu.make_async_copy(left_hbm.at[source], left_ring.at[ring], sems.at[0, ring]),
            pltpu.make_async_copy(right_hbm.at[source], right_ring.at[ring], sems.at[1, ring]),
        ]

    def start(i):
        @pl.when(i < total)
        def _():
            for copy in fetch(i):
                copy.start()

    def wait(i):
        @pl.when(i < total)
        def _():
            for copy in fetch(i):
                copy.wait()

    if first_part:
        start(0)

        @pl.loop(0, sums.shape[0])
        def _(q):
            sums[q] = jnp.zeros(sums.shape[1:], sums.dtype)

    zero = jnp.zeros((kernel_size, patch), jnp.bfloat16)

    def first(i, ring, at, ref, u):
        for e in range(QUAD):
            slot = plan_ref[layout.slot + (i * STEP + at) * QUAD + e]
            right = right_ring[ring, at * QUAD + e]
            kern = kern_ref[jnp.maximum(slot, 0)]
            kern = jnp.where(slot >= 0, kern, jnp.zeros_like(kern))
            spread = jnp.concatenate(
                [jnp.concatenate([right, zero], axis=1), jnp.concatenate([zero, right], axis=1)], axis=0
            )
            out = jnp.dot(kern, spread, preferred_element_type=jnp.float32).astype(jnp.bfloat16)
            top = slice(e * 2 * kernel_size, (e * 2 + 1) * kernel_size)
            low = slice((e * 2 + 1) * kernel_size, (e * 2 + 2) * kernel_size)
            ref[u, top, :] = out
            ref[u, low, :patch] = -out[:, patch:]
            ref[u, low, patch:] = out[:, :patch]

    def second(i, ring, at, ref, u):
        left = jnp.concatenate([left_ring[ring, at * QUAD + e] for e in range(QUAD)], axis=1)
        q = plan_ref[layout.anchor + i * STEP + at]
        sums[q] += jnp.dot(left, ref[u], preferred_element_type=jnp.float32)

    if first_part:
        wait(0)
        start(1)
        for u in range(UNROLL):
            first(0, 0, u, mixed[0], u)

    @pl.loop(begin, end)
    def _(i):
        here = lax.rem(i, RING)
        there = lax.rem(i + 1, RING)
        start(i + 2)
        if first_part:
            wait(i + 1)
        else:
            pl.when(i > begin)(lambda: wait(i + 1))
        for u in range(UNROLL):
            first(i, here, UNROLL + u, mixed[1], u)
            second(i, here, u, mixed[0], u)
        for u in range(UNROLL):
            first(i + 1, there, u, mixed[0], u)
            second(i, here, UNROLL + u, mixed[1], u)

    if first_part:
        wait(end + 1)
    if not halo:
        return
    low = lax.broadcasted_iota(jnp.int32, (kernel_size, patch), 1) < kernel_size
    take = functools.partial(strip, sums, row_slots, col_slots, kernel_size)
    for plane in range(2):
        behind = 0.0
        for tile in range(col_slots // 2):
            even = take(plane, row_slots, 2 * tile)
            odd = pltpu.roll(take(plane, row_slots, 2 * tile + 1), kernel_size, 1)
            row_ref[plane, :, tile * patch : (tile + 1) * patch] = (
                even + jnp.where(low, behind, odd)
            ).astype(row_ref.dtype)
            behind = odd
    for a in range(row_slots + 1):
        real = pltpu.roll(take(0, a, col_slots - 1), kernel_size, 1)
        imag = take(1, a, col_slots - 1)
        edge = jnp.where(low, real, imag)
        if a < row_slots:
            col_ref[a * kernel_size : (a + 1) * kernel_size, :] = edge.astype(col_ref.dtype)
        else:
            corner_ref[...] = edge.astype(corner_ref.dtype)


def grid_part(plan, part, kernels, left, right, carried, halo, layout):
    kernel_size = kernels.shape[1]
    patch = left.shape[1]
    row_slots, col_slots = TILE_U // kernel_size, TILE_V // kernel_size
    smem = pl.BlockSpec(memory_space=pltpu.SMEM)
    vmem = pl.BlockSpec(memory_space=pltpu.VMEM)
    hbm = pl.BlockSpec(memory_space=pl.ANY)
    first_part = carried is None
    carried = [] if first_part else [in_vmem(array) for array in carried]
    mixed_shape = (UNROLL, QUAD * 2 * kernel_size, 2 * patch)
    out_shape = [
        pltpu.VMEM((row_slots * col_slots, patch, 2 * patch), jnp.float32),
        pltpu.VMEM((RING, STEP * QUAD) + left.shape[1:], left.dtype),
        pltpu.VMEM((RING, STEP * QUAD) + right.shape[1:], right.dtype),
        pltpu.VMEM(mixed_shape, jnp.bfloat16),
    ]
    if halo:
        out_shape += [
            jax.ShapeDtypeStruct((2, kernel_size, TILE_V), jnp.bfloat16),
            jax.ShapeDtypeStruct((TILE_U, 2 * kernel_size), jnp.bfloat16),
            jax.ShapeDtypeStruct((kernel_size, 2 * kernel_size), jnp.bfloat16),
        ]
    out = pl.pallas_call(
        functools.partial(
            grid_body,
            part=part,
            first_part=first_part,
            halo=halo,
            layout=layout,
            row_slots=row_slots,
            col_slots=col_slots,
        ),
        in_specs=[smem, vmem, hbm, hbm] + [vmem] * len(carried),
        out_specs=[vmem] * len(out_shape),
        out_shape=out_shape,
        input_output_aliases={4 + i: i for i in range(len(carried))},
        scratch_shapes=[
            pltpu.VMEM(mixed_shape, jnp.bfloat16),
            pltpu.SemaphoreType.DMA((2, RING)),
        ],
        compiler_params=pltpu.CompilerParams(vmem_limit_bytes=12 * 2**20),
        name="grid_part",
    )(plan, in_vmem(kernels), in_hbm(left), in_hbm(right), *carried)
    return out[:4], out[4:]


def merge_body(sums, row_ref, col_ref, corner_ref, out_ref):
    kernel_size = row_ref.shape[1]
    patch = sums.shape[1]
    row_slots = out_ref.shape[1] // kernel_size
    col_slots = out_ref.shape[2] // kernel_size
    low = lax.broadcasted_iota(jnp.int32, (kernel_size, patch), 1) < kernel_size
    take = functools.partial(strip, sums, row_slots, col_slots, kernel_size)
    for a in range(row_slots):
        rows = slice(a * kernel_size, (a + 1) * kernel_size)
        edge = col_ref[rows, :].astype(jnp.float32)
        if a == 0:
            edge = edge + corner_ref[...].astype(jnp.float32)
        for plane in range(2):
            behind = edge if plane == 0 else pltpu.roll(edge, kernel_size, 1)
            for tile in range(col_slots // 2):
                lanes = slice(tile * patch, (tile + 1) * patch)
                odd = pltpu.roll(take(plane, a, 2 * tile + 1), kernel_size, 1)
                value = take(plane, a, 2 * tile) + jnp.where(low, behind, odd)
                if a == 0:
                    value = value + row_ref[plane, :, lanes].astype(jnp.float32)
                out_ref[plane, rows, lanes] = value
                behind = odd


def merge_tile(sums, row, col, corner):
    vmem = pl.BlockSpec(memory_space=pltpu.VMEM)
    return pl.pallas_call(
        merge_body,
        in_specs=[vmem] * 4,
        out_specs=vmem,
        out_shape=jax.ShapeDtypeStruct((2, TILE_U, TILE_V), jnp.float32),
        compiler_params=pltpu.CompilerParams(vmem_limit_bytes=8 * 2**20),
        name="merge_tile",
    )(in_vmem(sums), row, col, corner)


def shards(
    aperture_amp,
    aperture_phase,
    plane_depths,
    send_list,
    send_count,
    vis_left,
    vis_right,
    block_slot,
    block_pos,
    block_count,
):
    kernel_size = vis_right.shape[1]
    tiles, capacity = send_list.shape[1:]
    both = ("tu", "tv")
    outgoing = make_kernels(
        aperture_amp, aperture_phase, plane_depths, send_list[0].T, send_count, kernel_size
    )
    outgoing = outgoing.reshape((tiles, capacity) + outgoing.shape[1:])
    arrived = lax.all_to_all(outgoing, both, split_axis=0, concat_axis=0, tiled=True)
    received = arrived.reshape((-1,) + arrived.shape[2:])
    layout = Layout(block_pos.shape[0], (TILE_U // kernel_size) * (TILE_V // kernel_size))
    plan, left, right = plan_blocks(block_pos, block_slot, block_count, vis_left, vis_right, layout)
    carried, (row, col, corner) = grid_part(plan, 0, received, left, right, None, True, layout)
    row = from_behind(row, "tu", 1)
    col = from_behind(col, "tv", 1)
    rows, cols = lax.axis_size("tu"), lax.axis_size("tv")
    diagonal = [
        (i * cols + j, (i + 1) * cols + j + 1) for i in range(rows - 1) for j in range(cols - 1)
    ]
    corner = lax.ppermute(corner, both, diagonal)
    carried, _ = grid_part(plan, 1, received, left, right, carried, False, layout)
    return merge_tile(carried[0], row, col, corner)


def solution(mesh):
    placed = (
        P(("tu", "tv"), None, None),
        P(("tu", "tv"), None, None),
        P(),
        P(("tu", "tv"), None, None),
        P(("tu", "tv"), None),
        P(("tu", "tv"), None, None),
        P(("tu", "tv"), None, None),
        P(("tu", "tv")),
        P(("tu", "tv")),
        P(("tu", "tv")),
    )
    return jax.shard_map(
        shards, mesh=mesh, in_specs=placed, out_specs=P(None, "tu", "tv"), check_vma=False
    )
```

```python
import functools
import math

import jax
import jax.numpy as jnp
import numpy as np
from jax import lax
from jax.experimental import pallas as pl
from jax.experimental.pallas import tpu as pltpu
from jax.sharding import PartitionSpec as P

TILE_U = 256
TILE_V = 512
QUAD = 4
UNROLL = 4
STEP = 2 * UNROLL
RING = 4

def _fit(fn, degree):
    span = math.pi ** 2
    nodes = 0.5 * span * (1.0 - np.cos(np.pi * (np.arange(400) + 0.5) / 400))
    cheb = np.polynomial.chebyshev.Chebyshev.fit(nodes, fn(np.sqrt(nodes)), degree, domain=[0, span])
    return [float(c) for c in cheb.convert(kind=np.polynomial.Polynomial).coef]


COS_POLY = _fit(np.cos, 6)
SIN_POLY = _fit(lambda x: np.sin(x) / x, 5)


def horner(coefs, u):
    total = jnp.full_like(u, coefs[-1])
    for coef in coefs[-2::-1]:
        total = total * u + coef
    return total


def cos_sin(x):
    u = x * x
    return horner(COS_POLY, u), x * horner(SIN_POLY, u)


def from_behind(block, axis, distance):
    devices = range(lax.axis_size(axis))
    route = [(i - distance, i) for i in devices if i - distance in devices]
    return lax.ppermute(block, axis, route)


def in_hbm(array):
    return pltpu.with_memory_space_constraint(array, pltpu.HBM)


def in_vmem(array):
    return pltpu.with_memory_space_constraint(array, pltpu.VMEM)


def kernels_body(
    list_hbm, count_hbm, depth_hbm, amp_hbm, phase_hbm, out_ref,
    chosen_list, count, depth, amp, phase, table, screen, halves, made, small_sems, bulk_sems,
):
    screens, size, _ = amp.shape
    planes = depth.shape[0]
    kernel_size = out_ref.shape[1]
    small = [
        pltpu.make_async_copy(depth_hbm, depth, small_sems.at[0]),
        pltpu.make_async_copy(list_hbm, chosen_list, small_sems.at[1]),
        pltpu.make_async_copy(count_hbm, count, small_sems.at[2]),
    ]
    for copy in small:
        copy.start()

    def bulk(s):
        return [
            pltpu.make_async_copy(amp_hbm.at[s], amp.at[s], bulk_sems.at[0, s]),
            pltpu.make_async_copy(phase_hbm.at[s], phase.at[s], bulk_sems.at[1, s]),
        ]

    for s in range(screens):
        for copy in bulk(s):
            copy.start()

    frequency = lax.broadcasted_iota(jnp.int32, (kernel_size, size), 0) - kernel_size // 2
    cells = lax.broadcasted_iota(jnp.int32, (kernel_size, size), 1)
    turns = frequency.astype(jnp.float32) * cells.astype(jnp.float32) / size
    real_f, imag_f = cos_sin((2.0 * math.pi) * (turns - jnp.round(turns)))
    real_f = real_f.astype(jnp.bfloat16).astype(jnp.float32)
    imag_f = (-imag_f).astype(jnp.bfloat16).astype(jnp.float32)
    place = (lax.broadcasted_iota(jnp.int32, (1, size), 1).astype(jnp.float32) - size // 2) / size
    square = place * place
    for copy in small:
        copy.wait()
    for p in range(planes):
        turns = depth[p] * square
        real_e, imag_e = cos_sin((2.0 * math.pi) * (turns - jnp.round(turns)))
        real_g = (real_f * real_e - imag_f * imag_e).astype(jnp.bfloat16)
        imag_g = (real_f * imag_e + imag_f * real_e).astype(jnp.bfloat16)
        top = slice(p * 2 * kernel_size, (p * 2 + 1) * kernel_size)
        low = slice((p * 2 + 1) * kernel_size, (p * 2 + 2) * kernel_size)
        table[top, :size] = real_g
        table[top, size:] = -imag_g
        table[low, :size] = imag_g
        table[low, size:] = real_g

    @pl.loop(0, screens)
    def _(s):
        for copy in bulk(s):
            copy.wait()
        magnitude = amp[s].astype(jnp.float32)
        real_e, imag_e = cos_sin(phase[s].astype(jnp.float32))
        screen[:size, :] = (magnitude * real_e).astype(jnp.bfloat16)
        screen[size:, :] = (magnitude * imag_e).astype(jnp.bfloat16)
        product = jnp.dot(table[...], screen[...], preferred_element_type=jnp.float32).astype(jnp.bfloat16)
        for p in range(planes):
            base = p * 2 * kernel_size
            halves[s, p, :, :size] = product[base : base + kernel_size]
            halves[s, p, :, size:] = product[base + kernel_size : base + 2 * kernel_size]

    for p in range(planes):
        second = lax.dot_general(
            jnp.concatenate([halves[s, p] for s in range(screens)], axis=0),
            table[p * 2 * kernel_size : (p + 1) * 2 * kernel_size, :],
            (((1,), (1,)), ((), ())),
            preferred_element_type=jnp.float32,
        )
        second = (second * (1.0 / size)).astype(jnp.bfloat16)
        for s in range(screens):
            made[s * planes + p] = second[s * kernel_size : (s + 1) * kernel_size]

    capacity, tiles = chosen_list.shape

    @pl.loop(0, tiles)
    def _(t):
        for c in range(capacity):
            chosen = made[chosen_list[c, t]]
            out_ref[t * capacity + c] = jnp.where(c < count[0, t], chosen, jnp.zeros_like(chosen))


def make_kernels(aperture_amp, aperture_phase, plane_depths, chosen_list, counts, kernel_size):
    screens, size, _ = aperture_amp.shape
    planes = plane_depths.shape[0]
    capacity, tiles = chosen_list.shape
    hbm = pl.BlockSpec(memory_space=pl.ANY)
    return pl.pallas_call(
        kernels_body,
        in_specs=[hbm] * 5,
        out_specs=pl.BlockSpec(memory_space=pltpu.VMEM),
        out_shape=pltpu.VMEM((tiles * capacity, kernel_size, 2 * kernel_size), jnp.bfloat16),
        scratch_shapes=[
            pltpu.SMEM((capacity, tiles), jnp.int32),
            pltpu.SMEM((1, tiles), jnp.int32),
            pltpu.SMEM((planes,), jnp.float32),
            pltpu.VMEM((screens, size, size), jnp.bfloat16),
            pltpu.VMEM((screens, size, size), jnp.bfloat16),
            pltpu.VMEM((planes * 2 * kernel_size, 2 * size), jnp.bfloat16),
            pltpu.VMEM((2 * size, size), jnp.bfloat16),
            pltpu.VMEM((screens, planes, kernel_size, 2 * size), jnp.bfloat16),
            pltpu.VMEM((screens * planes, kernel_size, 2 * kernel_size), jnp.bfloat16),
            pltpu.SemaphoreType.DMA((3,)),
            pltpu.SemaphoreType.DMA((2, screens)),
        ],
        compiler_params=pltpu.CompilerParams(vmem_limit_bytes=32 * 2**20),
        name="make_kernels",
    )(*map(in_hbm, (chosen_list, counts, plane_depths, aperture_amp, aperture_phase)))


class Layout:
    def __init__(self, blocks, anchors):
        self.parts = 2
        quads = (blocks + (QUAD - 1) * anchors) // QUAD + 1 + self.parts * (STEP - 1)
        self.quads = (quads + STEP - 1) // STEP * STEP
        self.anchor = self.parts + 1
        self.slot = self.anchor + self.quads
        self.total = self.slot + (self.quads + UNROLL) * QUAD


def plan_body(
    pos_ref, slot_ref, count_ref, left_hbm, right_hbm, plan_ref, left_out, right_out,
    left_ref, right_ref, tally, cursor, sems, *, layout, row_slots, col_slots,
):
    anchors = row_slots * col_slots
    border = row_slots + col_slots - 1
    live = count_ref[0]

    def copies(block, place):
        return [
            pltpu.make_async_copy(left_hbm.at[block], left_ref.at[place], sems.at[0]),
            pltpu.make_async_copy(right_hbm.at[block], right_ref.at[place], sems.at[1]),
        ]

    def put(block, place, slot):
        plan_ref[layout.slot + place] = slot
        for copy in copies(block, place):
            copy.start()

    @pl.loop(0, anchors)
    def _(q):
        tally[q] = 0

    @pl.loop(0, live)
    def _(j):
        q = pos_ref[j]
        tally[q] = tally[q] + 1

    def lay(rank, quad):
        inner = rank - border
        q = jnp.where(
            rank < col_slots,
            (row_slots - 1) * col_slots + rank,
            jnp.where(
                rank < border,
                (rank - col_slots) * col_slots + col_slots - 1,
                (inner // (col_slots - 1)) * col_slots + lax.rem(inner, col_slots - 1),
            ),
        )
        number = tally[q]
        quads = (number + QUAD - 1) // QUAD
        cursor[q] = quad * QUAD

        @pl.loop(0, quads)
        def _(i):
            plan_ref[layout.anchor + quad + i] = q

        @pl.loop(quad * QUAD + number, (quad + quads) * QUAD)
        def _(i):
            put(0, i, -1)

        return quad + quads

    quad = 0
    begin = 0
    plan_ref[0] = 0
    for part, end in enumerate([border, anchors]):
        quad = lax.fori_loop(begin, end, lay, quad)
        begin = end
        full = ((quad + STEP - 1) // STEP) * STEP

        @pl.loop(quad, full)
        def _(i):
            plan_ref[layout.anchor + i] = 0
            for e in range(QUAD):
                put(0, i * QUAD + e, -1)

        quad = full
        plan_ref[part + 1] = quad

    @pl.loop(quad * QUAD, (quad + UNROLL) * QUAD)
    def _(i):
        plan_ref[layout.slot + i] = -1

    @pl.loop(0, live)
    def _(j):
        q = pos_ref[j]
        at = cursor[q]
        cursor[q] = at + 1
        put(j, at, slot_ref[j])

    @pl.loop(0, quad * QUAD)
    def _(i):
        for copy in copies(0, 0):
            copy.wait()

    chunk = STEP * QUAD

    def writes(i):
        rows = pl.ds(i * chunk, chunk)
        return [
            pltpu.make_async_copy(left_ref.at[rows], left_out.at[rows], sems.at[2]),
            pltpu.make_async_copy(right_ref.at[rows], right_out.at[rows], sems.at[3]),
        ]

    @pl.loop(0, quad // STEP)
    def _(i):
        for copy in writes(i):
            copy.start()

    @pl.loop(0, quad // STEP)
    def _(i):
        for copy in writes(i):
            copy.wait()


def plan_blocks(block_pos, block_slot, block_count, vis_left, vis_right, layout):
    kernel_size = vis_right.shape[1]
    row_slots, col_slots = TILE_U // kernel_size, TILE_V // kernel_size
    smem = pl.BlockSpec(memory_space=pltpu.SMEM)
    hbm = pl.BlockSpec(memory_space=pl.ANY)
    places = layout.quads * QUAD
    return pl.pallas_call(
        functools.partial(plan_body, layout=layout, row_slots=row_slots, col_slots=col_slots),
        in_specs=[smem] * 3 + [hbm] * 2,
        out_specs=[smem, hbm, hbm],
        out_shape=[
            jax.ShapeDtypeStruct((layout.total,), jnp.int32),
            pltpu.HBM((places,) + vis_left.shape[1:], vis_left.dtype),
            pltpu.HBM((places,) + vis_right.shape[1:], vis_right.dtype),
        ],
        scratch_shapes=[
            pltpu.VMEM((places,) + vis_left.shape[1:], vis_left.dtype),
            pltpu.VMEM((places,) + vis_right.shape[1:], vis_right.dtype),
            pltpu.SMEM((row_slots * col_slots,), jnp.int32),
            pltpu.SMEM((row_slots * col_slots,), jnp.int32),
            pltpu.SemaphoreType.DMA((4,)),
        ],
        compiler_params=pltpu.CompilerParams(vmem_limit_bytes=36 * 2**20),
        name="plan_blocks",
    )(block_pos, block_slot, block_count, in_hbm(vis_left), in_hbm(vis_right))


def strip(sums, row_slots, col_slots, kernel_size, plane, a, col):
    patch = sums.shape[1]
    lanes = slice(plane * patch, (plane + 1) * patch)
    total = None
    if a < row_slots:
        total = sums[a * col_slots + col, :kernel_size, lanes]
    if a > 0:
        above = sums[(a - 1) * col_slots + col, kernel_size:, lanes]
        total = above if total is None else total + above
    return total


def grid_body(
    plan_ref, kern_ref, left_hbm, right_hbm, *rest, part, first_part, halo, layout, row_slots, col_slots
):
    if not first_part:
        rest = rest[4:]
    sums, left_ring, right_ring, ahead, *rest = rest
    if halo:
        row_ref, col_ref, corner_ref, *rest = rest
    behind_ref, sems = rest
    mixed = (ahead, behind_ref)
    slots, kernel_size, _ = kern_ref.shape
    patch = left_hbm.shape[1]
    chunk = STEP * QUAD
    begin = plan_ref[part] // STEP
    end = plan_ref[part + 1] // STEP
    total = plan_ref[layout.parts] // STEP

    def fetch(i):
        source = pl.ds(i * chunk, chunk)
        ring = lax.rem(i, RING)
        return [
            pltpu.make_async_copy(left_hbm.at[source], left_ring.at[ring], sems.at[0, ring]),
            pltpu.make_async_copy(right_hbm.at[source], right_ring.at[ring], sems.at[1, ring]),
        ]

    def start(i):
        @pl.when(i < total)
        def _():
            for copy in fetch(i):
                copy.start()

    def wait(i):
        @pl.when(i < total)
        def _():
            for copy in fetch(i):
                copy.wait()

    if first_part:
        start(0)

        @pl.loop(0, sums.shape[0])
        def _(q):
            sums[q] = jnp.zeros(sums.shape[1:], sums.dtype)

    zero = jnp.zeros((kernel_size, patch), jnp.bfloat16)

    def first(i, ring, at, ref, u):
        for e in range(QUAD):
            slot = plan_ref[layout.slot + (i * STEP + at) * QUAD + e]
            right = right_ring[ring, at * QUAD + e]
            kern = kern_ref[jnp.maximum(slot, 0)]
            kern = jnp.where(slot >= 0, kern, jnp.zeros_like(kern))
            spread = jnp.concatenate(
                [jnp.concatenate([right, zero], axis=1), jnp.concatenate([zero, right], axis=1)], axis=0
            )
            out = jnp.dot(kern, spread, preferred_element_type=jnp.float32).astype(jnp.bfloat16)
            top = slice(e * 2 * kernel_size, (e * 2 + 1) * kernel_size)
            low = slice((e * 2 + 1) * kernel_size, (e * 2 + 2) * kernel_size)
            ref[u, top, :] = out
            ref[u, low, :patch] = -out[:, patch:]
            ref[u, low, patch:] = out[:, :patch]

    def second(i, ring, at, ref, u):
        left = jnp.concatenate([left_ring[ring, at * QUAD + e] for e in range(QUAD)], axis=1)
        q = plan_ref[layout.anchor + i * STEP + at]
        sums[q] += jnp.dot(left, ref[u], preferred_element_type=jnp.float32)

    if first_part:
        wait(0)
        start(1)
        start(2)
        for u in range(UNROLL):
            first(0, 0, u, mixed[0], u)

    @pl.loop(begin, end)
    def _(i):
        here = lax.rem(i, RING)
        there = lax.rem(i + 1, RING)
        start(i + 3)
        if first_part:
            wait(i + 1)
        else:
            pl.when(i > begin + 1)(lambda: wait(i + 1))
        for u in range(UNROLL):
            first(i, here, UNROLL + u, mixed[1], u)
            second(i, here, u, mixed[0], u)
        for u in range(UNROLL):
            first(i + 1, there, u, mixed[0], u)
            second(i, here, UNROLL + u, mixed[1], u)

    if first_part:
        wait(end + 1)
        wait(end + 2)
    if not halo:
        return
    low = lax.broadcasted_iota(jnp.int32, (kernel_size, patch), 1) < kernel_size
    take = functools.partial(strip, sums, row_slots, col_slots, kernel_size)
    for plane in range(2):
        behind = 0.0
        for tile in range(col_slots // 2):
            even = take(plane, row_slots, 2 * tile)
            odd = pltpu.roll(take(plane, row_slots, 2 * tile + 1), kernel_size, 1)
            row_ref[plane, :, tile * patch : (tile + 1) * patch] = (
                even + jnp.where(low, behind, odd)
            ).astype(row_ref.dtype)
            behind = odd
    for a in range(row_slots + 1):
        real = pltpu.roll(take(0, a, col_slots - 1), kernel_size, 1)
        imag = take(1, a, col_slots - 1)
        edge = jnp.where(low, real, imag)
        if a < row_slots:
            col_ref[a * kernel_size : (a + 1) * kernel_size, :] = edge.astype(col_ref.dtype)
        else:
            corner_ref[...] = edge.astype(corner_ref.dtype)


def grid_part(plan, part, kernels, left, right, carried, halo, layout):
    kernel_size = kernels.shape[1]
    patch = left.shape[1]
    row_slots, col_slots = TILE_U // kernel_size, TILE_V // kernel_size
    smem = pl.BlockSpec(memory_space=pltpu.SMEM)
    vmem = pl.BlockSpec(memory_space=pltpu.VMEM)
    hbm = pl.BlockSpec(memory_space=pl.ANY)
    first_part = carried is None
    carried = [] if first_part else [in_vmem(array) for array in carried]
    mixed_shape = (UNROLL, QUAD * 2 * kernel_size, 2 * patch)
    out_shape = [
        pltpu.VMEM((row_slots * col_slots, patch, 2 * patch), jnp.float32),
        pltpu.VMEM((RING, STEP * QUAD) + left.shape[1:], left.dtype),
        pltpu.VMEM((RING, STEP * QUAD) + right.shape[1:], right.dtype),
        pltpu.VMEM(mixed_shape, jnp.bfloat16),
    ]
    if halo:
        out_shape += [
            jax.ShapeDtypeStruct((2, kernel_size, TILE_V), jnp.bfloat16),
            jax.ShapeDtypeStruct((TILE_U, 2 * kernel_size), jnp.bfloat16),
            jax.ShapeDtypeStruct((kernel_size, 2 * kernel_size), jnp.bfloat16),
        ]
    out = pl.pallas_call(
        functools.partial(
            grid_body,
            part=part,
            first_part=first_part,
            halo=halo,
            layout=layout,
            row_slots=row_slots,
            col_slots=col_slots,
        ),
        in_specs=[smem, vmem, hbm, hbm] + [vmem] * len(carried),
        out_specs=[vmem] * len(out_shape),
        out_shape=out_shape,
        input_output_aliases={4 + i: i for i in range(len(carried))},
        scratch_shapes=[
            pltpu.VMEM(mixed_shape, jnp.bfloat16),
            pltpu.SemaphoreType.DMA((2, RING)),
        ],
        compiler_params=pltpu.CompilerParams(vmem_limit_bytes=12 * 2**20),
        name="grid_part",
    )(plan, in_vmem(kernels), in_hbm(left), in_hbm(right), *carried)
    return out[:4], out[4:]


def merge_body(sums, row_ref, col_ref, corner_ref, out_ref):
    kernel_size = row_ref.shape[1]
    patch = sums.shape[1]
    row_slots = out_ref.shape[1] // kernel_size
    col_slots = out_ref.shape[2] // kernel_size
    low = lax.broadcasted_iota(jnp.int32, (kernel_size, patch), 1) < kernel_size
    take = functools.partial(strip, sums, row_slots, col_slots, kernel_size)
    for a in range(row_slots):
        rows = slice(a * kernel_size, (a + 1) * kernel_size)
        edge = col_ref[rows, :].astype(jnp.float32)
        if a == 0:
            edge = edge + corner_ref[...].astype(jnp.float32)
        for plane in range(2):
            behind = edge if plane == 0 else pltpu.roll(edge, kernel_size, 1)
            for tile in range(col_slots // 2):
                lanes = slice(tile * patch, (tile + 1) * patch)
                odd = pltpu.roll(take(plane, a, 2 * tile + 1), kernel_size, 1)
                value = take(plane, a, 2 * tile) + jnp.where(low, behind, odd)
                if a == 0:
                    value = value + row_ref[plane, :, lanes].astype(jnp.float32)
                out_ref[plane, rows, lanes] = value
                behind = odd


def merge_tile(sums, row, col, corner):
    vmem = pl.BlockSpec(memory_space=pltpu.VMEM)
    return pl.pallas_call(
        merge_body,
        in_specs=[vmem] * 4,
        out_specs=vmem,
        out_shape=jax.ShapeDtypeStruct((2, TILE_U, TILE_V), jnp.float32),
        compiler_params=pltpu.CompilerParams(vmem_limit_bytes=8 * 2**20),
        name="merge_tile",
    )(in_vmem(sums), row, col, corner)


def shards(
    aperture_amp,
    aperture_phase,
    plane_depths,
    send_list,
    send_count,
    vis_left,
    vis_right,
    block_slot,
    block_pos,
    block_count,
):
    kernel_size = vis_right.shape[1]
    tiles, capacity = send_list.shape[1:]
    both = ("tu", "tv")
    outgoing = make_kernels(
        aperture_amp, aperture_phase, plane_depths, send_list[0].T, send_count, kernel_size
    )
    outgoing = outgoing.reshape((tiles, capacity) + outgoing.shape[1:])
    arrived = lax.all_to_all(outgoing, both, split_axis=0, concat_axis=0, tiled=True)
    received = arrived.reshape((-1,) + arrived.shape[2:])
    layout = Layout(block_pos.shape[0], (TILE_U // kernel_size) * (TILE_V // kernel_size))
    plan, left, right = plan_blocks(block_pos, block_slot, block_count, vis_left, vis_right, layout)
    carried, (row, col, corner) = grid_part(plan, 0, received, left, right, None, True, layout)
    row = from_behind(row, "tu", 1)
    col = from_behind(col, "tv", 1)
    rows, cols = lax.axis_size("tu"), lax.axis_size("tv")
    diagonal = [
        (i * cols + j, (i + 1) * cols + j + 1) for i in range(rows - 1) for j in range(cols - 1)
    ]
    corner = lax.ppermute(corner, both, diagonal)
    carried, _ = grid_part(plan, 1, received, left, right, carried, False, layout)
    return merge_tile(carried[0], row, col, corner)


def solution(mesh):
    placed = (
        P(("tu", "tv"), None, None),
        P(("tu", "tv"), None, None),
        P(),
        P(("tu", "tv"), None, None),
        P(("tu", "tv"), None),
        P(("tu", "tv"), None, None),
        P(("tu", "tv"), None, None),
        P(("tu", "tv")),
        P(("tu", "tv")),
        P(("tu", "tv")),
    )
    return jax.shard_map(
        shards, mesh=mesh, in_specs=placed, out_specs=P(None, "tu", "tv"), check_vma=False
    )
```

```python
import functools
import math

import jax
import jax.numpy as jnp
import numpy as np
from jax import lax
from jax.experimental import pallas as pl
from jax.experimental.pallas import tpu as pltpu
from jax.sharding import PartitionSpec as P

TILE_U = 256
TILE_V = 512
QUAD = 4
UNROLL = 4
STEP = 2 * UNROLL
RING = 4

def _fit(fn, degree):
    span = math.pi ** 2
    nodes = 0.5 * span * (1.0 - np.cos(np.pi * (np.arange(400) + 0.5) / 400))
    cheb = np.polynomial.chebyshev.Chebyshev.fit(nodes, fn(np.sqrt(nodes)), degree, domain=[0, span])
    return [float(c) for c in cheb.convert(kind=np.polynomial.Polynomial).coef]


COS_POLY = _fit(np.cos, 6)
SIN_POLY = _fit(lambda x: np.sin(x) / x, 5)


def horner(coefs, u):
    total = jnp.full_like(u, coefs[-1])
    for coef in coefs[-2::-1]:
        total = total * u + coef
    return total


def cos_sin(x):
    u = x * x
    return horner(COS_POLY, u), x * horner(SIN_POLY, u)


def from_behind(block, axis, distance):
    devices = range(lax.axis_size(axis))
    route = [(i - distance, i) for i in devices if i - distance in devices]
    return lax.ppermute(block, axis, route)


def in_hbm(array):
    return pltpu.with_memory_space_constraint(array, pltpu.HBM)


def in_vmem(array):
    return pltpu.with_memory_space_constraint(array, pltpu.VMEM)


def in_smem(array):
    return pltpu.with_memory_space_constraint(array, pltpu.SMEM)


def kernels_body(
    list_hbm, count_hbm, depth_hbm, amp_hbm, phase_hbm, out_ref,
    chosen_list, count, depth, amp, phase, table, screen, halves, made, small_sems, bulk_sems,
):
    screens, size, _ = amp.shape
    planes = depth.shape[0]
    kernel_size = out_ref.shape[1]
    small = [
        pltpu.make_async_copy(depth_hbm, depth, small_sems.at[0]),
        pltpu.make_async_copy(list_hbm, chosen_list, small_sems.at[1]),
        pltpu.make_async_copy(count_hbm, count, small_sems.at[2]),
    ]
    for copy in small:
        copy.start()

    def bulk(s):
        return [
            pltpu.make_async_copy(amp_hbm.at[s], amp.at[s], bulk_sems.at[0, s]),
            pltpu.make_async_copy(phase_hbm.at[s], phase.at[s], bulk_sems.at[1, s]),
        ]

    for s in range(screens):
        for copy in bulk(s):
            copy.start()

    frequency = lax.broadcasted_iota(jnp.int32, (kernel_size, size), 0) - kernel_size // 2
    cells = lax.broadcasted_iota(jnp.int32, (kernel_size, size), 1)
    turns = frequency.astype(jnp.float32) * cells.astype(jnp.float32) / size
    real_f, imag_f = cos_sin((2.0 * math.pi) * (turns - jnp.round(turns)))
    real_f = real_f.astype(jnp.bfloat16).astype(jnp.float32)
    imag_f = (-imag_f).astype(jnp.bfloat16).astype(jnp.float32)
    place = (lax.broadcasted_iota(jnp.int32, (1, size), 1).astype(jnp.float32) - size // 2) / size
    square = place * place
    for copy in small:
        copy.wait()
    for p in range(planes):
        turns = depth[p] * square
        real_e, imag_e = cos_sin((2.0 * math.pi) * (turns - jnp.round(turns)))
        real_g = (real_f * real_e - imag_f * imag_e).astype(jnp.bfloat16)
        imag_g = (real_f * imag_e + imag_f * real_e).astype(jnp.bfloat16)
        top = slice(p * 2 * kernel_size, (p * 2 + 1) * kernel_size)
        low = slice((p * 2 + 1) * kernel_size, (p * 2 + 2) * kernel_size)
        table[top, :size] = real_g
        table[top, size:] = -imag_g
        table[low, :size] = imag_g
        table[low, size:] = real_g

    @pl.loop(0, screens)
    def _(s):
        for copy in bulk(s):
            copy.wait()
        magnitude = amp[s].astype(jnp.float32)
        real_e, imag_e = cos_sin(phase[s].astype(jnp.float32))
        screen[:size, :] = (magnitude * real_e).astype(jnp.bfloat16)
        screen[size:, :] = (magnitude * imag_e).astype(jnp.bfloat16)
        product = jnp.dot(table[...], screen[...], preferred_element_type=jnp.float32).astype(jnp.bfloat16)
        for p in range(planes):
            base = p * 2 * kernel_size
            halves[s, p, :, :size] = product[base : base + kernel_size]
            halves[s, p, :, size:] = product[base + kernel_size : base + 2 * kernel_size]

    for p in range(planes):
        second = lax.dot_general(
            jnp.concatenate([halves[s, p] for s in range(screens)], axis=0),
            table[p * 2 * kernel_size : (p + 1) * 2 * kernel_size, :],
            (((1,), (1,)), ((), ())),
            preferred_element_type=jnp.float32,
        )
        second = (second * (1.0 / size)).astype(jnp.bfloat16)
        for s in range(screens):
            made[s * planes + p] = second[s * kernel_size : (s + 1) * kernel_size]

    capacity, tiles = chosen_list.shape

    @pl.loop(0, tiles)
    def _(t):
        for c in range(capacity):
            chosen = made[chosen_list[c, t]]
            out_ref[t * capacity + c] = jnp.where(c < count[0, t], chosen, jnp.zeros_like(chosen))


def make_kernels(aperture_amp, aperture_phase, plane_depths, chosen_list, counts, kernel_size):
    screens, size, _ = aperture_amp.shape
    planes = plane_depths.shape[0]
    capacity, tiles = chosen_list.shape
    hbm = pl.BlockSpec(memory_space=pl.ANY)
    return pl.pallas_call(
        kernels_body,
        in_specs=[hbm] * 5,
        out_specs=pl.BlockSpec(memory_space=pltpu.VMEM),
        out_shape=pltpu.VMEM((tiles * capacity, kernel_size, 2 * kernel_size), jnp.bfloat16),
        scratch_shapes=[
            pltpu.SMEM((capacity, tiles), jnp.int32),
            pltpu.SMEM((1, tiles), jnp.int32),
            pltpu.SMEM((planes,), jnp.float32),
            pltpu.VMEM((screens, size, size), jnp.bfloat16),
            pltpu.VMEM((screens, size, size), jnp.bfloat16),
            pltpu.VMEM((planes * 2 * kernel_size, 2 * size), jnp.bfloat16),
            pltpu.VMEM((2 * size, size), jnp.bfloat16),
            pltpu.VMEM((screens, planes, kernel_size, 2 * size), jnp.bfloat16),
            pltpu.VMEM((screens * planes, kernel_size, 2 * kernel_size), jnp.bfloat16),
            pltpu.SemaphoreType.DMA((3,)),
            pltpu.SemaphoreType.DMA((2, screens)),
        ],
        compiler_params=pltpu.CompilerParams(vmem_limit_bytes=32 * 2**20),
        name="make_kernels",
    )(*map(in_hbm, (chosen_list, counts, plane_depths, aperture_amp, aperture_phase)))


class Layout:
    def __init__(self, blocks, anchors):
        self.parts = 3
        quads = (blocks + (QUAD - 1) * anchors) // QUAD + 1 + self.parts * (STEP - 1)
        self.quads = (quads + STEP - 1) // STEP * STEP
        self.anchor = self.parts + 1
        self.slot = self.anchor + self.quads
        self.total = self.slot + (self.quads + UNROLL) * QUAD


def plan_body(
    pos_ref, slot_ref, count_ref, left_hbm, right_hbm, plan_ref, left_out, right_out,
    left_ref, right_ref, tally, cursor, sems, *, layout, row_slots, col_slots,
):
    anchors = row_slots * col_slots
    border = row_slots + col_slots - 1
    live = count_ref[0]

    def copies(block, place):
        return [
            pltpu.make_async_copy(left_hbm.at[block], left_ref.at[place], sems.at[0]),
            pltpu.make_async_copy(right_hbm.at[block], right_ref.at[place], sems.at[1]),
        ]

    def put(block, place, slot):
        plan_ref[layout.slot + place] = slot
        for copy in copies(block, place):
            copy.start()

    @pl.loop(0, anchors)
    def _(q):
        tally[q] = 0

    @pl.loop(0, live)
    def _(j):
        q = pos_ref[j]
        tally[q] = tally[q] + 1

    def lay(rank, quad):
        inner = rank - border
        q = jnp.where(
            rank < row_slots,
            rank * col_slots + col_slots - 1,
            jnp.where(
                rank < border,
                (row_slots - 1) * col_slots + rank - row_slots,
                (inner // (col_slots - 1)) * col_slots + lax.rem(inner, col_slots - 1),
            ),
        )
        number = tally[q]
        quads = (number + QUAD - 1) // QUAD
        cursor[q] = quad * QUAD

        @pl.loop(0, quads)
        def _(i):
            plan_ref[layout.anchor + quad + i] = q

        @pl.loop(quad * QUAD + number, (quad + quads) * QUAD)
        def _(i):
            put(0, i, -1)

        return quad + quads

    quad = 0
    begin = 0
    plan_ref[0] = 0
    for part, end in enumerate([row_slots, border, anchors]):
        quad = lax.fori_loop(begin, end, lay, quad)
        begin = end
        full = ((quad + STEP - 1) // STEP) * STEP

        @pl.loop(quad, full)
        def _(i):
            plan_ref[layout.anchor + i] = 0
            for e in range(QUAD):
                put(0, i * QUAD + e, -1)

        quad = full
        plan_ref[part + 1] = quad

    @pl.loop(quad * QUAD, (quad + UNROLL) * QUAD)
    def _(i):
        plan_ref[layout.slot + i] = -1

    @pl.loop(0, live)
    def _(j):
        q = pos_ref[j]
        at = cursor[q]
        cursor[q] = at + 1
        put(j, at, slot_ref[j])

    chunk = STEP * QUAD

    @pl.loop(0, quad // STEP)
    def _(i):
        rows = pl.ds(0, chunk)
        pltpu.make_async_copy(left_hbm.at[rows], left_ref.at[rows], sems.at[0]).wait()
        pltpu.make_async_copy(right_hbm.at[rows], right_ref.at[rows], sems.at[1]).wait()

    def writes(i):
        rows = pl.ds(i * chunk, chunk)
        return [
            pltpu.make_async_copy(left_ref.at[rows], left_out.at[rows], sems.at[2]),
            pltpu.make_async_copy(right_ref.at[rows], right_out.at[rows], sems.at[3]),
        ]

    @pl.loop(0, quad // STEP)
    def _(i):
        for copy in writes(i):
            copy.start()

    @pl.loop(0, quad // STEP)
    def _(i):
        for copy in writes(i):
            copy.wait()


def plan_blocks(block_pos, block_slot, block_count, vis_left, vis_right, layout):
    kernel_size = vis_right.shape[1]
    row_slots, col_slots = TILE_U // kernel_size, TILE_V // kernel_size
    smem = pl.BlockSpec(memory_space=pltpu.SMEM)
    hbm = pl.BlockSpec(memory_space=pl.ANY)
    places = layout.quads * QUAD
    return pl.pallas_call(
        functools.partial(plan_body, layout=layout, row_slots=row_slots, col_slots=col_slots),
        in_specs=[smem] * 3 + [hbm] * 2,
        out_specs=[smem, hbm, hbm],
        out_shape=[
            pltpu.SMEM((layout.total,), jnp.int32),
            pltpu.HBM((places,) + vis_left.shape[1:], vis_left.dtype),
            pltpu.HBM((places,) + vis_right.shape[1:], vis_right.dtype),
        ],
        scratch_shapes=[
            pltpu.VMEM((places,) + vis_left.shape[1:], vis_left.dtype),
            pltpu.VMEM((places,) + vis_right.shape[1:], vis_right.dtype),
            pltpu.SMEM((row_slots * col_slots,), jnp.int32),
            pltpu.SMEM((row_slots * col_slots,), jnp.int32),
            pltpu.SemaphoreType.DMA((4,)),
        ],
        compiler_params=pltpu.CompilerParams(vmem_limit_bytes=36 * 2**20),
        name="plan_blocks",
    )(block_pos, block_slot, block_count, in_hbm(vis_left), in_hbm(vis_right))


def strip(sums, row_slots, col_slots, kernel_size, plane, a, col):
    patch = sums.shape[1]
    lanes = slice(plane * patch, (plane + 1) * patch)
    total = None
    if a < row_slots:
        total = sums[a * col_slots + col, :kernel_size, lanes]
    if a > 0:
        above = sums[(a - 1) * col_slots + col, kernel_size:, lanes]
        total = above if total is None else total + above
    return total


def grid_body(
    plan_ref, kern_ref, left_hbm, right_hbm, *rest, part, first_part, layout, row_slots, col_slots
):
    if not first_part:
        rest = rest[4:]
    sums, left_ring, right_ring, ahead, *rest = rest
    if first_part:
        col_ref, *rest = rest
    behind_ref, sems = rest
    mixed = (ahead, behind_ref)
    slots, kernel_size, _ = kern_ref.shape
    patch = left_hbm.shape[1]
    chunk = STEP * QUAD
    begin = plan_ref[part] // STEP
    end = plan_ref[part + 1] // STEP
    total = plan_ref[layout.parts] // STEP

    def fetch(i):
        source = pl.ds(i * chunk, chunk)
        ring = lax.rem(i, RING)
        return [
            pltpu.make_async_copy(left_hbm.at[source], left_ring.at[ring], sems.at[0, ring]),
            pltpu.make_async_copy(right_hbm.at[source], right_ring.at[ring], sems.at[1, ring]),
        ]

    def start(i):
        @pl.when(i < total)
        def _():
            for copy in fetch(i):
                copy.start()

    def wait_new(i):
        if first_part:
            wait(i)
        else:
            pl.when(i > begin + 2)(lambda: wait(i))

    def wait(i):
        @pl.when(i < total)
        def _():
            for copy in fetch(i):
                copy.wait()

    if first_part:
        start(0)

        @pl.loop(0, sums.shape[0])
        def _(q):
            sums[q] = jnp.zeros(sums.shape[1:], sums.dtype)

    zero = jnp.zeros((kernel_size, patch), jnp.bfloat16)

    def first(i, ring, at, ref, u):
        for e in range(QUAD):
            slot = plan_ref[layout.slot + (i * STEP + at) * QUAD + e]
            right = right_ring[ring, at * QUAD + e]
            kern = kern_ref[jnp.maximum(slot, 0)]
            kern = jnp.where(slot >= 0, kern, jnp.zeros_like(kern))
            spread = jnp.concatenate(
                [jnp.concatenate([right, zero], axis=1), jnp.concatenate([zero, right], axis=1)], axis=0
            )
            out = jnp.dot(kern, spread, preferred_element_type=jnp.float32).astype(jnp.bfloat16)
            top = slice(e * 2 * kernel_size, (e * 2 + 1) * kernel_size)
            low = slice((e * 2 + 1) * kernel_size, (e * 2 + 2) * kernel_size)
            ref[u, top, :] = out
            ref[u, low, :patch] = -out[:, patch:]
            ref[u, low, patch:] = out[:, :patch]

    def second(i, ring, at, ref, u):
        left = jnp.concatenate([left_ring[ring, at * QUAD + e] for e in range(QUAD)], axis=1)
        q = plan_ref[layout.anchor + i * STEP + at]
        sums[q] += jnp.dot(left, ref[u], preferred_element_type=jnp.float32)

    if first_part:
        wait(0)
        start(1)
        start(2)
        for u in range(UNROLL):
            first(0, 0, u, mixed[0], u)

    @pl.loop(begin, end)
    def _(i):
        here = lax.rem(i, RING)
        there = lax.rem(i + 1, RING)
        start(i + 3)
        wait_new(i + 1)
        for u in range(UNROLL):
            first(i, here, UNROLL + u, mixed[1], u)
            second(i, here, u, mixed[0], u)
        for u in range(UNROLL):
            first(i + 1, there, u, mixed[0], u)
            second(i, here, UNROLL + u, mixed[1], u)

    wait_new(end + 1)
    wait_new(end + 2)
    if not first_part:
        return
    low = lax.broadcasted_iota(jnp.int32, (kernel_size, patch), 1) < kernel_size
    take = functools.partial(strip, sums, row_slots, col_slots, kernel_size)
    for a in range(row_slots + 1):
        real = pltpu.roll(take(0, a, col_slots - 1), kernel_size, 1)
        edge = jnp.where(low, real, take(1, a, col_slots - 1))
        col_ref[a * kernel_size : (a + 1) * kernel_size, :] = edge.astype(col_ref.dtype)


def row_body(before, col_ref, sums, row_ref, *, row_slots, col_slots):
    kernel_size = row_ref.shape[1]
    patch = sums.shape[1]
    low = lax.broadcasted_iota(jnp.int32, (kernel_size, patch), 1) < kernel_size
    take = functools.partial(strip, sums, row_slots, col_slots, kernel_size)
    corner = col_ref[row_slots * kernel_size :, :].astype(jnp.float32)
    for plane in range(2):
        behind = corner if plane == 0 else pltpu.roll(corner, kernel_size, 1)
        for tile in range(col_slots // 2):
            odd = pltpu.roll(take(plane, row_slots, 2 * tile + 1), kernel_size, 1)
            value = take(plane, row_slots, 2 * tile) + jnp.where(low, behind, odd)
            row_ref[plane, :, tile * patch : (tile + 1) * patch] = value.astype(row_ref.dtype)
            behind = odd


def row_halo(sums, col, kernel_size):
    vmem = pl.BlockSpec(memory_space=pltpu.VMEM)
    return pl.pallas_call(
        functools.partial(row_body, row_slots=TILE_U // kernel_size, col_slots=TILE_V // kernel_size),
        in_specs=[vmem] * 2,
        out_specs=[vmem] * 2,
        out_shape=[
            pltpu.VMEM(sums.shape, sums.dtype),
            pltpu.VMEM((2, kernel_size, TILE_V), jnp.bfloat16),
        ],
        input_output_aliases={0: 0},
        compiler_params=pltpu.CompilerParams(vmem_limit_bytes=4 * 2**20),
        name="row_halo",
    )(in_vmem(sums), in_vmem(col))


def grid_part(plan, part, kernels, left, right, carried, layout):
    kernel_size = kernels.shape[1]
    patch = left.shape[1]
    row_slots, col_slots = TILE_U // kernel_size, TILE_V // kernel_size
    smem = pl.BlockSpec(memory_space=pltpu.SMEM)
    vmem = pl.BlockSpec(memory_space=pltpu.VMEM)
    hbm = pl.BlockSpec(memory_space=pl.ANY)
    first_part = carried is None
    carried = [] if first_part else [in_vmem(array) for array in carried]
    mixed_shape = (UNROLL, QUAD * 2 * kernel_size, 2 * patch)
    out_shape = [
        pltpu.VMEM((row_slots * col_slots, patch, 2 * patch), jnp.float32),
        pltpu.VMEM((RING, STEP * QUAD) + left.shape[1:], left.dtype),
        pltpu.VMEM((RING, STEP * QUAD) + right.shape[1:], right.dtype),
        pltpu.VMEM(mixed_shape, jnp.bfloat16),
    ]
    if first_part:
        out_shape.append(pltpu.VMEM((TILE_U + kernel_size, 2 * kernel_size), jnp.bfloat16))
    out = pl.pallas_call(
        functools.partial(
            grid_body,
            part=part,
            first_part=first_part,
            layout=layout,
            row_slots=row_slots,
            col_slots=col_slots,
        ),
        in_specs=[smem, vmem, hbm, hbm] + [vmem] * len(carried),
        out_specs=[vmem] * len(out_shape),
        out_shape=out_shape,
        input_output_aliases={4 + i: i for i in range(len(carried))},
        scratch_shapes=[
            pltpu.VMEM(mixed_shape, jnp.bfloat16),
            pltpu.SemaphoreType.DMA((2, RING)),
        ],
        compiler_params=pltpu.CompilerParams(vmem_limit_bytes=12 * 2**20),
        name="grid_part",
    )(in_smem(plan), in_vmem(kernels), in_hbm(left), in_hbm(right), *carried)
    return out[:4], out[4:]


def merge_body(sums, row_ref, col_ref, out_ref):
    kernel_size = row_ref.shape[1]
    patch = sums.shape[1]
    row_slots = out_ref.shape[1] // kernel_size
    col_slots = out_ref.shape[2] // kernel_size
    low = lax.broadcasted_iota(jnp.int32, (kernel_size, patch), 1) < kernel_size
    take = functools.partial(strip, sums, row_slots, col_slots, kernel_size)
    for a in range(row_slots):
        rows = slice(a * kernel_size, (a + 1) * kernel_size)
        edge = col_ref[rows, :].astype(jnp.float32)
        for plane in range(2):
            behind = edge if plane == 0 else pltpu.roll(edge, kernel_size, 1)
            for tile in range(col_slots // 2):
                lanes = slice(tile * patch, (tile + 1) * patch)
                odd = pltpu.roll(take(plane, a, 2 * tile + 1), kernel_size, 1)
                value = take(plane, a, 2 * tile) + jnp.where(low, behind, odd)
                if a == 0:
                    value = value + row_ref[plane, :, lanes].astype(jnp.float32)
                out_ref[plane, rows, lanes] = value
                behind = odd


def merge_tile(sums, row, col):
    vmem = pl.BlockSpec(memory_space=pltpu.VMEM)
    return pl.pallas_call(
        merge_body,
        in_specs=[vmem] * 3,
        out_specs=vmem,
        out_shape=jax.ShapeDtypeStruct((2, TILE_U, TILE_V), jnp.float32),
        compiler_params=pltpu.CompilerParams(vmem_limit_bytes=8 * 2**20),
        name="merge_tile",
    )(*map(in_vmem, (sums, row, col)))


def shards(
    aperture_amp,
    aperture_phase,
    plane_depths,
    send_list,
    send_count,
    vis_left,
    vis_right,
    block_slot,
    block_pos,
    block_count,
):
    kernel_size = vis_right.shape[1]
    tiles, capacity = send_list.shape[1:]
    both = ("tu", "tv")
    outgoing = make_kernels(
        aperture_amp, aperture_phase, plane_depths, send_list[0].T, send_count, kernel_size
    )
    outgoing = outgoing.reshape((tiles, capacity) + outgoing.shape[1:])
    arrived = lax.all_to_all(outgoing, both, split_axis=0, concat_axis=0, tiled=True)
    received = arrived.reshape((-1,) + arrived.shape[2:])
    layout = Layout(block_pos.shape[0], (TILE_U // kernel_size) * (TILE_V // kernel_size))
    plan, left, right = plan_blocks(block_pos, block_slot, block_count, vis_left, vis_right, layout)
    carried, (col,) = grid_part(plan, 0, received, left, right, None, layout)
    col = from_behind(col, "tv", 1)
    carried, _ = grid_part(plan, 1, received, left, right, carried, layout)
    sums, row = row_halo(carried[0], col, kernel_size)
    row = from_behind(row, "tu", 1)
    carried, _ = grid_part(plan, 2, received, left, right, [sums, *carried[1:]], layout)
    return merge_tile(carried[0], row, col)


def solution(mesh):
    placed = (
        P(("tu", "tv"), None, None),
        P(("tu", "tv"), None, None),
        P(),
        P(("tu", "tv"), None, None),
        P(("tu", "tv"), None),
        P(("tu", "tv"), None, None),
        P(("tu", "tv"), None, None),
        P(("tu", "tv")),
        P(("tu", "tv")),
        P(("tu", "tv")),
    )
    return jax.shard_map(
        shards, mesh=mesh, in_specs=placed, out_specs=P(None, "tu", "tv"), check_vma=False
    )
```

```python
import functools
import math

import jax
import jax.numpy as jnp
import numpy as np
from jax import lax
from jax.experimental import pallas as pl
from jax.experimental.pallas import tpu as pltpu
from jax.sharding import PartitionSpec as P

TILE_U = 256
TILE_V = 512
QUAD = 4
UNROLL = 4
STEP = 2 * UNROLL
RING = 4

def _fit(fn, degree):
    span = math.pi ** 2
    nodes = 0.5 * span * (1.0 - np.cos(np.pi * (np.arange(400) + 0.5) / 400))
    cheb = np.polynomial.chebyshev.Chebyshev.fit(nodes, fn(np.sqrt(nodes)), degree, domain=[0, span])
    return [float(c) for c in cheb.convert(kind=np.polynomial.Polynomial).coef]


COS_POLY = _fit(np.cos, 6)
SIN_POLY = _fit(lambda x: np.sin(x) / x, 5)


def horner(coefs, u):
    total = jnp.full_like(u, coefs[-1])
    for coef in coefs[-2::-1]:
        total = total * u + coef
    return total


def cos_sin(x):
    u = x * x
    return horner(COS_POLY, u), x * horner(SIN_POLY, u)


def from_behind(block, axis, distance):
    devices = range(lax.axis_size(axis))
    route = [(i - distance, i) for i in devices if i - distance in devices]
    return lax.ppermute(block, axis, route)


def in_hbm(array):
    return pltpu.with_memory_space_constraint(array, pltpu.HBM)


def in_vmem(array):
    return pltpu.with_memory_space_constraint(array, pltpu.VMEM)


def in_smem(array):
    return pltpu.with_memory_space_constraint(array, pltpu.SMEM)


def kernels_body(
    list_hbm, count_hbm, depth_hbm, amp_hbm, phase_hbm, out_ref,
    chosen_list, count, depth, amp, phase, table, screen, halves, made, small_sems, bulk_sems,
):
    screens, size, _ = amp.shape
    planes = depth.shape[0]
    kernel_size = out_ref.shape[1]
    small = [
        pltpu.make_async_copy(depth_hbm, depth, small_sems.at[0]),
        pltpu.make_async_copy(list_hbm, chosen_list, small_sems.at[1]),
        pltpu.make_async_copy(count_hbm, count, small_sems.at[2]),
    ]
    for copy in small:
        copy.start()

    def bulk(s):
        return [
            pltpu.make_async_copy(amp_hbm.at[s], amp.at[s], bulk_sems.at[0, s]),
            pltpu.make_async_copy(phase_hbm.at[s], phase.at[s], bulk_sems.at[1, s]),
        ]

    for copy in bulk(0):
        copy.start()

    frequency = lax.broadcasted_iota(jnp.int32, (kernel_size, size), 0) - kernel_size // 2
    cells = lax.broadcasted_iota(jnp.int32, (kernel_size, size), 1)
    turns = frequency.astype(jnp.float32) * cells.astype(jnp.float32) / size
    real_f, imag_f = cos_sin((2.0 * math.pi) * (turns - jnp.round(turns)))
    real_f = real_f.astype(jnp.bfloat16).astype(jnp.float32)
    imag_f = (-imag_f).astype(jnp.bfloat16).astype(jnp.float32)
    place = (lax.broadcasted_iota(jnp.int32, (1, size), 1).astype(jnp.float32) - size // 2) / size
    square = place * place
    for copy in small:
        copy.wait()
    for s in range(1, screens):
        for copy in bulk(s):
            copy.start()
    for p in range(planes):
        turns = depth[p] * square
        real_e, imag_e = cos_sin((2.0 * math.pi) * (turns - jnp.round(turns)))
        real_g = (real_f * real_e - imag_f * imag_e).astype(jnp.bfloat16)
        imag_g = (real_f * imag_e + imag_f * real_e).astype(jnp.bfloat16)
        top = slice(p * 2 * kernel_size, (p * 2 + 1) * kernel_size)
        low = slice((p * 2 + 1) * kernel_size, (p * 2 + 2) * kernel_size)
        table[top, :size] = real_g
        table[top, size:] = -imag_g
        table[low, :size] = imag_g
        table[low, size:] = real_g

    @pl.loop(0, screens)
    def _(s):
        for copy in bulk(s):
            copy.wait()
        magnitude = amp[s].astype(jnp.float32)
        real_e, imag_e = cos_sin(phase[s].astype(jnp.float32))
        screen[:size, :] = (magnitude * real_e).astype(jnp.bfloat16)
        screen[size:, :] = (magnitude * imag_e).astype(jnp.bfloat16)
        product = jnp.dot(table[...], screen[...], preferred_element_type=jnp.float32).astype(jnp.bfloat16)
        for p in range(planes):
            base = p * 2 * kernel_size
            halves[s, p, :, :size] = product[base : base + kernel_size]
            halves[s, p, :, size:] = product[base + kernel_size : base + 2 * kernel_size]

    for p in range(planes):
        second = lax.dot_general(
            jnp.concatenate([halves[s, p] for s in range(screens)], axis=0),
            table[p * 2 * kernel_size : (p + 1) * 2 * kernel_size, :],
            (((1,), (1,)), ((), ())),
            preferred_element_type=jnp.float32,
        )
        second = (second * (1.0 / size)).astype(jnp.bfloat16)
        for s in range(screens):
            made[s * planes + p] = second[s * kernel_size : (s + 1) * kernel_size]

    capacity, tiles = chosen_list.shape

    @pl.loop(0, tiles)
    def _(t):
        for c in range(capacity):
            chosen = made[chosen_list[c, t]]
            out_ref[t * capacity + c] = jnp.where(c < count[0, t], chosen, jnp.zeros_like(chosen))


def make_kernels(aperture_amp, aperture_phase, plane_depths, chosen_list, counts, kernel_size):
    screens, size, _ = aperture_amp.shape
    planes = plane_depths.shape[0]
    capacity, tiles = chosen_list.shape
    hbm = pl.BlockSpec(memory_space=pl.ANY)
    return pl.pallas_call(
        kernels_body,
        in_specs=[hbm] * 5,
        out_specs=pl.BlockSpec(memory_space=pltpu.VMEM),
        out_shape=pltpu.VMEM((tiles * capacity, kernel_size, 2 * kernel_size), jnp.bfloat16),
        scratch_shapes=[
            pltpu.SMEM((capacity, tiles), jnp.int32),
            pltpu.SMEM((1, tiles), jnp.int32),
            pltpu.SMEM((planes,), jnp.float32),
            pltpu.VMEM((screens, size, size), jnp.bfloat16),
            pltpu.VMEM((screens, size, size), jnp.bfloat16),
            pltpu.VMEM((planes * 2 * kernel_size, 2 * size), jnp.bfloat16),
            pltpu.VMEM((2 * size, size), jnp.bfloat16),
            pltpu.VMEM((screens, planes, kernel_size, 2 * size), jnp.bfloat16),
            pltpu.VMEM((screens * planes, kernel_size, 2 * kernel_size), jnp.bfloat16),
            pltpu.SemaphoreType.DMA((3,)),
            pltpu.SemaphoreType.DMA((2, screens)),
        ],
        compiler_params=pltpu.CompilerParams(vmem_limit_bytes=32 * 2**20),
        name="make_kernels",
    )(*map(in_hbm, (chosen_list, counts, plane_depths, aperture_amp, aperture_phase)))


class Layout:
    def __init__(self, blocks, anchors):
        self.parts = 3
        quads = (blocks + (QUAD - 1) * anchors) // QUAD + 1 + self.parts * (STEP - 1)
        self.quads = (quads + STEP - 1) // STEP * STEP
        self.anchor = self.parts + 1
        self.slot = self.anchor + self.quads
        self.total = self.slot + (self.quads + UNROLL) * QUAD


def plan_body(
    pos_ref, slot_ref, count_ref, left_hbm, right_hbm, plan_ref, left_out, right_out,
    left_ref, right_ref, tally, cursor, sems, *, layout, row_slots, col_slots,
):
    anchors = row_slots * col_slots
    border = row_slots + col_slots - 1
    live = count_ref[0]

    def copies(block, place):
        return [
            pltpu.make_async_copy(left_hbm.at[block], left_ref.at[place], sems.at[0]),
            pltpu.make_async_copy(right_hbm.at[block], right_ref.at[place], sems.at[1]),
        ]

    def put(block, place, slot):
        plan_ref[layout.slot + place] = slot
        for copy in copies(block, place):
            copy.start()

    @pl.loop(0, anchors)
    def _(q):
        tally[q] = 0

    @pl.loop(0, live)
    def _(j):
        q = pos_ref[j]
        tally[q] = tally[q] + 1

    def lay(rank, quad):
        inner = rank - border
        q = jnp.where(
            rank < row_slots,
            rank * col_slots + col_slots - 1,
            jnp.where(
                rank < border,
                (row_slots - 1) * col_slots + rank - row_slots,
                (inner // (col_slots - 1)) * col_slots + lax.rem(inner, col_slots - 1),
            ),
        )
        number = tally[q]
        quads = (number + QUAD - 1) // QUAD
        cursor[q] = quad * QUAD

        @pl.loop(0, quads)
        def _(i):
            plan_ref[layout.anchor + quad + i] = q

        @pl.loop(quad * QUAD + number, (quad + quads) * QUAD)
        def _(i):
            put(0, i, -1)

        return quad + quads

    quad = 0
    begin = 0
    plan_ref[0] = 0
    for part, end in enumerate([row_slots, border, anchors]):
        quad = lax.fori_loop(begin, end, lay, quad)
        begin = end
        full = ((quad + STEP - 1) // STEP) * STEP

        @pl.loop(quad, full)
        def _(i):
            plan_ref[layout.anchor + i] = 0
            for e in range(QUAD):
                put(0, i * QUAD + e, -1)

        quad = full
        plan_ref[part + 1] = quad

    @pl.loop(quad * QUAD, (quad + UNROLL) * QUAD)
    def _(i):
        plan_ref[layout.slot + i] = -1

    @pl.loop(0, live)
    def _(j):
        q = pos_ref[j]
        at = cursor[q]
        cursor[q] = at + 1
        put(j, at, slot_ref[j])

    chunk = STEP * QUAD

    @pl.loop(0, quad // STEP)
    def _(i):
        rows = pl.ds(0, chunk)
        pltpu.make_async_copy(left_hbm.at[rows], left_ref.at[rows], sems.at[0]).wait()
        pltpu.make_async_copy(right_hbm.at[rows], right_ref.at[rows], sems.at[1]).wait()

    def writes(i):
        rows = pl.ds(i * chunk, chunk)
        return [
            pltpu.make_async_copy(left_ref.at[rows], left_out.at[rows], sems.at[2]),
            pltpu.make_async_copy(right_ref.at[rows], right_out.at[rows], sems.at[3]),
        ]

    @pl.loop(0, quad // STEP)
    def _(i):
        for copy in writes(i):
            copy.start()

    @pl.loop(0, quad // STEP)
    def _(i):
        for copy in writes(i):
            copy.wait()


def plan_blocks(block_pos, block_slot, block_count, vis_left, vis_right, layout):
    kernel_size = vis_right.shape[1]
    row_slots, col_slots = TILE_U // kernel_size, TILE_V // kernel_size
    smem = pl.BlockSpec(memory_space=pltpu.SMEM)
    hbm = pl.BlockSpec(memory_space=pl.ANY)
    places = layout.quads * QUAD
    return pl.pallas_call(
        functools.partial(plan_body, layout=layout, row_slots=row_slots, col_slots=col_slots),
        in_specs=[smem] * 3 + [hbm] * 2,
        out_specs=[smem, hbm, hbm],
        out_shape=[
            pltpu.SMEM((layout.total,), jnp.int32),
            pltpu.HBM((places,) + vis_left.shape[1:], vis_left.dtype),
            pltpu.HBM((places,) + vis_right.shape[1:], vis_right.dtype),
        ],
        scratch_shapes=[
            pltpu.VMEM((places,) + vis_left.shape[1:], vis_left.dtype),
            pltpu.VMEM((places,) + vis_right.shape[1:], vis_right.dtype),
            pltpu.SMEM((row_slots * col_slots,), jnp.int32),
            pltpu.SMEM((row_slots * col_slots,), jnp.int32),
            pltpu.SemaphoreType.DMA((4,)),
        ],
        compiler_params=pltpu.CompilerParams(vmem_limit_bytes=36 * 2**20),
        name="plan_blocks",
    )(block_pos, block_slot, block_count, in_hbm(vis_left), in_hbm(vis_right))


def strip(sums, row_slots, col_slots, kernel_size, plane, a, col):
    patch = sums.shape[1]
    lanes = slice(plane * patch, (plane + 1) * patch)
    total = None
    if a < row_slots:
        total = sums[a * col_slots + col, :kernel_size, lanes]
    if a > 0:
        above = sums[(a - 1) * col_slots + col, kernel_size:, lanes]
        total = above if total is None else total + above
    return total


def grid_body(
    plan_ref, kern_ref, left_hbm, right_hbm, *rest, part, first_part, layout, row_slots, col_slots
):
    if not first_part:
        rest = rest[4:]
    sums, left_ring, right_ring, ahead, *rest = rest
    if first_part:
        col_ref, *rest = rest
    behind_ref, sems = rest
    mixed = (ahead, behind_ref)
    slots, kernel_size, _ = kern_ref.shape
    patch = left_hbm.shape[1]
    chunk = STEP * QUAD
    begin = plan_ref[part] // STEP
    end = plan_ref[part + 1] // STEP
    limit = jnp.minimum(plan_ref[layout.parts] // STEP, end + 2)

    def fetch(i):
        source = pl.ds(i * chunk, chunk)
        ring = lax.rem(i, RING)
        return [
            pltpu.make_async_copy(left_hbm.at[source], left_ring.at[ring], sems.at[0, ring]),
            pltpu.make_async_copy(right_hbm.at[source], right_ring.at[ring], sems.at[1, ring]),
        ]

    def start(i):
        @pl.when(i < limit)
        def _():
            for copy in fetch(i):
                copy.start()

    def wait_new(i):
        if first_part:
            wait(i)
        else:
            pl.when(i > begin + 1)(lambda: wait(i))

    def wait(i):
        @pl.when(i < limit)
        def _():
            for copy in fetch(i):
                copy.wait()

    if first_part:
        start(0)

        @pl.loop(0, sums.shape[0])
        def _(q):
            sums[q] = jnp.zeros(sums.shape[1:], sums.dtype)

    zero = jnp.zeros((kernel_size, patch), jnp.bfloat16)

    def first(i, ring, at, ref, u):
        for e in range(QUAD):
            slot = plan_ref[layout.slot + (i * STEP + at) * QUAD + e]
            right = right_ring[ring, at * QUAD + e]
            kern = kern_ref[jnp.maximum(slot, 0)]
            kern = jnp.where(slot >= 0, kern, jnp.zeros_like(kern))
            spread = jnp.concatenate(
                [jnp.concatenate([right, zero], axis=1), jnp.concatenate([zero, right], axis=1)], axis=0
            )
            out = jnp.dot(kern, spread, preferred_element_type=jnp.float32).astype(jnp.bfloat16)
            top = slice(e * 2 * kernel_size, (e * 2 + 1) * kernel_size)
            low = slice((e * 2 + 1) * kernel_size, (e * 2 + 2) * kernel_size)
            ref[u, top, :] = out
            ref[u, low, :patch] = -out[:, patch:]
            ref[u, low, patch:] = out[:, :patch]

    def second(i, ring, at, ref, u):
        left = jnp.concatenate([left_ring[ring, at * QUAD + e] for e in range(QUAD)], axis=1)
        q = plan_ref[layout.anchor + i * STEP + at]
        sums[q] += jnp.dot(left, ref[u], preferred_element_type=jnp.float32)

    if first_part:
        wait(0)
        start(1)
        start(2)
        for u in range(UNROLL):
            first(0, 0, u, mixed[0], u)
    else:
        start(begin + 2)

    @pl.loop(begin, end)
    def _(i):
        here = lax.rem(i, RING)
        there = lax.rem(i + 1, RING)
        start(i + 3)
        wait_new(i + 1)
        for u in range(UNROLL):
            first(i, here, UNROLL + u, mixed[1], u)
            second(i, here, u, mixed[0], u)
        for u in range(UNROLL):
            first(i + 1, there, u, mixed[0], u)
            second(i, here, UNROLL + u, mixed[1], u)

    wait_new(end + 1)
    if not first_part:
        return
    low = lax.broadcasted_iota(jnp.int32, (kernel_size, patch), 1) < kernel_size
    take = functools.partial(strip, sums, row_slots, col_slots, kernel_size)
    for a in range(row_slots + 1):
        real = pltpu.roll(take(0, a, col_slots - 1), kernel_size, 1)
        edge = jnp.where(low, real, take(1, a, col_slots - 1))
        col_ref[a * kernel_size : (a + 1) * kernel_size, :] = edge.astype(col_ref.dtype)


def row_body(before, col_ref, sums, row_ref, *, row_slots, col_slots):
    kernel_size = row_ref.shape[1]
    patch = sums.shape[1]
    low = lax.broadcasted_iota(jnp.int32, (kernel_size, patch), 1) < kernel_size
    take = functools.partial(strip, sums, row_slots, col_slots, kernel_size)
    corner = col_ref[row_slots * kernel_size :, :].astype(jnp.float32)
    for plane in range(2):
        behind = corner if plane == 0 else pltpu.roll(corner, kernel_size, 1)
        for tile in range(col_slots // 2):
            odd = pltpu.roll(take(plane, row_slots, 2 * tile + 1), kernel_size, 1)
            value = take(plane, row_slots, 2 * tile) + jnp.where(low, behind, odd)
            row_ref[plane, :, tile * patch : (tile + 1) * patch] = value.astype(row_ref.dtype)
            behind = odd


def row_halo(sums, col, kernel_size):
    vmem = pl.BlockSpec(memory_space=pltpu.VMEM)
    return pl.pallas_call(
        functools.partial(row_body, row_slots=TILE_U // kernel_size, col_slots=TILE_V // kernel_size),
        in_specs=[vmem] * 2,
        out_specs=[vmem] * 2,
        out_shape=[
            pltpu.VMEM(sums.shape, sums.dtype),
            pltpu.VMEM((2, kernel_size, TILE_V), jnp.bfloat16),
        ],
        input_output_aliases={0: 0},
        compiler_params=pltpu.CompilerParams(vmem_limit_bytes=4 * 2**20),
        name="row_halo",
    )(in_vmem(sums), in_vmem(col))


def grid_part(plan, part, kernels, left, right, carried, layout):
    kernel_size = kernels.shape[1]
    patch = left.shape[1]
    row_slots, col_slots = TILE_U // kernel_size, TILE_V // kernel_size
    smem = pl.BlockSpec(memory_space=pltpu.SMEM)
    vmem = pl.BlockSpec(memory_space=pltpu.VMEM)
    hbm = pl.BlockSpec(memory_space=pl.ANY)
    first_part = carried is None
    carried = [] if first_part else [in_vmem(array) for array in carried]
    mixed_shape = (UNROLL, QUAD * 2 * kernel_size, 2 * patch)
    out_shape = [
        pltpu.VMEM((row_slots * col_slots, patch, 2 * patch), jnp.float32),
        pltpu.VMEM((RING, STEP * QUAD) + left.shape[1:], left.dtype),
        pltpu.VMEM((RING, STEP * QUAD) + right.shape[1:], right.dtype),
        pltpu.VMEM(mixed_shape, jnp.bfloat16),
    ]
    if first_part:
        out_shape.append(pltpu.VMEM((TILE_U + kernel_size, 2 * kernel_size), jnp.bfloat16))
    out = pl.pallas_call(
        functools.partial(
            grid_body,
            part=part,
            first_part=first_part,
            layout=layout,
            row_slots=row_slots,
            col_slots=col_slots,
        ),
        in_specs=[smem, vmem, hbm, hbm] + [vmem] * len(carried),
        out_specs=[vmem] * len(out_shape),
        out_shape=out_shape,
        input_output_aliases={4 + i: i for i in range(len(carried))},
        scratch_shapes=[
            pltpu.VMEM(mixed_shape, jnp.bfloat16),
            pltpu.SemaphoreType.DMA((2, RING)),
        ],
        compiler_params=pltpu.CompilerParams(vmem_limit_bytes=12 * 2**20),
        name="grid_part",
    )(in_smem(plan), in_vmem(kernels), in_hbm(left), in_hbm(right), *carried)
    return out[:4], out[4:]


def merge_body(sums, row_ref, col_ref, out_hbm, out_ref, sems):
    kernel_size = row_ref.shape[1]
    patch = sums.shape[1]
    row_slots = out_ref.shape[1] // kernel_size
    col_slots = out_ref.shape[2] // kernel_size
    low = lax.broadcasted_iota(jnp.int32, (kernel_size, patch), 1) < kernel_size
    take = functools.partial(strip, sums, row_slots, col_slots, kernel_size)
    for a in range(row_slots):
        rows = slice(a * kernel_size, (a + 1) * kernel_size)
        edge = col_ref[rows, :].astype(jnp.float32)
        for plane in range(2):
            behind = edge if plane == 0 else pltpu.roll(edge, kernel_size, 1)
            for tile in range(col_slots // 2):
                lanes = slice(tile * patch, (tile + 1) * patch)
                odd = pltpu.roll(take(plane, a, 2 * tile + 1), kernel_size, 1)
                value = take(plane, a, 2 * tile) + jnp.where(low, behind, odd)
                if a == 0:
                    value = value + row_ref[plane, :, lanes].astype(jnp.float32)
                out_ref[plane, rows, lanes] = value
                behind = odd
        pltpu.make_async_copy(out_ref.at[:, rows], out_hbm.at[:, rows], sems.at[a]).start()
    for a in range(row_slots):
        rows = slice(a * kernel_size, (a + 1) * kernel_size)
        pltpu.make_async_copy(out_ref.at[:, rows], out_hbm.at[:, rows], sems.at[a]).wait()


def merge_tile(sums, row, col):
    vmem = pl.BlockSpec(memory_space=pltpu.VMEM)
    return pl.pallas_call(
        merge_body,
        in_specs=[vmem] * 3,
        out_specs=pl.BlockSpec(memory_space=pl.ANY),
        out_shape=jax.ShapeDtypeStruct((2, TILE_U, TILE_V), jnp.float32),
        scratch_shapes=[
            pltpu.VMEM((2, TILE_U, TILE_V), jnp.float32),
            pltpu.SemaphoreType.DMA((TILE_U // row.shape[1],)),
        ],
        compiler_params=pltpu.CompilerParams(vmem_limit_bytes=8 * 2**20),
        name="merge_tile",
    )(*map(in_vmem, (sums, row, col)))


def shards(
    aperture_amp,
    aperture_phase,
    plane_depths,
    send_list,
    send_count,
    vis_left,
    vis_right,
    block_slot,
    block_pos,
    block_count,
):
    kernel_size = vis_right.shape[1]
    tiles, capacity = send_list.shape[1:]
    both = ("tu", "tv")
    outgoing = make_kernels(
        aperture_amp, aperture_phase, plane_depths, send_list[0].T, send_count, kernel_size
    )
    outgoing = outgoing.reshape((tiles, capacity) + outgoing.shape[1:])
    arrived = lax.all_to_all(outgoing, both, split_axis=0, concat_axis=0, tiled=True)
    received = arrived.reshape((-1,) + arrived.shape[2:])
    layout = Layout(block_pos.shape[0], (TILE_U // kernel_size) * (TILE_V // kernel_size))
    plan, left, right = plan_blocks(block_pos, block_slot, block_count, vis_left, vis_right, layout)
    carried, (col,) = grid_part(plan, 0, received, left, right, None, layout)
    col = from_behind(col, "tv", 1)
    carried, _ = grid_part(plan, 1, received, left, right, carried, layout)
    sums, row = row_halo(carried[0], col, kernel_size)
    row = from_behind(row, "tu", 1)
    carried, _ = grid_part(plan, 2, received, left, right, [sums, *carried[1:]], layout)
    return merge_tile(carried[0], row, col)


def solution(mesh):
    placed = (
        P(("tu", "tv"), None, None),
        P(("tu", "tv"), None, None),
        P(),
        P(("tu", "tv"), None, None),
        P(("tu", "tv"), None),
        P(("tu", "tv"), None, None),
        P(("tu", "tv"), None, None),
        P(("tu", "tv")),
        P(("tu", "tv")),
        P(("tu", "tv")),
    )
    return jax.shard_map(
        shards, mesh=mesh, in_specs=placed, out_specs=P(None, "tu", "tv"), check_vma=False
    )
```

```python
import functools
import math

import jax
import jax.numpy as jnp
import numpy as np
from jax import lax
from jax.experimental import pallas as pl
from jax.experimental.pallas import tpu as pltpu
from jax.sharding import PartitionSpec as P

TILE_U = 256
TILE_V = 512
QUAD = 4
UNROLL = 4
STEP = 2 * UNROLL
RING = 4

def _fit(fn, degree):
    span = math.pi ** 2
    nodes = 0.5 * span * (1.0 - np.cos(np.pi * (np.arange(400) + 0.5) / 400))
    cheb = np.polynomial.chebyshev.Chebyshev.fit(nodes, fn(np.sqrt(nodes)), degree, domain=[0, span])
    return [float(c) for c in cheb.convert(kind=np.polynomial.Polynomial).coef]


COS_POLY = _fit(np.cos, 6)
SIN_POLY = _fit(lambda x: np.sin(x) / x, 5)


def horner(coefs, u):
    total = jnp.full_like(u, coefs[-1])
    for coef in coefs[-2::-1]:
        total = total * u + coef
    return total


def cos_sin(x):
    u = x * x
    return horner(COS_POLY, u), x * horner(SIN_POLY, u)


def from_behind(block, axis, distance):
    devices = range(lax.axis_size(axis))
    route = [(i - distance, i) for i in devices if i - distance in devices]
    return lax.ppermute(block, axis, route)


def in_hbm(array):
    return pltpu.with_memory_space_constraint(array, pltpu.HBM)


def in_vmem(array):
    return pltpu.with_memory_space_constraint(array, pltpu.VMEM)


def in_smem(array):
    return pltpu.with_memory_space_constraint(array, pltpu.SMEM)


def kernels_body(
    list_hbm, count_hbm, depth_hbm, amp_hbm, phase_hbm, out_ref,
    chosen_list, count, depth, amp, phase, table, screen, halves, made, small_sems, bulk_sems,
):
    screens, size, _ = amp.shape
    planes = depth.shape[0]
    kernel_size = out_ref.shape[1]
    small = [
        pltpu.make_async_copy(depth_hbm, depth, small_sems.at[0]),
        pltpu.make_async_copy(list_hbm, chosen_list, small_sems.at[1]),
        pltpu.make_async_copy(count_hbm, count, small_sems.at[2]),
    ]
    for copy in small:
        copy.start()

    def bulk(s):
        return [
            pltpu.make_async_copy(amp_hbm.at[s], amp.at[s], bulk_sems.at[0, s]),
            pltpu.make_async_copy(phase_hbm.at[s], phase.at[s], bulk_sems.at[1, s]),
        ]

    for copy in bulk(0):
        copy.start()

    frequency = lax.broadcasted_iota(jnp.int32, (kernel_size, size), 0) - kernel_size // 2
    cells = lax.broadcasted_iota(jnp.int32, (kernel_size, size), 1)
    turns = frequency.astype(jnp.float32) * cells.astype(jnp.float32) / size
    real_f, imag_f = cos_sin((2.0 * math.pi) * (turns - jnp.round(turns)))
    real_f = real_f.astype(jnp.bfloat16).astype(jnp.float32)
    imag_f = (-imag_f).astype(jnp.bfloat16).astype(jnp.float32)
    place = (lax.broadcasted_iota(jnp.int32, (1, size), 1).astype(jnp.float32) - size // 2) / size
    square = place * place
    for copy in small:
        copy.wait()
    for s in range(1, screens):
        for copy in bulk(s):
            copy.start()
    for p in range(planes):
        turns = depth[p] * square
        real_e, imag_e = cos_sin((2.0 * math.pi) * (turns - jnp.round(turns)))
        real_g = (real_f * real_e - imag_f * imag_e).astype(jnp.bfloat16)
        imag_g = (real_f * imag_e + imag_f * real_e).astype(jnp.bfloat16)
        top = slice(p * 2 * kernel_size, (p * 2 + 1) * kernel_size)
        low = slice((p * 2 + 1) * kernel_size, (p * 2 + 2) * kernel_size)
        table[top, :size] = real_g
        table[top, size:] = -imag_g
        table[low, :size] = imag_g
        table[low, size:] = real_g

    @pl.loop(0, screens)
    def _(s):
        for copy in bulk(s):
            copy.wait()
        magnitude = amp[s].astype(jnp.float32)
        real_e, imag_e = cos_sin(phase[s].astype(jnp.float32))
        screen[:size, :] = (magnitude * real_e).astype(jnp.bfloat16)
        screen[size:, :] = (magnitude * imag_e).astype(jnp.bfloat16)
        product = jnp.dot(table[...], screen[...], preferred_element_type=jnp.float32).astype(jnp.bfloat16)
        for p in range(planes):
            base = p * 2 * kernel_size
            halves[s, p, :, :size] = product[base : base + kernel_size]
            halves[s, p, :, size:] = product[base + kernel_size : base + 2 * kernel_size]

    for p in range(planes):
        second = lax.dot_general(
            jnp.concatenate([halves[s, p] for s in range(screens)], axis=0),
            table[p * 2 * kernel_size : (p + 1) * 2 * kernel_size, :],
            (((1,), (1,)), ((), ())),
            preferred_element_type=jnp.float32,
        )
        second = (second * (1.0 / size)).astype(jnp.bfloat16)
        for s in range(screens):
            made[s * planes + p] = second[s * kernel_size : (s + 1) * kernel_size]

    capacity, tiles = chosen_list.shape

    @pl.loop(0, tiles)
    def _(t):
        for c in range(capacity):
            chosen = made[chosen_list[c, t]]
            out_ref[t * capacity + c] = jnp.where(c < count[0, t], chosen, jnp.zeros_like(chosen))


def make_kernels(aperture_amp, aperture_phase, plane_depths, chosen_list, counts, kernel_size):
    screens, size, _ = aperture_amp.shape
    planes = plane_depths.shape[0]
    capacity, tiles = chosen_list.shape
    hbm = pl.BlockSpec(memory_space=pl.ANY)
    return pl.pallas_call(
        kernels_body,
        in_specs=[hbm] * 5,
        out_specs=pl.BlockSpec(memory_space=pltpu.VMEM),
        out_shape=pltpu.VMEM((tiles * capacity, kernel_size, 2 * kernel_size), jnp.bfloat16),
        scratch_shapes=[
            pltpu.SMEM((capacity, tiles), jnp.int32),
            pltpu.SMEM((1, tiles), jnp.int32),
            pltpu.SMEM((planes,), jnp.float32),
            pltpu.VMEM((screens, size, size), jnp.bfloat16),
            pltpu.VMEM((screens, size, size), jnp.bfloat16),
            pltpu.VMEM((planes * 2 * kernel_size, 2 * size), jnp.bfloat16),
            pltpu.VMEM((2 * size, size), jnp.bfloat16),
            pltpu.VMEM((screens, planes, kernel_size, 2 * size), jnp.bfloat16),
            pltpu.VMEM((screens * planes, kernel_size, 2 * kernel_size), jnp.bfloat16),
            pltpu.SemaphoreType.DMA((3,)),
            pltpu.SemaphoreType.DMA((2, screens)),
        ],
        compiler_params=pltpu.CompilerParams(vmem_limit_bytes=32 * 2**20),
        name="make_kernels",
    )(*map(in_hbm, (chosen_list, counts, plane_depths, aperture_amp, aperture_phase)))


class Layout:
    def __init__(self, blocks, anchors):
        self.parts = 3
        quads = (blocks + (QUAD - 1) * anchors) // QUAD + 1
        self.quads = (quads + STEP - 1) // STEP * STEP
        self.anchor = self.parts + 1
        self.slot = self.anchor + self.quads
        self.total = self.slot + (self.quads + UNROLL) * QUAD


def plan_body(
    pos_ref, slot_ref, count_ref, left_hbm, right_hbm, plan_ref, left_out, right_out,
    left_ref, right_ref, tally, cursor, sems, *, layout, row_slots, col_slots,
):
    anchors = row_slots * col_slots
    border = row_slots + col_slots - 1
    live = count_ref[0]

    def copies(block, place):
        return [
            pltpu.make_async_copy(left_hbm.at[block], left_ref.at[place], sems.at[0]),
            pltpu.make_async_copy(right_hbm.at[block], right_ref.at[place], sems.at[1]),
        ]

    def put(block, place, slot):
        plan_ref[layout.slot + place] = slot
        for copy in copies(block, place):
            copy.start()

    @pl.loop(0, anchors)
    def _(q):
        tally[q] = 0

    @pl.loop(0, live)
    def _(j):
        q = pos_ref[j]
        tally[q] = tally[q] + 1

    def lay(rank, quad):
        inner = rank - border
        q = jnp.where(
            rank < row_slots,
            rank * col_slots + col_slots - 1,
            jnp.where(
                rank < border,
                (row_slots - 1) * col_slots + rank - row_slots,
                (inner // (col_slots - 1)) * col_slots + lax.rem(inner, col_slots - 1),
            ),
        )
        number = tally[q]
        quads = (number + QUAD - 1) // QUAD
        cursor[q] = quad * QUAD

        @pl.loop(0, quads)
        def _(i):
            plan_ref[layout.anchor + quad + i] = q

        @pl.loop(quad * QUAD + number, (quad + quads) * QUAD)
        def _(i):
            put(0, i, -1)

        return quad + quads

    quad = 0
    begin = 0
    plan_ref[0] = 0
    for part, end in enumerate([row_slots, border, anchors]):
        quad = lax.fori_loop(begin, end, lay, quad)
        begin = end
        plan_ref[part + 1] = ((quad + STEP - 1) // STEP) * STEP

    full = ((quad + STEP - 1) // STEP) * STEP

    @pl.loop(quad, full)
    def _(i):
        plan_ref[layout.anchor + i] = 0
        for e in range(QUAD):
            put(0, i * QUAD + e, -1)

    quad = full

    @pl.loop(quad * QUAD, (quad + UNROLL) * QUAD)
    def _(i):
        plan_ref[layout.slot + i] = -1

    @pl.loop(0, live)
    def _(j):
        q = pos_ref[j]
        at = cursor[q]
        cursor[q] = at + 1
        put(j, at, slot_ref[j])

    chunk = STEP * QUAD

    @pl.loop(0, quad // STEP)
    def _(i):
        rows = pl.ds(0, chunk)
        pltpu.make_async_copy(left_hbm.at[rows], left_ref.at[rows], sems.at[0]).wait()
        pltpu.make_async_copy(right_hbm.at[rows], right_ref.at[rows], sems.at[1]).wait()

    def writes(i):
        rows = pl.ds(i * chunk, chunk)
        return [
            pltpu.make_async_copy(left_ref.at[rows], left_out.at[rows], sems.at[2]),
            pltpu.make_async_copy(right_ref.at[rows], right_out.at[rows], sems.at[3]),
        ]

    @pl.loop(0, quad // STEP)
    def _(i):
        for copy in writes(i):
            copy.start()

    @pl.loop(0, quad // STEP)
    def _(i):
        for copy in writes(i):
            copy.wait()


def plan_blocks(block_pos, block_slot, block_count, vis_left, vis_right, layout):
    kernel_size = vis_right.shape[1]
    row_slots, col_slots = TILE_U // kernel_size, TILE_V // kernel_size
    smem = pl.BlockSpec(memory_space=pltpu.SMEM)
    hbm = pl.BlockSpec(memory_space=pl.ANY)
    places = layout.quads * QUAD
    return pl.pallas_call(
        functools.partial(plan_body, layout=layout, row_slots=row_slots, col_slots=col_slots),
        in_specs=[smem] * 3 + [hbm] * 2,
        out_specs=[smem, hbm, hbm],
        out_shape=[
            pltpu.SMEM((layout.total,), jnp.int32),
            pltpu.HBM((places,) + vis_left.shape[1:], vis_left.dtype),
            pltpu.HBM((places,) + vis_right.shape[1:], vis_right.dtype),
        ],
        scratch_shapes=[
            pltpu.VMEM((places,) + vis_left.shape[1:], vis_left.dtype),
            pltpu.VMEM((places,) + vis_right.shape[1:], vis_right.dtype),
            pltpu.SMEM((row_slots * col_slots,), jnp.int32),
            pltpu.SMEM((row_slots * col_slots,), jnp.int32),
            pltpu.SemaphoreType.DMA((4,)),
        ],
        compiler_params=pltpu.CompilerParams(vmem_limit_bytes=36 * 2**20),
        name="plan_blocks",
    )(block_pos, block_slot, block_count, in_hbm(vis_left), in_hbm(vis_right))


def strip(sums, row_slots, col_slots, kernel_size, plane, a, col):
    patch = sums.shape[1]
    lanes = slice(plane * patch, (plane + 1) * patch)
    total = None
    if a < row_slots:
        total = sums[a * col_slots + col, :kernel_size, lanes]
    if a > 0:
        above = sums[(a - 1) * col_slots + col, kernel_size:, lanes]
        total = above if total is None else total + above
    return total


def grid_body(
    plan_ref, kern_ref, left_hbm, right_hbm, *rest, part, first_part, layout, row_slots, col_slots
):
    if not first_part:
        rest = rest[4:]
    sums, left_ring, right_ring, ahead, *rest = rest
    if first_part:
        col_ref, *rest = rest
    behind_ref, sems = rest
    mixed = (ahead, behind_ref)
    slots, kernel_size, _ = kern_ref.shape
    patch = left_hbm.shape[1]
    chunk = STEP * QUAD
    begin = plan_ref[part] // STEP
    end = plan_ref[part + 1] // STEP
    limit = jnp.minimum(plan_ref[layout.parts] // STEP, end + 2)

    def fetch(i):
        source = pl.ds(i * chunk, chunk)
        ring = lax.rem(i, RING)
        return [
            pltpu.make_async_copy(left_hbm.at[source], left_ring.at[ring], sems.at[0, ring]),
            pltpu.make_async_copy(right_hbm.at[source], right_ring.at[ring], sems.at[1, ring]),
        ]

    def start(i):
        @pl.when(i < limit)
        def _():
            for copy in reversed(fetch(i)):
                copy.start()

    def wait_new(i):
        if first_part:
            wait(i)
        else:
            pl.when(i > begin + 1)(lambda: wait(i))

    def wait(i):
        @pl.when(i < limit)
        def _():
            for copy in fetch(i):
                copy.wait()

    if first_part:
        start(0)

        @pl.loop(0, sums.shape[0])
        def _(q):
            sums[q] = jnp.zeros(sums.shape[1:], sums.dtype)

    zero = jnp.zeros((kernel_size, patch), jnp.bfloat16)

    def first(i, ring, at, ref, u):
        for e in range(QUAD):
            slot = plan_ref[layout.slot + (i * STEP + at) * QUAD + e]
            right = right_ring[ring, at * QUAD + e]
            kern = kern_ref[jnp.maximum(slot, 0)]
            kern = jnp.where(slot >= 0, kern, jnp.zeros_like(kern))
            spread = jnp.concatenate(
                [jnp.concatenate([right, zero], axis=1), jnp.concatenate([zero, right], axis=1)], axis=0
            )
            out = jnp.dot(kern, spread, preferred_element_type=jnp.float32).astype(jnp.bfloat16)
            top = slice(e * 2 * kernel_size, (e * 2 + 1) * kernel_size)
            low = slice((e * 2 + 1) * kernel_size, (e * 2 + 2) * kernel_size)
            ref[u, top, :] = out
            ref[u, low, :patch] = -out[:, patch:]
            ref[u, low, patch:] = out[:, :patch]

    def second(i, ring, at, ref, u):
        left = jnp.concatenate([left_ring[ring, at * QUAD + e] for e in range(QUAD)], axis=1)
        q = plan_ref[layout.anchor + i * STEP + at]
        sums[q] += jnp.dot(left, ref[u], preferred_element_type=jnp.float32)

    if first_part:
        fetch(0)[1].wait()
        start(1)
        for u in range(UNROLL):
            first(0, 0, u, mixed[0], u)
        fetch(0)[0].wait()
        start(2)
    else:
        start(begin + 2)

    @pl.loop(begin, end)
    def _(i):
        here = lax.rem(i, RING)
        there = lax.rem(i + 1, RING)
        start(i + 3)
        wait_new(i + 1)
        for u in range(UNROLL):
            first(i, here, UNROLL + u, mixed[1], u)
            second(i, here, u, mixed[0], u)
        for u in range(UNROLL):
            first(i + 1, there, u, mixed[0], u)
            second(i, here, UNROLL + u, mixed[1], u)

    wait_new(end + 1)
    if not first_part:
        return
    low = lax.broadcasted_iota(jnp.int32, (kernel_size, patch), 1) < kernel_size
    take = functools.partial(strip, sums, row_slots, col_slots, kernel_size)
    for a in range(row_slots + 1):
        real = pltpu.roll(take(0, a, col_slots - 1), kernel_size, 1)
        edge = jnp.where(low, real, take(1, a, col_slots - 1))
        col_ref[a * kernel_size : (a + 1) * kernel_size, :] = edge.astype(col_ref.dtype)


def row_body(before, col_ref, sums, row_ref, *, row_slots, col_slots):
    kernel_size = row_ref.shape[1]
    patch = sums.shape[1]
    low = lax.broadcasted_iota(jnp.int32, (kernel_size, patch), 1) < kernel_size
    take = functools.partial(strip, sums, row_slots, col_slots, kernel_size)
    corner = col_ref[row_slots * kernel_size :, :].astype(jnp.float32)
    for plane in range(2):
        behind = corner if plane == 0 else pltpu.roll(corner, kernel_size, 1)
        for tile in range(col_slots // 2):
            odd = pltpu.roll(take(plane, row_slots, 2 * tile + 1), kernel_size, 1)
            value = take(plane, row_slots, 2 * tile) + jnp.where(low, behind, odd)
            row_ref[plane, :, tile * patch : (tile + 1) * patch] = value.astype(row_ref.dtype)
            behind = odd


def row_halo(sums, col, kernel_size):
    vmem = pl.BlockSpec(memory_space=pltpu.VMEM)
    return pl.pallas_call(
        functools.partial(row_body, row_slots=TILE_U // kernel_size, col_slots=TILE_V // kernel_size),
        in_specs=[vmem] * 2,
        out_specs=[vmem] * 2,
        out_shape=[
            pltpu.VMEM(sums.shape, sums.dtype),
            pltpu.VMEM((2, kernel_size, TILE_V), jnp.bfloat16),
        ],
        input_output_aliases={0: 0},
        compiler_params=pltpu.CompilerParams(vmem_limit_bytes=4 * 2**20),
        name="row_halo",
    )(in_vmem(sums), in_vmem(col))


def grid_part(plan, part, kernels, left, right, carried, layout):
    kernel_size = kernels.shape[1]
    patch = left.shape[1]
    row_slots, col_slots = TILE_U // kernel_size, TILE_V // kernel_size
    smem = pl.BlockSpec(memory_space=pltpu.SMEM)
    vmem = pl.BlockSpec(memory_space=pltpu.VMEM)
    hbm = pl.BlockSpec(memory_space=pl.ANY)
    first_part = carried is None
    carried = [] if first_part else [in_vmem(array) for array in carried]
    mixed_shape = (UNROLL, QUAD * 2 * kernel_size, 2 * patch)
    out_shape = [
        pltpu.VMEM((row_slots * col_slots, patch, 2 * patch), jnp.float32),
        pltpu.VMEM((RING, STEP * QUAD) + left.shape[1:], left.dtype),
        pltpu.VMEM((RING, STEP * QUAD) + right.shape[1:], right.dtype),
        pltpu.VMEM(mixed_shape, jnp.bfloat16),
    ]
    if first_part:
        out_shape.append(pltpu.VMEM((TILE_U + kernel_size, 2 * kernel_size), jnp.bfloat16))
    out = pl.pallas_call(
        functools.partial(
            grid_body,
            part=part,
            first_part=first_part,
            layout=layout,
            row_slots=row_slots,
            col_slots=col_slots,
        ),
        in_specs=[smem, vmem, hbm, hbm] + [vmem] * len(carried),
        out_specs=[vmem] * len(out_shape),
        out_shape=out_shape,
        input_output_aliases={4 + i: i for i in range(len(carried))},
        scratch_shapes=[
            pltpu.VMEM(mixed_shape, jnp.bfloat16),
            pltpu.SemaphoreType.DMA((2, RING)),
        ],
        compiler_params=pltpu.CompilerParams(vmem_limit_bytes=12 * 2**20),
        name="grid_part",
    )(in_smem(plan), in_vmem(kernels), in_hbm(left), in_hbm(right), *carried)
    return out[:4], out[4:]


def merge_body(sums, row_ref, col_ref, out_hbm, out_ref, sems):
    kernel_size = row_ref.shape[1]
    patch = sums.shape[1]
    row_slots = out_ref.shape[1] // kernel_size
    col_slots = out_ref.shape[2] // kernel_size
    low = lax.broadcasted_iota(jnp.int32, (kernel_size, patch), 1) < kernel_size
    take = functools.partial(strip, sums, row_slots, col_slots, kernel_size)
    for a in range(row_slots):
        rows = slice(a * kernel_size, (a + 1) * kernel_size)
        edge = col_ref[rows, :].astype(jnp.float32)
        for plane in range(2):
            behind = edge if plane == 0 else pltpu.roll(edge, kernel_size, 1)
            for tile in range(col_slots // 2):
                lanes = slice(tile * patch, (tile + 1) * patch)
                odd = pltpu.roll(take(plane, a, 2 * tile + 1), kernel_size, 1)
                value = take(plane, a, 2 * tile) + jnp.where(low, behind, odd)
                if a == 0:
                    value = value + row_ref[plane, :, lanes].astype(jnp.float32)
                out_ref[plane, rows, lanes] = value
                behind = odd
        pltpu.make_async_copy(out_ref.at[:, rows], out_hbm.at[:, rows], sems.at[a]).start()
    for a in range(row_slots):
        rows = slice(a * kernel_size, (a + 1) * kernel_size)
        pltpu.make_async_copy(out_ref.at[:, rows], out_hbm.at[:, rows], sems.at[a]).wait()


def merge_tile(sums, row, col):
    vmem = pl.BlockSpec(memory_space=pltpu.VMEM)
    return pl.pallas_call(
        merge_body,
        in_specs=[vmem] * 3,
        out_specs=pl.BlockSpec(memory_space=pl.ANY),
        out_shape=jax.ShapeDtypeStruct((2, TILE_U, TILE_V), jnp.float32),
        scratch_shapes=[
            pltpu.VMEM((2, TILE_U, TILE_V), jnp.float32),
            pltpu.SemaphoreType.DMA((TILE_U // row.shape[1],)),
        ],
        compiler_params=pltpu.CompilerParams(vmem_limit_bytes=8 * 2**20),
        name="merge_tile",
    )(*map(in_vmem, (sums, row, col)))


def shards(
    aperture_amp,
    aperture_phase,
    plane_depths,
    send_list,
    send_count,
    vis_left,
    vis_right,
    block_slot,
    block_pos,
    block_count,
):
    kernel_size = vis_right.shape[1]
    tiles, capacity = send_list.shape[1:]
    both = ("tu", "tv")
    outgoing = make_kernels(
        aperture_amp, aperture_phase, plane_depths, send_list[0].T, send_count, kernel_size
    )
    outgoing = outgoing.reshape((tiles, capacity) + outgoing.shape[1:])
    arrived = lax.all_to_all(outgoing, both, split_axis=0, concat_axis=0, tiled=True)
    received = arrived.reshape((-1,) + arrived.shape[2:])
    layout = Layout(block_pos.shape[0], (TILE_U // kernel_size) * (TILE_V // kernel_size))
    plan, left, right = plan_blocks(block_pos, block_slot, block_count, vis_left, vis_right, layout)
    carried, (col,) = grid_part(plan, 0, received, left, right, None, layout)
    col = from_behind(col, "tv", 1)
    carried, _ = grid_part(plan, 1, received, left, right, carried, layout)
    sums, row = row_halo(carried[0], col, kernel_size)
    row = from_behind(row, "tu", 1)
    carried, _ = grid_part(plan, 2, received, left, right, [sums, *carried[1:]], layout)
    return merge_tile(carried[0], row, col)


def solution(mesh):
    placed = (
        P(("tu", "tv"), None, None),
        P(("tu", "tv"), None, None),
        P(),
        P(("tu", "tv"), None, None),
        P(("tu", "tv"), None),
        P(("tu", "tv"), None, None),
        P(("tu", "tv"), None, None),
        P(("tu", "tv")),
        P(("tu", "tv")),
        P(("tu", "tv")),
    )
    return jax.shard_map(
        shards, mesh=mesh, in_specs=placed, out_specs=P(None, "tu", "tv"), check_vma=False
    )
```

```python
import functools
import math

import jax
import jax.numpy as jnp
import numpy as np
from jax import lax
from jax.experimental import pallas as pl
from jax.experimental.pallas import tpu as pltpu
from jax.sharding import PartitionSpec as P

TILE_U = 256
TILE_V = 512
QUAD = 4
UNROLL = 4
STEP = 2 * UNROLL
RING = 4
LEFT, RIGHT = 0, 1

def _fit(fn, degree):
    span = math.pi ** 2
    nodes = 0.5 * span * (1.0 - np.cos(np.pi * (np.arange(400) + 0.5) / 400))
    cheb = np.polynomial.chebyshev.Chebyshev.fit(nodes, fn(np.sqrt(nodes)), degree, domain=[0, span])
    return [float(c) for c in cheb.convert(kind=np.polynomial.Polynomial).coef]


COS_POLY = _fit(np.cos, 6)
SIN_POLY = _fit(lambda x: np.sin(x) / x, 5)


def horner(coefs, u):
    total = jnp.full_like(u, coefs[-1])
    for coef in coefs[-2::-1]:
        total = total * u + coef
    return total


def cos_sin(x):
    u = x * x
    return horner(COS_POLY, u), x * horner(SIN_POLY, u)


def from_behind(block, axis, distance):
    devices = range(lax.axis_size(axis))
    route = [(i - distance, i) for i in devices if i - distance in devices]
    return lax.ppermute(block, axis, route)


def in_hbm(array):
    return pltpu.with_memory_space_constraint(array, pltpu.HBM)


def in_vmem(array):
    return pltpu.with_memory_space_constraint(array, pltpu.VMEM)


def in_smem(array):
    return pltpu.with_memory_space_constraint(array, pltpu.SMEM)


def kernels_body(
    list_hbm, count_hbm, depth_hbm, amp_hbm, phase_hbm, out_ref,
    chosen_list, count, depth, amp, phase, table, screen, halves, made, small_sems, bulk_sems,
):
    screens, size, _ = amp.shape
    planes = depth.shape[0]
    kernel_size = out_ref.shape[1]
    small = [
        pltpu.make_async_copy(depth_hbm, depth, small_sems.at[0]),
        pltpu.make_async_copy(list_hbm, chosen_list, small_sems.at[1]),
        pltpu.make_async_copy(count_hbm, count, small_sems.at[2]),
    ]
    for copy in small:
        copy.start()

    def bulk(s):
        return [
            pltpu.make_async_copy(amp_hbm.at[s], amp.at[s], bulk_sems.at[0, s]),
            pltpu.make_async_copy(phase_hbm.at[s], phase.at[s], bulk_sems.at[1, s]),
        ]

    for copy in bulk(0):
        copy.start()

    frequency = lax.broadcasted_iota(jnp.int32, (kernel_size, size), 0) - kernel_size // 2
    cells = lax.broadcasted_iota(jnp.int32, (kernel_size, size), 1)
    turns = frequency.astype(jnp.float32) * cells.astype(jnp.float32) / size
    real_f, imag_f = cos_sin((2.0 * math.pi) * (turns - jnp.round(turns)))
    real_f = real_f.astype(jnp.bfloat16).astype(jnp.float32)
    imag_f = (-imag_f).astype(jnp.bfloat16).astype(jnp.float32)
    place = (lax.broadcasted_iota(jnp.int32, (1, size), 1).astype(jnp.float32) - size // 2) / size
    square = place * place
    for copy in small:
        copy.wait()
    for s in range(1, screens):
        for copy in bulk(s):
            copy.start()
    for p in range(planes):
        turns = depth[p] * square
        real_e, imag_e = cos_sin((2.0 * math.pi) * (turns - jnp.round(turns)))
        real_g = (real_f * real_e - imag_f * imag_e).astype(jnp.bfloat16)
        imag_g = (real_f * imag_e + imag_f * real_e).astype(jnp.bfloat16)
        top = slice(p * 2 * kernel_size, (p * 2 + 1) * kernel_size)
        low = slice((p * 2 + 1) * kernel_size, (p * 2 + 2) * kernel_size)
        table[top, :size] = real_g
        table[top, size:] = -imag_g
        table[low, :size] = imag_g
        table[low, size:] = real_g

    @pl.loop(0, screens)
    def _(s):
        for copy in bulk(s):
            copy.wait()
        magnitude = amp[s].astype(jnp.float32)
        real_e, imag_e = cos_sin(phase[s].astype(jnp.float32))
        screen[:size, :] = (magnitude * real_e).astype(jnp.bfloat16)
        screen[size:, :] = (magnitude * imag_e).astype(jnp.bfloat16)
        product = jnp.dot(table[...], screen[...], preferred_element_type=jnp.float32).astype(jnp.bfloat16)
        for p in range(planes):
            base = p * 2 * kernel_size
            halves[s, p, :, :size] = product[base : base + kernel_size]
            halves[s, p, :, size:] = product[base + kernel_size : base + 2 * kernel_size]

    for p in range(planes):
        second = lax.dot_general(
            jnp.concatenate([halves[s, p] for s in range(screens)], axis=0),
            table[p * 2 * kernel_size : (p + 1) * 2 * kernel_size, :],
            (((1,), (1,)), ((), ())),
            preferred_element_type=jnp.float32,
        )
        second = (second * (1.0 / size)).astype(jnp.bfloat16)
        for s in range(screens):
            made[s * planes + p] = second[s * kernel_size : (s + 1) * kernel_size]

    capacity, tiles = chosen_list.shape

    @pl.loop(0, tiles)
    def _(t):
        for c in range(capacity):
            chosen = made[chosen_list[c, t]]
            out_ref[t * capacity + c] = jnp.where(c < count[0, t], chosen, jnp.zeros_like(chosen))


def make_kernels(aperture_amp, aperture_phase, plane_depths, chosen_list, counts, kernel_size):
    screens, size, _ = aperture_amp.shape
    planes = plane_depths.shape[0]
    capacity, tiles = chosen_list.shape
    hbm = pl.BlockSpec(memory_space=pl.ANY)
    return pl.pallas_call(
        kernels_body,
        in_specs=[hbm] * 5,
        out_specs=pl.BlockSpec(memory_space=pltpu.VMEM),
        out_shape=pltpu.VMEM((tiles * capacity, kernel_size, 2 * kernel_size), jnp.bfloat16),
        scratch_shapes=[
            pltpu.SMEM((capacity, tiles), jnp.int32),
            pltpu.SMEM((1, tiles), jnp.int32),
            pltpu.SMEM((planes,), jnp.float32),
            pltpu.VMEM((screens, size, size), jnp.bfloat16),
            pltpu.VMEM((screens, size, size), jnp.bfloat16),
            pltpu.VMEM((planes * 2 * kernel_size, 2 * size), jnp.bfloat16),
            pltpu.VMEM((2 * size, size), jnp.bfloat16),
            pltpu.VMEM((screens, planes, kernel_size, 2 * size), jnp.bfloat16),
            pltpu.VMEM((screens * planes, kernel_size, 2 * kernel_size), jnp.bfloat16),
            pltpu.SemaphoreType.DMA((3,)),
            pltpu.SemaphoreType.DMA((2, screens)),
        ],
        compiler_params=pltpu.CompilerParams(vmem_limit_bytes=32 * 2**20),
        name="make_kernels",
    )(*map(in_hbm, (chosen_list, counts, plane_depths, aperture_amp, aperture_phase)))


class Layout:
    def __init__(self, blocks, anchors):
        self.parts = 3
        quads = (blocks + (QUAD - 1) * anchors) // QUAD + 1
        self.quads = (quads + STEP - 1) // STEP * STEP
        self.anchor = self.parts + 1
        self.slot = self.anchor + self.quads
        self.total = self.slot + (self.quads + UNROLL) * QUAD


def plan_body(
    pos_ref, slot_ref, count_ref, left_hbm, right_hbm, plan_ref, left_out, right_out,
    left_ref, right_ref, tally, cursor, sems, *, layout, row_slots, col_slots,
):
    anchors = row_slots * col_slots
    border = row_slots + col_slots - 1
    live = count_ref[0]

    def copies(block, place):
        return [
            pltpu.make_async_copy(left_hbm.at[block], left_ref.at[place], sems.at[0]),
            pltpu.make_async_copy(right_hbm.at[block], right_ref.at[place], sems.at[1]),
        ]

    def put(block, place, slot):
        plan_ref[layout.slot + place] = slot
        for copy in copies(block, place):
            copy.start()

    @pl.loop(0, anchors)
    def _(q):
        tally[q] = 0

    @pl.loop(0, live)
    def _(j):
        q = pos_ref[j]
        tally[q] = tally[q] + 1

    def lay(rank, quad):
        inner = rank - border
        q = jnp.where(
            rank < row_slots,
            rank * col_slots + col_slots - 1,
            jnp.where(
                rank < border,
                (row_slots - 1) * col_slots + rank - row_slots,
                (inner // (col_slots - 1)) * col_slots + lax.rem(inner, col_slots - 1),
            ),
        )
        number = tally[q]
        quads = (number + QUAD - 1) // QUAD
        cursor[q] = quad * QUAD

        @pl.loop(0, quads)
        def _(i):
            plan_ref[layout.anchor + quad + i] = q

        @pl.loop(quad * QUAD + number, (quad + quads) * QUAD)
        def _(i):
            put(0, i, -1)

        return quad + quads

    quad = 0
    begin = 0
    plan_ref[0] = 0
    for part, end in enumerate([row_slots, border, anchors]):
        quad = lax.fori_loop(begin, end, lay, quad)
        begin = end
        plan_ref[part + 1] = ((quad + STEP - 1) // STEP) * STEP

    full = ((quad + STEP - 1) // STEP) * STEP

    @pl.loop(quad, full)
    def _(i):
        plan_ref[layout.anchor + i] = 0
        for e in range(QUAD):
            put(0, i * QUAD + e, -1)

    quad = full

    @pl.loop(quad * QUAD, (quad + UNROLL) * QUAD)
    def _(i):
        plan_ref[layout.slot + i] = -1

    @pl.loop(0, live)
    def _(j):
        q = pos_ref[j]
        at = cursor[q]
        cursor[q] = at + 1
        put(j, at, slot_ref[j])

    chunk = STEP * QUAD

    @pl.loop(0, quad // STEP)
    def _(i):
        rows = pl.ds(0, chunk)
        pltpu.make_async_copy(left_hbm.at[rows], left_ref.at[rows], sems.at[0]).wait()
        pltpu.make_async_copy(right_hbm.at[rows], right_ref.at[rows], sems.at[1]).wait()

    def writes(i):
        rows = pl.ds(i * chunk, chunk)
        return [
            pltpu.make_async_copy(left_ref.at[rows], left_out.at[rows], sems.at[2]),
            pltpu.make_async_copy(right_ref.at[rows], right_out.at[rows], sems.at[3]),
        ]

    @pl.loop(0, quad // STEP)
    def _(i):
        for copy in writes(i):
            copy.start()

    @pl.loop(0, quad // STEP)
    def _(i):
        for copy in writes(i):
            copy.wait()


def plan_blocks(block_pos, block_slot, block_count, vis_left, vis_right, layout):
    kernel_size = vis_right.shape[1]
    row_slots, col_slots = TILE_U // kernel_size, TILE_V // kernel_size
    smem = pl.BlockSpec(memory_space=pltpu.SMEM)
    hbm = pl.BlockSpec(memory_space=pl.ANY)
    places = layout.quads * QUAD
    return pl.pallas_call(
        functools.partial(plan_body, layout=layout, row_slots=row_slots, col_slots=col_slots),
        in_specs=[smem] * 3 + [hbm] * 2,
        out_specs=[smem, hbm, hbm],
        out_shape=[
            pltpu.SMEM((layout.total,), jnp.int32),
            pltpu.HBM((places,) + vis_left.shape[1:], vis_left.dtype),
            pltpu.HBM((places,) + vis_right.shape[1:], vis_right.dtype),
        ],
        scratch_shapes=[
            pltpu.VMEM((places,) + vis_left.shape[1:], vis_left.dtype),
            pltpu.VMEM((places,) + vis_right.shape[1:], vis_right.dtype),
            pltpu.SMEM((row_slots * col_slots,), jnp.int32),
            pltpu.SMEM((row_slots * col_slots,), jnp.int32),
            pltpu.SemaphoreType.DMA((4,)),
        ],
        compiler_params=pltpu.CompilerParams(vmem_limit_bytes=36 * 2**20),
        name="plan_blocks",
    )(block_pos, block_slot, block_count, in_hbm(vis_left), in_hbm(vis_right))


def strip(sums, row_slots, col_slots, kernel_size, plane, a, col):
    patch = sums.shape[1]
    lanes = slice(plane * patch, (plane + 1) * patch)
    total = None
    if a < row_slots:
        total = sums[a * col_slots + col, :kernel_size, lanes]
    if a > 0:
        above = sums[(a - 1) * col_slots + col, kernel_size:, lanes]
        total = above if total is None else total + above
    return total


def grid_body(
    plan_ref, kern_ref, left_hbm, right_hbm, *rest, part, first_part, layout, row_slots, col_slots
):
    if not first_part:
        rest = rest[4:]
    sums, left_ring, right_ring, ahead, *rest = rest
    if first_part:
        col_ref, *rest = rest
    behind_ref, sems = rest
    mixed = (ahead, behind_ref)
    slots, kernel_size, _ = kern_ref.shape
    patch = left_hbm.shape[1]
    chunk = STEP * QUAD
    begin = plan_ref[part] // STEP
    end = plan_ref[part + 1] // STEP
    limit = jnp.minimum(plan_ref[layout.parts] // STEP, end + 2)

    def fetch(i):
        source = pl.ds(i * chunk, chunk)
        ring = lax.rem(i, RING)
        return [
            pltpu.make_async_copy(left_hbm.at[source], left_ring.at[ring], sems.at[0, ring]),
            pltpu.make_async_copy(right_hbm.at[source], right_ring.at[ring], sems.at[1, ring]),
        ]

    def start(i, which):
        @pl.when(i < limit)
        def _():
            fetch(i)[which].start()

    def wait(i, which):
        fresh = (i < limit) if first_part else ((i < limit) & (i > begin + 1))

        @pl.when(fresh)
        def _():
            fetch(i)[which].wait()

    if first_part:
        start(0, RIGHT)
        start(1, RIGHT)
        start(0, LEFT)

        @pl.loop(0, sums.shape[0])
        def _(q):
            sums[q] = jnp.zeros(sums.shape[1:], sums.dtype)

    zero = jnp.zeros((kernel_size, patch), jnp.bfloat16)

    def first(i, ring, at, ref, u):
        for e in range(QUAD):
            slot = plan_ref[layout.slot + (i * STEP + at) * QUAD + e]
            right = right_ring[ring, at * QUAD + e]
            kern = kern_ref[jnp.maximum(slot, 0)]
            kern = jnp.where(slot >= 0, kern, jnp.zeros_like(kern))
            spread = jnp.concatenate(
                [jnp.concatenate([right, zero], axis=1), jnp.concatenate([zero, right], axis=1)], axis=0
            )
            out = jnp.dot(kern, spread, preferred_element_type=jnp.float32).astype(jnp.bfloat16)
            top = slice(e * 2 * kernel_size, (e * 2 + 1) * kernel_size)
            low = slice((e * 2 + 1) * kernel_size, (e * 2 + 2) * kernel_size)
            ref[u, top, :] = out
            ref[u, low, :patch] = -out[:, patch:]
            ref[u, low, patch:] = out[:, :patch]

    def second(i, ring, at, ref, u):
        left = jnp.concatenate([left_ring[ring, at * QUAD + e] for e in range(QUAD)], axis=1)
        q = plan_ref[layout.anchor + i * STEP + at]
        sums[q] += jnp.dot(left, ref[u], preferred_element_type=jnp.float32)

    if first_part:
        wait(0, RIGHT)
        start(1, LEFT)
        for u in range(UNROLL):
            first(0, 0, u, mixed[0], u)
    start(begin + 2, RIGHT)
    start(begin + 2, LEFT)

    @pl.loop(begin, end)
    def _(i):
        here = lax.rem(i, RING)
        there = lax.rem(i + 1, RING)
        start(i + 3, RIGHT)
        start(i + 3, LEFT)
        wait(i, LEFT)
        wait(i + 1, RIGHT)
        for u in range(UNROLL):
            first(i, here, UNROLL + u, mixed[1], u)
            second(i, here, u, mixed[0], u)
        for u in range(UNROLL):
            first(i + 1, there, u, mixed[0], u)
            second(i, here, UNROLL + u, mixed[1], u)

    wait(end, LEFT)
    wait(end + 1, LEFT)
    wait(end + 1, RIGHT)
    if not first_part:
        return
    low = lax.broadcasted_iota(jnp.int32, (kernel_size, patch), 1) < kernel_size
    take = functools.partial(strip, sums, row_slots, col_slots, kernel_size)
    for a in range(row_slots + 1):
        real = pltpu.roll(take(0, a, col_slots - 1), kernel_size, 1)
        edge = jnp.where(low, real, take(1, a, col_slots - 1))
        col_ref[a * kernel_size : (a + 1) * kernel_size, :] = edge.astype(col_ref.dtype)


def row_body(before, col_ref, sums, row_ref, *, row_slots, col_slots):
    kernel_size = row_ref.shape[1]
    patch = sums.shape[1]
    low = lax.broadcasted_iota(jnp.int32, (kernel_size, patch), 1) < kernel_size
    take = functools.partial(strip, sums, row_slots, col_slots, kernel_size)
    corner = col_ref[row_slots * kernel_size :, :].astype(jnp.float32)
    for plane in range(2):
        behind = corner if plane == 0 else pltpu.roll(corner, kernel_size, 1)
        for tile in range(col_slots // 2):
            odd = pltpu.roll(take(plane, row_slots, 2 * tile + 1), kernel_size, 1)
            value = take(plane, row_slots, 2 * tile) + jnp.where(low, behind, odd)
            row_ref[plane, :, tile * patch : (tile + 1) * patch] = value.astype(row_ref.dtype)
            behind = odd


def row_halo(sums, col, kernel_size):
    vmem = pl.BlockSpec(memory_space=pltpu.VMEM)
    return pl.pallas_call(
        functools.partial(row_body, row_slots=TILE_U // kernel_size, col_slots=TILE_V // kernel_size),
        in_specs=[vmem] * 2,
        out_specs=[vmem] * 2,
        out_shape=[
            pltpu.VMEM(sums.shape, sums.dtype),
            pltpu.VMEM((2, kernel_size, TILE_V), jnp.bfloat16),
        ],
        input_output_aliases={0: 0},
        compiler_params=pltpu.CompilerParams(vmem_limit_bytes=4 * 2**20),
        name="row_halo",
    )(in_vmem(sums), in_vmem(col))


def grid_part(plan, part, kernels, left, right, carried, layout):
    kernel_size = kernels.shape[1]
    patch = left.shape[1]
    row_slots, col_slots = TILE_U // kernel_size, TILE_V // kernel_size
    smem = pl.BlockSpec(memory_space=pltpu.SMEM)
    vmem = pl.BlockSpec(memory_space=pltpu.VMEM)
    hbm = pl.BlockSpec(memory_space=pl.ANY)
    first_part = carried is None
    carried = [] if first_part else [in_vmem(array) for array in carried]
    mixed_shape = (UNROLL, QUAD * 2 * kernel_size, 2 * patch)
    out_shape = [
        pltpu.VMEM((row_slots * col_slots, patch, 2 * patch), jnp.float32),
        pltpu.VMEM((RING, STEP * QUAD) + left.shape[1:], left.dtype),
        pltpu.VMEM((RING, STEP * QUAD) + right.shape[1:], right.dtype),
        pltpu.VMEM(mixed_shape, jnp.bfloat16),
    ]
    if first_part:
        out_shape.append(pltpu.VMEM((TILE_U + kernel_size, 2 * kernel_size), jnp.bfloat16))
    out = pl.pallas_call(
        functools.partial(
            grid_body,
            part=part,
            first_part=first_part,
            layout=layout,
            row_slots=row_slots,
            col_slots=col_slots,
        ),
        in_specs=[smem, vmem, hbm, hbm] + [vmem] * len(carried),
        out_specs=[vmem] * len(out_shape),
        out_shape=out_shape,
        input_output_aliases={4 + i: i for i in range(len(carried))},
        scratch_shapes=[
            pltpu.VMEM(mixed_shape, jnp.bfloat16),
            pltpu.SemaphoreType.DMA((2, RING)),
        ],
        compiler_params=pltpu.CompilerParams(vmem_limit_bytes=12 * 2**20),
        name="grid_part",
    )(in_smem(plan), in_vmem(kernels), in_hbm(left), in_hbm(right), *carried)
    return out[:4], out[4:]


def merge_body(sums, row_ref, col_ref, out_hbm, out_ref, sems):
    kernel_size = row_ref.shape[1]
    patch = sums.shape[1]
    row_slots = out_ref.shape[1] // kernel_size
    col_slots = out_ref.shape[2] // kernel_size
    low = lax.broadcasted_iota(jnp.int32, (kernel_size, patch), 1) < kernel_size
    take = functools.partial(strip, sums, row_slots, col_slots, kernel_size)
    for a in range(row_slots):
        rows = slice(a * kernel_size, (a + 1) * kernel_size)
        edge = col_ref[rows, :].astype(jnp.float32)
        for plane in range(2):
            behind = edge if plane == 0 else pltpu.roll(edge, kernel_size, 1)
            for tile in range(col_slots // 2):
                lanes = slice(tile * patch, (tile + 1) * patch)
                odd = pltpu.roll(take(plane, a, 2 * tile + 1), kernel_size, 1)
                value = take(plane, a, 2 * tile) + jnp.where(low, behind, odd)
                if a == 0:
                    value = value + row_ref[plane, :, lanes].astype(jnp.float32)
                out_ref[plane, rows, lanes] = value
                behind = odd
        pltpu.make_async_copy(out_ref.at[:, rows], out_hbm.at[:, rows], sems.at[a]).start()
    for a in range(row_slots):
        rows = slice(a * kernel_size, (a + 1) * kernel_size)
        pltpu.make_async_copy(out_ref.at[:, rows], out_hbm.at[:, rows], sems.at[a]).wait()


def merge_tile(sums, row, col):
    vmem = pl.BlockSpec(memory_space=pltpu.VMEM)
    return pl.pallas_call(
        merge_body,
        in_specs=[vmem] * 3,
        out_specs=pl.BlockSpec(memory_space=pl.ANY),
        out_shape=jax.ShapeDtypeStruct((2, TILE_U, TILE_V), jnp.float32),
        scratch_shapes=[
            pltpu.VMEM((2, TILE_U, TILE_V), jnp.float32),
            pltpu.SemaphoreType.DMA((TILE_U // row.shape[1],)),
        ],
        compiler_params=pltpu.CompilerParams(vmem_limit_bytes=8 * 2**20),
        name="merge_tile",
    )(*map(in_vmem, (sums, row, col)))


def shards(
    aperture_amp,
    aperture_phase,
    plane_depths,
    send_list,
    send_count,
    vis_left,
    vis_right,
    block_slot,
    block_pos,
    block_count,
):
    kernel_size = vis_right.shape[1]
    tiles, capacity = send_list.shape[1:]
    both = ("tu", "tv")
    outgoing = make_kernels(
        aperture_amp, aperture_phase, plane_depths, send_list[0].T, send_count, kernel_size
    )
    outgoing = outgoing.reshape((tiles, capacity) + outgoing.shape[1:])
    arrived = lax.all_to_all(outgoing, both, split_axis=0, concat_axis=0, tiled=True)
    received = arrived.reshape((-1,) + arrived.shape[2:])
    layout = Layout(block_pos.shape[0], (TILE_U // kernel_size) * (TILE_V // kernel_size))
    plan, left, right = plan_blocks(block_pos, block_slot, block_count, vis_left, vis_right, layout)
    carried, (col,) = grid_part(plan, 0, received, left, right, None, layout)
    col = from_behind(col, "tv", 1)
    carried, _ = grid_part(plan, 1, received, left, right, carried, layout)
    sums, row = row_halo(carried[0], col, kernel_size)
    row = from_behind(row, "tu", 1)
    carried, _ = grid_part(plan, 2, received, left, right, [sums, *carried[1:]], layout)
    return merge_tile(carried[0], row, col)


def solution(mesh):
    placed = (
        P(("tu", "tv"), None, None),
        P(("tu", "tv"), None, None),
        P(),
        P(("tu", "tv"), None, None),
        P(("tu", "tv"), None),
        P(("tu", "tv"), None, None),
        P(("tu", "tv"), None, None),
        P(("tu", "tv")),
        P(("tu", "tv")),
        P(("tu", "tv")),
    )
    return jax.shard_map(
        shards, mesh=mesh, in_specs=placed, out_specs=P(None, "tu", "tv"), check_vma=False
    )
```

```python
import functools
import math

import jax
import jax.numpy as jnp
import numpy as np
from jax import lax
from jax.experimental import pallas as pl
from jax.experimental.pallas import tpu as pltpu
from jax.sharding import PartitionSpec as P

TILE_U = 256
TILE_V = 512
QUAD = 4
UNROLL = 4
STEP = 2 * UNROLL
RING = 4
LEFT, RIGHT = 0, 1

def _fit(fn, degree):
    span = math.pi ** 2
    nodes = 0.5 * span * (1.0 - np.cos(np.pi * (np.arange(400) + 0.5) / 400))
    cheb = np.polynomial.chebyshev.Chebyshev.fit(nodes, fn(np.sqrt(nodes)), degree, domain=[0, span])
    return [float(c) for c in cheb.convert(kind=np.polynomial.Polynomial).coef]


COS_POLY = _fit(np.cos, 6)
SIN_POLY = _fit(lambda x: np.sin(x) / x, 5)


def horner(coefs, u):
    total = jnp.full_like(u, coefs[-1])
    for coef in coefs[-2::-1]:
        total = total * u + coef
    return total


def cos_sin(x):
    u = x * x
    return horner(COS_POLY, u), x * horner(SIN_POLY, u)


def around(block, axis):
    devices = lax.axis_size(axis)
    return lax.ppermute(block, axis, [(i, (i + 1) % devices) for i in range(devices)])


def past_first(axis, halo):
    return jnp.where(lax.axis_index(axis) > 0, halo.astype(jnp.float32), 0.0)


def in_hbm(array):
    return pltpu.with_memory_space_constraint(array, pltpu.HBM)


def in_vmem(array):
    return pltpu.with_memory_space_constraint(array, pltpu.VMEM)


def in_smem(array):
    return pltpu.with_memory_space_constraint(array, pltpu.SMEM)


def kernels_body(
    list_hbm, count_hbm, depth_hbm, amp_hbm, phase_hbm, out_ref,
    chosen_list, count, depth, amp, phase, table, screen, halves, made, small_sems, bulk_sems,
):
    screens, size, _ = amp.shape
    planes = depth.shape[0]
    kernel_size = out_ref.shape[1]
    small = [
        pltpu.make_async_copy(depth_hbm, depth, small_sems.at[0]),
        pltpu.make_async_copy(list_hbm, chosen_list, small_sems.at[1]),
        pltpu.make_async_copy(count_hbm, count, small_sems.at[2]),
    ]
    for copy in small:
        copy.start()

    def bulk(s):
        return [
            pltpu.make_async_copy(amp_hbm.at[s], amp.at[s], bulk_sems.at[0, s]),
            pltpu.make_async_copy(phase_hbm.at[s], phase.at[s], bulk_sems.at[1, s]),
        ]

    for copy in bulk(0):
        copy.start()

    frequency = lax.broadcasted_iota(jnp.int32, (kernel_size, size), 0) - kernel_size // 2
    cells = lax.broadcasted_iota(jnp.int32, (kernel_size, size), 1)
    turns = frequency.astype(jnp.float32) * cells.astype(jnp.float32) / size
    real_f, imag_f = cos_sin((2.0 * math.pi) * (turns - jnp.round(turns)))
    real_f = real_f.astype(jnp.bfloat16).astype(jnp.float32)
    imag_f = (-imag_f).astype(jnp.bfloat16).astype(jnp.float32)
    place = (lax.broadcasted_iota(jnp.int32, (1, size), 1).astype(jnp.float32) - size // 2) / size
    square = place * place
    for copy in small:
        copy.wait()
    for s in range(1, screens):
        for copy in bulk(s):
            copy.start()
    for p in range(planes):
        turns = depth[p] * square
        real_e, imag_e = cos_sin((2.0 * math.pi) * (turns - jnp.round(turns)))
        real_g = (real_f * real_e - imag_f * imag_e).astype(jnp.bfloat16)
        imag_g = (real_f * imag_e + imag_f * real_e).astype(jnp.bfloat16)
        top = slice(p * 2 * kernel_size, (p * 2 + 1) * kernel_size)
        low = slice((p * 2 + 1) * kernel_size, (p * 2 + 2) * kernel_size)
        table[top, :size] = real_g
        table[top, size:] = -imag_g
        table[low, :size] = imag_g
        table[low, size:] = real_g

    @pl.loop(0, screens)
    def _(s):
        for copy in bulk(s):
            copy.wait()
        magnitude = amp[s].astype(jnp.float32)
        real_e, imag_e = cos_sin(phase[s].astype(jnp.float32))
        screen[:size, :] = (magnitude * real_e).astype(jnp.bfloat16)
        screen[size:, :] = (magnitude * imag_e).astype(jnp.bfloat16)
        product = jnp.dot(table[...], screen[...], preferred_element_type=jnp.float32).astype(jnp.bfloat16)
        for p in range(planes):
            base = p * 2 * kernel_size
            halves[s, p, :, :size] = product[base : base + kernel_size]
            halves[s, p, :, size:] = product[base + kernel_size : base + 2 * kernel_size]

    for p in range(planes):
        second = lax.dot_general(
            jnp.concatenate([halves[s, p] for s in range(screens)], axis=0),
            table[p * 2 * kernel_size : (p + 1) * 2 * kernel_size, :],
            (((1,), (1,)), ((), ())),
            preferred_element_type=jnp.float32,
        )
        second = (second * (1.0 / size)).astype(jnp.bfloat16)
        for s in range(screens):
            made[s * planes + p] = second[s * kernel_size : (s + 1) * kernel_size]

    capacity, tiles = chosen_list.shape

    @pl.loop(0, tiles)
    def _(t):
        for c in range(capacity):
            chosen = made[chosen_list[c, t]]
            out_ref[t * capacity + c] = jnp.where(c < count[0, t], chosen, jnp.zeros_like(chosen))


def make_kernels(aperture_amp, aperture_phase, plane_depths, chosen_list, counts, kernel_size):
    screens, size, _ = aperture_amp.shape
    planes = plane_depths.shape[0]
    capacity, tiles = chosen_list.shape
    hbm = pl.BlockSpec(memory_space=pl.ANY)
    return pl.pallas_call(
        kernels_body,
        in_specs=[hbm] * 5,
        out_specs=pl.BlockSpec(memory_space=pltpu.VMEM),
        out_shape=pltpu.VMEM((tiles * capacity, kernel_size, 2 * kernel_size), jnp.bfloat16),
        scratch_shapes=[
            pltpu.SMEM((capacity, tiles), jnp.int32),
            pltpu.SMEM((1, tiles), jnp.int32),
            pltpu.SMEM((planes,), jnp.float32),
            pltpu.VMEM((screens, size, size), jnp.bfloat16),
            pltpu.VMEM((screens, size, size), jnp.bfloat16),
            pltpu.VMEM((planes * 2 * kernel_size, 2 * size), jnp.bfloat16),
            pltpu.VMEM((2 * size, size), jnp.bfloat16),
            pltpu.VMEM((screens, planes, kernel_size, 2 * size), jnp.bfloat16),
            pltpu.VMEM((screens * planes, kernel_size, 2 * kernel_size), jnp.bfloat16),
            pltpu.SemaphoreType.DMA((3,)),
            pltpu.SemaphoreType.DMA((2, screens)),
        ],
        compiler_params=pltpu.CompilerParams(vmem_limit_bytes=32 * 2**20),
        name="make_kernels",
    )(*map(in_hbm, (chosen_list, counts, plane_depths, aperture_amp, aperture_phase)))


class Layout:
    def __init__(self, blocks, anchors):
        self.parts = 3
        quads = (blocks + (QUAD - 1) * anchors) // QUAD + 1
        self.quads = (quads + STEP - 1) // STEP * STEP
        self.anchor = self.parts + 1
        self.slot = self.anchor + self.quads
        self.total = self.slot + (self.quads + UNROLL) * QUAD


def plan_body(
    pos_ref, slot_ref, count_ref, left_hbm, right_hbm, plan_ref, left_out, right_out,
    left_ref, right_ref, tally, cursor, sems, *, layout, row_slots, col_slots,
):
    anchors = row_slots * col_slots
    border = row_slots + col_slots - 1
    live = count_ref[0]

    def copies(block, place):
        return [
            pltpu.make_async_copy(left_hbm.at[block], left_ref.at[place], sems.at[0]),
            pltpu.make_async_copy(right_hbm.at[block], right_ref.at[place], sems.at[1]),
        ]

    def put(block, place, slot):
        plan_ref[layout.slot + place] = slot
        for copy in copies(block, place):
            copy.start()

    @pl.loop(0, anchors)
    def _(q):
        tally[q] = 0

    @pl.loop(0, live)
    def _(j):
        q = pos_ref[j]
        tally[q] = tally[q] + 1

    def lay(rank, quad):
        inner = rank - border
        q = jnp.where(
            rank < row_slots,
            rank * col_slots + col_slots - 1,
            jnp.where(
                rank < border,
                (row_slots - 1) * col_slots + rank - row_slots,
                (inner // (col_slots - 1)) * col_slots + lax.rem(inner, col_slots - 1),
            ),
        )
        number = tally[q]
        quads = (number + QUAD - 1) // QUAD
        cursor[q] = quad * QUAD

        @pl.loop(0, quads)
        def _(i):
            plan_ref[layout.anchor + quad + i] = q

        @pl.loop(quad * QUAD + number, (quad + quads) * QUAD)
        def _(i):
            put(0, i, -1)

        return quad + quads

    quad = 0
    begin = 0
    plan_ref[0] = 0
    for part, end in enumerate([row_slots, border, anchors]):
        quad = lax.fori_loop(begin, end, lay, quad)
        begin = end
        plan_ref[part + 1] = ((quad + STEP - 1) // STEP) * STEP

    full = ((quad + STEP - 1) // STEP) * STEP

    @pl.loop(quad, full)
    def _(i):
        plan_ref[layout.anchor + i] = 0
        for e in range(QUAD):
            put(0, i * QUAD + e, -1)

    quad = full

    @pl.loop(quad * QUAD, (quad + UNROLL) * QUAD)
    def _(i):
        plan_ref[layout.slot + i] = -1

    @pl.loop(0, live)
    def _(j):
        q = pos_ref[j]
        at = cursor[q]
        cursor[q] = at + 1
        put(j, at, slot_ref[j])

    chunk = STEP * QUAD

    @pl.loop(0, quad // STEP)
    def _(i):
        rows = pl.ds(0, chunk)
        pltpu.make_async_copy(left_hbm.at[rows], left_ref.at[rows], sems.at[0]).wait()
        pltpu.make_async_copy(right_hbm.at[rows], right_ref.at[rows], sems.at[1]).wait()

    def writes(i):
        rows = pl.ds(i * chunk, chunk)
        return [
            pltpu.make_async_copy(left_ref.at[rows], left_out.at[rows], sems.at[2]),
            pltpu.make_async_copy(right_ref.at[rows], right_out.at[rows], sems.at[3]),
        ]

    @pl.loop(0, quad // STEP)
    def _(i):
        for copy in writes(i):
            copy.start()

    @pl.loop(0, quad // STEP)
    def _(i):
        for copy in writes(i):
            copy.wait()


def plan_blocks(block_pos, block_slot, block_count, vis_left, vis_right, layout):
    kernel_size = vis_right.shape[1]
    row_slots, col_slots = TILE_U // kernel_size, TILE_V // kernel_size
    smem = pl.BlockSpec(memory_space=pltpu.SMEM)
    hbm = pl.BlockSpec(memory_space=pl.ANY)
    places = layout.quads * QUAD
    return pl.pallas_call(
        functools.partial(plan_body, layout=layout, row_slots=row_slots, col_slots=col_slots),
        in_specs=[smem] * 3 + [hbm] * 2,
        out_specs=[smem, hbm, hbm],
        out_shape=[
            pltpu.SMEM((layout.total,), jnp.int32),
            pltpu.HBM((places,) + vis_left.shape[1:], vis_left.dtype),
            pltpu.HBM((places,) + vis_right.shape[1:], vis_right.dtype),
        ],
        scratch_shapes=[
            pltpu.VMEM((places,) + vis_left.shape[1:], vis_left.dtype),
            pltpu.VMEM((places,) + vis_right.shape[1:], vis_right.dtype),
            pltpu.SMEM((row_slots * col_slots,), jnp.int32),
            pltpu.SMEM((row_slots * col_slots,), jnp.int32),
            pltpu.SemaphoreType.DMA((4,)),
        ],
        compiler_params=pltpu.CompilerParams(vmem_limit_bytes=36 * 2**20),
        name="plan_blocks",
    )(block_pos, block_slot, block_count, in_hbm(vis_left), in_hbm(vis_right))


def strip(sums, row_slots, col_slots, kernel_size, plane, a, col):
    patch = sums.shape[1]
    lanes = slice(plane * patch, (plane + 1) * patch)
    total = None
    if a < row_slots:
        total = sums[a * col_slots + col, :kernel_size, lanes]
    if a > 0:
        above = sums[(a - 1) * col_slots + col, kernel_size:, lanes]
        total = above if total is None else total + above
    return total


def grid_body(
    plan_ref, kern_ref, left_hbm, right_hbm, *rest, part, first_part, layout, row_slots, col_slots
):
    if not first_part:
        rest = rest[4:]
    sums, left_ring, right_ring, ahead, *rest = rest
    if first_part:
        col_ref, *rest = rest
    behind_ref, sems = rest
    mixed = (ahead, behind_ref)
    slots, kernel_size, _ = kern_ref.shape
    patch = left_hbm.shape[1]
    chunk = STEP * QUAD
    begin = plan_ref[part] // STEP
    end = plan_ref[part + 1] // STEP
    limit = jnp.minimum(plan_ref[layout.parts] // STEP, end + 2)

    def fetch(i):
        source = pl.ds(i * chunk, chunk)
        ring = lax.rem(i, RING)
        return [
            pltpu.make_async_copy(left_hbm.at[source], left_ring.at[ring], sems.at[0, ring]),
            pltpu.make_async_copy(right_hbm.at[source], right_ring.at[ring], sems.at[1, ring]),
        ]

    def start(i, which):
        @pl.when(i < limit)
        def _():
            fetch(i)[which].start()

    def wait(i, which):
        fresh = (i < limit) if first_part else ((i < limit) & (i > begin + 1))

        @pl.when(fresh)
        def _():
            fetch(i)[which].wait()

    if first_part:
        start(0, RIGHT)
        start(1, RIGHT)
        start(0, LEFT)

        @pl.loop(0, sums.shape[0])
        def _(q):
            sums[q] = jnp.zeros(sums.shape[1:], sums.dtype)

    zero = jnp.zeros((kernel_size, patch), jnp.bfloat16)

    def first(i, ring, at, ref, u):
        for e in range(QUAD):
            slot = plan_ref[layout.slot + (i * STEP + at) * QUAD + e]
            right = right_ring[ring, at * QUAD + e]
            kern = kern_ref[jnp.maximum(slot, 0)]
            kern = jnp.where(slot >= 0, kern, jnp.zeros_like(kern))
            spread = jnp.concatenate(
                [jnp.concatenate([right, zero], axis=1), jnp.concatenate([zero, right], axis=1)], axis=0
            )
            out = jnp.dot(kern, spread, preferred_element_type=jnp.float32).astype(jnp.bfloat16)
            top = slice(e * 2 * kernel_size, (e * 2 + 1) * kernel_size)
            low = slice((e * 2 + 1) * kernel_size, (e * 2 + 2) * kernel_size)
            ref[u, top, :] = out
            ref[u, low, :patch] = -out[:, patch:]
            ref[u, low, patch:] = out[:, :patch]

    def second(i, ring, at, ref, u):
        left = jnp.concatenate([left_ring[ring, at * QUAD + e] for e in range(QUAD)], axis=1)
        q = plan_ref[layout.anchor + i * STEP + at]
        sums[q] += jnp.dot(left, ref[u], preferred_element_type=jnp.float32)

    if first_part:
        wait(0, RIGHT)
        start(1, LEFT)
        for u in range(UNROLL):
            first(0, 0, u, mixed[0], u)
    start(begin + 2, RIGHT)
    start(begin + 2, LEFT)

    @pl.loop(begin, end)
    def _(i):
        here = lax.rem(i, RING)
        there = lax.rem(i + 1, RING)
        start(i + 3, RIGHT)
        start(i + 3, LEFT)
        wait(i, LEFT)
        wait(i + 1, RIGHT)
        for u in range(UNROLL):
            first(i, here, UNROLL + u, mixed[1], u)
            second(i, here, u, mixed[0], u)
        for u in range(UNROLL):
            first(i + 1, there, u, mixed[0], u)
            second(i, here, UNROLL + u, mixed[1], u)

    wait(end, LEFT)
    wait(end + 1, LEFT)
    wait(end + 1, RIGHT)
    if not first_part:
        return
    low = lax.broadcasted_iota(jnp.int32, (kernel_size, patch), 1) < kernel_size
    take = functools.partial(strip, sums, row_slots, col_slots, kernel_size)
    for a in range(row_slots + 1):
        real = pltpu.roll(take(0, a, col_slots - 1), kernel_size, 1)
        edge = jnp.where(low, real, take(1, a, col_slots - 1))
        col_ref[a * kernel_size : (a + 1) * kernel_size, :] = edge.astype(col_ref.dtype)


def row_body(before, col_ref, sums, row_ref, *, row_slots, col_slots):
    kernel_size = row_ref.shape[1]
    patch = sums.shape[1]
    low = lax.broadcasted_iota(jnp.int32, (kernel_size, patch), 1) < kernel_size
    take = functools.partial(strip, sums, row_slots, col_slots, kernel_size)
    corner = past_first("tv", col_ref[row_slots * kernel_size :, :])
    for plane in range(2):
        behind = corner if plane == 0 else pltpu.roll(corner, kernel_size, 1)
        for tile in range(col_slots // 2):
            odd = pltpu.roll(take(plane, row_slots, 2 * tile + 1), kernel_size, 1)
            value = take(plane, row_slots, 2 * tile) + jnp.where(low, behind, odd)
            row_ref[plane, :, tile * patch : (tile + 1) * patch] = value.astype(row_ref.dtype)
            behind = odd


def row_halo(sums, col, kernel_size):
    vmem = pl.BlockSpec(memory_space=pltpu.VMEM)
    return pl.pallas_call(
        functools.partial(row_body, row_slots=TILE_U // kernel_size, col_slots=TILE_V // kernel_size),
        in_specs=[vmem] * 2,
        out_specs=[vmem] * 2,
        out_shape=[
            pltpu.VMEM(sums.shape, sums.dtype),
            pltpu.VMEM((2, kernel_size, TILE_V), jnp.bfloat16),
        ],
        input_output_aliases={0: 0},
        compiler_params=pltpu.CompilerParams(vmem_limit_bytes=4 * 2**20),
        name="row_halo",
    )(in_vmem(sums), in_vmem(col))


def grid_part(plan, part, kernels, left, right, carried, layout):
    kernel_size = kernels.shape[1]
    patch = left.shape[1]
    row_slots, col_slots = TILE_U // kernel_size, TILE_V // kernel_size
    smem = pl.BlockSpec(memory_space=pltpu.SMEM)
    vmem = pl.BlockSpec(memory_space=pltpu.VMEM)
    hbm = pl.BlockSpec(memory_space=pl.ANY)
    first_part = carried is None
    carried = [] if first_part else [in_vmem(array) for array in carried]
    mixed_shape = (UNROLL, QUAD * 2 * kernel_size, 2 * patch)
    out_shape = [
        pltpu.VMEM((row_slots * col_slots, patch, 2 * patch), jnp.float32),
        pltpu.VMEM((RING, STEP * QUAD) + left.shape[1:], left.dtype),
        pltpu.VMEM((RING, STEP * QUAD) + right.shape[1:], right.dtype),
        pltpu.VMEM(mixed_shape, jnp.bfloat16),
    ]
    if first_part:
        out_shape.append(pltpu.VMEM((TILE_U + kernel_size, 2 * kernel_size), jnp.bfloat16))
    out = pl.pallas_call(
        functools.partial(
            grid_body,
            part=part,
            first_part=first_part,
            layout=layout,
            row_slots=row_slots,
            col_slots=col_slots,
        ),
        in_specs=[smem, vmem, hbm, hbm] + [vmem] * len(carried),
        out_specs=[vmem] * len(out_shape),
        out_shape=out_shape,
        input_output_aliases={4 + i: i for i in range(len(carried))},
        scratch_shapes=[
            pltpu.VMEM(mixed_shape, jnp.bfloat16),
            pltpu.SemaphoreType.DMA((2, RING)),
        ],
        compiler_params=pltpu.CompilerParams(vmem_limit_bytes=12 * 2**20),
        name="grid_part",
    )(in_smem(plan), in_vmem(kernels), in_hbm(left), in_hbm(right), *carried)
    return out[:4], out[4:]


def merge_body(sums, row_ref, col_ref, out_hbm, out_ref, sems):
    kernel_size = row_ref.shape[1]
    patch = sums.shape[1]
    row_slots = out_ref.shape[1] // kernel_size
    col_slots = out_ref.shape[2] // kernel_size
    low = lax.broadcasted_iota(jnp.int32, (kernel_size, patch), 1) < kernel_size
    take = functools.partial(strip, sums, row_slots, col_slots, kernel_size)
    for a in range(row_slots):
        rows = slice(a * kernel_size, (a + 1) * kernel_size)
        edge = past_first("tv", col_ref[rows, :])
        for plane in range(2):
            behind = edge if plane == 0 else pltpu.roll(edge, kernel_size, 1)
            for tile in range(col_slots // 2):
                lanes = slice(tile * patch, (tile + 1) * patch)
                odd = pltpu.roll(take(plane, a, 2 * tile + 1), kernel_size, 1)
                value = take(plane, a, 2 * tile) + jnp.where(low, behind, odd)
                if a == 0:
                    value = value + past_first("tu", row_ref[plane, :, lanes])
                out_ref[plane, rows, lanes] = value
                behind = odd
        pltpu.make_async_copy(out_ref.at[:, rows], out_hbm.at[:, rows], sems.at[a]).start()
    for a in range(row_slots):
        rows = slice(a * kernel_size, (a + 1) * kernel_size)
        pltpu.make_async_copy(out_ref.at[:, rows], out_hbm.at[:, rows], sems.at[a]).wait()


def merge_tile(sums, row, col):
    vmem = pl.BlockSpec(memory_space=pltpu.VMEM)
    return pl.pallas_call(
        merge_body,
        in_specs=[vmem] * 3,
        out_specs=pl.BlockSpec(memory_space=pl.ANY),
        out_shape=jax.ShapeDtypeStruct((2, TILE_U, TILE_V), jnp.float32),
        scratch_shapes=[
            pltpu.VMEM((2, TILE_U, TILE_V), jnp.float32),
            pltpu.SemaphoreType.DMA((TILE_U // row.shape[1],)),
        ],
        compiler_params=pltpu.CompilerParams(vmem_limit_bytes=8 * 2**20),
        name="merge_tile",
    )(*map(in_vmem, (sums, row, col)))


def shards(
    aperture_amp,
    aperture_phase,
    plane_depths,
    send_list,
    send_count,
    vis_left,
    vis_right,
    block_slot,
    block_pos,
    block_count,
):
    kernel_size = vis_right.shape[1]
    tiles, capacity = send_list.shape[1:]
    both = ("tu", "tv")
    outgoing = make_kernels(
        aperture_amp, aperture_phase, plane_depths, send_list[0].T, send_count, kernel_size
    )
    outgoing = outgoing.reshape((tiles, capacity) + outgoing.shape[1:])
    arrived = lax.all_to_all(outgoing, both, split_axis=0, concat_axis=0, tiled=True)
    received = arrived.reshape((-1,) + arrived.shape[2:])
    layout = Layout(block_pos.shape[0], (TILE_U // kernel_size) * (TILE_V // kernel_size))
    plan, left, right = plan_blocks(block_pos, block_slot, block_count, vis_left, vis_right, layout)
    carried, (col,) = grid_part(plan, 0, received, left, right, None, layout)
    col = around(col, "tv")
    carried, _ = grid_part(plan, 1, received, left, right, carried, layout)
    sums, row = row_halo(carried[0], col, kernel_size)
    row = around(row, "tu")
    carried, _ = grid_part(plan, 2, received, left, right, [sums, *carried[1:]], layout)
    return merge_tile(carried[0], row, col)


def solution(mesh):
    placed = (
        P(("tu", "tv"), None, None),
        P(("tu", "tv"), None, None),
        P(),
        P(("tu", "tv"), None, None),
        P(("tu", "tv"), None),
        P(("tu", "tv"), None, None),
        P(("tu", "tv"), None, None),
        P(("tu", "tv")),
        P(("tu", "tv")),
        P(("tu", "tv")),
    )
    return jax.shard_map(
        shards, mesh=mesh, in_specs=placed, out_specs=P(None, "tu", "tv"), check_vma=False
    )
```

```python
import functools
import math

import jax
import jax.numpy as jnp
import numpy as np
from jax import lax
from jax.experimental import pallas as pl
from jax.experimental.pallas import tpu as pltpu
from jax.sharding import PartitionSpec as P

TILE_U = 256
TILE_V = 512
QUAD = 4
UNROLL = 4
STEP = 2 * UNROLL
RING = 4
LEFT, RIGHT = 0, 1

def _fit(fn, degree):
    span = math.pi ** 2
    nodes = 0.5 * span * (1.0 - np.cos(np.pi * (np.arange(400) + 0.5) / 400))
    cheb = np.polynomial.chebyshev.Chebyshev.fit(nodes, fn(np.sqrt(nodes)), degree, domain=[0, span])
    return [float(c) for c in cheb.convert(kind=np.polynomial.Polynomial).coef]


COS_POLY = _fit(np.cos, 6)
SIN_POLY = _fit(lambda x: np.sin(x) / x, 5)


def horner(coefs, u):
    total = jnp.full_like(u, coefs[-1])
    for coef in coefs[-2::-1]:
        total = total * u + coef
    return total


def cos_sin(x):
    u = x * x
    return horner(COS_POLY, u), x * horner(SIN_POLY, u)


def around(block, axis):
    devices = lax.axis_size(axis)
    return lax.ppermute(block, axis, [(i, (i + 1) % devices) for i in range(devices)])


def past_first(axis, halo):
    return jnp.where(lax.axis_index(axis) > 0, halo.astype(jnp.float32), 0.0)


def in_hbm(array):
    return pltpu.with_memory_space_constraint(array, pltpu.HBM)


def in_vmem(array):
    return pltpu.with_memory_space_constraint(array, pltpu.VMEM)


def in_smem(array):
    return pltpu.with_memory_space_constraint(array, pltpu.SMEM)


def kernels_body(
    list_hbm, count_hbm, depth_hbm, amp_hbm, phase_hbm, out_ref,
    chosen_list, count, depth, amp, phase, table, screen, halves, made, small_sems, bulk_sems,
):
    screens, size, _ = amp.shape
    planes = depth.shape[0]
    kernel_size = out_ref.shape[1]
    small = [
        pltpu.make_async_copy(depth_hbm, depth, small_sems.at[0]),
        pltpu.make_async_copy(list_hbm, chosen_list, small_sems.at[1]),
        pltpu.make_async_copy(count_hbm, count, small_sems.at[2]),
    ]
    for copy in small:
        copy.start()

    def bulk(s):
        return [
            pltpu.make_async_copy(amp_hbm.at[s], amp.at[s], bulk_sems.at[0, s]),
            pltpu.make_async_copy(phase_hbm.at[s], phase.at[s], bulk_sems.at[1, s]),
        ]

    for copy in bulk(0):
        copy.start()

    frequency = lax.broadcasted_iota(jnp.int32, (kernel_size, size), 0) - kernel_size // 2
    cells = lax.broadcasted_iota(jnp.int32, (kernel_size, size), 1)
    turns = frequency.astype(jnp.float32) * cells.astype(jnp.float32) / size
    real_f, imag_f = cos_sin((2.0 * math.pi) * (turns - jnp.round(turns)))
    real_f = real_f.astype(jnp.bfloat16).astype(jnp.float32)
    imag_f = (-imag_f).astype(jnp.bfloat16).astype(jnp.float32)
    place = (lax.broadcasted_iota(jnp.int32, (1, size), 1).astype(jnp.float32) - size // 2) / size
    square = place * place
    for copy in small:
        copy.wait()
    for s in range(1, screens):
        for copy in bulk(s):
            copy.start()
    for p in range(planes):
        turns = depth[p] * square
        real_e, imag_e = cos_sin((2.0 * math.pi) * (turns - jnp.round(turns)))
        real_g = (real_f * real_e - imag_f * imag_e).astype(jnp.bfloat16)
        imag_g = (real_f * imag_e + imag_f * real_e).astype(jnp.bfloat16)
        top = slice(p * 2 * kernel_size, (p * 2 + 1) * kernel_size)
        low = slice((p * 2 + 1) * kernel_size, (p * 2 + 2) * kernel_size)
        table[top, :size] = real_g
        table[top, size:] = -imag_g
        table[low, :size] = imag_g
        table[low, size:] = real_g

    @pl.loop(0, screens)
    def _(s):
        for copy in bulk(s):
            copy.wait()
        magnitude = amp[s].astype(jnp.float32)
        real_e, imag_e = cos_sin(phase[s].astype(jnp.float32))
        screen[:size, :] = (magnitude * real_e).astype(jnp.bfloat16)
        screen[size:, :] = (magnitude * imag_e).astype(jnp.bfloat16)
        product = jnp.dot(table[...], screen[...], preferred_element_type=jnp.float32).astype(jnp.bfloat16)
        for p in range(planes):
            base = p * 2 * kernel_size
            halves[s, p, :, :size] = product[base : base + kernel_size]
            halves[s, p, :, size:] = product[base + kernel_size : base + 2 * kernel_size]

    for p in range(planes):
        second = lax.dot_general(
            jnp.concatenate([halves[s, p] for s in range(screens)], axis=0),
            table[p * 2 * kernel_size : (p + 1) * 2 * kernel_size, :],
            (((1,), (1,)), ((), ())),
            preferred_element_type=jnp.float32,
        )
        second = (second * (1.0 / size)).astype(jnp.bfloat16)
        for s in range(screens):
            made[s * planes + p] = second[s * kernel_size : (s + 1) * kernel_size]

    capacity, tiles = chosen_list.shape

    @pl.loop(0, tiles)
    def _(t):
        for c in range(capacity):
            chosen = made[chosen_list[c, t]]
            out_ref[t * capacity + c] = jnp.where(c < count[0, t], chosen, jnp.zeros_like(chosen))


def make_kernels(aperture_amp, aperture_phase, plane_depths, chosen_list, counts, kernel_size):
    screens, size, _ = aperture_amp.shape
    planes = plane_depths.shape[0]
    capacity, tiles = chosen_list.shape
    hbm = pl.BlockSpec(memory_space=pl.ANY)
    return pl.pallas_call(
        kernels_body,
        in_specs=[hbm] * 5,
        out_specs=pl.BlockSpec(memory_space=pltpu.VMEM),
        out_shape=pltpu.VMEM((tiles * capacity, kernel_size, 2 * kernel_size), jnp.bfloat16),
        scratch_shapes=[
            pltpu.SMEM((capacity, tiles), jnp.int32),
            pltpu.SMEM((1, tiles), jnp.int32),
            pltpu.SMEM((planes,), jnp.float32),
            pltpu.VMEM((screens, size, size), jnp.bfloat16),
            pltpu.VMEM((screens, size, size), jnp.bfloat16),
            pltpu.VMEM((planes * 2 * kernel_size, 2 * size), jnp.bfloat16),
            pltpu.VMEM((2 * size, size), jnp.bfloat16),
            pltpu.VMEM((screens, planes, kernel_size, 2 * size), jnp.bfloat16),
            pltpu.VMEM((screens * planes, kernel_size, 2 * kernel_size), jnp.bfloat16),
            pltpu.SemaphoreType.DMA((3,)),
            pltpu.SemaphoreType.DMA((2, screens)),
        ],
        compiler_params=pltpu.CompilerParams(vmem_limit_bytes=32 * 2**20),
        name="make_kernels",
    )(*map(in_hbm, (chosen_list, counts, plane_depths, aperture_amp, aperture_phase)))


class Layout:
    def __init__(self, blocks, anchors):
        self.parts = 3
        quads = (blocks + (QUAD - 1) * anchors) // QUAD + 1
        self.quads = (quads + STEP - 1) // STEP * STEP
        self.anchor = self.parts + 1
        self.slot = self.anchor + self.quads
        self.total = self.slot + (self.quads + UNROLL) * QUAD


def plan_body(
    pos_ref, slot_ref, count_ref, left_hbm, right_hbm, plan_ref, left_out, right_out,
    left_ref, right_ref, tally, cursor, sems, *, layout, row_slots, col_slots,
):
    anchors = row_slots * col_slots
    border = row_slots + col_slots - 1
    live = count_ref[0]

    def copies(block, place):
        return [
            pltpu.make_async_copy(left_hbm.at[block], left_ref.at[place], sems.at[0]),
            pltpu.make_async_copy(right_hbm.at[block], right_ref.at[place], sems.at[1]),
        ]

    def put(block, place, slot):
        plan_ref[layout.slot + place] = slot
        for copy in copies(block, place):
            copy.start()

    @pl.loop(0, anchors)
    def _(q):
        tally[q] = 0

    @pl.loop(0, live)
    def _(j):
        q = pos_ref[j]
        tally[q] = tally[q] + 1

    def lay(rank, quad):
        inner = rank - border
        q = jnp.where(
            rank < row_slots,
            rank * col_slots + col_slots - 1,
            jnp.where(
                rank < border,
                (row_slots - 1) * col_slots + rank - row_slots,
                (inner // (col_slots - 1)) * col_slots + lax.rem(inner, col_slots - 1),
            ),
        )
        number = tally[q]
        quads = (number + QUAD - 1) // QUAD
        cursor[q] = quad * QUAD

        @pl.loop(0, quads)
        def _(i):
            plan_ref[layout.anchor + quad + i] = q

        @pl.loop(quad * QUAD + number, (quad + quads) * QUAD)
        def _(i):
            put(0, i, -1)

        return quad + quads

    quad = 0
    begin = 0
    plan_ref[0] = 0
    for part, end in enumerate([row_slots, border, anchors]):
        quad = lax.fori_loop(begin, end, lay, quad)
        begin = end
        plan_ref[part + 1] = ((quad + STEP - 1) // STEP) * STEP

    full = ((quad + STEP - 1) // STEP) * STEP
    plan_ref[2] = jnp.maximum(plan_ref[2], (full // STEP) * 3 // 7 * STEP)

    @pl.loop(quad, full)
    def _(i):
        plan_ref[layout.anchor + i] = 0
        for e in range(QUAD):
            put(0, i * QUAD + e, -1)

    quad = full

    @pl.loop(quad * QUAD, (quad + UNROLL) * QUAD)
    def _(i):
        plan_ref[layout.slot + i] = -1

    @pl.loop(0, live)
    def _(j):
        q = pos_ref[j]
        at = cursor[q]
        cursor[q] = at + 1
        put(j, at, slot_ref[j])

    chunk = STEP * QUAD

    @pl.loop(0, quad // STEP)
    def _(i):
        rows = pl.ds(0, chunk)
        pltpu.make_async_copy(left_hbm.at[rows], left_ref.at[rows], sems.at[0]).wait()
        pltpu.make_async_copy(right_hbm.at[rows], right_ref.at[rows], sems.at[1]).wait()

    def writes(i):
        rows = pl.ds(i * chunk, chunk)
        return [
            pltpu.make_async_copy(left_ref.at[rows], left_out.at[rows], sems.at[2]),
            pltpu.make_async_copy(right_ref.at[rows], right_out.at[rows], sems.at[3]),
        ]

    @pl.loop(0, quad // STEP)
    def _(i):
        for copy in writes(i):
            copy.start()

    @pl.loop(0, quad // STEP)
    def _(i):
        for copy in writes(i):
            copy.wait()


def plan_blocks(block_pos, block_slot, block_count, vis_left, vis_right, layout):
    kernel_size = vis_right.shape[1]
    row_slots, col_slots = TILE_U // kernel_size, TILE_V // kernel_size
    smem = pl.BlockSpec(memory_space=pltpu.SMEM)
    hbm = pl.BlockSpec(memory_space=pl.ANY)
    places = layout.quads * QUAD
    return pl.pallas_call(
        functools.partial(plan_body, layout=layout, row_slots=row_slots, col_slots=col_slots),
        in_specs=[smem] * 3 + [hbm] * 2,
        out_specs=[smem, hbm, hbm],
        out_shape=[
            pltpu.SMEM((layout.total,), jnp.int32),
            pltpu.HBM((places,) + vis_left.shape[1:], vis_left.dtype),
            pltpu.HBM((places,) + vis_right.shape[1:], vis_right.dtype),
        ],
        scratch_shapes=[
            pltpu.VMEM((places,) + vis_left.shape[1:], vis_left.dtype),
            pltpu.VMEM((places,) + vis_right.shape[1:], vis_right.dtype),
            pltpu.SMEM((row_slots * col_slots,), jnp.int32),
            pltpu.SMEM((row_slots * col_slots,), jnp.int32),
            pltpu.SemaphoreType.DMA((4,)),
        ],
        compiler_params=pltpu.CompilerParams(vmem_limit_bytes=36 * 2**20),
        name="plan_blocks",
    )(block_pos, block_slot, block_count, in_hbm(vis_left), in_hbm(vis_right))


def strip(sums, row_slots, col_slots, kernel_size, plane, a, col):
    patch = sums.shape[1]
    lanes = slice(plane * patch, (plane + 1) * patch)
    total = None
    if a < row_slots:
        total = sums[a * col_slots + col, :kernel_size, lanes]
    if a > 0:
        above = sums[(a - 1) * col_slots + col, kernel_size:, lanes]
        total = above if total is None else total + above
    return total


def grid_body(
    plan_ref, kern_ref, left_hbm, right_hbm, *rest, part, first_part, layout, row_slots, col_slots
):
    if not first_part:
        rest = rest[4:]
    sums, left_ring, right_ring, ahead, *rest = rest
    if first_part:
        col_ref, *rest = rest
    behind_ref, sems = rest
    mixed = (ahead, behind_ref)
    slots, kernel_size, _ = kern_ref.shape
    patch = left_hbm.shape[1]
    chunk = STEP * QUAD
    begin = plan_ref[part] // STEP
    end = plan_ref[part + 1] // STEP
    limit = jnp.minimum(plan_ref[layout.parts] // STEP, end + 2)

    def fetch(i):
        source = pl.ds(i * chunk, chunk)
        ring = lax.rem(i, RING)
        return [
            pltpu.make_async_copy(left_hbm.at[source], left_ring.at[ring], sems.at[0, ring]),
            pltpu.make_async_copy(right_hbm.at[source], right_ring.at[ring], sems.at[1, ring]),
        ]

    def start(i, which):
        @pl.when(i < limit)
        def _():
            fetch(i)[which].start()

    def wait(i, which):
        fresh = (i < limit) if first_part else ((i < limit) & (i > begin + 1))

        @pl.when(fresh)
        def _():
            fetch(i)[which].wait()

    if first_part:
        start(0, RIGHT)
        start(1, RIGHT)
        start(0, LEFT)

        @pl.loop(0, sums.shape[0])
        def _(q):
            sums[q] = jnp.zeros(sums.shape[1:], sums.dtype)

    zero = jnp.zeros((kernel_size, patch), jnp.bfloat16)

    def first(i, ring, at, ref, u):
        for e in range(QUAD):
            slot = plan_ref[layout.slot + (i * STEP + at) * QUAD + e]
            right = right_ring[ring, at * QUAD + e]
            kern = kern_ref[jnp.maximum(slot, 0)]
            kern = jnp.where(slot >= 0, kern, jnp.zeros_like(kern))
            spread = jnp.concatenate(
                [jnp.concatenate([right, zero], axis=1), jnp.concatenate([zero, right], axis=1)], axis=0
            )
            out = jnp.dot(kern, spread, preferred_element_type=jnp.float32).astype(jnp.bfloat16)
            top = slice(e * 2 * kernel_size, (e * 2 + 1) * kernel_size)
            low = slice((e * 2 + 1) * kernel_size, (e * 2 + 2) * kernel_size)
            ref[u, top, :] = out
            ref[u, low, :patch] = -out[:, patch:]
            ref[u, low, patch:] = out[:, :patch]

    def second(i, ring, at, ref, u):
        left = jnp.concatenate([left_ring[ring, at * QUAD + e] for e in range(QUAD)], axis=1)
        q = plan_ref[layout.anchor + i * STEP + at]
        sums[q] += jnp.dot(left, ref[u], preferred_element_type=jnp.float32)

    if first_part:
        wait(0, RIGHT)
        start(1, LEFT)
        for u in range(UNROLL):
            first(0, 0, u, mixed[0], u)
    start(begin + 2, RIGHT)
    start(begin + 2, LEFT)

    @pl.loop(begin, end)
    def _(i):
        here = lax.rem(i, RING)
        there = lax.rem(i + 1, RING)
        start(i + 3, RIGHT)
        start(i + 3, LEFT)
        wait(i, LEFT)
        wait(i + 1, RIGHT)
        for u in range(UNROLL):
            first(i, here, UNROLL + u, mixed[1], u)
            second(i, here, u, mixed[0], u)
        for u in range(UNROLL):
            first(i + 1, there, u, mixed[0], u)
            second(i, here, UNROLL + u, mixed[1], u)

    wait(end, LEFT)
    wait(end + 1, LEFT)
    wait(end + 1, RIGHT)
    if not first_part:
        return
    low = lax.broadcasted_iota(jnp.int32, (kernel_size, patch), 1) < kernel_size
    take = functools.partial(strip, sums, row_slots, col_slots, kernel_size)
    for a in range(row_slots + 1):
        real = pltpu.roll(take(0, a, col_slots - 1), kernel_size, 1)
        edge = jnp.where(low, real, take(1, a, col_slots - 1))
        col_ref[a * kernel_size : (a + 1) * kernel_size, :] = edge.astype(col_ref.dtype)


def row_body(before, col_ref, sums, row_ref, *, row_slots, col_slots):
    kernel_size = row_ref.shape[1]
    patch = sums.shape[1]
    low = lax.broadcasted_iota(jnp.int32, (kernel_size, patch), 1) < kernel_size
    take = functools.partial(strip, sums, row_slots, col_slots, kernel_size)
    corner = past_first("tv", col_ref[row_slots * kernel_size :, :])
    for plane in range(2):
        behind = corner if plane == 0 else pltpu.roll(corner, kernel_size, 1)
        for tile in range(col_slots // 2):
            odd = pltpu.roll(take(plane, row_slots, 2 * tile + 1), kernel_size, 1)
            value = take(plane, row_slots, 2 * tile) + jnp.where(low, behind, odd)
            row_ref[plane, :, tile * patch : (tile + 1) * patch] = value.astype(row_ref.dtype)
            behind = odd


def row_halo(sums, col, kernel_size):
    vmem = pl.BlockSpec(memory_space=pltpu.VMEM)
    return pl.pallas_call(
        functools.partial(row_body, row_slots=TILE_U // kernel_size, col_slots=TILE_V // kernel_size),
        in_specs=[vmem] * 2,
        out_specs=[vmem] * 2,
        out_shape=[
            pltpu.VMEM(sums.shape, sums.dtype),
            pltpu.VMEM((2, kernel_size, TILE_V), jnp.bfloat16),
        ],
        input_output_aliases={0: 0},
        compiler_params=pltpu.CompilerParams(vmem_limit_bytes=4 * 2**20),
        name="row_halo",
    )(in_vmem(sums), in_vmem(col))


def grid_part(plan, part, kernels, left, right, carried, layout):
    kernel_size = kernels.shape[1]
    patch = left.shape[1]
    row_slots, col_slots = TILE_U // kernel_size, TILE_V // kernel_size
    smem = pl.BlockSpec(memory_space=pltpu.SMEM)
    vmem = pl.BlockSpec(memory_space=pltpu.VMEM)
    hbm = pl.BlockSpec(memory_space=pl.ANY)
    first_part = carried is None
    carried = [] if first_part else [in_vmem(array) for array in carried]
    mixed_shape = (UNROLL, QUAD * 2 * kernel_size, 2 * patch)
    out_shape = [
        pltpu.VMEM((row_slots * col_slots, patch, 2 * patch), jnp.float32),
        pltpu.VMEM((RING, STEP * QUAD) + left.shape[1:], left.dtype),
        pltpu.VMEM((RING, STEP * QUAD) + right.shape[1:], right.dtype),
        pltpu.VMEM(mixed_shape, jnp.bfloat16),
    ]
    if first_part:
        out_shape.append(pltpu.VMEM((TILE_U + kernel_size, 2 * kernel_size), jnp.bfloat16))
    out = pl.pallas_call(
        functools.partial(
            grid_body,
            part=part,
            first_part=first_part,
            layout=layout,
            row_slots=row_slots,
            col_slots=col_slots,
        ),
        in_specs=[smem, vmem, hbm, hbm] + [vmem] * len(carried),
        out_specs=[vmem] * len(out_shape),
        out_shape=out_shape,
        input_output_aliases={4 + i: i for i in range(len(carried))},
        scratch_shapes=[
            pltpu.VMEM(mixed_shape, jnp.bfloat16),
            pltpu.SemaphoreType.DMA((2, RING)),
        ],
        compiler_params=pltpu.CompilerParams(vmem_limit_bytes=12 * 2**20),
        name="grid_part",
    )(in_smem(plan), in_vmem(kernels), in_hbm(left), in_hbm(right), *carried)
    return out[:4], out[4:]


def merge_body(sums, row_ref, col_ref, out_hbm, out_ref, sems):
    kernel_size = row_ref.shape[1]
    patch = sums.shape[1]
    row_slots = out_ref.shape[1] // kernel_size
    col_slots = out_ref.shape[2] // kernel_size
    low = lax.broadcasted_iota(jnp.int32, (kernel_size, patch), 1) < kernel_size
    take = functools.partial(strip, sums, row_slots, col_slots, kernel_size)
    for a in range(row_slots):
        rows = slice(a * kernel_size, (a + 1) * kernel_size)
        edge = past_first("tv", col_ref[rows, :])
        for plane in range(2):
            behind = edge if plane == 0 else pltpu.roll(edge, kernel_size, 1)
            for tile in range(col_slots // 2):
                lanes = slice(tile * patch, (tile + 1) * patch)
                odd = pltpu.roll(take(plane, a, 2 * tile + 1), kernel_size, 1)
                value = take(plane, a, 2 * tile) + jnp.where(low, behind, odd)
                if a == 0:
                    value = value + past_first("tu", row_ref[plane, :, lanes])
                out_ref[plane, rows, lanes] = value
                behind = odd
        pltpu.make_async_copy(out_ref.at[:, rows], out_hbm.at[:, rows], sems.at[a]).start()
    for a in range(row_slots):
        rows = slice(a * kernel_size, (a + 1) * kernel_size)
        pltpu.make_async_copy(out_ref.at[:, rows], out_hbm.at[:, rows], sems.at[a]).wait()


def merge_tile(sums, row, col):
    vmem = pl.BlockSpec(memory_space=pltpu.VMEM)
    return pl.pallas_call(
        merge_body,
        in_specs=[vmem] * 3,
        out_specs=pl.BlockSpec(memory_space=pl.ANY),
        out_shape=jax.ShapeDtypeStruct((2, TILE_U, TILE_V), jnp.float32),
        scratch_shapes=[
            pltpu.VMEM((2, TILE_U, TILE_V), jnp.float32),
            pltpu.SemaphoreType.DMA((TILE_U // row.shape[1],)),
        ],
        compiler_params=pltpu.CompilerParams(vmem_limit_bytes=8 * 2**20),
        name="merge_tile",
    )(*map(in_vmem, (sums, row, col)))


def shards(
    aperture_amp,
    aperture_phase,
    plane_depths,
    send_list,
    send_count,
    vis_left,
    vis_right,
    block_slot,
    block_pos,
    block_count,
):
    kernel_size = vis_right.shape[1]
    tiles, capacity = send_list.shape[1:]
    both = ("tu", "tv")
    outgoing = make_kernels(
        aperture_amp, aperture_phase, plane_depths, send_list[0].T, send_count, kernel_size
    )
    outgoing = outgoing.reshape((tiles, capacity) + outgoing.shape[1:])
    arrived = lax.all_to_all(outgoing, both, split_axis=0, concat_axis=0, tiled=True)
    received = arrived.reshape((-1,) + arrived.shape[2:])
    layout = Layout(block_pos.shape[0], (TILE_U // kernel_size) * (TILE_V // kernel_size))
    plan, left, right = plan_blocks(block_pos, block_slot, block_count, vis_left, vis_right, layout)
    carried, (col,) = grid_part(plan, 0, received, left, right, None, layout)
    col = around(col, "tv")
    carried, _ = grid_part(plan, 1, received, left, right, carried, layout)
    sums, row = row_halo(carried[0], col, kernel_size)
    row = around(row, "tu")
    carried, _ = grid_part(plan, 2, received, left, right, [sums, *carried[1:]], layout)
    return merge_tile(carried[0], row, col)


def solution(mesh):
    placed = (
        P(("tu", "tv"), None, None),
        P(("tu", "tv"), None, None),
        P(),
        P(("tu", "tv"), None, None),
        P(("tu", "tv"), None),
        P(("tu", "tv"), None, None),
        P(("tu", "tv"), None, None),
        P(("tu", "tv")),
        P(("tu", "tv")),
        P(("tu", "tv")),
    )
    return jax.shard_map(
        shards, mesh=mesh, in_specs=placed, out_specs=P(None, "tu", "tv"), check_vma=False
    )
```

```python
import functools
import math

import jax
import jax.numpy as jnp
import numpy as np
from jax import lax
from jax.experimental import pallas as pl
from jax.experimental.pallas import tpu as pltpu
from jax.sharding import PartitionSpec as P

TILE_U = 256
TILE_V = 512
QUAD = 4
UNROLL = 4
STEP = 2 * UNROLL
RING = 4
LEFT, RIGHT = 0, 1

def _fit(fn, degree):
    span = math.pi ** 2
    nodes = 0.5 * span * (1.0 - np.cos(np.pi * (np.arange(400) + 0.5) / 400))
    cheb = np.polynomial.chebyshev.Chebyshev.fit(nodes, fn(np.sqrt(nodes)), degree, domain=[0, span])
    return [float(c) for c in cheb.convert(kind=np.polynomial.Polynomial).coef]


COS_POLY = _fit(np.cos, 6)
SIN_POLY = _fit(lambda x: np.sin(x) / x, 5)


def horner(coefs, u):
    total = jnp.full_like(u, coefs[-1])
    for coef in coefs[-2::-1]:
        total = total * u + coef
    return total


def cos_sin(x):
    u = x * x
    return horner(COS_POLY, u), x * horner(SIN_POLY, u)


def around(block, axes):
    sizes = [lax.axis_size(axis) for axis in axes]
    route = []
    for place in np.ndindex(*sizes):
        target = [(i + 1) % n for i, n in zip(place, sizes)]
        route.append((int(np.ravel_multi_index(place, sizes)), int(np.ravel_multi_index(target, sizes))))
    return lax.ppermute(block, axes, route)


def past_first(axes, halo):
    real = functools.reduce(jnp.logical_and, [lax.axis_index(axis) > 0 for axis in axes])
    return jnp.where(real, halo.astype(jnp.float32), 0.0)


def in_hbm(array):
    return pltpu.with_memory_space_constraint(array, pltpu.HBM)


def in_vmem(array):
    return pltpu.with_memory_space_constraint(array, pltpu.VMEM)


def in_smem(array):
    return pltpu.with_memory_space_constraint(array, pltpu.SMEM)


def kernels_body(
    list_hbm, count_hbm, depth_hbm, amp_hbm, phase_hbm, out_ref,
    chosen_list, count, depth, amp, phase, table, screen, halves, made, small_sems, bulk_sems,
):
    screens, size, _ = amp.shape
    planes = depth.shape[0]
    kernel_size = out_ref.shape[1]
    small = [
        pltpu.make_async_copy(depth_hbm, depth, small_sems.at[0]),
        pltpu.make_async_copy(list_hbm, chosen_list, small_sems.at[1]),
        pltpu.make_async_copy(count_hbm, count, small_sems.at[2]),
    ]
    for copy in small:
        copy.start()

    def bulk(s):
        return [
            pltpu.make_async_copy(amp_hbm.at[s], amp.at[s], bulk_sems.at[0, s]),
            pltpu.make_async_copy(phase_hbm.at[s], phase.at[s], bulk_sems.at[1, s]),
        ]

    for copy in bulk(0):
        copy.start()

    frequency = lax.broadcasted_iota(jnp.int32, (kernel_size, size), 0) - kernel_size // 2
    cells = lax.broadcasted_iota(jnp.int32, (kernel_size, size), 1)
    turns = frequency.astype(jnp.float32) * cells.astype(jnp.float32) / size
    real_f, imag_f = cos_sin((2.0 * math.pi) * (turns - jnp.round(turns)))
    real_f = real_f.astype(jnp.bfloat16).astype(jnp.float32)
    imag_f = (-imag_f).astype(jnp.bfloat16).astype(jnp.float32)
    place = (lax.broadcasted_iota(jnp.int32, (1, size), 1).astype(jnp.float32) - size // 2) / size
    square = place * place
    for copy in small:
        copy.wait()
    for s in range(1, screens):
        for copy in bulk(s):
            copy.start()
    for p in range(planes):
        turns = depth[p] * square
        real_e, imag_e = cos_sin((2.0 * math.pi) * (turns - jnp.round(turns)))
        real_g = (real_f * real_e - imag_f * imag_e).astype(jnp.bfloat16)
        imag_g = (real_f * imag_e + imag_f * real_e).astype(jnp.bfloat16)
        top = slice(p * 2 * kernel_size, (p * 2 + 1) * kernel_size)
        low = slice((p * 2 + 1) * kernel_size, (p * 2 + 2) * kernel_size)
        table[top, :size] = real_g
        table[top, size:] = -imag_g
        table[low, :size] = imag_g
        table[low, size:] = real_g

    @pl.loop(0, screens)
    def _(s):
        for copy in bulk(s):
            copy.wait()
        magnitude = amp[s].astype(jnp.float32)
        real_e, imag_e = cos_sin(phase[s].astype(jnp.float32))
        screen[:size, :] = (magnitude * real_e).astype(jnp.bfloat16)
        screen[size:, :] = (magnitude * imag_e).astype(jnp.bfloat16)
        product = jnp.dot(table[...], screen[...], preferred_element_type=jnp.float32).astype(jnp.bfloat16)
        for p in range(planes):
            base = p * 2 * kernel_size
            halves[s, p, :, :size] = product[base : base + kernel_size]
            halves[s, p, :, size:] = product[base + kernel_size : base + 2 * kernel_size]

    for p in range(planes):
        second = lax.dot_general(
            jnp.concatenate([halves[s, p] for s in range(screens)], axis=0),
            table[p * 2 * kernel_size : (p + 1) * 2 * kernel_size, :],
            (((1,), (1,)), ((), ())),
            preferred_element_type=jnp.float32,
        )
        second = (second * (1.0 / size)).astype(jnp.bfloat16)
        for s in range(screens):
            made[s * planes + p] = second[s * kernel_size : (s + 1) * kernel_size]

    capacity, tiles = chosen_list.shape

    @pl.loop(0, tiles)
    def _(t):
        for c in range(capacity):
            chosen = made[chosen_list[c, t]]
            out_ref[t * capacity + c] = jnp.where(c < count[0, t], chosen, jnp.zeros_like(chosen))


def make_kernels(aperture_amp, aperture_phase, plane_depths, chosen_list, counts, kernel_size):
    screens, size, _ = aperture_amp.shape
    planes = plane_depths.shape[0]
    capacity, tiles = chosen_list.shape
    hbm = pl.BlockSpec(memory_space=pl.ANY)
    return pl.pallas_call(
        kernels_body,
        in_specs=[hbm] * 5,
        out_specs=pl.BlockSpec(memory_space=pltpu.VMEM),
        out_shape=pltpu.VMEM((tiles * capacity, kernel_size, 2 * kernel_size), jnp.bfloat16),
        scratch_shapes=[
            pltpu.SMEM((capacity, tiles), jnp.int32),
            pltpu.SMEM((1, tiles), jnp.int32),
            pltpu.SMEM((planes,), jnp.float32),
            pltpu.VMEM((screens, size, size), jnp.bfloat16),
            pltpu.VMEM((screens, size, size), jnp.bfloat16),
            pltpu.VMEM((planes * 2 * kernel_size, 2 * size), jnp.bfloat16),
            pltpu.VMEM((2 * size, size), jnp.bfloat16),
            pltpu.VMEM((screens, planes, kernel_size, 2 * size), jnp.bfloat16),
            pltpu.VMEM((screens * planes, kernel_size, 2 * kernel_size), jnp.bfloat16),
            pltpu.SemaphoreType.DMA((3,)),
            pltpu.SemaphoreType.DMA((2, screens)),
        ],
        compiler_params=pltpu.CompilerParams(vmem_limit_bytes=32 * 2**20),
        name="make_kernels",
    )(*map(in_hbm, (chosen_list, counts, plane_depths, aperture_amp, aperture_phase)))


class Layout:
    def __init__(self, blocks, anchors):
        self.parts = 3
        quads = (blocks + (QUAD - 1) * anchors) // QUAD + 1
        self.quads = (quads + STEP - 1) // STEP * STEP
        self.anchor = self.parts + 1
        self.slot = self.anchor + self.quads
        self.total = self.slot + (self.quads + UNROLL) * QUAD


def plan_body(
    pos_ref, slot_ref, count_ref, left_hbm, right_hbm, plan_ref, left_out, right_out,
    left_ref, right_ref, tally, cursor, sems, *, layout, row_slots, col_slots,
):
    anchors = row_slots * col_slots
    border = row_slots + col_slots - 1
    live = count_ref[0]

    def copies(block, place):
        return [
            pltpu.make_async_copy(left_hbm.at[block], left_ref.at[place], sems.at[0]),
            pltpu.make_async_copy(right_hbm.at[block], right_ref.at[place], sems.at[1]),
        ]

    def put(block, place, slot):
        plan_ref[layout.slot + place] = slot
        for copy in copies(block, place):
            copy.start()

    @pl.loop(0, anchors)
    def _(q):
        tally[q] = 0

    @pl.loop(0, live)
    def _(j):
        q = pos_ref[j]
        tally[q] = tally[q] + 1

    def lay(rank, quad):
        inner = rank - border
        q = jnp.where(
            rank < row_slots,
            rank * col_slots + col_slots - 1,
            jnp.where(
                rank < border,
                (row_slots - 1) * col_slots + rank - row_slots,
                (inner // (col_slots - 1)) * col_slots + lax.rem(inner, col_slots - 1),
            ),
        )
        number = tally[q]
        quads = (number + QUAD - 1) // QUAD
        cursor[q] = quad * QUAD

        @pl.loop(0, quads)
        def _(i):
            plan_ref[layout.anchor + quad + i] = q

        @pl.loop(quad * QUAD + number, (quad + quads) * QUAD)
        def _(i):
            put(0, i, -1)

        return quad + quads

    quad = 0
    begin = 0
    plan_ref[0] = 0
    for part, end in enumerate([row_slots, border, anchors]):
        quad = lax.fori_loop(begin, end, lay, quad)
        begin = end
        plan_ref[part + 1] = ((quad + STEP - 1) // STEP) * STEP

    full = ((quad + STEP - 1) // STEP) * STEP

    @pl.loop(quad, full)
    def _(i):
        plan_ref[layout.anchor + i] = 0
        for e in range(QUAD):
            put(0, i * QUAD + e, -1)

    quad = full

    @pl.loop(quad * QUAD, (quad + UNROLL) * QUAD)
    def _(i):
        plan_ref[layout.slot + i] = -1

    @pl.loop(0, live)
    def _(j):
        q = pos_ref[j]
        at = cursor[q]
        cursor[q] = at + 1
        put(j, at, slot_ref[j])

    chunk = STEP * QUAD

    @pl.loop(0, quad // STEP)
    def _(i):
        rows = pl.ds(0, chunk)
        pltpu.make_async_copy(left_hbm.at[rows], left_ref.at[rows], sems.at[0]).wait()
        pltpu.make_async_copy(right_hbm.at[rows], right_ref.at[rows], sems.at[1]).wait()

    def writes(i):
        rows = pl.ds(i * chunk, chunk)
        return [
            pltpu.make_async_copy(left_ref.at[rows], left_out.at[rows], sems.at[2]),
            pltpu.make_async_copy(right_ref.at[rows], right_out.at[rows], sems.at[3]),
        ]

    @pl.loop(0, quad // STEP)
    def _(i):
        for copy in writes(i):
            copy.start()

    @pl.loop(0, quad // STEP)
    def _(i):
        for copy in writes(i):
            copy.wait()


def plan_blocks(block_pos, block_slot, block_count, vis_left, vis_right, layout):
    kernel_size = vis_right.shape[1]
    row_slots, col_slots = TILE_U // kernel_size, TILE_V // kernel_size
    smem = pl.BlockSpec(memory_space=pltpu.SMEM)
    hbm = pl.BlockSpec(memory_space=pl.ANY)
    places = layout.quads * QUAD
    return pl.pallas_call(
        functools.partial(plan_body, layout=layout, row_slots=row_slots, col_slots=col_slots),
        in_specs=[smem] * 3 + [hbm] * 2,
        out_specs=[smem, hbm, hbm],
        out_shape=[
            pltpu.SMEM((layout.total,), jnp.int32),
            pltpu.HBM((places,) + vis_left.shape[1:], vis_left.dtype),
            pltpu.HBM((places,) + vis_right.shape[1:], vis_right.dtype),
        ],
        scratch_shapes=[
            pltpu.VMEM((places,) + vis_left.shape[1:], vis_left.dtype),
            pltpu.VMEM((places,) + vis_right.shape[1:], vis_right.dtype),
            pltpu.SMEM((row_slots * col_slots,), jnp.int32),
            pltpu.SMEM((row_slots * col_slots,), jnp.int32),
            pltpu.SemaphoreType.DMA((4,)),
        ],
        compiler_params=pltpu.CompilerParams(vmem_limit_bytes=36 * 2**20),
        name="plan_blocks",
    )(block_pos, block_slot, block_count, in_hbm(vis_left), in_hbm(vis_right))


def strip(sums, row_slots, col_slots, kernel_size, plane, a, col):
    patch = sums.shape[1]
    lanes = slice(plane * patch, (plane + 1) * patch)
    total = None
    if a < row_slots:
        total = sums[a * col_slots + col, :kernel_size, lanes]
    if a > 0:
        above = sums[(a - 1) * col_slots + col, kernel_size:, lanes]
        total = above if total is None else total + above
    return total


def grid_body(
    plan_ref, kern_ref, left_hbm, right_hbm, *rest, part, first_part, layout, row_slots, col_slots
):
    if not first_part:
        rest = rest[4:]
    sums, left_ring, right_ring, ahead, *rest = rest
    if part == 0:
        col_ref, corner_ref, *rest = rest
    if part == 1:
        row_ref, *rest = rest
    behind_ref, sems = rest
    mixed = (ahead, behind_ref)
    slots, kernel_size, _ = kern_ref.shape
    patch = left_hbm.shape[1]
    chunk = STEP * QUAD
    begin = plan_ref[part] // STEP
    end = plan_ref[part + 1] // STEP
    limit = jnp.minimum(plan_ref[layout.parts] // STEP, end + 2)

    def fetch(i):
        source = pl.ds(i * chunk, chunk)
        ring = lax.rem(i, RING)
        return [
            pltpu.make_async_copy(left_hbm.at[source], left_ring.at[ring], sems.at[0, ring]),
            pltpu.make_async_copy(right_hbm.at[source], right_ring.at[ring], sems.at[1, ring]),
        ]

    def start(i, which):
        @pl.when(i < limit)
        def _():
            fetch(i)[which].start()

    def wait(i, which):
        fresh = (i < limit) if first_part else ((i < limit) & (i > begin + 1))

        @pl.when(fresh)
        def _():
            fetch(i)[which].wait()

    if first_part:
        start(0, RIGHT)
        start(1, RIGHT)
        start(0, LEFT)

        @pl.loop(0, sums.shape[0])
        def _(q):
            sums[q] = jnp.zeros(sums.shape[1:], sums.dtype)

    zero = jnp.zeros((kernel_size, patch), jnp.bfloat16)

    def first(i, ring, at, ref, u):
        for e in range(QUAD):
            slot = plan_ref[layout.slot + (i * STEP + at) * QUAD + e]
            right = right_ring[ring, at * QUAD + e]
            kern = kern_ref[jnp.maximum(slot, 0)]
            kern = jnp.where(slot >= 0, kern, jnp.zeros_like(kern))
            spread = jnp.concatenate(
                [jnp.concatenate([right, zero], axis=1), jnp.concatenate([zero, right], axis=1)], axis=0
            )
            out = jnp.dot(kern, spread, preferred_element_type=jnp.float32).astype(jnp.bfloat16)
            top = slice(e * 2 * kernel_size, (e * 2 + 1) * kernel_size)
            low = slice((e * 2 + 1) * kernel_size, (e * 2 + 2) * kernel_size)
            ref[u, top, :] = out
            ref[u, low, :patch] = -out[:, patch:]
            ref[u, low, patch:] = out[:, :patch]

    def second(i, ring, at, ref, u):
        left = jnp.concatenate([left_ring[ring, at * QUAD + e] for e in range(QUAD)], axis=1)
        q = plan_ref[layout.anchor + i * STEP + at]
        sums[q] += jnp.dot(left, ref[u], preferred_element_type=jnp.float32)

    if first_part:
        wait(0, RIGHT)
        start(1, LEFT)
        for u in range(UNROLL):
            first(0, 0, u, mixed[0], u)
    start(begin + 2, RIGHT)
    start(begin + 2, LEFT)

    @pl.loop(begin, end)
    def _(i):
        here = lax.rem(i, RING)
        there = lax.rem(i + 1, RING)
        start(i + 3, RIGHT)
        start(i + 3, LEFT)
        wait(i, LEFT)
        wait(i + 1, RIGHT)
        for u in range(UNROLL):
            first(i, here, UNROLL + u, mixed[1], u)
            second(i, here, u, mixed[0], u)
        for u in range(UNROLL):
            first(i + 1, there, u, mixed[0], u)
            second(i, here, UNROLL + u, mixed[1], u)

    wait(end, LEFT)
    wait(end + 1, LEFT)
    wait(end + 1, RIGHT)
    if part > 1:
        return
    low = lax.broadcasted_iota(jnp.int32, (kernel_size, patch), 1) < kernel_size
    take = functools.partial(strip, sums, row_slots, col_slots, kernel_size)
    if part == 0:
        for a in range(row_slots + 1):
            real = pltpu.roll(take(0, a, col_slots - 1), kernel_size, 1)
            edge = jnp.where(low, real, take(1, a, col_slots - 1)).astype(col_ref.dtype)
            if a < row_slots:
                col_ref[a * kernel_size : (a + 1) * kernel_size, :] = edge
            else:
                corner_ref[...] = edge
        return
    for plane in range(2):
        behind = 0.0
        for tile in range(col_slots // 2):
            odd = pltpu.roll(take(plane, row_slots, 2 * tile + 1), kernel_size, 1)
            value = take(plane, row_slots, 2 * tile) + jnp.where(low, behind, odd)
            row_ref[plane, :, tile * patch : (tile + 1) * patch] = value.astype(row_ref.dtype)
            behind = odd


def grid_part(plan, part, kernels, left, right, carried, layout):
    kernel_size = kernels.shape[1]
    patch = left.shape[1]
    row_slots, col_slots = TILE_U // kernel_size, TILE_V // kernel_size
    smem = pl.BlockSpec(memory_space=pltpu.SMEM)
    vmem = pl.BlockSpec(memory_space=pltpu.VMEM)
    hbm = pl.BlockSpec(memory_space=pl.ANY)
    first_part = carried is None
    carried = [] if first_part else [in_vmem(array) for array in carried]
    mixed_shape = (UNROLL, QUAD * 2 * kernel_size, 2 * patch)
    out_shape = [
        pltpu.VMEM((row_slots * col_slots, patch, 2 * patch), jnp.float32),
        pltpu.VMEM((RING, STEP * QUAD) + left.shape[1:], left.dtype),
        pltpu.VMEM((RING, STEP * QUAD) + right.shape[1:], right.dtype),
        pltpu.VMEM(mixed_shape, jnp.bfloat16),
    ]
    if part == 0:
        out_shape.append(pltpu.VMEM((TILE_U, 2 * kernel_size), jnp.bfloat16))
        out_shape.append(pltpu.VMEM((kernel_size, 2 * kernel_size), jnp.bfloat16))
    if part == 1:
        out_shape.append(pltpu.VMEM((2, kernel_size, TILE_V), jnp.bfloat16))
    out = pl.pallas_call(
        functools.partial(
            grid_body,
            part=part,
            first_part=first_part,
            layout=layout,
            row_slots=row_slots,
            col_slots=col_slots,
        ),
        in_specs=[smem, vmem, hbm, hbm] + [vmem] * len(carried),
        out_specs=[vmem] * len(out_shape),
        out_shape=out_shape,
        input_output_aliases={4 + i: i for i in range(len(carried))},
        scratch_shapes=[
            pltpu.VMEM(mixed_shape, jnp.bfloat16),
            pltpu.SemaphoreType.DMA((2, RING)),
        ],
        compiler_params=pltpu.CompilerParams(vmem_limit_bytes=12 * 2**20),
        cost_estimate=pl.CostEstimate(flops=2 * 10**9, bytes_accessed=10**7, transcendentals=0),
        name="grid_part",
    )(in_smem(plan), in_vmem(kernels), in_hbm(left), in_hbm(right), *carried)
    return out[:4], out[4:]


def merge_body(sums, row_ref, col_ref, corner_ref, out_hbm, out_ref, sems):
    kernel_size = row_ref.shape[1]
    patch = sums.shape[1]
    row_slots = out_ref.shape[1] // kernel_size
    col_slots = out_ref.shape[2] // kernel_size
    low = lax.broadcasted_iota(jnp.int32, (kernel_size, patch), 1) < kernel_size
    take = functools.partial(strip, sums, row_slots, col_slots, kernel_size)
    for a in range(row_slots):
        rows = slice(a * kernel_size, (a + 1) * kernel_size)
        edge = past_first(["tv"], col_ref[rows, :])
        if a == 0:
            edge = edge + past_first(["tu", "tv"], corner_ref[...])
        for plane in range(2):
            behind = edge if plane == 0 else pltpu.roll(edge, kernel_size, 1)
            for tile in range(col_slots // 2):
                lanes = slice(tile * patch, (tile + 1) * patch)
                odd = pltpu.roll(take(plane, a, 2 * tile + 1), kernel_size, 1)
                value = take(plane, a, 2 * tile) + jnp.where(low, behind, odd)
                if a == 0:
                    value = value + past_first(["tu"], row_ref[plane, :, lanes])
                out_ref[plane, rows, lanes] = value
                behind = odd
        pltpu.make_async_copy(out_ref.at[:, rows], out_hbm.at[:, rows], sems.at[a]).start()
    for a in range(row_slots):
        rows = slice(a * kernel_size, (a + 1) * kernel_size)
        pltpu.make_async_copy(out_ref.at[:, rows], out_hbm.at[:, rows], sems.at[a]).wait()


def merge_tile(sums, row, col, corner):
    vmem = pl.BlockSpec(memory_space=pltpu.VMEM)
    return pl.pallas_call(
        merge_body,
        in_specs=[vmem] * 4,
        out_specs=pl.BlockSpec(memory_space=pl.ANY),
        out_shape=jax.ShapeDtypeStruct((2, TILE_U, TILE_V), jnp.float32),
        scratch_shapes=[
            pltpu.VMEM((2, TILE_U, TILE_V), jnp.float32),
            pltpu.SemaphoreType.DMA((TILE_U // row.shape[1],)),
        ],
        compiler_params=pltpu.CompilerParams(vmem_limit_bytes=8 * 2**20),
        name="merge_tile",
    )(*map(in_vmem, (sums, row, col, corner)))


def shards(
    aperture_amp,
    aperture_phase,
    plane_depths,
    send_list,
    send_count,
    vis_left,
    vis_right,
    block_slot,
    block_pos,
    block_count,
):
    kernel_size = vis_right.shape[1]
    tiles, capacity = send_list.shape[1:]
    both = ("tu", "tv")
    outgoing = make_kernels(
        aperture_amp, aperture_phase, plane_depths, send_list[0].T, send_count, kernel_size
    )
    outgoing = outgoing.reshape((tiles, capacity) + outgoing.shape[1:])
    arrived = lax.all_to_all(outgoing, both, split_axis=0, concat_axis=0, tiled=True)
    received = arrived.reshape((-1,) + arrived.shape[2:])
    layout = Layout(block_pos.shape[0], (TILE_U // kernel_size) * (TILE_V // kernel_size))
    plan, left, right = plan_blocks(block_pos, block_slot, block_count, vis_left, vis_right, layout)
    carried, (col, corner) = grid_part(plan, 0, received, left, right, None, layout)
    col = around(col, ("tv",))
    corner = around(corner, ("tu", "tv"))
    carried, (row,) = grid_part(plan, 1, received, left, right, carried, layout)
    row = around(row, ("tu",))
    carried, _ = grid_part(plan, 2, received, left, right, carried, layout)
    return merge_tile(carried[0], row, col, corner)


def solution(mesh):
    placed = (
        P(("tu", "tv"), None, None),
        P(("tu", "tv"), None, None),
        P(),
        P(("tu", "tv"), None, None),
        P(("tu", "tv"), None),
        P(("tu", "tv"), None, None),
        P(("tu", "tv"), None, None),
        P(("tu", "tv")),
        P(("tu", "tv")),
        P(("tu", "tv")),
    )
    return jax.shard_map(
        shards, mesh=mesh, in_specs=placed, out_specs=P(None, "tu", "tv"), check_vma=False
    )
```

```python
import functools
import math

import jax
import jax.numpy as jnp
import numpy as np
from jax import lax
from jax.experimental import pallas as pl
from jax.experimental.pallas import tpu as pltpu
from jax.sharding import PartitionSpec as P

TILE_U = 256
TILE_V = 512
QUAD = 4
UNROLL = 4
STEP = 2 * UNROLL
RING = 4
LEFT, RIGHT = 0, 1

def _fit(fn, degree):
    span = math.pi ** 2
    nodes = 0.5 * span * (1.0 - np.cos(np.pi * (np.arange(400) + 0.5) / 400))
    cheb = np.polynomial.chebyshev.Chebyshev.fit(nodes, fn(np.sqrt(nodes)), degree, domain=[0, span])
    return [float(c) for c in cheb.convert(kind=np.polynomial.Polynomial).coef]


COS_POLY = _fit(np.cos, 6)
SIN_POLY = _fit(lambda x: np.sin(x) / x, 5)


def horner(coefs, u):
    total = jnp.full_like(u, coefs[-1])
    for coef in coefs[-2::-1]:
        total = total * u + coef
    return total


def cos_sin(x):
    u = x * x
    return horner(COS_POLY, u), x * horner(SIN_POLY, u)


def around(block, axes):
    sizes = [lax.axis_size(axis) for axis in axes]
    route = []
    for place in np.ndindex(*sizes):
        target = [(i + 1) % n for i, n in zip(place, sizes)]
        route.append((int(np.ravel_multi_index(place, sizes)), int(np.ravel_multi_index(target, sizes))))
    return lax.ppermute(block, axes, route)


def past_first(axes, halo):
    real = functools.reduce(jnp.logical_and, [lax.axis_index(axis) > 0 for axis in axes])
    return jnp.where(real, halo.astype(jnp.float32), 0.0)


def in_hbm(array):
    return pltpu.with_memory_space_constraint(array, pltpu.HBM)


def in_vmem(array):
    return pltpu.with_memory_space_constraint(array, pltpu.VMEM)


def in_smem(array):
    return pltpu.with_memory_space_constraint(array, pltpu.SMEM)


def kernels_body(
    list_hbm, count_hbm, depth_hbm, amp_hbm, phase_hbm, out_ref,
    chosen_list, count, depth, amp, phase, table, screen, halves, made, small_sems, bulk_sems,
):
    screens, size, _ = amp.shape
    planes = depth.shape[0]
    kernel_size = out_ref.shape[1]
    small = [
        pltpu.make_async_copy(depth_hbm, depth, small_sems.at[0]),
        pltpu.make_async_copy(list_hbm, chosen_list, small_sems.at[1]),
        pltpu.make_async_copy(count_hbm, count, small_sems.at[2]),
    ]
    for copy in small:
        copy.start()

    def bulk(s):
        return [
            pltpu.make_async_copy(amp_hbm.at[s], amp.at[s], bulk_sems.at[0, s]),
            pltpu.make_async_copy(phase_hbm.at[s], phase.at[s], bulk_sems.at[1, s]),
        ]

    for copy in bulk(0):
        copy.start()

    frequency = lax.broadcasted_iota(jnp.int32, (kernel_size, size), 0) - kernel_size // 2
    cells = lax.broadcasted_iota(jnp.int32, (kernel_size, size), 1)
    turns = frequency.astype(jnp.float32) * cells.astype(jnp.float32) / size
    real_f, imag_f = cos_sin((2.0 * math.pi) * (turns - jnp.round(turns)))
    real_f = real_f.astype(jnp.bfloat16).astype(jnp.float32)
    imag_f = (-imag_f).astype(jnp.bfloat16).astype(jnp.float32)
    place = (lax.broadcasted_iota(jnp.int32, (1, size), 1).astype(jnp.float32) - size // 2) / size
    square = place * place
    for copy in small:
        copy.wait()
    for s in range(1, screens):
        for copy in bulk(s):
            copy.start()
    for p in range(planes):
        turns = depth[p] * square
        real_e, imag_e = cos_sin((2.0 * math.pi) * (turns - jnp.round(turns)))
        real_g = (real_f * real_e - imag_f * imag_e).astype(jnp.bfloat16)
        imag_g = (real_f * imag_e + imag_f * real_e).astype(jnp.bfloat16)
        top = slice(p * 2 * kernel_size, (p * 2 + 1) * kernel_size)
        low = slice((p * 2 + 1) * kernel_size, (p * 2 + 2) * kernel_size)
        table[top, :size] = real_g
        table[top, size:] = -imag_g
        table[low, :size] = imag_g
        table[low, size:] = real_g

    @pl.loop(0, screens)
    def _(s):
        for copy in bulk(s):
            copy.wait()
        magnitude = amp[s].astype(jnp.float32)
        real_e, imag_e = cos_sin(phase[s].astype(jnp.float32))
        screen[:size, :] = (magnitude * real_e).astype(jnp.bfloat16)
        screen[size:, :] = (magnitude * imag_e).astype(jnp.bfloat16)
        product = jnp.dot(table[...], screen[...], preferred_element_type=jnp.float32).astype(jnp.bfloat16)
        for p in range(planes):
            base = p * 2 * kernel_size
            halves[s, p, :, :size] = product[base : base + kernel_size]
            halves[s, p, :, size:] = product[base + kernel_size : base + 2 * kernel_size]

    for p in range(planes):
        second = lax.dot_general(
            jnp.concatenate([halves[s, p] for s in range(screens)], axis=0),
            table[p * 2 * kernel_size : (p + 1) * 2 * kernel_size, :],
            (((1,), (1,)), ((), ())),
            preferred_element_type=jnp.float32,
        )
        second = (second * (1.0 / size)).astype(jnp.bfloat16)
        for s in range(screens):
            made[s * planes + p] = second[s * kernel_size : (s + 1) * kernel_size]

    capacity, tiles = chosen_list.shape

    @pl.loop(0, tiles)
    def _(t):
        for c in range(capacity):
            chosen = made[chosen_list[c, t]]
            out_ref[t * capacity + c] = jnp.where(c < count[0, t], chosen, jnp.zeros_like(chosen))


def make_kernels(aperture_amp, aperture_phase, plane_depths, chosen_list, counts, kernel_size):
    screens, size, _ = aperture_amp.shape
    planes = plane_depths.shape[0]
    capacity, tiles = chosen_list.shape
    hbm = pl.BlockSpec(memory_space=pl.ANY)
    return pl.pallas_call(
        kernels_body,
        in_specs=[hbm] * 5,
        out_specs=pl.BlockSpec(memory_space=pltpu.VMEM),
        out_shape=pltpu.VMEM((tiles * capacity, kernel_size, 2 * kernel_size), jnp.bfloat16),
        scratch_shapes=[
            pltpu.SMEM((capacity, tiles), jnp.int32),
            pltpu.SMEM((1, tiles), jnp.int32),
            pltpu.SMEM((planes,), jnp.float32),
            pltpu.VMEM((screens, size, size), jnp.bfloat16),
            pltpu.VMEM((screens, size, size), jnp.bfloat16),
            pltpu.VMEM((planes * 2 * kernel_size, 2 * size), jnp.bfloat16),
            pltpu.VMEM((2 * size, size), jnp.bfloat16),
            pltpu.VMEM((screens, planes, kernel_size, 2 * size), jnp.bfloat16),
            pltpu.VMEM((screens * planes, kernel_size, 2 * kernel_size), jnp.bfloat16),
            pltpu.SemaphoreType.DMA((3,)),
            pltpu.SemaphoreType.DMA((2, screens)),
        ],
        compiler_params=pltpu.CompilerParams(vmem_limit_bytes=32 * 2**20),
        name="make_kernels",
    )(*map(in_hbm, (chosen_list, counts, plane_depths, aperture_amp, aperture_phase)))


class Layout:
    def __init__(self, blocks, anchors):
        self.parts = 2
        quads = (blocks + (QUAD - 1) * anchors) // QUAD + 1
        self.quads = (quads + STEP - 1) // STEP * STEP
        self.anchor = self.parts + 1
        self.slot = self.anchor + self.quads
        self.total = self.slot + (self.quads + UNROLL) * QUAD


def plan_body(
    pos_ref, slot_ref, count_ref, left_hbm, right_hbm, plan_ref, left_out, right_out,
    left_ref, right_ref, tally, cursor, sems, *, layout, row_slots, col_slots,
):
    anchors = row_slots * col_slots
    border = row_slots + col_slots - 1
    live = count_ref[0]

    def copies(block, place):
        return [
            pltpu.make_async_copy(left_hbm.at[block], left_ref.at[place], sems.at[0]),
            pltpu.make_async_copy(right_hbm.at[block], right_ref.at[place], sems.at[1]),
        ]

    def put(block, place, slot):
        plan_ref[layout.slot + place] = slot
        for copy in copies(block, place):
            copy.start()

    @pl.loop(0, anchors)
    def _(q):
        tally[q] = 0

    @pl.loop(0, live)
    def _(j):
        q = pos_ref[j]
        tally[q] = tally[q] + 1

    def lay(rank, quad):
        inner = rank - border
        q = jnp.where(
            rank < row_slots,
            rank * col_slots + col_slots - 1,
            jnp.where(
                rank < border,
                (row_slots - 1) * col_slots + rank - row_slots,
                (inner // (col_slots - 1)) * col_slots + lax.rem(inner, col_slots - 1),
            ),
        )
        number = tally[q]
        quads = (number + QUAD - 1) // QUAD
        cursor[q] = quad * QUAD

        @pl.loop(0, quads)
        def _(i):
            plan_ref[layout.anchor + quad + i] = q

        @pl.loop(quad * QUAD + number, (quad + quads) * QUAD)
        def _(i):
            put(0, i, -1)

        return quad + quads

    quad = 0
    begin = 0
    plan_ref[0] = 0
    for part, end in enumerate([border, anchors]):
        quad = lax.fori_loop(begin, end, lay, quad)
        begin = end
        plan_ref[part + 1] = ((quad + STEP - 1) // STEP) * STEP

    full = ((quad + STEP - 1) // STEP) * STEP

    @pl.loop(quad, full)
    def _(i):
        plan_ref[layout.anchor + i] = 0
        for e in range(QUAD):
            put(0, i * QUAD + e, -1)

    quad = full

    @pl.loop(quad * QUAD, (quad + UNROLL) * QUAD)
    def _(i):
        plan_ref[layout.slot + i] = -1

    @pl.loop(0, live)
    def _(j):
        q = pos_ref[j]
        at = cursor[q]
        cursor[q] = at + 1
        put(j, at, slot_ref[j])

    chunk = STEP * QUAD

    @pl.loop(0, quad // STEP)
    def _(i):
        rows = pl.ds(0, chunk)
        pltpu.make_async_copy(left_hbm.at[rows], left_ref.at[rows], sems.at[0]).wait()
        pltpu.make_async_copy(right_hbm.at[rows], right_ref.at[rows], sems.at[1]).wait()

    def writes(i):
        rows = pl.ds(i * chunk, chunk)
        return [
            pltpu.make_async_copy(left_ref.at[rows], left_out.at[rows], sems.at[2]),
            pltpu.make_async_copy(right_ref.at[rows], right_out.at[rows], sems.at[3]),
        ]

    @pl.loop(0, quad // STEP)
    def _(i):
        for copy in writes(i):
            copy.start()

    @pl.loop(0, quad // STEP)
    def _(i):
        for copy in writes(i):
            copy.wait()


def plan_blocks(block_pos, block_slot, block_count, vis_left, vis_right, layout):
    kernel_size = vis_right.shape[1]
    row_slots, col_slots = TILE_U // kernel_size, TILE_V // kernel_size
    smem = pl.BlockSpec(memory_space=pltpu.SMEM)
    hbm = pl.BlockSpec(memory_space=pl.ANY)
    places = layout.quads * QUAD
    return pl.pallas_call(
        functools.partial(plan_body, layout=layout, row_slots=row_slots, col_slots=col_slots),
        in_specs=[smem] * 3 + [hbm] * 2,
        out_specs=[smem, hbm, hbm],
        out_shape=[
            pltpu.SMEM((layout.total,), jnp.int32),
            pltpu.HBM((places,) + vis_left.shape[1:], vis_left.dtype),
            pltpu.HBM((places,) + vis_right.shape[1:], vis_right.dtype),
        ],
        scratch_shapes=[
            pltpu.VMEM((places,) + vis_left.shape[1:], vis_left.dtype),
            pltpu.VMEM((places,) + vis_right.shape[1:], vis_right.dtype),
            pltpu.SMEM((row_slots * col_slots,), jnp.int32),
            pltpu.SMEM((row_slots * col_slots,), jnp.int32),
            pltpu.SemaphoreType.DMA((4,)),
        ],
        compiler_params=pltpu.CompilerParams(vmem_limit_bytes=36 * 2**20),
        name="plan_blocks",
    )(block_pos, block_slot, block_count, in_hbm(vis_left), in_hbm(vis_right))


def strip(sums, row_slots, col_slots, kernel_size, plane, a, col):
    patch = sums.shape[1]
    lanes = slice(plane * patch, (plane + 1) * patch)
    total = None
    if a < row_slots:
        total = sums[a * col_slots + col, :kernel_size, lanes]
    if a > 0:
        above = sums[(a - 1) * col_slots + col, kernel_size:, lanes]
        total = above if total is None else total + above
    return total


def grid_body(
    plan_ref, kern_ref, left_hbm, right_hbm, *rest, part, first_part, layout, row_slots, col_slots
):
    if not first_part:
        rest = rest[4:]
    sums, left_ring, right_ring, ahead, *rest = rest
    if first_part:
        row_ref, col_ref, corner_ref, *rest = rest
    behind_ref, sems = rest
    mixed = (ahead, behind_ref)
    slots, kernel_size, _ = kern_ref.shape
    patch = left_hbm.shape[1]
    chunk = STEP * QUAD
    begin = plan_ref[part] // STEP
    end = plan_ref[part + 1] // STEP
    limit = jnp.minimum(plan_ref[layout.parts] // STEP, end + 2)

    def fetch(i):
        source = pl.ds(i * chunk, chunk)
        ring = lax.rem(i, RING)
        return [
            pltpu.make_async_copy(left_hbm.at[source], left_ring.at[ring], sems.at[0, ring]),
            pltpu.make_async_copy(right_hbm.at[source], right_ring.at[ring], sems.at[1, ring]),
        ]

    def start(i, which):
        @pl.when(i < limit)
        def _():
            fetch(i)[which].start()

    def wait(i, which):
        fresh = (i < limit) if first_part else ((i < limit) & (i > begin + 1))

        @pl.when(fresh)
        def _():
            fetch(i)[which].wait()

    if first_part:
        start(0, RIGHT)
        start(1, RIGHT)
        start(0, LEFT)

        @pl.loop(0, sums.shape[0])
        def _(q):
            sums[q] = jnp.zeros(sums.shape[1:], sums.dtype)

    zero = jnp.zeros((kernel_size, patch), jnp.bfloat16)

    def first(i, ring, at, ref, u):
        for e in range(QUAD):
            slot = plan_ref[layout.slot + (i * STEP + at) * QUAD + e]
            right = right_ring[ring, at * QUAD + e]
            kern = kern_ref[jnp.maximum(slot, 0)]
            kern = jnp.where(slot >= 0, kern, jnp.zeros_like(kern))
            spread = jnp.concatenate(
                [jnp.concatenate([right, zero], axis=1), jnp.concatenate([zero, right], axis=1)], axis=0
            )
            out = jnp.dot(kern, spread, preferred_element_type=jnp.float32).astype(jnp.bfloat16)
            top = slice(e * 2 * kernel_size, (e * 2 + 1) * kernel_size)
            low = slice((e * 2 + 1) * kernel_size, (e * 2 + 2) * kernel_size)
            ref[u, top, :] = out
            ref[u, low, :patch] = -out[:, patch:]
            ref[u, low, patch:] = out[:, :patch]

    def second(i, ring, at, ref, u):
        left = jnp.concatenate([left_ring[ring, at * QUAD + e] for e in range(QUAD)], axis=1)
        q = plan_ref[layout.anchor + i * STEP + at]
        sums[q] += jnp.dot(left, ref[u], preferred_element_type=jnp.float32)

    if first_part:
        wait(0, RIGHT)
        start(1, LEFT)
        for u in range(UNROLL):
            first(0, 0, u, mixed[0], u)
    start(begin + 2, RIGHT)
    start(begin + 2, LEFT)

    @pl.loop(begin, end)
    def _(i):
        here = lax.rem(i, RING)
        there = lax.rem(i + 1, RING)
        start(i + 3, RIGHT)
        start(i + 3, LEFT)
        wait(i, LEFT)
        wait(i + 1, RIGHT)
        for u in range(UNROLL):
            first(i, here, UNROLL + u, mixed[1], u)
            second(i, here, u, mixed[0], u)
        for u in range(UNROLL):
            first(i + 1, there, u, mixed[0], u)
            second(i, here, UNROLL + u, mixed[1], u)

    wait(end, LEFT)
    wait(end + 1, LEFT)
    wait(end + 1, RIGHT)
    if not first_part:
        return
    low = lax.broadcasted_iota(jnp.int32, (kernel_size, patch), 1) < kernel_size
    take = functools.partial(strip, sums, row_slots, col_slots, kernel_size)
    for a in range(row_slots + 1):
        real = pltpu.roll(take(0, a, col_slots - 1), kernel_size, 1)
        edge = jnp.where(low, real, take(1, a, col_slots - 1)).astype(col_ref.dtype)
        if a < row_slots:
            col_ref[a * kernel_size : (a + 1) * kernel_size, :] = edge
        else:
            corner_ref[...] = edge
    for plane in range(2):
        behind = 0.0
        for tile in range(col_slots // 2):
            odd = pltpu.roll(take(plane, row_slots, 2 * tile + 1), kernel_size, 1)
            value = take(plane, row_slots, 2 * tile) + jnp.where(low, behind, odd)
            row_ref[plane, :, tile * patch : (tile + 1) * patch] = value.astype(row_ref.dtype)
            behind = odd


def grid_part(plan, part, kernels, left, right, carried, layout):
    kernel_size = kernels.shape[1]
    patch = left.shape[1]
    row_slots, col_slots = TILE_U // kernel_size, TILE_V // kernel_size
    smem = pl.BlockSpec(memory_space=pltpu.SMEM)
    vmem = pl.BlockSpec(memory_space=pltpu.VMEM)
    hbm = pl.BlockSpec(memory_space=pl.ANY)
    first_part = carried is None
    carried = [] if first_part else [in_vmem(array) for array in carried]
    mixed_shape = (UNROLL, QUAD * 2 * kernel_size, 2 * patch)
    out_shape = [
        pltpu.VMEM((row_slots * col_slots, patch, 2 * patch), jnp.float32),
        pltpu.VMEM((RING, STEP * QUAD) + left.shape[1:], left.dtype),
        pltpu.VMEM((RING, STEP * QUAD) + right.shape[1:], right.dtype),
        pltpu.VMEM(mixed_shape, jnp.bfloat16),
    ]
    if first_part:
        out_shape += [
            pltpu.VMEM((2, kernel_size, TILE_V), jnp.bfloat16),
            pltpu.VMEM((TILE_U, 2 * kernel_size), jnp.bfloat16),
            pltpu.VMEM((kernel_size, 2 * kernel_size), jnp.bfloat16),
        ]
    out = pl.pallas_call(
        functools.partial(
            grid_body,
            part=part,
            first_part=first_part,
            layout=layout,
            row_slots=row_slots,
            col_slots=col_slots,
        ),
        in_specs=[smem, vmem, hbm, hbm] + [vmem] * len(carried),
        out_specs=[vmem] * len(out_shape),
        out_shape=out_shape,
        input_output_aliases={4 + i: i for i in range(len(carried))},
        scratch_shapes=[
            pltpu.VMEM(mixed_shape, jnp.bfloat16),
            pltpu.SemaphoreType.DMA((2, RING)),
        ],
        compiler_params=pltpu.CompilerParams(vmem_limit_bytes=12 * 2**20),
        cost_estimate=pl.CostEstimate(flops=2 * 10**9, bytes_accessed=10**7, transcendentals=0),
        name="grid_part",
    )(in_smem(plan), in_vmem(kernels), in_hbm(left), in_hbm(right), *carried)
    return out[:4], out[4:]


def merge_body(sums, row_ref, col_ref, corner_ref, out_hbm, out_ref, sems):
    kernel_size = row_ref.shape[1]
    patch = sums.shape[1]
    row_slots = out_ref.shape[1] // kernel_size
    col_slots = out_ref.shape[2] // kernel_size
    low = lax.broadcasted_iota(jnp.int32, (kernel_size, patch), 1) < kernel_size
    take = functools.partial(strip, sums, row_slots, col_slots, kernel_size)
    for a in range(row_slots):
        rows = slice(a * kernel_size, (a + 1) * kernel_size)
        edge = past_first(["tv"], col_ref[rows, :])
        if a == 0:
            edge = edge + past_first(["tu", "tv"], corner_ref[...])
        for plane in range(2):
            behind = edge if plane == 0 else pltpu.roll(edge, kernel_size, 1)
            for tile in range(col_slots // 2):
                lanes = slice(tile * patch, (tile + 1) * patch)
                odd = pltpu.roll(take(plane, a, 2 * tile + 1), kernel_size, 1)
                value = take(plane, a, 2 * tile) + jnp.where(low, behind, odd)
                if a == 0:
                    value = value + past_first(["tu"], row_ref[plane, :, lanes])
                out_ref[plane, rows, lanes] = value
                behind = odd
        pltpu.make_async_copy(out_ref.at[:, rows], out_hbm.at[:, rows], sems.at[a]).start()
    for a in range(row_slots):
        rows = slice(a * kernel_size, (a + 1) * kernel_size)
        pltpu.make_async_copy(out_ref.at[:, rows], out_hbm.at[:, rows], sems.at[a]).wait()


def merge_tile(sums, row, col, corner):
    vmem = pl.BlockSpec(memory_space=pltpu.VMEM)
    return pl.pallas_call(
        merge_body,
        in_specs=[vmem] * 4,
        out_specs=pl.BlockSpec(memory_space=pl.ANY),
        out_shape=jax.ShapeDtypeStruct((2, TILE_U, TILE_V), jnp.float32),
        scratch_shapes=[
            pltpu.VMEM((2, TILE_U, TILE_V), jnp.float32),
            pltpu.SemaphoreType.DMA((TILE_U // row.shape[1],)),
        ],
        compiler_params=pltpu.CompilerParams(vmem_limit_bytes=8 * 2**20),
        name="merge_tile",
    )(*map(in_vmem, (sums, row, col, corner)))


def shards(
    aperture_amp,
    aperture_phase,
    plane_depths,
    send_list,
    send_count,
    vis_left,
    vis_right,
    block_slot,
    block_pos,
    block_count,
):
    kernel_size = vis_right.shape[1]
    tiles, capacity = send_list.shape[1:]
    both = ("tu", "tv")
    outgoing = make_kernels(
        aperture_amp, aperture_phase, plane_depths, send_list[0].T, send_count, kernel_size
    )
    outgoing = outgoing.reshape((tiles, capacity) + outgoing.shape[1:])
    arrived = lax.all_to_all(outgoing, both, split_axis=0, concat_axis=0, tiled=True)
    received = arrived.reshape((-1,) + arrived.shape[2:])
    layout = Layout(block_pos.shape[0], (TILE_U // kernel_size) * (TILE_V // kernel_size))
    plan, left, right = plan_blocks(block_pos, block_slot, block_count, vis_left, vis_right, layout)
    carried, (row, col, corner) = grid_part(plan, 0, received, left, right, None, layout)
    row = around(row, ("tu",))
    col = around(col, ("tv",))
    corner = around(corner, ("tu", "tv"))
    carried, _ = grid_part(plan, 1, received, left, right, carried, layout)
    return merge_tile(carried[0], row, col, corner)


def solution(mesh):
    placed = (
        P(("tu", "tv"), None, None),
        P(("tu", "tv"), None, None),
        P(),
        P(("tu", "tv"), None, None),
        P(("tu", "tv"), None),
        P(("tu", "tv"), None, None),
        P(("tu", "tv"), None, None),
        P(("tu", "tv")),
        P(("tu", "tv")),
        P(("tu", "tv")),
    )
    return jax.shard_map(
        shards, mesh=mesh, in_specs=placed, out_specs=P(None, "tu", "tv"), check_vma=False
    )
```

```python
import functools
import math

import jax
import jax.numpy as jnp
import numpy as np
from jax import lax
from jax.experimental import pallas as pl
from jax.experimental.pallas import tpu as pltpu
from jax.sharding import PartitionSpec as P

TILE_U = 256
TILE_V = 512
QUAD = 4
UNROLL = 4
STEP = 2 * UNROLL
RING = 4
LEFT, RIGHT = 0, 1

def _fit(fn, degree):
    span = math.pi ** 2
    nodes = 0.5 * span * (1.0 - np.cos(np.pi * (np.arange(400) + 0.5) / 400))
    cheb = np.polynomial.chebyshev.Chebyshev.fit(nodes, fn(np.sqrt(nodes)), degree, domain=[0, span])
    return [float(c) for c in cheb.convert(kind=np.polynomial.Polynomial).coef]


COS_POLY = _fit(np.cos, 6)
SIN_POLY = _fit(lambda x: np.sin(x) / x, 5)


def horner(coefs, u):
    total = jnp.full_like(u, coefs[-1])
    for coef in coefs[-2::-1]:
        total = total * u + coef
    return total


def cos_sin(x):
    u = x * x
    return horner(COS_POLY, u), x * horner(SIN_POLY, u)


def around(block, axes):
    sizes = [lax.axis_size(axis) for axis in axes]
    route = []
    for place in np.ndindex(*sizes):
        target = [(i + 1) % n for i, n in zip(place, sizes)]
        route.append((int(np.ravel_multi_index(place, sizes)), int(np.ravel_multi_index(target, sizes))))
    return lax.ppermute(block, axes, route)


def past_first(axes, halo):
    real = functools.reduce(jnp.logical_and, [lax.axis_index(axis) > 0 for axis in axes])
    return jnp.where(real, halo.astype(jnp.float32), 0.0)


def in_hbm(array):
    return pltpu.with_memory_space_constraint(array, pltpu.HBM)


def in_vmem(array):
    return pltpu.with_memory_space_constraint(array, pltpu.VMEM)


def in_smem(array):
    return pltpu.with_memory_space_constraint(array, pltpu.SMEM)


def kernels_body(
    list_hbm, count_hbm, depth_hbm, amp_hbm, phase_hbm, out_ref,
    chosen_list, count, depth, amp, phase, table, screen, halves, made, small_sems, bulk_sems,
):
    screens, size, _ = amp.shape
    planes = depth.shape[0]
    kernel_size = out_ref.shape[1]
    small = [
        pltpu.make_async_copy(depth_hbm, depth, small_sems.at[0]),
        pltpu.make_async_copy(list_hbm, chosen_list, small_sems.at[1]),
        pltpu.make_async_copy(count_hbm, count, small_sems.at[2]),
    ]
    for copy in small:
        copy.start()

    def bulk(s):
        return [
            pltpu.make_async_copy(amp_hbm.at[s], amp.at[s], bulk_sems.at[0, s]),
            pltpu.make_async_copy(phase_hbm.at[s], phase.at[s], bulk_sems.at[1, s]),
        ]

    for copy in bulk(0):
        copy.start()

    frequency = lax.broadcasted_iota(jnp.int32, (kernel_size, size), 0) - kernel_size // 2
    cells = lax.broadcasted_iota(jnp.int32, (kernel_size, size), 1)
    turns = frequency.astype(jnp.float32) * cells.astype(jnp.float32) / size
    real_f, imag_f = cos_sin((2.0 * math.pi) * (turns - jnp.round(turns)))
    real_f = real_f.astype(jnp.bfloat16).astype(jnp.float32)
    imag_f = (-imag_f).astype(jnp.bfloat16).astype(jnp.float32)
    place = (lax.broadcasted_iota(jnp.int32, (1, size), 1).astype(jnp.float32) - size // 2) / size
    square = place * place
    for copy in small:
        copy.wait()
    for s in range(1, screens):
        for copy in bulk(s):
            copy.start()
    for p in range(planes):
        turns = depth[p] * square
        real_e, imag_e = cos_sin((2.0 * math.pi) * (turns - jnp.round(turns)))
        real_g = (real_f * real_e - imag_f * imag_e).astype(jnp.bfloat16)
        imag_g = (real_f * imag_e + imag_f * real_e).astype(jnp.bfloat16)
        top = slice(p * 2 * kernel_size, (p * 2 + 1) * kernel_size)
        low = slice((p * 2 + 1) * kernel_size, (p * 2 + 2) * kernel_size)
        table[top, :size] = real_g
        table[top, size:] = -imag_g
        table[low, :size] = imag_g
        table[low, size:] = real_g

    @pl.loop(0, screens)
    def _(s):
        for copy in bulk(s):
            copy.wait()
        magnitude = amp[s].astype(jnp.float32)
        real_e, imag_e = cos_sin(phase[s].astype(jnp.float32))
        screen[:size, :] = (magnitude * real_e).astype(jnp.bfloat16)
        screen[size:, :] = (magnitude * imag_e).astype(jnp.bfloat16)
        product = jnp.dot(table[...], screen[...], preferred_element_type=jnp.float32).astype(jnp.bfloat16)
        for p in range(planes):
            base = p * 2 * kernel_size
            halves[s, p, :, :size] = product[base : base + kernel_size]
            halves[s, p, :, size:] = product[base + kernel_size : base + 2 * kernel_size]

    for p in range(planes):
        second = lax.dot_general(
            jnp.concatenate([halves[s, p] for s in range(screens)], axis=0),
            table[p * 2 * kernel_size : (p + 1) * 2 * kernel_size, :],
            (((1,), (1,)), ((), ())),
            preferred_element_type=jnp.float32,
        )
        second = (second * (1.0 / size)).astype(jnp.bfloat16)
        for s in range(screens):
            made[s * planes + p] = second[s * kernel_size : (s + 1) * kernel_size]

    capacity, tiles = chosen_list.shape

    @pl.loop(0, tiles)
    def _(t):
        for c in range(capacity):
            chosen = made[chosen_list[c, t]]
            out_ref[t * capacity + c] = jnp.where(c < count[0, t], chosen, jnp.zeros_like(chosen))


def make_kernels(aperture_amp, aperture_phase, plane_depths, chosen_list, counts, kernel_size):
    screens, size, _ = aperture_amp.shape
    planes = plane_depths.shape[0]
    capacity, tiles = chosen_list.shape
    hbm = pl.BlockSpec(memory_space=pl.ANY)
    return pl.pallas_call(
        kernels_body,
        in_specs=[hbm] * 5,
        out_specs=pl.BlockSpec(memory_space=pltpu.VMEM),
        out_shape=pltpu.VMEM((tiles * capacity, kernel_size, 2 * kernel_size), jnp.bfloat16),
        scratch_shapes=[
            pltpu.SMEM((capacity, tiles), jnp.int32),
            pltpu.SMEM((1, tiles), jnp.int32),
            pltpu.SMEM((planes,), jnp.float32),
            pltpu.VMEM((screens, size, size), jnp.bfloat16),
            pltpu.VMEM((screens, size, size), jnp.bfloat16),
            pltpu.VMEM((planes * 2 * kernel_size, 2 * size), jnp.bfloat16),
            pltpu.VMEM((2 * size, size), jnp.bfloat16),
            pltpu.VMEM((screens, planes, kernel_size, 2 * size), jnp.bfloat16),
            pltpu.VMEM((screens * planes, kernel_size, 2 * kernel_size), jnp.bfloat16),
            pltpu.SemaphoreType.DMA((3,)),
            pltpu.SemaphoreType.DMA((2, screens)),
        ],
        compiler_params=pltpu.CompilerParams(vmem_limit_bytes=32 * 2**20),
        name="make_kernels",
    )(*map(in_hbm, (chosen_list, counts, plane_depths, aperture_amp, aperture_phase)))


class Layout:
    def __init__(self, blocks, anchors):
        self.parts = 2
        quads = (blocks + (QUAD - 1) * anchors) // QUAD + 1
        self.quads = (quads + STEP - 1) // STEP * STEP
        self.anchor = self.parts + 1
        self.slot = self.anchor + self.quads
        self.total = self.slot + (self.quads + UNROLL) * QUAD


def plan_body(
    pos_ref, slot_ref, count_ref, left_hbm, right_hbm, plan_ref, left_out, right_out,
    left_ref, right_ref, tally, cursor, sems, *, layout, row_slots, col_slots,
):
    anchors = row_slots * col_slots
    border = row_slots + col_slots - 1
    live = count_ref[0]

    def copies(block, place):
        return [
            pltpu.make_async_copy(left_hbm.at[block], left_ref.at[place], sems.at[0]),
            pltpu.make_async_copy(right_hbm.at[block], right_ref.at[place], sems.at[1]),
        ]

    def put(block, place, slot):
        plan_ref[layout.slot + place] = slot
        for copy in copies(block, place):
            copy.start()

    @pl.loop(0, anchors)
    def _(q):
        tally[q] = 0

    @pl.loop(0, live)
    def _(j):
        q = pos_ref[j]
        tally[q] = tally[q] + 1

    def lay(rank, quad):
        inner = rank - border
        q = jnp.where(
            rank < row_slots,
            rank * col_slots + col_slots - 1,
            jnp.where(
                rank < border,
                (row_slots - 1) * col_slots + rank - row_slots,
                (inner // (col_slots - 1)) * col_slots + lax.rem(inner, col_slots - 1),
            ),
        )
        number = tally[q]
        quads = (number + QUAD - 1) // QUAD
        cursor[q] = quad * QUAD

        @pl.loop(0, quads)
        def _(i):
            plan_ref[layout.anchor + quad + i] = q

        @pl.loop(quad * QUAD + number, (quad + quads) * QUAD)
        def _(i):
            put(0, i, -1)

        return quad + quads

    quad = 0
    begin = 0
    plan_ref[0] = 0
    for part, end in enumerate([border, anchors]):
        quad = lax.fori_loop(begin, end, lay, quad)
        begin = end
        plan_ref[part + 1] = ((quad + STEP - 1) // STEP) * STEP

    full = ((quad + STEP - 1) // STEP) * STEP

    @pl.loop(quad, full)
    def _(i):
        plan_ref[layout.anchor + i] = 0
        for e in range(QUAD):
            put(0, i * QUAD + e, -1)

    quad = full

    @pl.loop(quad * QUAD, (quad + UNROLL) * QUAD)
    def _(i):
        plan_ref[layout.slot + i] = -1

    @pl.loop(0, live)
    def _(j):
        q = pos_ref[j]
        at = cursor[q]
        cursor[q] = at + 1
        put(j, at, slot_ref[j])

    chunk = STEP * QUAD

    @pl.loop(0, quad // STEP)
    def _(i):
        rows = pl.ds(0, chunk)
        pltpu.make_async_copy(left_hbm.at[rows], left_ref.at[rows], sems.at[0]).wait()
        pltpu.make_async_copy(right_hbm.at[rows], right_ref.at[rows], sems.at[1]).wait()

    def writes(i):
        rows = pl.ds(i * chunk, chunk)
        return [
            pltpu.make_async_copy(left_ref.at[rows], left_out.at[rows], sems.at[2]),
            pltpu.make_async_copy(right_ref.at[rows], right_out.at[rows], sems.at[3]),
        ]

    @pl.loop(0, quad // STEP)
    def _(i):
        for copy in writes(i):
            copy.start()

    @pl.loop(0, quad // STEP)
    def _(i):
        for copy in writes(i):
            copy.wait()


def plan_blocks(block_pos, block_slot, block_count, vis_left, vis_right, layout):
    kernel_size = vis_right.shape[1]
    row_slots, col_slots = TILE_U // kernel_size, TILE_V // kernel_size
    smem = pl.BlockSpec(memory_space=pltpu.SMEM)
    hbm = pl.BlockSpec(memory_space=pl.ANY)
    places = layout.quads * QUAD
    return pl.pallas_call(
        functools.partial(plan_body, layout=layout, row_slots=row_slots, col_slots=col_slots),
        in_specs=[smem] * 3 + [hbm] * 2,
        out_specs=[smem, hbm, hbm],
        out_shape=[
            pltpu.SMEM((layout.total,), jnp.int32),
            pltpu.HBM((places,) + vis_left.shape[1:], vis_left.dtype),
            pltpu.HBM((places,) + vis_right.shape[1:], vis_right.dtype),
        ],
        scratch_shapes=[
            pltpu.VMEM((places,) + vis_left.shape[1:], vis_left.dtype),
            pltpu.VMEM((places,) + vis_right.shape[1:], vis_right.dtype),
            pltpu.SMEM((row_slots * col_slots,), jnp.int32),
            pltpu.SMEM((row_slots * col_slots,), jnp.int32),
            pltpu.SemaphoreType.DMA((4,)),
        ],
        compiler_params=pltpu.CompilerParams(vmem_limit_bytes=36 * 2**20),
        name="plan_blocks",
    )(block_pos, block_slot, block_count, in_hbm(vis_left), in_hbm(vis_right))


def strip(sums, row_slots, col_slots, kernel_size, plane, a, col):
    patch = sums.shape[1]
    lanes = slice(plane * patch, (plane + 1) * patch)
    total = None
    if a < row_slots:
        total = sums[a * col_slots + col, :kernel_size, lanes]
    if a > 0:
        above = sums[(a - 1) * col_slots + col, kernel_size:, lanes]
        total = above if total is None else total + above
    return total


def grid_body(
    plan_ref, kern_ref, left_hbm, right_hbm, *rest, part, first_part, layout, row_slots, col_slots
):
    if not first_part:
        rest = rest[4:]
    sums, left_ring, right_ring, ahead, *rest = rest
    if first_part:
        row_ref, col_ref, corner_ref, *rest = rest
    behind_ref, sems = rest
    mixed = (ahead, behind_ref)
    slots, kernel_size, _ = kern_ref.shape
    patch = left_hbm.shape[1]
    chunk = STEP * QUAD
    begin = plan_ref[part] // STEP
    end = plan_ref[part + 1] // STEP
    limit = jnp.minimum(plan_ref[layout.parts] // STEP, end + 2)

    def fetch(i):
        source = pl.ds(i * chunk, chunk)
        ring = lax.rem(i, RING)
        return [
            pltpu.make_async_copy(left_hbm.at[source], left_ring.at[ring], sems.at[0, ring]),
            pltpu.make_async_copy(right_hbm.at[source], right_ring.at[ring], sems.at[1, ring]),
        ]

    def start(i, which):
        @pl.when(i < limit)
        def _():
            fetch(i)[which].start()

    def wait(i, which):
        fresh = (i < limit) if first_part else ((i < limit) & (i > begin + 1))

        @pl.when(fresh)
        def _():
            fetch(i)[which].wait()

    if first_part:
        start(0, RIGHT)
        start(1, RIGHT)
        start(0, LEFT)

        @pl.loop(0, sums.shape[0])
        def _(q):
            sums[q] = jnp.zeros(sums.shape[1:], sums.dtype)

    zero = jnp.zeros((kernel_size, patch), jnp.bfloat16)

    def first(i, ring, at, ref, u):
        for e in range(QUAD):
            slot = plan_ref[layout.slot + (i * STEP + at) * QUAD + e]
            right = right_ring[ring, at * QUAD + e]
            kern = kern_ref[jnp.maximum(slot, 0)]
            kern = jnp.where(slot >= 0, kern, jnp.zeros_like(kern))
            spread = jnp.concatenate(
                [jnp.concatenate([right, zero], axis=1), jnp.concatenate([zero, right], axis=1)], axis=0
            )
            out = jnp.dot(kern, spread, preferred_element_type=jnp.float32).astype(jnp.bfloat16)
            top = slice(e * 2 * kernel_size, (e * 2 + 1) * kernel_size)
            low = slice((e * 2 + 1) * kernel_size, (e * 2 + 2) * kernel_size)
            ref[u, top, :] = out
            ref[u, low, :patch] = -out[:, patch:]
            ref[u, low, patch:] = out[:, :patch]

    def second(i, ring, at, ref, u):
        left = jnp.concatenate([left_ring[ring, at * QUAD + e] for e in range(QUAD)], axis=1)
        q = plan_ref[layout.anchor + i * STEP + at]
        sums[q] += jnp.dot(left, ref[u], preferred_element_type=jnp.float32)

    if first_part:
        wait(0, RIGHT)
        start(1, LEFT)
        for u in range(UNROLL):
            first(0, 0, u, mixed[0], u)
    start(begin + 2, RIGHT)
    start(begin + 2, LEFT)

    @pl.loop(begin, end)
    def _(i):
        here = lax.rem(i, RING)
        there = lax.rem(i + 1, RING)
        start(i + 3, RIGHT)
        start(i + 3, LEFT)
        wait(i, LEFT)
        wait(i + 1, RIGHT)
        for u in range(UNROLL):
            first(i, here, UNROLL + u, mixed[1], u)
            second(i, here, u, mixed[0], u)
        for u in range(UNROLL):
            first(i + 1, there, u, mixed[0], u)
            second(i, here, UNROLL + u, mixed[1], u)

    wait(end, LEFT)
    wait(end + 1, LEFT)
    wait(end + 1, RIGHT)
    if not first_part:
        return
    low = lax.broadcasted_iota(jnp.int32, (kernel_size, patch), 1) < kernel_size
    take = functools.partial(strip, sums, row_slots, col_slots, kernel_size)
    for a in range(row_slots + 1):
        real = pltpu.roll(take(0, a, col_slots - 1), kernel_size, 1)
        edge = jnp.where(low, real, take(1, a, col_slots - 1)).astype(col_ref.dtype)
        if a < row_slots:
            col_ref[a * kernel_size : (a + 1) * kernel_size, :] = edge
        else:
            corner_ref[...] = edge
    for plane in range(2):
        behind = 0.0
        for tile in range(col_slots // 2):
            odd = pltpu.roll(take(plane, row_slots, 2 * tile + 1), kernel_size, 1)
            value = take(plane, row_slots, 2 * tile) + jnp.where(low, behind, odd)
            row_ref[plane, :, tile * patch : (tile + 1) * patch] = value.astype(row_ref.dtype)
            behind = odd


def grid_part(plan, part, kernels, left, right, carried, layout):
    kernel_size = kernels.shape[1]
    patch = left.shape[1]
    row_slots, col_slots = TILE_U // kernel_size, TILE_V // kernel_size
    smem = pl.BlockSpec(memory_space=pltpu.SMEM)
    vmem = pl.BlockSpec(memory_space=pltpu.VMEM)
    hbm = pl.BlockSpec(memory_space=pl.ANY)
    first_part = carried is None
    carried = [] if first_part else [in_vmem(array) for array in carried]
    mixed_shape = (UNROLL, QUAD * 2 * kernel_size, 2 * patch)
    out_shape = [
        pltpu.VMEM((row_slots * col_slots, patch, 2 * patch), jnp.float32),
        pltpu.VMEM((RING, STEP * QUAD) + left.shape[1:], left.dtype),
        pltpu.VMEM((RING, STEP * QUAD) + right.shape[1:], right.dtype),
        pltpu.VMEM(mixed_shape, jnp.bfloat16),
    ]
    if first_part:
        out_shape += [
            pltpu.VMEM((2, kernel_size, TILE_V), jnp.bfloat16),
            pltpu.VMEM((TILE_U, 2 * kernel_size), jnp.bfloat16),
            pltpu.VMEM((kernel_size, 2 * kernel_size), jnp.bfloat16),
        ]
    out = pl.pallas_call(
        functools.partial(
            grid_body,
            part=part,
            first_part=first_part,
            layout=layout,
            row_slots=row_slots,
            col_slots=col_slots,
        ),
        in_specs=[smem, vmem, hbm, hbm] + [vmem] * len(carried),
        out_specs=[vmem] * len(out_shape),
        out_shape=out_shape,
        input_output_aliases={4 + i: i for i in range(len(carried))},
        scratch_shapes=[
            pltpu.VMEM(mixed_shape, jnp.bfloat16),
            pltpu.SemaphoreType.DMA((2, RING)),
        ],
        compiler_params=pltpu.CompilerParams(vmem_limit_bytes=12 * 2**20),
        name="grid_part",
    )(in_smem(plan), in_vmem(kernels), in_hbm(left), in_hbm(right), *carried)
    return out[:4], out[4:]


def merge_body(sums, row_ref, col_ref, corner_ref, out_hbm, out_ref, sems):
    kernel_size = row_ref.shape[1]
    patch = sums.shape[1]
    row_slots = out_ref.shape[1] // kernel_size
    col_slots = out_ref.shape[2] // kernel_size
    low = lax.broadcasted_iota(jnp.int32, (kernel_size, patch), 1) < kernel_size
    take = functools.partial(strip, sums, row_slots, col_slots, kernel_size)
    for a in range(row_slots):
        rows = slice(a * kernel_size, (a + 1) * kernel_size)
        edge = past_first(["tv"], col_ref[rows, :])
        if a == 0:
            edge = edge + past_first(["tu", "tv"], corner_ref[...])
        for plane in range(2):
            behind = edge if plane == 0 else pltpu.roll(edge, kernel_size, 1)
            for tile in range(col_slots // 2):
                lanes = slice(tile * patch, (tile + 1) * patch)
                odd = pltpu.roll(take(plane, a, 2 * tile + 1), kernel_size, 1)
                value = take(plane, a, 2 * tile) + jnp.where(low, behind, odd)
                if a == 0:
                    value = value + past_first(["tu"], row_ref[plane, :, lanes])
                out_ref[plane, rows, lanes] = value
                behind = odd
        pltpu.make_async_copy(out_ref.at[:, rows], out_hbm.at[:, rows], sems.at[a]).start()
    for a in range(row_slots):
        rows = slice(a * kernel_size, (a + 1) * kernel_size)
        pltpu.make_async_copy(out_ref.at[:, rows], out_hbm.at[:, rows], sems.at[a]).wait()


def merge_tile(sums, row, col, corner):
    vmem = pl.BlockSpec(memory_space=pltpu.VMEM)
    return pl.pallas_call(
        merge_body,
        in_specs=[vmem] * 4,
        out_specs=pl.BlockSpec(memory_space=pl.ANY),
        out_shape=jax.ShapeDtypeStruct((2, TILE_U, TILE_V), jnp.float32),
        scratch_shapes=[
            pltpu.VMEM((2, TILE_U, TILE_V), jnp.float32),
            pltpu.SemaphoreType.DMA((TILE_U // row.shape[1],)),
        ],
        compiler_params=pltpu.CompilerParams(vmem_limit_bytes=8 * 2**20),
        name="merge_tile",
    )(*map(in_vmem, (sums, row, col, corner)))


def shards(
    aperture_amp,
    aperture_phase,
    plane_depths,
    send_list,
    send_count,
    vis_left,
    vis_right,
    block_slot,
    block_pos,
    block_count,
):
    kernel_size = vis_right.shape[1]
    tiles, capacity = send_list.shape[1:]
    both = ("tu", "tv")
    outgoing = make_kernels(
        aperture_amp, aperture_phase, plane_depths, send_list[0].T, send_count, kernel_size
    )
    outgoing = outgoing.reshape((tiles, capacity) + outgoing.shape[1:])
    arrived = lax.all_to_all(outgoing, both, split_axis=0, concat_axis=0, tiled=True)
    received = arrived.reshape((-1,) + arrived.shape[2:])
    layout = Layout(block_pos.shape[0], (TILE_U // kernel_size) * (TILE_V // kernel_size))
    plan, left, right = plan_blocks(block_pos, block_slot, block_count, vis_left, vis_right, layout)
    carried, (row, col, corner) = grid_part(plan, 0, received, left, right, None, layout)
    row = around(row, ("tu",))
    col = around(col, ("tv",))
    corner = around(corner, ("tu", "tv"))
    carried, _ = grid_part(plan, 1, received, left, right, carried, layout)
    return merge_tile(carried[0], row, col, corner)


def solution(mesh):
    placed = (
        P(("tu", "tv"), None, None),
        P(("tu", "tv"), None, None),
        P(),
        P(("tu", "tv"), None, None),
        P(("tu", "tv"), None),
        P(("tu", "tv"), None, None),
        P(("tu", "tv"), None, None),
        P(("tu", "tv")),
        P(("tu", "tv")),
        P(("tu", "tv")),
    )
    return jax.shard_map(
        shards, mesh=mesh, in_specs=placed, out_specs=P(None, "tu", "tv"), check_vma=False
    )
```

```python
import functools
import math

import jax
import jax.numpy as jnp
import numpy as np
from jax import lax
from jax.experimental import pallas as pl
from jax.experimental.pallas import tpu as pltpu
from jax.sharding import PartitionSpec as P

TILE_U = 256
TILE_V = 512
QUAD = 4
UNROLL = 8
STEP = 2 * UNROLL
RING = 4
LEFT, RIGHT = 0, 1

def _fit(fn, degree):
    span = math.pi ** 2
    nodes = 0.5 * span * (1.0 - np.cos(np.pi * (np.arange(400) + 0.5) / 400))
    cheb = np.polynomial.chebyshev.Chebyshev.fit(nodes, fn(np.sqrt(nodes)), degree, domain=[0, span])
    return [float(c) for c in cheb.convert(kind=np.polynomial.Polynomial).coef]


COS_POLY = _fit(np.cos, 6)
SIN_POLY = _fit(lambda x: np.sin(x) / x, 5)


def horner(coefs, u):
    total = jnp.full_like(u, coefs[-1])
    for coef in coefs[-2::-1]:
        total = total * u + coef
    return total


def cos_sin(x):
    u = x * x
    return horner(COS_POLY, u), x * horner(SIN_POLY, u)


def around(block, axes):
    sizes = [lax.axis_size(axis) for axis in axes]
    route = []
    for place in np.ndindex(*sizes):
        target = [(i + 1) % n for i, n in zip(place, sizes)]
        route.append((int(np.ravel_multi_index(place, sizes)), int(np.ravel_multi_index(target, sizes))))
    return lax.ppermute(block, axes, route)


def past_first(axes, halo):
    real = functools.reduce(jnp.logical_and, [lax.axis_index(axis) > 0 for axis in axes])
    return jnp.where(real, halo.astype(jnp.float32), 0.0)


def in_hbm(array):
    return pltpu.with_memory_space_constraint(array, pltpu.HBM)


def in_vmem(array):
    return pltpu.with_memory_space_constraint(array, pltpu.VMEM)


def in_smem(array):
    return pltpu.with_memory_space_constraint(array, pltpu.SMEM)


def kernels_body(
    list_hbm, count_hbm, depth_hbm, amp_hbm, phase_hbm, out_ref,
    chosen_list, count, depth, amp, phase, table, screen, halves, made, small_sems, bulk_sems,
):
    screens, size, _ = amp.shape
    planes = depth.shape[0]
    kernel_size = out_ref.shape[1]
    small = [
        pltpu.make_async_copy(depth_hbm, depth, small_sems.at[0]),
        pltpu.make_async_copy(list_hbm, chosen_list, small_sems.at[1]),
        pltpu.make_async_copy(count_hbm, count, small_sems.at[2]),
    ]
    for copy in small:
        copy.start()

    def bulk(s):
        return [
            pltpu.make_async_copy(amp_hbm.at[s], amp.at[s], bulk_sems.at[0, s]),
            pltpu.make_async_copy(phase_hbm.at[s], phase.at[s], bulk_sems.at[1, s]),
        ]

    for copy in bulk(0):
        copy.start()

    frequency = lax.broadcasted_iota(jnp.int32, (kernel_size, size), 0) - kernel_size // 2
    cells = lax.broadcasted_iota(jnp.int32, (kernel_size, size), 1)
    turns = frequency.astype(jnp.float32) * cells.astype(jnp.float32) / size
    real_f, imag_f = cos_sin((2.0 * math.pi) * (turns - jnp.round(turns)))
    real_f = real_f.astype(jnp.bfloat16).astype(jnp.float32)
    imag_f = (-imag_f).astype(jnp.bfloat16).astype(jnp.float32)
    place = (lax.broadcasted_iota(jnp.int32, (1, size), 1).astype(jnp.float32) - size // 2) / size
    square = place * place
    for copy in small:
        copy.wait()
    for s in range(1, screens):
        for copy in bulk(s):
            copy.start()
    for p in range(planes):
        turns = depth[p] * square
        real_e, imag_e = cos_sin((2.0 * math.pi) * (turns - jnp.round(turns)))
        real_g = (real_f * real_e - imag_f * imag_e).astype(jnp.bfloat16)
        imag_g = (real_f * imag_e + imag_f * real_e).astype(jnp.bfloat16)
        top = slice(p * 2 * kernel_size, (p * 2 + 1) * kernel_size)
        low = slice((p * 2 + 1) * kernel_size, (p * 2 + 2) * kernel_size)
        table[top, :size] = real_g
        table[top, size:] = -imag_g
        table[low, :size] = imag_g
        table[low, size:] = real_g

    @pl.loop(0, screens)
    def _(s):
        for copy in bulk(s):
            copy.wait()
        magnitude = amp[s].astype(jnp.float32)
        real_e, imag_e = cos_sin(phase[s].astype(jnp.float32))
        screen[:size, :] = (magnitude * real_e).astype(jnp.bfloat16)
        screen[size:, :] = (magnitude * imag_e).astype(jnp.bfloat16)
        product = jnp.dot(table[...], screen[...], preferred_element_type=jnp.float32).astype(jnp.bfloat16)
        for p in range(planes):
            base = p * 2 * kernel_size
            halves[s, p, :, :size] = product[base : base + kernel_size]
            halves[s, p, :, size:] = product[base + kernel_size : base + 2 * kernel_size]

    for p in range(planes):
        second = lax.dot_general(
            jnp.concatenate([halves[s, p] for s in range(screens)], axis=0),
            table[p * 2 * kernel_size : (p + 1) * 2 * kernel_size, :],
            (((1,), (1,)), ((), ())),
            preferred_element_type=jnp.float32,
        )
        second = (second * (1.0 / size)).astype(jnp.bfloat16)
        for s in range(screens):
            made[s * planes + p] = second[s * kernel_size : (s + 1) * kernel_size]

    capacity, tiles = chosen_list.shape

    @pl.loop(0, tiles)
    def _(t):
        for c in range(capacity):
            chosen = made[chosen_list[c, t]]
            out_ref[t * capacity + c] = jnp.where(c < count[0, t], chosen, jnp.zeros_like(chosen))


def make_kernels(aperture_amp, aperture_phase, plane_depths, chosen_list, counts, kernel_size):
    screens, size, _ = aperture_amp.shape
    planes = plane_depths.shape[0]
    capacity, tiles = chosen_list.shape
    hbm = pl.BlockSpec(memory_space=pl.ANY)
    return pl.pallas_call(
        kernels_body,
        in_specs=[hbm] * 5,
        out_specs=pl.BlockSpec(memory_space=pltpu.VMEM),
        out_shape=pltpu.VMEM((tiles * capacity, kernel_size, 2 * kernel_size), jnp.bfloat16),
        scratch_shapes=[
            pltpu.SMEM((capacity, tiles), jnp.int32),
            pltpu.SMEM((1, tiles), jnp.int32),
            pltpu.SMEM((planes,), jnp.float32),
            pltpu.VMEM((screens, size, size), jnp.bfloat16),
            pltpu.VMEM((screens, size, size), jnp.bfloat16),
            pltpu.VMEM((planes * 2 * kernel_size, 2 * size), jnp.bfloat16),
            pltpu.VMEM((2 * size, size), jnp.bfloat16),
            pltpu.VMEM((screens, planes, kernel_size, 2 * size), jnp.bfloat16),
            pltpu.VMEM((screens * planes, kernel_size, 2 * kernel_size), jnp.bfloat16),
            pltpu.SemaphoreType.DMA((3,)),
            pltpu.SemaphoreType.DMA((2, screens)),
        ],
        compiler_params=pltpu.CompilerParams(vmem_limit_bytes=32 * 2**20),
        name="make_kernels",
    )(*map(in_hbm, (chosen_list, counts, plane_depths, aperture_amp, aperture_phase)))


class Layout:
    def __init__(self, blocks, anchors):
        self.parts = 2
        quads = (blocks + (QUAD - 1) * anchors) // QUAD + 1
        self.quads = (quads + STEP - 1) // STEP * STEP
        self.anchor = self.parts + 1
        self.slot = self.anchor + self.quads
        self.total = self.slot + (self.quads + UNROLL) * QUAD


def plan_body(
    pos_ref, slot_ref, count_ref, left_hbm, right_hbm, plan_ref, left_out, right_out,
    left_ref, right_ref, tally, cursor, sems, *, layout, row_slots, col_slots,
):
    anchors = row_slots * col_slots
    border = row_slots + col_slots - 1
    live = count_ref[0]

    def copies(block, place):
        return [
            pltpu.make_async_copy(left_hbm.at[block], left_ref.at[place], sems.at[0]),
            pltpu.make_async_copy(right_hbm.at[block], right_ref.at[place], sems.at[1]),
        ]

    def put(block, place, slot):
        plan_ref[layout.slot + place] = slot
        for copy in copies(block, place):
            copy.start()

    @pl.loop(0, anchors)
    def _(q):
        tally[q] = 0

    @pl.loop(0, live)
    def _(j):
        q = pos_ref[j]
        tally[q] = tally[q] + 1

    def lay(rank, quad):
        inner = rank - border
        q = jnp.where(
            rank < row_slots,
            rank * col_slots + col_slots - 1,
            jnp.where(
                rank < border,
                (row_slots - 1) * col_slots + rank - row_slots,
                (inner // (col_slots - 1)) * col_slots + lax.rem(inner, col_slots - 1),
            ),
        )
        number = tally[q]
        quads = (number + QUAD - 1) // QUAD
        cursor[q] = quad * QUAD

        @pl.loop(0, quads)
        def _(i):
            plan_ref[layout.anchor + quad + i] = q

        @pl.loop(quad * QUAD + number, (quad + quads) * QUAD)
        def _(i):
            put(0, i, -1)

        return quad + quads

    quad = 0
    begin = 0
    plan_ref[0] = 0
    for part, end in enumerate([border, anchors]):
        quad = lax.fori_loop(begin, end, lay, quad)
        begin = end
        plan_ref[part + 1] = ((quad + STEP - 1) // STEP) * STEP

    full = ((quad + STEP - 1) // STEP) * STEP

    @pl.loop(quad, full)
    def _(i):
        plan_ref[layout.anchor + i] = 0
        for e in range(QUAD):
            put(0, i * QUAD + e, -1)

    quad = full

    @pl.loop(quad * QUAD, (quad + UNROLL) * QUAD)
    def _(i):
        plan_ref[layout.slot + i] = -1

    @pl.loop(0, live)
    def _(j):
        q = pos_ref[j]
        at = cursor[q]
        cursor[q] = at + 1
        put(j, at, slot_ref[j])

    chunk = STEP * QUAD

    @pl.loop(0, quad // STEP)
    def _(i):
        rows = pl.ds(0, chunk)
        pltpu.make_async_copy(left_hbm.at[rows], left_ref.at[rows], sems.at[0]).wait()
        pltpu.make_async_copy(right_hbm.at[rows], right_ref.at[rows], sems.at[1]).wait()

    def writes(i):
        rows = pl.ds(i * chunk, chunk)
        return [
            pltpu.make_async_copy(left_ref.at[rows], left_out.at[rows], sems.at[2]),
            pltpu.make_async_copy(right_ref.at[rows], right_out.at[rows], sems.at[3]),
        ]

    @pl.loop(0, quad // STEP)
    def _(i):
        for copy in writes(i):
            copy.start()

    @pl.loop(0, quad // STEP)
    def _(i):
        for copy in writes(i):
            copy.wait()


def plan_blocks(block_pos, block_slot, block_count, vis_left, vis_right, layout):
    kernel_size = vis_right.shape[1]
    row_slots, col_slots = TILE_U // kernel_size, TILE_V // kernel_size
    smem = pl.BlockSpec(memory_space=pltpu.SMEM)
    hbm = pl.BlockSpec(memory_space=pl.ANY)
    places = layout.quads * QUAD
    return pl.pallas_call(
        functools.partial(plan_body, layout=layout, row_slots=row_slots, col_slots=col_slots),
        in_specs=[smem] * 3 + [hbm] * 2,
        out_specs=[smem, hbm, hbm],
        out_shape=[
            pltpu.SMEM((layout.total,), jnp.int32),
            pltpu.HBM((places,) + vis_left.shape[1:], vis_left.dtype),
            pltpu.HBM((places,) + vis_right.shape[1:], vis_right.dtype),
        ],
        scratch_shapes=[
            pltpu.VMEM((places,) + vis_left.shape[1:], vis_left.dtype),
            pltpu.VMEM((places,) + vis_right.shape[1:], vis_right.dtype),
            pltpu.SMEM((row_slots * col_slots,), jnp.int32),
            pltpu.SMEM((row_slots * col_slots,), jnp.int32),
            pltpu.SemaphoreType.DMA((4,)),
        ],
        compiler_params=pltpu.CompilerParams(vmem_limit_bytes=36 * 2**20),
        name="plan_blocks",
    )(block_pos, block_slot, block_count, in_hbm(vis_left), in_hbm(vis_right))


def strip(sums, row_slots, col_slots, kernel_size, plane, a, col):
    patch = sums.shape[1]
    lanes = slice(plane * patch, (plane + 1) * patch)
    total = None
    if a < row_slots:
        total = sums[a * col_slots + col, :kernel_size, lanes]
    if a > 0:
        above = sums[(a - 1) * col_slots + col, kernel_size:, lanes]
        total = above if total is None else total + above
    return total


def grid_body(
    plan_ref, kern_ref, left_hbm, right_hbm, *rest, part, first_part, layout, row_slots, col_slots
):
    if not first_part:
        rest = rest[4:]
    sums, left_ring, right_ring, ahead, *rest = rest
    if first_part:
        row_ref, col_ref, corner_ref, *rest = rest
    behind_ref, sems = rest
    mixed = (ahead, behind_ref)
    slots, kernel_size, _ = kern_ref.shape
    patch = left_hbm.shape[1]
    chunk = STEP * QUAD
    begin = plan_ref[part] // STEP
    end = plan_ref[part + 1] // STEP
    limit = jnp.minimum(plan_ref[layout.parts] // STEP, end + 2)

    def fetch(i):
        source = pl.ds(i * chunk, chunk)
        ring = lax.rem(i, RING)
        return [
            pltpu.make_async_copy(left_hbm.at[source], left_ring.at[ring], sems.at[0, ring]),
            pltpu.make_async_copy(right_hbm.at[source], right_ring.at[ring], sems.at[1, ring]),
        ]

    def start(i, which):
        @pl.when(i < limit)
        def _():
            fetch(i)[which].start()

    def wait(i, which):
        fresh = (i < limit) if first_part else ((i < limit) & (i > begin + 1))

        @pl.when(fresh)
        def _():
            fetch(i)[which].wait()

    if first_part:
        start(0, RIGHT)
        start(1, RIGHT)
        start(0, LEFT)

        @pl.loop(0, sums.shape[0])
        def _(q):
            sums[q] = jnp.zeros(sums.shape[1:], sums.dtype)

    zero = jnp.zeros((kernel_size, patch), jnp.bfloat16)

    def first(i, ring, at, ref, u):
        for e in range(QUAD):
            slot = plan_ref[layout.slot + (i * STEP + at) * QUAD + e]
            right = right_ring[ring, at * QUAD + e]
            kern = kern_ref[jnp.maximum(slot, 0)]
            kern = jnp.where(slot >= 0, kern, jnp.zeros_like(kern))
            spread = jnp.concatenate(
                [jnp.concatenate([right, zero], axis=1), jnp.concatenate([zero, right], axis=1)], axis=0
            )
            out = jnp.dot(kern, spread, preferred_element_type=jnp.float32).astype(jnp.bfloat16)
            top = slice(e * 2 * kernel_size, (e * 2 + 1) * kernel_size)
            low = slice((e * 2 + 1) * kernel_size, (e * 2 + 2) * kernel_size)
            ref[u, top, :] = out
            ref[u, low, :patch] = -out[:, patch:]
            ref[u, low, patch:] = out[:, :patch]

    def second(i, ring, at, ref, u):
        left = jnp.concatenate([left_ring[ring, at * QUAD + e] for e in range(QUAD)], axis=1)
        q = plan_ref[layout.anchor + i * STEP + at]
        sums[q] += jnp.dot(left, ref[u], preferred_element_type=jnp.float32)

    if first_part:
        wait(0, RIGHT)
        start(1, LEFT)
        for u in range(UNROLL):
            first(0, 0, u, mixed[0], u)
    start(begin + 2, RIGHT)
    start(begin + 2, LEFT)

    @pl.loop(begin, end)
    def _(i):
        here = lax.rem(i, RING)
        there = lax.rem(i + 1, RING)
        start(i + 3, RIGHT)
        start(i + 3, LEFT)
        wait(i, LEFT)
        wait(i + 1, RIGHT)
        for u in range(UNROLL):
            first(i, here, UNROLL + u, mixed[1], u)
            second(i, here, u, mixed[0], u)
        for u in range(UNROLL):
            first(i + 1, there, u, mixed[0], u)
            second(i, here, UNROLL + u, mixed[1], u)

    wait(end, LEFT)
    wait(end + 1, LEFT)
    wait(end + 1, RIGHT)
    if not first_part:
        return
    low = lax.broadcasted_iota(jnp.int32, (kernel_size, patch), 1) < kernel_size
    take = functools.partial(strip, sums, row_slots, col_slots, kernel_size)
    for a in range(row_slots + 1):
        real = pltpu.roll(take(0, a, col_slots - 1), kernel_size, 1)
        edge = jnp.where(low, real, take(1, a, col_slots - 1)).astype(col_ref.dtype)
        if a < row_slots:
            col_ref[a * kernel_size : (a + 1) * kernel_size, :] = edge
        else:
            corner_ref[...] = edge
    for plane in range(2):
        behind = 0.0
        for tile in range(col_slots // 2):
            odd = pltpu.roll(take(plane, row_slots, 2 * tile + 1), kernel_size, 1)
            value = take(plane, row_slots, 2 * tile) + jnp.where(low, behind, odd)
            row_ref[plane, :, tile * patch : (tile + 1) * patch] = value.astype(row_ref.dtype)
            behind = odd


def grid_part(plan, part, kernels, left, right, carried, layout):
    kernel_size = kernels.shape[1]
    patch = left.shape[1]
    row_slots, col_slots = TILE_U // kernel_size, TILE_V // kernel_size
    smem = pl.BlockSpec(memory_space=pltpu.SMEM)
    vmem = pl.BlockSpec(memory_space=pltpu.VMEM)
    hbm = pl.BlockSpec(memory_space=pl.ANY)
    first_part = carried is None
    carried = [] if first_part else [in_vmem(array) for array in carried]
    mixed_shape = (UNROLL, QUAD * 2 * kernel_size, 2 * patch)
    out_shape = [
        pltpu.VMEM((row_slots * col_slots, patch, 2 * patch), jnp.float32),
        pltpu.VMEM((RING, STEP * QUAD) + left.shape[1:], left.dtype),
        pltpu.VMEM((RING, STEP * QUAD) + right.shape[1:], right.dtype),
        pltpu.VMEM(mixed_shape, jnp.bfloat16),
    ]
    if first_part:
        out_shape += [
            pltpu.VMEM((2, kernel_size, TILE_V), jnp.bfloat16),
            pltpu.VMEM((TILE_U, 2 * kernel_size), jnp.bfloat16),
            pltpu.VMEM((kernel_size, 2 * kernel_size), jnp.bfloat16),
        ]
    out = pl.pallas_call(
        functools.partial(
            grid_body,
            part=part,
            first_part=first_part,
            layout=layout,
            row_slots=row_slots,
            col_slots=col_slots,
        ),
        in_specs=[smem, vmem, hbm, hbm] + [vmem] * len(carried),
        out_specs=[vmem] * len(out_shape),
        out_shape=out_shape,
        input_output_aliases={4 + i: i for i in range(len(carried))},
        scratch_shapes=[
            pltpu.VMEM(mixed_shape, jnp.bfloat16),
            pltpu.SemaphoreType.DMA((2, RING)),
        ],
        compiler_params=pltpu.CompilerParams(vmem_limit_bytes=12 * 2**20),
        name="grid_part",
    )(in_smem(plan), in_vmem(kernels), in_hbm(left), in_hbm(right), *carried)
    return out[:4], out[4:]


def merge_body(sums, row_ref, col_ref, corner_ref, out_hbm, out_ref, sems):
    kernel_size = row_ref.shape[1]
    patch = sums.shape[1]
    row_slots = out_ref.shape[1] // kernel_size
    col_slots = out_ref.shape[2] // kernel_size
    low = lax.broadcasted_iota(jnp.int32, (kernel_size, patch), 1) < kernel_size
    take = functools.partial(strip, sums, row_slots, col_slots, kernel_size)
    for a in range(row_slots):
        rows = slice(a * kernel_size, (a + 1) * kernel_size)
        edge = past_first(["tv"], col_ref[rows, :])
        if a == 0:
            edge = edge + past_first(["tu", "tv"], corner_ref[...])
        for plane in range(2):
            behind = edge if plane == 0 else pltpu.roll(edge, kernel_size, 1)
            for tile in range(col_slots // 2):
                lanes = slice(tile * patch, (tile + 1) * patch)
                odd = pltpu.roll(take(plane, a, 2 * tile + 1), kernel_size, 1)
                value = take(plane, a, 2 * tile) + jnp.where(low, behind, odd)
                if a == 0:
                    value = value + past_first(["tu"], row_ref[plane, :, lanes])
                out_ref[plane, rows, lanes] = value
                behind = odd
        pltpu.make_async_copy(out_ref.at[:, rows], out_hbm.at[:, rows], sems.at[a]).start()
    for a in range(row_slots):
        rows = slice(a * kernel_size, (a + 1) * kernel_size)
        pltpu.make_async_copy(out_ref.at[:, rows], out_hbm.at[:, rows], sems.at[a]).wait()


def merge_tile(sums, row, col, corner):
    vmem = pl.BlockSpec(memory_space=pltpu.VMEM)
    return pl.pallas_call(
        merge_body,
        in_specs=[vmem] * 4,
        out_specs=pl.BlockSpec(memory_space=pl.ANY),
        out_shape=jax.ShapeDtypeStruct((2, TILE_U, TILE_V), jnp.float32),
        scratch_shapes=[
            pltpu.VMEM((2, TILE_U, TILE_V), jnp.float32),
            pltpu.SemaphoreType.DMA((TILE_U // row.shape[1],)),
        ],
        compiler_params=pltpu.CompilerParams(vmem_limit_bytes=8 * 2**20),
        name="merge_tile",
    )(*map(in_vmem, (sums, row, col, corner)))


def shards(
    aperture_amp,
    aperture_phase,
    plane_depths,
    send_list,
    send_count,
    vis_left,
    vis_right,
    block_slot,
    block_pos,
    block_count,
):
    kernel_size = vis_right.shape[1]
    tiles, capacity = send_list.shape[1:]
    both = ("tu", "tv")
    outgoing = make_kernels(
        aperture_amp, aperture_phase, plane_depths, send_list[0].T, send_count, kernel_size
    )
    outgoing = outgoing.reshape((tiles, capacity) + outgoing.shape[1:])
    arrived = lax.all_to_all(outgoing, both, split_axis=0, concat_axis=0, tiled=True)
    received = arrived.reshape((-1,) + arrived.shape[2:])
    layout = Layout(block_pos.shape[0], (TILE_U // kernel_size) * (TILE_V // kernel_size))
    plan, left, right = plan_blocks(block_pos, block_slot, block_count, vis_left, vis_right, layout)
    carried, (row, col, corner) = grid_part(plan, 0, received, left, right, None, layout)
    row = around(row, ("tu",))
    col = around(col, ("tv",))
    corner = around(corner, ("tu", "tv"))
    carried, _ = grid_part(plan, 1, received, left, right, carried, layout)
    return merge_tile(carried[0], row, col, corner)


def solution(mesh):
    placed = (
        P(("tu", "tv"), None, None),
        P(("tu", "tv"), None, None),
        P(),
        P(("tu", "tv"), None, None),
        P(("tu", "tv"), None),
        P(("tu", "tv"), None, None),
        P(("tu", "tv"), None, None),
        P(("tu", "tv")),
        P(("tu", "tv")),
        P(("tu", "tv")),
    )
    return jax.shard_map(
        shards, mesh=mesh, in_specs=placed, out_specs=P(None, "tu", "tv"), check_vma=False
    )
```

```python
import functools
import math

import jax
import jax.numpy as jnp
import numpy as np
from jax import lax
from jax.experimental import pallas as pl
from jax.experimental.pallas import tpu as pltpu
from jax.sharding import PartitionSpec as P

TILE_U = 256
TILE_V = 512
QUAD = 4
UNROLL = 8
STEP = 2 * UNROLL
RING = 4
LEFT, RIGHT = 0, 1

def _fit(fn, degree):
    span = math.pi ** 2
    nodes = 0.5 * span * (1.0 - np.cos(np.pi * (np.arange(400) + 0.5) / 400))
    cheb = np.polynomial.chebyshev.Chebyshev.fit(nodes, fn(np.sqrt(nodes)), degree, domain=[0, span])
    return [float(c) for c in cheb.convert(kind=np.polynomial.Polynomial).coef]


COS_POLY = _fit(np.cos, 6)
SIN_POLY = _fit(lambda x: np.sin(x) / x, 5)


def horner(coefs, u):
    total = jnp.full_like(u, coefs[-1])
    for coef in coefs[-2::-1]:
        total = total * u + coef
    return total


def cos_sin(x):
    u = x * x
    return horner(COS_POLY, u), x * horner(SIN_POLY, u)


def around(block, axes):
    sizes = [lax.axis_size(axis) for axis in axes]
    route = []
    for place in np.ndindex(*sizes):
        target = [(i + 1) % n for i, n in zip(place, sizes)]
        route.append((int(np.ravel_multi_index(place, sizes)), int(np.ravel_multi_index(target, sizes))))
    return lax.ppermute(block, axes, route)


def past_first(axes, halo):
    real = functools.reduce(jnp.logical_and, [lax.axis_index(axis) > 0 for axis in axes])
    return jnp.where(real, halo.astype(jnp.float32), 0.0)


def in_hbm(array):
    return pltpu.with_memory_space_constraint(array, pltpu.HBM)


def in_vmem(array):
    return pltpu.with_memory_space_constraint(array, pltpu.VMEM)


def in_smem(array):
    return pltpu.with_memory_space_constraint(array, pltpu.SMEM)


def kernels_body(
    list_hbm, count_hbm, depth_hbm, amp_hbm, phase_hbm, out_ref,
    chosen_list, count, depth, amp, phase, table, screen, halves, made, small_sems, bulk_sems,
):
    screens, size, _ = amp.shape
    planes = depth.shape[0]
    kernel_size = out_ref.shape[1]
    small = [
        pltpu.make_async_copy(depth_hbm, depth, small_sems.at[0]),
        pltpu.make_async_copy(list_hbm, chosen_list, small_sems.at[1]),
        pltpu.make_async_copy(count_hbm, count, small_sems.at[2]),
    ]
    for copy in small:
        copy.start()

    def bulk(s):
        return [
            pltpu.make_async_copy(amp_hbm.at[s], amp.at[s], bulk_sems.at[0, s]),
            pltpu.make_async_copy(phase_hbm.at[s], phase.at[s], bulk_sems.at[1, s]),
        ]

    for copy in bulk(0):
        copy.start()

    frequency = lax.broadcasted_iota(jnp.int32, (kernel_size, size), 0) - kernel_size // 2
    cells = lax.broadcasted_iota(jnp.int32, (kernel_size, size), 1)
    turns = frequency.astype(jnp.float32) * cells.astype(jnp.float32) / size
    real_f, imag_f = cos_sin((2.0 * math.pi) * (turns - jnp.round(turns)))
    real_f = real_f.astype(jnp.bfloat16).astype(jnp.float32)
    imag_f = (-imag_f).astype(jnp.bfloat16).astype(jnp.float32)
    place = (lax.broadcasted_iota(jnp.int32, (1, size), 1).astype(jnp.float32) - size // 2) / size
    square = place * place
    for copy in small:
        copy.wait()
    for s in range(1, screens):
        for copy in bulk(s):
            copy.start()
    for p in range(planes):
        turns = depth[p] * square
        real_e, imag_e = cos_sin((2.0 * math.pi) * (turns - jnp.round(turns)))
        real_g = (real_f * real_e - imag_f * imag_e).astype(jnp.bfloat16)
        imag_g = (real_f * imag_e + imag_f * real_e).astype(jnp.bfloat16)
        top = slice(p * 2 * kernel_size, (p * 2 + 1) * kernel_size)
        low = slice((p * 2 + 1) * kernel_size, (p * 2 + 2) * kernel_size)
        table[top, :size] = real_g
        table[top, size:] = -imag_g
        table[low, :size] = imag_g
        table[low, size:] = real_g

    @pl.loop(0, screens)
    def _(s):
        for copy in bulk(s):
            copy.wait()
        magnitude = amp[s].astype(jnp.float32)
        real_e, imag_e = cos_sin(phase[s].astype(jnp.float32))
        screen[:size, :] = (magnitude * real_e).astype(jnp.bfloat16)
        screen[size:, :] = (magnitude * imag_e).astype(jnp.bfloat16)
        product = jnp.dot(table[...], screen[...], preferred_element_type=jnp.float32).astype(jnp.bfloat16)
        for p in range(planes):
            base = p * 2 * kernel_size
            halves[s, p, :, :size] = product[base : base + kernel_size]
            halves[s, p, :, size:] = product[base + kernel_size : base + 2 * kernel_size]

    for p in range(planes):
        second = lax.dot_general(
            jnp.concatenate([halves[s, p] for s in range(screens)], axis=0),
            table[p * 2 * kernel_size : (p + 1) * 2 * kernel_size, :],
            (((1,), (1,)), ((), ())),
            preferred_element_type=jnp.float32,
        )
        second = (second * (1.0 / size)).astype(jnp.bfloat16)
        for s in range(screens):
            made[s * planes + p] = second[s * kernel_size : (s + 1) * kernel_size]

    capacity, tiles = chosen_list.shape

    @pl.loop(0, tiles, unroll=8)
    def _(t):
        for c in range(capacity):
            chosen = made[chosen_list[c, t]]
            out_ref[t * capacity + c] = jnp.where(c < count[0, t], chosen, jnp.zeros_like(chosen))


def make_kernels(aperture_amp, aperture_phase, plane_depths, chosen_list, counts, kernel_size):
    screens, size, _ = aperture_amp.shape
    planes = plane_depths.shape[0]
    capacity, tiles = chosen_list.shape
    hbm = pl.BlockSpec(memory_space=pl.ANY)
    return pl.pallas_call(
        kernels_body,
        in_specs=[hbm] * 5,
        out_specs=pl.BlockSpec(memory_space=pltpu.VMEM),
        out_shape=pltpu.VMEM((tiles * capacity, kernel_size, 2 * kernel_size), jnp.bfloat16),
        scratch_shapes=[
            pltpu.SMEM((capacity, tiles), jnp.int32),
            pltpu.SMEM((1, tiles), jnp.int32),
            pltpu.SMEM((planes,), jnp.float32),
            pltpu.VMEM((screens, size, size), jnp.bfloat16),
            pltpu.VMEM((screens, size, size), jnp.bfloat16),
            pltpu.VMEM((planes * 2 * kernel_size, 2 * size), jnp.bfloat16),
            pltpu.VMEM((2 * size, size), jnp.bfloat16),
            pltpu.VMEM((screens, planes, kernel_size, 2 * size), jnp.bfloat16),
            pltpu.VMEM((screens * planes, kernel_size, 2 * kernel_size), jnp.bfloat16),
            pltpu.SemaphoreType.DMA((3,)),
            pltpu.SemaphoreType.DMA((2, screens)),
        ],
        compiler_params=pltpu.CompilerParams(vmem_limit_bytes=32 * 2**20),
        name="make_kernels",
    )(*map(in_hbm, (chosen_list, counts, plane_depths, aperture_amp, aperture_phase)))


class Layout:
    def __init__(self, blocks, anchors):
        self.parts = 2
        quads = (blocks + (QUAD - 1) * anchors) // QUAD + 1
        self.quads = (quads + STEP - 1) // STEP * STEP
        self.anchor = self.parts + 1
        self.slot = self.anchor + self.quads
        self.total = self.slot + (self.quads + UNROLL) * QUAD


def plan_body(
    pos_ref, slot_ref, count_ref, left_hbm, right_hbm, plan_ref, left_out, right_out,
    left_ref, right_ref, tally, cursor, sems, *, layout, row_slots, col_slots,
):
    anchors = row_slots * col_slots
    border = row_slots + col_slots - 1
    live = count_ref[0]

    def copies(block, place):
        return [
            pltpu.make_async_copy(left_hbm.at[block], left_ref.at[place], sems.at[0]),
            pltpu.make_async_copy(right_hbm.at[block], right_ref.at[place], sems.at[1]),
        ]

    def put(block, place, slot):
        plan_ref[layout.slot + place] = slot
        for copy in copies(block, place):
            copy.start()

    @pl.loop(0, anchors)
    def _(q):
        tally[q] = 0

    @pl.loop(0, live)
    def _(j):
        q = pos_ref[j]
        tally[q] = tally[q] + 1

    def lay(rank, quad):
        inner = rank - border
        q = jnp.where(
            rank < row_slots,
            rank * col_slots + col_slots - 1,
            jnp.where(
                rank < border,
                (row_slots - 1) * col_slots + rank - row_slots,
                (inner // (col_slots - 1)) * col_slots + lax.rem(inner, col_slots - 1),
            ),
        )
        number = tally[q]
        quads = (number + QUAD - 1) // QUAD
        cursor[q] = quad * QUAD

        @pl.loop(0, quads)
        def _(i):
            plan_ref[layout.anchor + quad + i] = q

        @pl.loop(quad * QUAD + number, (quad + quads) * QUAD)
        def _(i):
            put(0, i, -1)

        return quad + quads

    quad = 0
    begin = 0
    plan_ref[0] = 0
    for part, end in enumerate([border, anchors]):
        quad = lax.fori_loop(begin, end, lay, quad)
        begin = end
        plan_ref[part + 1] = ((quad + STEP - 1) // STEP) * STEP

    full = ((quad + STEP - 1) // STEP) * STEP

    @pl.loop(quad, full)
    def _(i):
        plan_ref[layout.anchor + i] = 0
        for e in range(QUAD):
            put(0, i * QUAD + e, -1)

    quad = full

    @pl.loop(quad * QUAD, (quad + UNROLL) * QUAD)
    def _(i):
        plan_ref[layout.slot + i] = -1

    @pl.loop(0, live)
    def _(j):
        q = pos_ref[j]
        at = cursor[q]
        cursor[q] = at + 1
        put(j, at, slot_ref[j])

    chunk = STEP * QUAD

    @pl.loop(0, quad // STEP)
    def _(i):
        rows = pl.ds(0, chunk)
        pltpu.make_async_copy(left_hbm.at[rows], left_ref.at[rows], sems.at[0]).wait()
        pltpu.make_async_copy(right_hbm.at[rows], right_ref.at[rows], sems.at[1]).wait()

    def writes(i):
        rows = pl.ds(i * chunk, chunk)
        return [
            pltpu.make_async_copy(left_ref.at[rows], left_out.at[rows], sems.at[2]),
            pltpu.make_async_copy(right_ref.at[rows], right_out.at[rows], sems.at[3]),
        ]

    @pl.loop(0, quad // STEP)
    def _(i):
        for copy in writes(i):
            copy.start()

    @pl.loop(0, quad // STEP)
    def _(i):
        for copy in writes(i):
            copy.wait()


def plan_blocks(block_pos, block_slot, block_count, vis_left, vis_right, layout):
    kernel_size = vis_right.shape[1]
    row_slots, col_slots = TILE_U // kernel_size, TILE_V // kernel_size
    smem = pl.BlockSpec(memory_space=pltpu.SMEM)
    hbm = pl.BlockSpec(memory_space=pl.ANY)
    places = layout.quads * QUAD
    return pl.pallas_call(
        functools.partial(plan_body, layout=layout, row_slots=row_slots, col_slots=col_slots),
        in_specs=[smem] * 3 + [hbm] * 2,
        out_specs=[smem, hbm, hbm],
        out_shape=[
            pltpu.SMEM((layout.total,), jnp.int32),
            pltpu.HBM((places,) + vis_left.shape[1:], vis_left.dtype),
            pltpu.HBM((places,) + vis_right.shape[1:], vis_right.dtype),
        ],
        scratch_shapes=[
            pltpu.VMEM((places,) + vis_left.shape[1:], vis_left.dtype),
            pltpu.VMEM((places,) + vis_right.shape[1:], vis_right.dtype),
            pltpu.SMEM((row_slots * col_slots,), jnp.int32),
            pltpu.SMEM((row_slots * col_slots,), jnp.int32),
            pltpu.SemaphoreType.DMA((4,)),
        ],
        compiler_params=pltpu.CompilerParams(vmem_limit_bytes=36 * 2**20),
        name="plan_blocks",
    )(block_pos, block_slot, block_count, in_hbm(vis_left), in_hbm(vis_right))


def strip(sums, row_slots, col_slots, kernel_size, plane, a, col):
    patch = sums.shape[1]
    lanes = slice(plane * patch, (plane + 1) * patch)
    total = None
    if a < row_slots:
        total = sums[a * col_slots + col, :kernel_size, lanes]
    if a > 0:
        above = sums[(a - 1) * col_slots + col, kernel_size:, lanes]
        total = above if total is None else total + above
    return total


def grid_body(
    plan_ref, kern_ref, left_hbm, right_hbm, *rest, part, first_part, layout, row_slots, col_slots
):
    if not first_part:
        rest = rest[4:]
    sums, left_ring, right_ring, ahead, *rest = rest
    if first_part:
        row_ref, col_ref, corner_ref, *rest = rest
    behind_ref, sems = rest
    mixed = (ahead, behind_ref)
    slots, kernel_size, _ = kern_ref.shape
    patch = left_hbm.shape[1]
    chunk = STEP * QUAD
    begin = plan_ref[part] // STEP
    end = plan_ref[part + 1] // STEP
    limit = jnp.minimum(plan_ref[layout.parts] // STEP, end + 2)

    def fetch(i):
        source = pl.ds(i * chunk, chunk)
        ring = lax.rem(i, RING)
        return [
            pltpu.make_async_copy(left_hbm.at[source], left_ring.at[ring], sems.at[0, ring]),
            pltpu.make_async_copy(right_hbm.at[source], right_ring.at[ring], sems.at[1, ring]),
        ]

    def start(i, which):
        @pl.when(i < limit)
        def _():
            fetch(i)[which].start()

    def wait(i, which):
        fresh = (i < limit) if first_part else ((i < limit) & (i > begin + 1))

        @pl.when(fresh)
        def _():
            fetch(i)[which].wait()

    if first_part:
        start(0, RIGHT)
        start(0, LEFT)

        @pl.loop(0, sums.shape[0])
        def _(q):
            sums[q] = jnp.zeros(sums.shape[1:], sums.dtype)

    zero = jnp.zeros((kernel_size, patch), jnp.bfloat16)

    def first(i, ring, at, ref, u):
        for e in range(QUAD):
            slot = plan_ref[layout.slot + (i * STEP + at) * QUAD + e]
            right = right_ring[ring, at * QUAD + e]
            kern = kern_ref[jnp.maximum(slot, 0)]
            kern = jnp.where(slot >= 0, kern, jnp.zeros_like(kern))
            spread = jnp.concatenate(
                [jnp.concatenate([right, zero], axis=1), jnp.concatenate([zero, right], axis=1)], axis=0
            )
            out = jnp.dot(kern, spread, preferred_element_type=jnp.float32).astype(jnp.bfloat16)
            top = slice(e * 2 * kernel_size, (e * 2 + 1) * kernel_size)
            low = slice((e * 2 + 1) * kernel_size, (e * 2 + 2) * kernel_size)
            ref[u, top, :] = out
            ref[u, low, :patch] = -out[:, patch:]
            ref[u, low, patch:] = out[:, :patch]

    def second(i, ring, at, ref, u):
        left = jnp.concatenate([left_ring[ring, at * QUAD + e] for e in range(QUAD)], axis=1)
        q = plan_ref[layout.anchor + i * STEP + at]
        sums[q] += jnp.dot(left, ref[u], preferred_element_type=jnp.float32)

    if first_part:
        wait(0, RIGHT)
        start(1, RIGHT)
        start(1, LEFT)
        for u in range(UNROLL):
            first(0, 0, u, mixed[0], u)
    start(begin + 2, RIGHT)
    start(begin + 2, LEFT)

    @pl.loop(begin, end)
    def _(i):
        here = lax.rem(i, RING)
        there = lax.rem(i + 1, RING)
        start(i + 3, RIGHT)
        start(i + 3, LEFT)
        wait(i, LEFT)
        wait(i + 1, RIGHT)
        for u in range(UNROLL):
            first(i, here, UNROLL + u, mixed[1], u)
            second(i, here, u, mixed[0], u)
        for u in range(UNROLL):
            first(i + 1, there, u, mixed[0], u)
            second(i, here, UNROLL + u, mixed[1], u)

    wait(end, LEFT)
    wait(end + 1, LEFT)
    wait(end + 1, RIGHT)
    if not first_part:
        return
    low = lax.broadcasted_iota(jnp.int32, (kernel_size, patch), 1) < kernel_size
    take = functools.partial(strip, sums, row_slots, col_slots, kernel_size)
    for a in range(row_slots + 1):
        real = pltpu.roll(take(0, a, col_slots - 1), kernel_size, 1)
        edge = jnp.where(low, real, take(1, a, col_slots - 1)).astype(col_ref.dtype)
        if a < row_slots:
            col_ref[a * kernel_size : (a + 1) * kernel_size, :] = edge
        else:
            corner_ref[...] = edge
    for plane in range(2):
        behind = 0.0
        for tile in range(col_slots // 2):
            odd = pltpu.roll(take(plane, row_slots, 2 * tile + 1), kernel_size, 1)
            value = take(plane, row_slots, 2 * tile) + jnp.where(low, behind, odd)
            row_ref[plane, :, tile * patch : (tile + 1) * patch] = value.astype(row_ref.dtype)
            behind = odd


def grid_part(plan, part, kernels, left, right, carried, layout):
    kernel_size = kernels.shape[1]
    patch = left.shape[1]
    row_slots, col_slots = TILE_U // kernel_size, TILE_V // kernel_size
    smem = pl.BlockSpec(memory_space=pltpu.SMEM)
    vmem = pl.BlockSpec(memory_space=pltpu.VMEM)
    hbm = pl.BlockSpec(memory_space=pl.ANY)
    first_part = carried is None
    carried = [] if first_part else [in_vmem(array) for array in carried]
    mixed_shape = (UNROLL, QUAD * 2 * kernel_size, 2 * patch)
    out_shape = [
        pltpu.VMEM((row_slots * col_slots, patch, 2 * patch), jnp.float32),
        pltpu.VMEM((RING, STEP * QUAD) + left.shape[1:], left.dtype),
        pltpu.VMEM((RING, STEP * QUAD) + right.shape[1:], right.dtype),
        pltpu.VMEM(mixed_shape, jnp.bfloat16),
    ]
    if first_part:
        out_shape += [
            pltpu.VMEM((2, kernel_size, TILE_V), jnp.bfloat16),
            pltpu.VMEM((TILE_U, 2 * kernel_size), jnp.bfloat16),
            pltpu.VMEM((kernel_size, 2 * kernel_size), jnp.bfloat16),
        ]
    out = pl.pallas_call(
        functools.partial(
            grid_body,
            part=part,
            first_part=first_part,
            layout=layout,
            row_slots=row_slots,
            col_slots=col_slots,
        ),
        in_specs=[smem, vmem, hbm, hbm] + [vmem] * len(carried),
        out_specs=[vmem] * len(out_shape),
        out_shape=out_shape,
        input_output_aliases={4 + i: i for i in range(len(carried))},
        scratch_shapes=[
            pltpu.VMEM(mixed_shape, jnp.bfloat16),
            pltpu.SemaphoreType.DMA((2, RING)),
        ],
        compiler_params=pltpu.CompilerParams(vmem_limit_bytes=12 * 2**20),
        name="grid_part",
    )(in_smem(plan), in_vmem(kernels), in_hbm(left), in_hbm(right), *carried)
    return out[:4], out[4:]


def merge_body(sums, row_ref, col_ref, corner_ref, out_hbm, out_ref, sems):
    kernel_size = row_ref.shape[1]
    patch = sums.shape[1]
    row_slots = out_ref.shape[1] // kernel_size
    col_slots = out_ref.shape[2] // kernel_size
    low = lax.broadcasted_iota(jnp.int32, (kernel_size, patch), 1) < kernel_size
    take = functools.partial(strip, sums, row_slots, col_slots, kernel_size)
    for a in range(row_slots):
        rows = slice(a * kernel_size, (a + 1) * kernel_size)
        edge = past_first(["tv"], col_ref[rows, :])
        if a == 0:
            edge = edge + past_first(["tu", "tv"], corner_ref[...])
        for plane in range(2):
            behind = edge if plane == 0 else pltpu.roll(edge, kernel_size, 1)
            for tile in range(col_slots // 2):
                lanes = slice(tile * patch, (tile + 1) * patch)
                odd = pltpu.roll(take(plane, a, 2 * tile + 1), kernel_size, 1)
                value = take(plane, a, 2 * tile) + jnp.where(low, behind, odd)
                if a == 0:
                    value = value + past_first(["tu"], row_ref[plane, :, lanes])
                out_ref[plane, rows, lanes] = value
                behind = odd
        pltpu.make_async_copy(out_ref.at[:, rows], out_hbm.at[:, rows], sems.at[a]).start()
    for a in range(row_slots):
        rows = slice(a * kernel_size, (a + 1) * kernel_size)
        pltpu.make_async_copy(out_ref.at[:, rows], out_hbm.at[:, rows], sems.at[a]).wait()


def merge_tile(sums, row, col, corner):
    vmem = pl.BlockSpec(memory_space=pltpu.VMEM)
    return pl.pallas_call(
        merge_body,
        in_specs=[vmem] * 4,
        out_specs=pl.BlockSpec(memory_space=pl.ANY),
        out_shape=jax.ShapeDtypeStruct((2, TILE_U, TILE_V), jnp.float32),
        scratch_shapes=[
            pltpu.VMEM((2, TILE_U, TILE_V), jnp.float32),
            pltpu.SemaphoreType.DMA((TILE_U // row.shape[1],)),
        ],
        compiler_params=pltpu.CompilerParams(vmem_limit_bytes=8 * 2**20),
        name="merge_tile",
    )(*map(in_vmem, (sums, row, col, corner)))


def shards(
    aperture_amp,
    aperture_phase,
    plane_depths,
    send_list,
    send_count,
    vis_left,
    vis_right,
    block_slot,
    block_pos,
    block_count,
):
    kernel_size = vis_right.shape[1]
    tiles, capacity = send_list.shape[1:]
    both = ("tu", "tv")
    outgoing = make_kernels(
        aperture_amp, aperture_phase, plane_depths, send_list[0].T, send_count, kernel_size
    )
    outgoing = outgoing.reshape((tiles, capacity) + outgoing.shape[1:])
    arrived = lax.all_to_all(outgoing, both, split_axis=0, concat_axis=0, tiled=True)
    received = arrived.reshape((-1,) + arrived.shape[2:])
    layout = Layout(block_pos.shape[0], (TILE_U // kernel_size) * (TILE_V // kernel_size))
    plan, left, right = plan_blocks(block_pos, block_slot, block_count, vis_left, vis_right, layout)
    carried, (row, col, corner) = grid_part(plan, 0, received, left, right, None, layout)
    row = around(row, ("tu",))
    col = around(col, ("tv",))
    corner = around(corner, ("tu", "tv"))
    carried, _ = grid_part(plan, 1, received, left, right, carried, layout)
    return merge_tile(carried[0], row, col, corner)


def solution(mesh):
    placed = (
        P(("tu", "tv"), None, None),
        P(("tu", "tv"), None, None),
        P(),
        P(("tu", "tv"), None, None),
        P(("tu", "tv"), None),
        P(("tu", "tv"), None, None),
        P(("tu", "tv"), None, None),
        P(("tu", "tv")),
        P(("tu", "tv")),
        P(("tu", "tv")),
    )
    return jax.shard_map(
        shards, mesh=mesh, in_specs=placed, out_specs=P(None, "tu", "tv"), check_vma=False
    )
```

```python
import functools
import math

import jax
import jax.numpy as jnp
import numpy as np
from jax import lax
from jax.experimental import pallas as pl
from jax.experimental.pallas import tpu as pltpu
from jax.sharding import PartitionSpec as P

TILE_U = 256
TILE_V = 512
QUAD = 4
UNROLL = 8
STEP = 2 * UNROLL
RING = 4
LEFT, RIGHT = 0, 1

def _fit(fn, degree):
    span = math.pi ** 2
    nodes = 0.5 * span * (1.0 - np.cos(np.pi * (np.arange(400) + 0.5) / 400))
    cheb = np.polynomial.chebyshev.Chebyshev.fit(nodes, fn(np.sqrt(nodes)), degree, domain=[0, span])
    return [float(c) for c in cheb.convert(kind=np.polynomial.Polynomial).coef]


COS_POLY = _fit(np.cos, 6)
SIN_POLY = _fit(lambda x: np.sin(x) / x, 5)


def horner(coefs, u):
    total = jnp.full_like(u, coefs[-1])
    for coef in coefs[-2::-1]:
        total = total * u + coef
    return total


def cos_sin(x):
    u = x * x
    return horner(COS_POLY, u), x * horner(SIN_POLY, u)


def around(block, axes):
    sizes = [lax.axis_size(axis) for axis in axes]
    route = []
    for place in np.ndindex(*sizes):
        target = [(i + 1) % n for i, n in zip(place, sizes)]
        route.append((int(np.ravel_multi_index(place, sizes)), int(np.ravel_multi_index(target, sizes))))
    return lax.ppermute(block, axes, route)


def to_next(block, axis):
    places = range(lax.axis_size(axis))

    def exchange(first):
        route = []
        for i in places:
            other = i + 1 if i % 2 == first else i - 1
            route.append((i, other if other in places else i))
        return lax.ppermute(block, axis, route)

    return exchange(0), exchange(1)


def past_first(axes, halo):
    real = functools.reduce(jnp.logical_and, [lax.axis_index(axis) > 0 for axis in axes])
    return jnp.where(real, halo.astype(jnp.float32), 0.0)


def in_hbm(array):
    return pltpu.with_memory_space_constraint(array, pltpu.HBM)


def in_vmem(array):
    return pltpu.with_memory_space_constraint(array, pltpu.VMEM)


def in_smem(array):
    return pltpu.with_memory_space_constraint(array, pltpu.SMEM)


def kernels_body(
    list_hbm, count_hbm, depth_hbm, amp_hbm, phase_hbm, out_ref,
    chosen_list, count, depth, amp, phase, table, screen, halves, made, small_sems, bulk_sems,
):
    screens, size, _ = amp.shape
    planes = depth.shape[0]
    kernel_size = out_ref.shape[1]
    small = [
        pltpu.make_async_copy(depth_hbm, depth, small_sems.at[0]),
        pltpu.make_async_copy(list_hbm, chosen_list, small_sems.at[1]),
        pltpu.make_async_copy(count_hbm, count, small_sems.at[2]),
    ]
    for copy in small:
        copy.start()

    def bulk(s):
        return [
            pltpu.make_async_copy(amp_hbm.at[s], amp.at[s], bulk_sems.at[0, s]),
            pltpu.make_async_copy(phase_hbm.at[s], phase.at[s], bulk_sems.at[1, s]),
        ]

    for copy in bulk(0):
        copy.start()

    frequency = lax.broadcasted_iota(jnp.int32, (kernel_size, size), 0) - kernel_size // 2
    cells = lax.broadcasted_iota(jnp.int32, (kernel_size, size), 1)
    turns = frequency.astype(jnp.float32) * cells.astype(jnp.float32) / size
    real_f, imag_f = cos_sin((2.0 * math.pi) * (turns - jnp.round(turns)))
    real_f = real_f.astype(jnp.bfloat16).astype(jnp.float32)
    imag_f = (-imag_f).astype(jnp.bfloat16).astype(jnp.float32)
    place = (lax.broadcasted_iota(jnp.int32, (1, size), 1).astype(jnp.float32) - size // 2) / size
    square = place * place
    for copy in small:
        copy.wait()
    for s in range(1, screens):
        for copy in bulk(s):
            copy.start()
    for p in range(planes):
        turns = depth[p] * square
        real_e, imag_e = cos_sin((2.0 * math.pi) * (turns - jnp.round(turns)))
        real_g = (real_f * real_e - imag_f * imag_e).astype(jnp.bfloat16)
        imag_g = (real_f * imag_e + imag_f * real_e).astype(jnp.bfloat16)
        top = slice(p * 2 * kernel_size, (p * 2 + 1) * kernel_size)
        low = slice((p * 2 + 1) * kernel_size, (p * 2 + 2) * kernel_size)
        table[top, :size] = real_g
        table[top, size:] = -imag_g
        table[low, :size] = imag_g
        table[low, size:] = real_g

    @pl.loop(0, screens)
    def _(s):
        for copy in bulk(s):
            copy.wait()
        magnitude = amp[s].astype(jnp.float32)
        real_e, imag_e = cos_sin(phase[s].astype(jnp.float32))
        screen[:size, :] = (magnitude * real_e).astype(jnp.bfloat16)
        screen[size:, :] = (magnitude * imag_e).astype(jnp.bfloat16)
        product = jnp.dot(table[...], screen[...], preferred_element_type=jnp.float32).astype(jnp.bfloat16)
        for p in range(planes):
            base = p * 2 * kernel_size
            halves[s, p, :, :size] = product[base : base + kernel_size]
            halves[s, p, :, size:] = product[base + kernel_size : base + 2 * kernel_size]

    for p in range(planes):
        second = lax.dot_general(
            jnp.concatenate([halves[s, p] for s in range(screens)], axis=0),
            table[p * 2 * kernel_size : (p + 1) * 2 * kernel_size, :],
            (((1,), (1,)), ((), ())),
            preferred_element_type=jnp.float32,
        )
        second = (second * (1.0 / size)).astype(jnp.bfloat16)
        for s in range(screens):
            made[s * planes + p] = second[s * kernel_size : (s + 1) * kernel_size]

    capacity, tiles = chosen_list.shape

    @pl.loop(0, tiles, unroll=8)
    def _(t):
        for c in range(capacity):
            chosen = made[chosen_list[c, t]]
            out_ref[t * capacity + c] = jnp.where(c < count[0, t], chosen, jnp.zeros_like(chosen))


def make_kernels(aperture_amp, aperture_phase, plane_depths, chosen_list, counts, kernel_size):
    screens, size, _ = aperture_amp.shape
    planes = plane_depths.shape[0]
    capacity, tiles = chosen_list.shape
    hbm = pl.BlockSpec(memory_space=pl.ANY)
    return pl.pallas_call(
        kernels_body,
        in_specs=[hbm] * 5,
        out_specs=pl.BlockSpec(memory_space=pltpu.VMEM),
        out_shape=pltpu.VMEM((tiles * capacity, kernel_size, 2 * kernel_size), jnp.bfloat16),
        scratch_shapes=[
            pltpu.SMEM((capacity, tiles), jnp.int32),
            pltpu.SMEM((1, tiles), jnp.int32),
            pltpu.SMEM((planes,), jnp.float32),
            pltpu.VMEM((screens, size, size), jnp.bfloat16),
            pltpu.VMEM((screens, size, size), jnp.bfloat16),
            pltpu.VMEM((planes * 2 * kernel_size, 2 * size), jnp.bfloat16),
            pltpu.VMEM((2 * size, size), jnp.bfloat16),
            pltpu.VMEM((screens, planes, kernel_size, 2 * size), jnp.bfloat16),
            pltpu.VMEM((screens * planes, kernel_size, 2 * kernel_size), jnp.bfloat16),
            pltpu.SemaphoreType.DMA((3,)),
            pltpu.SemaphoreType.DMA((2, screens)),
        ],
        compiler_params=pltpu.CompilerParams(vmem_limit_bytes=32 * 2**20),
        name="make_kernels",
    )(*map(in_hbm, (chosen_list, counts, plane_depths, aperture_amp, aperture_phase)))


class Layout:
    def __init__(self, blocks, anchors):
        self.parts = 2
        quads = (blocks + (QUAD - 1) * anchors) // QUAD + 1
        self.quads = (quads + STEP - 1) // STEP * STEP
        self.anchor = self.parts + 1
        self.slot = self.anchor + self.quads
        self.total = self.slot + (self.quads + UNROLL) * QUAD


def plan_body(
    pos_ref, slot_ref, count_ref, left_hbm, right_hbm, plan_ref, left_out, right_out,
    left_ref, right_ref, tally, cursor, sems, *, layout, row_slots, col_slots,
):
    anchors = row_slots * col_slots
    border = row_slots + col_slots - 1
    live = count_ref[0]

    def copies(block, place):
        return [
            pltpu.make_async_copy(left_hbm.at[block], left_ref.at[place], sems.at[0]),
            pltpu.make_async_copy(right_hbm.at[block], right_ref.at[place], sems.at[1]),
        ]

    def put(block, place, slot):
        plan_ref[layout.slot + place] = slot
        for copy in copies(block, place):
            copy.start()

    @pl.loop(0, anchors)
    def _(q):
        tally[q] = 0

    @pl.loop(0, live)
    def _(j):
        q = pos_ref[j]
        tally[q] = tally[q] + 1

    def lay(rank, quad):
        inner = rank - border
        q = jnp.where(
            rank < row_slots,
            rank * col_slots + col_slots - 1,
            jnp.where(
                rank < border,
                (row_slots - 1) * col_slots + rank - row_slots,
                (inner // (col_slots - 1)) * col_slots + lax.rem(inner, col_slots - 1),
            ),
        )
        number = tally[q]
        quads = (number + QUAD - 1) // QUAD
        cursor[q] = quad * QUAD

        @pl.loop(0, quads)
        def _(i):
            plan_ref[layout.anchor + quad + i] = q

        @pl.loop(quad * QUAD + number, (quad + quads) * QUAD)
        def _(i):
            put(0, i, -1)

        return quad + quads

    quad = 0
    begin = 0
    plan_ref[0] = 0
    for part, end in enumerate([border, anchors]):
        quad = lax.fori_loop(begin, end, lay, quad)
        begin = end
        plan_ref[part + 1] = ((quad + STEP - 1) // STEP) * STEP

    full = ((quad + STEP - 1) // STEP) * STEP

    @pl.loop(quad, full)
    def _(i):
        plan_ref[layout.anchor + i] = 0
        for e in range(QUAD):
            put(0, i * QUAD + e, -1)

    quad = full

    @pl.loop(quad * QUAD, (quad + UNROLL) * QUAD)
    def _(i):
        plan_ref[layout.slot + i] = -1

    @pl.loop(0, live)
    def _(j):
        q = pos_ref[j]
        at = cursor[q]
        cursor[q] = at + 1
        put(j, at, slot_ref[j])

    chunk = STEP * QUAD

    @pl.loop(0, quad // STEP)
    def _(i):
        rows = pl.ds(0, chunk)
        pltpu.make_async_copy(left_hbm.at[rows], left_ref.at[rows], sems.at[0]).wait()
        pltpu.make_async_copy(right_hbm.at[rows], right_ref.at[rows], sems.at[1]).wait()

    def writes(i):
        rows = pl.ds(i * chunk, chunk)
        return [
            pltpu.make_async_copy(left_ref.at[rows], left_out.at[rows], sems.at[2]),
            pltpu.make_async_copy(right_ref.at[rows], right_out.at[rows], sems.at[3]),
        ]

    @pl.loop(0, quad // STEP)
    def _(i):
        for copy in writes(i):
            copy.start()

    @pl.loop(0, quad // STEP)
    def _(i):
        for copy in writes(i):
            copy.wait()


def plan_blocks(block_pos, block_slot, block_count, vis_left, vis_right, layout):
    kernel_size = vis_right.shape[1]
    row_slots, col_slots = TILE_U // kernel_size, TILE_V // kernel_size
    smem = pl.BlockSpec(memory_space=pltpu.SMEM)
    hbm = pl.BlockSpec(memory_space=pl.ANY)
    places = layout.quads * QUAD
    return pl.pallas_call(
        functools.partial(plan_body, layout=layout, row_slots=row_slots, col_slots=col_slots),
        in_specs=[smem] * 3 + [hbm] * 2,
        out_specs=[smem, hbm, hbm],
        out_shape=[
            pltpu.SMEM((layout.total,), jnp.int32),
            pltpu.HBM((places,) + vis_left.shape[1:], vis_left.dtype),
            pltpu.HBM((places,) + vis_right.shape[1:], vis_right.dtype),
        ],
        scratch_shapes=[
            pltpu.VMEM((places,) + vis_left.shape[1:], vis_left.dtype),
            pltpu.VMEM((places,) + vis_right.shape[1:], vis_right.dtype),
            pltpu.SMEM((row_slots * col_slots,), jnp.int32),
            pltpu.SMEM((row_slots * col_slots,), jnp.int32),
            pltpu.SemaphoreType.DMA((4,)),
        ],
        compiler_params=pltpu.CompilerParams(vmem_limit_bytes=36 * 2**20),
        name="plan_blocks",
    )(block_pos, block_slot, block_count, in_hbm(vis_left), in_hbm(vis_right))


def strip(sums, row_slots, col_slots, kernel_size, plane, a, col):
    patch = sums.shape[1]
    lanes = slice(plane * patch, (plane + 1) * patch)
    total = None
    if a < row_slots:
        total = sums[a * col_slots + col, :kernel_size, lanes]
    if a > 0:
        above = sums[(a - 1) * col_slots + col, kernel_size:, lanes]
        total = above if total is None else total + above
    return total


def grid_body(
    plan_ref, kern_ref, left_hbm, right_hbm, *rest, part, first_part, layout, row_slots, col_slots
):
    if not first_part:
        rest = rest[4:]
    sums, left_ring, right_ring, ahead, *rest = rest
    if first_part:
        row_ref, col_ref, corner_ref, *rest = rest
    behind_ref, sems = rest
    mixed = (ahead, behind_ref)
    slots, kernel_size, _ = kern_ref.shape
    patch = left_hbm.shape[1]
    chunk = STEP * QUAD
    begin = plan_ref[part] // STEP
    end = plan_ref[part + 1] // STEP
    limit = jnp.minimum(plan_ref[layout.parts] // STEP, end + 2)

    def fetch(i):
        source = pl.ds(i * chunk, chunk)
        ring = lax.rem(i, RING)
        return [
            pltpu.make_async_copy(left_hbm.at[source], left_ring.at[ring], sems.at[0, ring]),
            pltpu.make_async_copy(right_hbm.at[source], right_ring.at[ring], sems.at[1, ring]),
        ]

    def start(i, which):
        @pl.when(i < limit)
        def _():
            fetch(i)[which].start()

    def wait(i, which):
        fresh = (i < limit) if first_part else ((i < limit) & (i > begin + 1))

        @pl.when(fresh)
        def _():
            fetch(i)[which].wait()

    if first_part:
        start(0, RIGHT)
        start(1, RIGHT)
        start(0, LEFT)

        @pl.loop(0, sums.shape[0])
        def _(q):
            sums[q] = jnp.zeros(sums.shape[1:], sums.dtype)

    zero = jnp.zeros((kernel_size, patch), jnp.bfloat16)

    def first(i, ring, at, ref, u):
        for e in range(QUAD):
            slot = plan_ref[layout.slot + (i * STEP + at) * QUAD + e]
            right = right_ring[ring, at * QUAD + e]
            kern = kern_ref[jnp.maximum(slot, 0)]
            kern = jnp.where(slot >= 0, kern, jnp.zeros_like(kern))
            spread = jnp.concatenate(
                [jnp.concatenate([right, zero], axis=1), jnp.concatenate([zero, right], axis=1)], axis=0
            )
            out = jnp.dot(kern, spread, preferred_element_type=jnp.float32).astype(jnp.bfloat16)
            top = slice(e * 2 * kernel_size, (e * 2 + 1) * kernel_size)
            low = slice((e * 2 + 1) * kernel_size, (e * 2 + 2) * kernel_size)
            ref[u, top, :] = out
            ref[u, low, :patch] = -out[:, patch:]
            ref[u, low, patch:] = out[:, :patch]

    def second(i, ring, at, ref, u):
        left = jnp.concatenate([left_ring[ring, at * QUAD + e] for e in range(QUAD)], axis=1)
        q = plan_ref[layout.anchor + i * STEP + at]
        sums[q] += jnp.dot(left, ref[u], preferred_element_type=jnp.float32)

    if first_part:
        wait(0, RIGHT)
        start(1, LEFT)
        for u in range(UNROLL):
            first(0, 0, u, mixed[0], u)
    start(begin + 2, RIGHT)
    start(begin + 2, LEFT)

    @pl.loop(begin, end)
    def _(i):
        here = lax.rem(i, RING)
        there = lax.rem(i + 1, RING)
        start(i + 3, RIGHT)
        start(i + 3, LEFT)
        wait(i, LEFT)
        wait(i + 1, RIGHT)
        for u in range(UNROLL):
            first(i, here, UNROLL + u, mixed[1], u)
            second(i, here, u, mixed[0], u)
        for u in range(UNROLL):
            first(i + 1, there, u, mixed[0], u)
            second(i, here, UNROLL + u, mixed[1], u)

    wait(end, LEFT)
    wait(end + 1, LEFT)
    wait(end + 1, RIGHT)
    if not first_part:
        return
    low = lax.broadcasted_iota(jnp.int32, (kernel_size, patch), 1) < kernel_size
    take = functools.partial(strip, sums, row_slots, col_slots, kernel_size)
    for a in range(row_slots + 1):
        real = pltpu.roll(take(0, a, col_slots - 1), kernel_size, 1)
        edge = jnp.where(low, real, take(1, a, col_slots - 1)).astype(col_ref.dtype)
        if a < row_slots:
            col_ref[a * kernel_size : (a + 1) * kernel_size, :] = edge
        else:
            corner_ref[...] = edge
    for plane in range(2):
        behind = 0.0
        for tile in range(col_slots // 2):
            odd = pltpu.roll(take(plane, row_slots, 2 * tile + 1), kernel_size, 1)
            value = take(plane, row_slots, 2 * tile) + jnp.where(low, behind, odd)
            row_ref[plane, :, tile * patch : (tile + 1) * patch] = value.astype(row_ref.dtype)
            behind = odd


def grid_part(plan, part, kernels, left, right, carried, layout):
    kernel_size = kernels.shape[1]
    patch = left.shape[1]
    row_slots, col_slots = TILE_U // kernel_size, TILE_V // kernel_size
    smem = pl.BlockSpec(memory_space=pltpu.SMEM)
    vmem = pl.BlockSpec(memory_space=pltpu.VMEM)
    hbm = pl.BlockSpec(memory_space=pl.ANY)
    first_part = carried is None
    carried = [] if first_part else [in_vmem(array) for array in carried]
    mixed_shape = (UNROLL, QUAD * 2 * kernel_size, 2 * patch)
    out_shape = [
        pltpu.VMEM((row_slots * col_slots, patch, 2 * patch), jnp.float32),
        pltpu.VMEM((RING, STEP * QUAD) + left.shape[1:], left.dtype),
        pltpu.VMEM((RING, STEP * QUAD) + right.shape[1:], right.dtype),
        pltpu.VMEM(mixed_shape, jnp.bfloat16),
    ]
    if first_part:
        out_shape += [
            pltpu.VMEM((2, kernel_size, TILE_V), jnp.bfloat16),
            pltpu.VMEM((TILE_U, 2 * kernel_size), jnp.bfloat16),
            pltpu.VMEM((kernel_size, 2 * kernel_size), jnp.bfloat16),
        ]
    out = pl.pallas_call(
        functools.partial(
            grid_body,
            part=part,
            first_part=first_part,
            layout=layout,
            row_slots=row_slots,
            col_slots=col_slots,
        ),
        in_specs=[smem, vmem, hbm, hbm] + [vmem] * len(carried),
        out_specs=[vmem] * len(out_shape),
        out_shape=out_shape,
        input_output_aliases={4 + i: i for i in range(len(carried))},
        scratch_shapes=[
            pltpu.VMEM(mixed_shape, jnp.bfloat16),
            pltpu.SemaphoreType.DMA((2, RING)),
        ],
        compiler_params=pltpu.CompilerParams(vmem_limit_bytes=12 * 2**20),
        name="grid_part",
    )(in_smem(plan), in_vmem(kernels), in_hbm(left), in_hbm(right), *carried)
    return out[:4], out[4:]


def merge_body(sums, even_ref, odd_ref, col_ref, corner_ref, out_hbm, out_ref, sems):
    kernel_size = even_ref.shape[1]
    patch = sums.shape[1]
    row_slots = out_ref.shape[1] // kernel_size
    col_slots = out_ref.shape[2] // kernel_size
    low = lax.broadcasted_iota(jnp.int32, (kernel_size, patch), 1) < kernel_size
    take = functools.partial(strip, sums, row_slots, col_slots, kernel_size)
    below_even = lax.axis_index("tu") % 2 == 1
    for a in range(row_slots):
        rows = slice(a * kernel_size, (a + 1) * kernel_size)
        edge = past_first(["tv"], col_ref[rows, :])
        if a == 0:
            edge = edge + past_first(["tu", "tv"], corner_ref[...])
        for plane in range(2):
            behind = edge if plane == 0 else pltpu.roll(edge, kernel_size, 1)
            for tile in range(col_slots // 2):
                lanes = slice(tile * patch, (tile + 1) * patch)
                odd = pltpu.roll(take(plane, a, 2 * tile + 1), kernel_size, 1)
                value = take(plane, a, 2 * tile) + jnp.where(low, behind, odd)
                if a == 0:
                    row = jnp.where(below_even, even_ref[plane, :, lanes], odd_ref[plane, :, lanes])
                    value = value + past_first(["tu"], row)
                out_ref[plane, rows, lanes] = value
                behind = odd
        pltpu.make_async_copy(out_ref.at[:, rows], out_hbm.at[:, rows], sems.at[a]).start()
    for a in range(row_slots):
        rows = slice(a * kernel_size, (a + 1) * kernel_size)
        pltpu.make_async_copy(out_ref.at[:, rows], out_hbm.at[:, rows], sems.at[a]).wait()


def merge_tile(sums, from_even, from_odd, col, corner):
    vmem = pl.BlockSpec(memory_space=pltpu.VMEM)
    return pl.pallas_call(
        merge_body,
        in_specs=[vmem] * 5,
        out_specs=pl.BlockSpec(memory_space=pl.ANY),
        out_shape=jax.ShapeDtypeStruct((2, TILE_U, TILE_V), jnp.float32),
        scratch_shapes=[
            pltpu.VMEM((2, TILE_U, TILE_V), jnp.float32),
            pltpu.SemaphoreType.DMA((TILE_U // from_even.shape[1],)),
        ],
        compiler_params=pltpu.CompilerParams(vmem_limit_bytes=8 * 2**20),
        name="merge_tile",
    )(*map(in_vmem, (sums, from_even, from_odd, col, corner)))


def shards(
    aperture_amp,
    aperture_phase,
    plane_depths,
    send_list,
    send_count,
    vis_left,
    vis_right,
    block_slot,
    block_pos,
    block_count,
):
    kernel_size = vis_right.shape[1]
    tiles, capacity = send_list.shape[1:]
    both = ("tu", "tv")
    outgoing = make_kernels(
        aperture_amp, aperture_phase, plane_depths, send_list[0].T, send_count, kernel_size
    )
    outgoing = outgoing.reshape((tiles, capacity) + outgoing.shape[1:])
    arrived = lax.all_to_all(outgoing, both, split_axis=0, concat_axis=0, tiled=True)
    received = arrived.reshape((-1,) + arrived.shape[2:])
    layout = Layout(block_pos.shape[0], (TILE_U // kernel_size) * (TILE_V // kernel_size))
    plan, left, right = plan_blocks(block_pos, block_slot, block_count, vis_left, vis_right, layout)
    carried, (row, col, corner) = grid_part(plan, 0, received, left, right, None, layout)
    from_even, from_odd = to_next(row, "tu")
    col = around(col, ("tv",))
    corner = around(corner, ("tu", "tv"))
    carried, _ = grid_part(plan, 1, received, left, right, carried, layout)
    return merge_tile(carried[0], from_even, from_odd, col, corner)


def solution(mesh):
    placed = (
        P(("tu", "tv"), None, None),
        P(("tu", "tv"), None, None),
        P(),
        P(("tu", "tv"), None, None),
        P(("tu", "tv"), None),
        P(("tu", "tv"), None, None),
        P(("tu", "tv"), None, None),
        P(("tu", "tv")),
        P(("tu", "tv")),
        P(("tu", "tv")),
    )
    return jax.shard_map(
        shards, mesh=mesh, in_specs=placed, out_specs=P(None, "tu", "tv"), check_vma=False
    )
```

```python
import functools
import math

import jax
import jax.numpy as jnp
import numpy as np
from jax import lax
from jax.experimental import pallas as pl
from jax.experimental.pallas import tpu as pltpu
from jax.sharding import PartitionSpec as P

TILE_U = 256
TILE_V = 512
QUAD = 4
UNROLL = 8
STEP = 2 * UNROLL
RING = 4
LEFT, RIGHT = 0, 1

def _fit(fn, degree):
    span = math.pi ** 2
    nodes = 0.5 * span * (1.0 - np.cos(np.pi * (np.arange(400) + 0.5) / 400))
    cheb = np.polynomial.chebyshev.Chebyshev.fit(nodes, fn(np.sqrt(nodes)), degree, domain=[0, span])
    return [float(c) for c in cheb.convert(kind=np.polynomial.Polynomial).coef]


COS_POLY = _fit(np.cos, 6)
SIN_POLY = _fit(lambda x: np.sin(x) / x, 5)


def horner(coefs, u):
    total = jnp.full_like(u, coefs[-1])
    for coef in coefs[-2::-1]:
        total = total * u + coef
    return total


def cos_sin(x):
    u = x * x
    return horner(COS_POLY, u), x * horner(SIN_POLY, u)


def around(block, axes):
    sizes = [lax.axis_size(axis) for axis in axes]
    route = []
    for place in np.ndindex(*sizes):
        target = [(i + 1) % n for i, n in zip(place, sizes)]
        route.append((int(np.ravel_multi_index(place, sizes)), int(np.ravel_multi_index(target, sizes))))
    return lax.ppermute(block, axes, route)


def past_first(axes, halo):
    real = functools.reduce(jnp.logical_and, [lax.axis_index(axis) > 0 for axis in axes])
    return jnp.where(real, halo.astype(jnp.float32), 0.0)


def in_hbm(array):
    return pltpu.with_memory_space_constraint(array, pltpu.HBM)


def in_vmem(array):
    return pltpu.with_memory_space_constraint(array, pltpu.VMEM)


def in_smem(array):
    return pltpu.with_memory_space_constraint(array, pltpu.SMEM)


def kernels_body(
    list_hbm, count_hbm, depth_hbm, amp_hbm, phase_hbm, out_ref,
    chosen_list, count, depth, amp, phase, table, screen, halves, made, small_sems, bulk_sems,
):
    screens, size, _ = amp.shape
    planes = depth.shape[0]
    kernel_size = out_ref.shape[1]
    small = [
        pltpu.make_async_copy(depth_hbm, depth, small_sems.at[0]),
        pltpu.make_async_copy(list_hbm, chosen_list, small_sems.at[1]),
        pltpu.make_async_copy(count_hbm, count, small_sems.at[2]),
    ]
    for copy in small:
        copy.start()

    halfway = size // 2
    row_halves = (slice(0, halfway), slice(halfway, size))

    def bulk(s, h):
        rows = row_halves[h]
        return [
            pltpu.make_async_copy(amp_hbm.at[s, rows], amp.at[s, rows], bulk_sems.at[h, s]),
            pltpu.make_async_copy(phase_hbm.at[s, rows], phase.at[s, rows], bulk_sems.at[2 + h, s]),
        ]

    for h in range(2):
        for copy in bulk(0, h):
            copy.start()

    frequency = lax.broadcasted_iota(jnp.int32, (kernel_size, size), 0) - kernel_size // 2
    cells = lax.broadcasted_iota(jnp.int32, (kernel_size, size), 1)
    turns = frequency.astype(jnp.float32) * cells.astype(jnp.float32) / size
    real_f, imag_f = cos_sin((2.0 * math.pi) * (turns - jnp.round(turns)))
    real_f = real_f.astype(jnp.bfloat16).astype(jnp.float32)
    imag_f = (-imag_f).astype(jnp.bfloat16).astype(jnp.float32)
    place = (lax.broadcasted_iota(jnp.int32, (1, size), 1).astype(jnp.float32) - size // 2) / size
    square = place * place
    for copy in small:
        copy.wait()
    for s in range(1, screens):
        for h in range(2):
            for copy in bulk(s, h):
                copy.start()
    for p in range(planes):
        turns = depth[p] * square
        real_e, imag_e = cos_sin((2.0 * math.pi) * (turns - jnp.round(turns)))
        real_g = (real_f * real_e - imag_f * imag_e).astype(jnp.bfloat16)
        imag_g = (real_f * imag_e + imag_f * real_e).astype(jnp.bfloat16)
        top = slice(p * 2 * kernel_size, (p * 2 + 1) * kernel_size)
        low = slice((p * 2 + 1) * kernel_size, (p * 2 + 2) * kernel_size)
        table[top, :size] = real_g
        table[top, size:] = -imag_g
        table[low, :size] = imag_g
        table[low, size:] = real_g

    @pl.loop(0, screens)
    def _(s):
        for h, rows in enumerate(row_halves):
            for copy in bulk(s, h):
                copy.wait()
            magnitude = amp[s, rows].astype(jnp.float32)
            real_e, imag_e = cos_sin(phase[s, rows].astype(jnp.float32))
            screen[rows, :] = (magnitude * real_e).astype(jnp.bfloat16)
            screen[slice(size + rows.start, size + rows.stop), :] = (magnitude * imag_e).astype(jnp.bfloat16)
        product = jnp.dot(table[...], screen[...], preferred_element_type=jnp.float32).astype(jnp.bfloat16)
        for p in range(planes):
            base = p * 2 * kernel_size
            halves[s, p, :, :size] = product[base : base + kernel_size]
            halves[s, p, :, size:] = product[base + kernel_size : base + 2 * kernel_size]

    for p in range(planes):
        second = lax.dot_general(
            jnp.concatenate([halves[s, p] for s in range(screens)], axis=0),
            table[p * 2 * kernel_size : (p + 1) * 2 * kernel_size, :],
            (((1,), (1,)), ((), ())),
            preferred_element_type=jnp.float32,
        )
        second = (second * (1.0 / size)).astype(jnp.bfloat16)
        for s in range(screens):
            made[s * planes + p] = second[s * kernel_size : (s + 1) * kernel_size]

    capacity, tiles = chosen_list.shape

    @pl.loop(0, tiles, unroll=8)
    def _(t):
        for c in range(capacity):
            chosen = made[chosen_list[c, t]]
            out_ref[t * capacity + c] = jnp.where(c < count[0, t], chosen, jnp.zeros_like(chosen))


def make_kernels(aperture_amp, aperture_phase, plane_depths, chosen_list, counts, kernel_size):
    screens, size, _ = aperture_amp.shape
    planes = plane_depths.shape[0]
    capacity, tiles = chosen_list.shape
    hbm = pl.BlockSpec(memory_space=pl.ANY)
    return pl.pallas_call(
        kernels_body,
        in_specs=[hbm] * 5,
        out_specs=pl.BlockSpec(memory_space=pltpu.VMEM),
        out_shape=pltpu.VMEM((tiles * capacity, kernel_size, 2 * kernel_size), jnp.bfloat16),
        scratch_shapes=[
            pltpu.SMEM((capacity, tiles), jnp.int32),
            pltpu.SMEM((1, tiles), jnp.int32),
            pltpu.SMEM((planes,), jnp.float32),
            pltpu.VMEM((screens, size, size), jnp.bfloat16),
            pltpu.VMEM((screens, size, size), jnp.bfloat16),
            pltpu.VMEM((planes * 2 * kernel_size, 2 * size), jnp.bfloat16),
            pltpu.VMEM((2 * size, size), jnp.bfloat16),
            pltpu.VMEM((screens, planes, kernel_size, 2 * size), jnp.bfloat16),
            pltpu.VMEM((screens * planes, kernel_size, 2 * kernel_size), jnp.bfloat16),
            pltpu.SemaphoreType.DMA((3,)),
            pltpu.SemaphoreType.DMA((4, screens)),
        ],
        compiler_params=pltpu.CompilerParams(vmem_limit_bytes=32 * 2**20),
        name="make_kernels",
    )(*map(in_hbm, (chosen_list, counts, plane_depths, aperture_amp, aperture_phase)))


class Layout:
    def __init__(self, blocks, anchors):
        self.parts = 2
        quads = (blocks + (QUAD - 1) * anchors) // QUAD + 1
        self.quads = (quads + STEP - 1) // STEP * STEP
        self.anchor = self.parts + 1
        self.slot = self.anchor + self.quads
        self.total = self.slot + (self.quads + UNROLL) * QUAD


def plan_body(
    pos_ref, slot_ref, count_ref, left_hbm, right_hbm, plan_ref, left_out, right_out,
    left_ref, right_ref, tally, cursor, sems, *, layout, row_slots, col_slots,
):
    anchors = row_slots * col_slots
    border = row_slots + col_slots - 1
    live = count_ref[0]

    def copies(block, place):
        return [
            pltpu.make_async_copy(left_hbm.at[block], left_ref.at[place], sems.at[0]),
            pltpu.make_async_copy(right_hbm.at[block], right_ref.at[place], sems.at[1]),
        ]

    def put(block, place, slot):
        plan_ref[layout.slot + place] = slot
        for copy in copies(block, place):
            copy.start()

    @pl.loop(0, anchors)
    def _(q):
        tally[q] = 0

    @pl.loop(0, live)
    def _(j):
        q = pos_ref[j]
        tally[q] = tally[q] + 1

    def lay(rank, quad):
        inner = rank - border
        q = jnp.where(
            rank < row_slots,
            rank * col_slots + col_slots - 1,
            jnp.where(
                rank < border,
                (row_slots - 1) * col_slots + rank - row_slots,
                (inner // (col_slots - 1)) * col_slots + lax.rem(inner, col_slots - 1),
            ),
        )
        number = tally[q]
        quads = (number + QUAD - 1) // QUAD
        cursor[q] = quad * QUAD

        @pl.loop(0, quads)
        def _(i):
            plan_ref[layout.anchor + quad + i] = q

        @pl.loop(quad * QUAD + number, (quad + quads) * QUAD)
        def _(i):
            put(0, i, -1)

        return quad + quads

    quad = 0
    begin = 0
    plan_ref[0] = 0
    for part, end in enumerate([border, anchors]):
        quad = lax.fori_loop(begin, end, lay, quad)
        begin = end
        plan_ref[part + 1] = ((quad + STEP - 1) // STEP) * STEP

    full = ((quad + STEP - 1) // STEP) * STEP

    @pl.loop(quad, full)
    def _(i):
        plan_ref[layout.anchor + i] = 0
        for e in range(QUAD):
            put(0, i * QUAD + e, -1)

    quad = full

    @pl.loop(quad * QUAD, (quad + UNROLL) * QUAD)
    def _(i):
        plan_ref[layout.slot + i] = -1

    @pl.loop(0, live)
    def _(j):
        q = pos_ref[j]
        at = cursor[q]
        cursor[q] = at + 1
        put(j, at, slot_ref[j])

    chunk = STEP * QUAD

    @pl.loop(0, quad // STEP)
    def _(i):
        rows = pl.ds(0, chunk)
        pltpu.make_async_copy(left_hbm.at[rows], left_ref.at[rows], sems.at[0]).wait()
        pltpu.make_async_copy(right_hbm.at[rows], right_ref.at[rows], sems.at[1]).wait()

    def writes(i):
        rows = pl.ds(i * chunk, chunk)
        return [
            pltpu.make_async_copy(left_ref.at[rows], left_out.at[rows], sems.at[2]),
            pltpu.make_async_copy(right_ref.at[rows], right_out.at[rows], sems.at[3]),
        ]

    @pl.loop(0, quad // STEP)
    def _(i):
        for copy in writes(i):
            copy.start()

    @pl.loop(0, quad // STEP)
    def _(i):
        for copy in writes(i):
            copy.wait()


def plan_blocks(block_pos, block_slot, block_count, vis_left, vis_right, layout):
    kernel_size = vis_right.shape[1]
    row_slots, col_slots = TILE_U // kernel_size, TILE_V // kernel_size
    smem = pl.BlockSpec(memory_space=pltpu.SMEM)
    hbm = pl.BlockSpec(memory_space=pl.ANY)
    places = layout.quads * QUAD
    return pl.pallas_call(
        functools.partial(plan_body, layout=layout, row_slots=row_slots, col_slots=col_slots),
        in_specs=[smem] * 3 + [hbm] * 2,
        out_specs=[smem, hbm, hbm],
        out_shape=[
            pltpu.SMEM((layout.total,), jnp.int32),
            pltpu.HBM((places,) + vis_left.shape[1:], vis_left.dtype),
            pltpu.HBM((places,) + vis_right.shape[1:], vis_right.dtype),
        ],
        scratch_shapes=[
            pltpu.VMEM((places,) + vis_left.shape[1:], vis_left.dtype),
            pltpu.VMEM((places,) + vis_right.shape[1:], vis_right.dtype),
            pltpu.SMEM((row_slots * col_slots,), jnp.int32),
            pltpu.SMEM((row_slots * col_slots,), jnp.int32),
            pltpu.SemaphoreType.DMA((4,)),
        ],
        compiler_params=pltpu.CompilerParams(vmem_limit_bytes=36 * 2**20),
        name="plan_blocks",
    )(block_pos, block_slot, block_count, in_hbm(vis_left), in_hbm(vis_right))


def strip(sums, row_slots, col_slots, kernel_size, plane, a, col):
    patch = sums.shape[1]
    lanes = slice(plane * patch, (plane + 1) * patch)
    total = None
    if a < row_slots:
        total = sums[a * col_slots + col, :kernel_size, lanes]
    if a > 0:
        above = sums[(a - 1) * col_slots + col, kernel_size:, lanes]
        total = above if total is None else total + above
    return total


def grid_body(
    plan_ref, kern_ref, left_hbm, right_hbm, *rest, part, first_part, layout, row_slots, col_slots
):
    if not first_part:
        rest = rest[4:]
    sums, left_ring, right_ring, ahead, *rest = rest
    if first_part:
        row_ref, col_ref, corner_ref, *rest = rest
    behind_ref, sems = rest
    mixed = (ahead, behind_ref)
    slots, kernel_size, _ = kern_ref.shape
    patch = left_hbm.shape[1]
    chunk = STEP * QUAD
    begin = plan_ref[part] // STEP
    end = plan_ref[part + 1] // STEP
    limit = jnp.minimum(plan_ref[layout.parts] // STEP, end + 2)

    def fetch(i):
        source = pl.ds(i * chunk, chunk)
        ring = lax.rem(i, RING)
        return [
            pltpu.make_async_copy(left_hbm.at[source], left_ring.at[ring], sems.at[0, ring]),
            pltpu.make_async_copy(right_hbm.at[source], right_ring.at[ring], sems.at[1, ring]),
        ]

    def start(i, which):
        @pl.when(i < limit)
        def _():
            fetch(i)[which].start()

    def wait(i, which):
        fresh = (i < limit) if first_part else ((i < limit) & (i > begin + 1))

        @pl.when(fresh)
        def _():
            fetch(i)[which].wait()

    if first_part:
        start(0, RIGHT)
        start(1, RIGHT)
        start(0, LEFT)

        @pl.loop(0, sums.shape[0])
        def _(q):
            sums[q] = jnp.zeros(sums.shape[1:], sums.dtype)

    zero = jnp.zeros((kernel_size, patch), jnp.bfloat16)

    def first(i, ring, at, ref, u):
        for e in range(QUAD):
            slot = plan_ref[layout.slot + (i * STEP + at) * QUAD + e]
            right = right_ring[ring, at * QUAD + e]
            kern = kern_ref[jnp.maximum(slot, 0)]
            kern = jnp.where(slot >= 0, kern, jnp.zeros_like(kern))
            spread = jnp.concatenate(
                [jnp.concatenate([right, zero], axis=1), jnp.concatenate([zero, right], axis=1)], axis=0
            )
            out = jnp.dot(kern, spread, preferred_element_type=jnp.float32).astype(jnp.bfloat16)
            top = slice(e * 2 * kernel_size, (e * 2 + 1) * kernel_size)
            low = slice((e * 2 + 1) * kernel_size, (e * 2 + 2) * kernel_size)
            ref[u, top, :] = out
            ref[u, low, :patch] = -out[:, patch:]
            ref[u, low, patch:] = out[:, :patch]

    def second(i, ring, at, ref, u):
        left = jnp.concatenate([left_ring[ring, at * QUAD + e] for e in range(QUAD)], axis=1)
        q = plan_ref[layout.anchor + i * STEP + at]
        sums[q] += jnp.dot(left, ref[u], preferred_element_type=jnp.float32)

    if first_part:
        wait(0, RIGHT)
        start(1, LEFT)
        for u in range(UNROLL):
            first(0, 0, u, mixed[0], u)
    start(begin + 2, RIGHT)
    start(begin + 2, LEFT)

    @pl.loop(begin, end)
    def _(i):
        here = lax.rem(i, RING)
        there = lax.rem(i + 1, RING)
        start(i + 3, RIGHT)
        start(i + 3, LEFT)
        wait(i, LEFT)
        wait(i + 1, RIGHT)
        for u in range(UNROLL):
            first(i, here, UNROLL + u, mixed[1], u)
            second(i, here, u, mixed[0], u)
        for u in range(UNROLL):
            first(i + 1, there, u, mixed[0], u)
            second(i, here, UNROLL + u, mixed[1], u)

    wait(end, LEFT)
    wait(end + 1, LEFT)
    wait(end + 1, RIGHT)
    if not first_part:
        return
    low = lax.broadcasted_iota(jnp.int32, (kernel_size, patch), 1) < kernel_size
    take = functools.partial(strip, sums, row_slots, col_slots, kernel_size)
    for a in range(row_slots + 1):
        real = pltpu.roll(take(0, a, col_slots - 1), kernel_size, 1)
        edge = jnp.where(low, real, take(1, a, col_slots - 1)).astype(col_ref.dtype)
        if a < row_slots:
            col_ref[a * kernel_size : (a + 1) * kernel_size, :] = edge
        else:
            corner_ref[...] = edge
    for plane in range(2):
        behind = 0.0
        for tile in range(col_slots // 2):
            odd = pltpu.roll(take(plane, row_slots, 2 * tile + 1), kernel_size, 1)
            value = take(plane, row_slots, 2 * tile) + jnp.where(low, behind, odd)
            row_ref[plane, :, tile * patch : (tile + 1) * patch] = value.astype(row_ref.dtype)
            behind = odd


def grid_part(plan, part, kernels, left, right, carried, layout):
    kernel_size = kernels.shape[1]
    patch = left.shape[1]
    row_slots, col_slots = TILE_U // kernel_size, TILE_V // kernel_size
    smem = pl.BlockSpec(memory_space=pltpu.SMEM)
    vmem = pl.BlockSpec(memory_space=pltpu.VMEM)
    hbm = pl.BlockSpec(memory_space=pl.ANY)
    first_part = carried is None
    carried = [] if first_part else [in_vmem(array) for array in carried]
    mixed_shape = (UNROLL, QUAD * 2 * kernel_size, 2 * patch)
    out_shape = [
        pltpu.VMEM((row_slots * col_slots, patch, 2 * patch), jnp.float32),
        pltpu.VMEM((RING, STEP * QUAD) + left.shape[1:], left.dtype),
        pltpu.VMEM((RING, STEP * QUAD) + right.shape[1:], right.dtype),
        pltpu.VMEM(mixed_shape, jnp.bfloat16),
    ]
    if first_part:
        out_shape += [
            pltpu.VMEM((2, kernel_size, TILE_V), jnp.bfloat16),
            pltpu.VMEM((TILE_U, 2 * kernel_size), jnp.bfloat16),
            pltpu.VMEM((kernel_size, 2 * kernel_size), jnp.bfloat16),
        ]
    out = pl.pallas_call(
        functools.partial(
            grid_body,
            part=part,
            first_part=first_part,
            layout=layout,
            row_slots=row_slots,
            col_slots=col_slots,
        ),
        in_specs=[smem, vmem, hbm, hbm] + [vmem] * len(carried),
        out_specs=[vmem] * len(out_shape),
        out_shape=out_shape,
        input_output_aliases={4 + i: i for i in range(len(carried))},
        scratch_shapes=[
            pltpu.VMEM(mixed_shape, jnp.bfloat16),
            pltpu.SemaphoreType.DMA((2, RING)),
        ],
        compiler_params=pltpu.CompilerParams(vmem_limit_bytes=12 * 2**20),
        name="grid_part",
    )(in_smem(plan), in_vmem(kernels), in_hbm(left), in_hbm(right), *carried)
    return out[:4], out[4:]


def merge_body(sums, row_ref, col_ref, corner_ref, out_hbm, out_ref, sems):
    kernel_size = row_ref.shape[1]
    patch = sums.shape[1]
    row_slots = out_ref.shape[1] // kernel_size
    col_slots = out_ref.shape[2] // kernel_size
    low = lax.broadcasted_iota(jnp.int32, (kernel_size, patch), 1) < kernel_size
    take = functools.partial(strip, sums, row_slots, col_slots, kernel_size)
    for a in range(row_slots):
        rows = slice(a * kernel_size, (a + 1) * kernel_size)
        edge = past_first(["tv"], col_ref[rows, :])
        if a == 0:
            edge = edge + past_first(["tu", "tv"], corner_ref[...])
        for plane in range(2):
            behind = edge if plane == 0 else pltpu.roll(edge, kernel_size, 1)
            for tile in range(col_slots // 2):
                lanes = slice(tile * patch, (tile + 1) * patch)
                odd = pltpu.roll(take(plane, a, 2 * tile + 1), kernel_size, 1)
                value = take(plane, a, 2 * tile) + jnp.where(low, behind, odd)
                if a == 0:
                    value = value + past_first(["tu"], row_ref[plane, :, lanes])
                out_ref[plane, rows, lanes] = value
                behind = odd
        pltpu.make_async_copy(out_ref.at[:, rows], out_hbm.at[:, rows], sems.at[a]).start()
    for a in range(row_slots):
        rows = slice(a * kernel_size, (a + 1) * kernel_size)
        pltpu.make_async_copy(out_ref.at[:, rows], out_hbm.at[:, rows], sems.at[a]).wait()


def merge_tile(sums, row, col, corner):
    vmem = pl.BlockSpec(memory_space=pltpu.VMEM)
    return pl.pallas_call(
        merge_body,
        in_specs=[vmem] * 4,
        out_specs=pl.BlockSpec(memory_space=pl.ANY),
        out_shape=jax.ShapeDtypeStruct((2, TILE_U, TILE_V), jnp.float32),
        scratch_shapes=[
            pltpu.VMEM((2, TILE_U, TILE_V), jnp.float32),
            pltpu.SemaphoreType.DMA((TILE_U // row.shape[1],)),
        ],
        compiler_params=pltpu.CompilerParams(vmem_limit_bytes=8 * 2**20),
        name="merge_tile",
    )(*map(in_vmem, (sums, row, col, corner)))


def shards(
    aperture_amp,
    aperture_phase,
    plane_depths,
    send_list,
    send_count,
    vis_left,
    vis_right,
    block_slot,
    block_pos,
    block_count,
):
    kernel_size = vis_right.shape[1]
    tiles, capacity = send_list.shape[1:]
    both = ("tu", "tv")
    outgoing = make_kernels(
        aperture_amp, aperture_phase, plane_depths, send_list[0].T, send_count, kernel_size
    )
    outgoing = outgoing.reshape((tiles, capacity) + outgoing.shape[1:])
    arrived = lax.all_to_all(outgoing, both, split_axis=0, concat_axis=0, tiled=True)
    received = arrived.reshape((-1,) + arrived.shape[2:])
    layout = Layout(block_pos.shape[0], (TILE_U // kernel_size) * (TILE_V // kernel_size))
    plan, left, right = plan_blocks(block_pos, block_slot, block_count, vis_left, vis_right, layout)
    carried, (row, col, corner) = grid_part(plan, 0, received, left, right, None, layout)
    row = around(row, ("tu",))
    col = around(col, ("tv",))
    corner = around(corner, ("tu", "tv"))
    carried, _ = grid_part(plan, 1, received, left, right, carried, layout)
    return merge_tile(carried[0], row, col, corner)


def solution(mesh):
    placed = (
        P(("tu", "tv"), None, None),
        P(("tu", "tv"), None, None),
        P(),
        P(("tu", "tv"), None, None),
        P(("tu", "tv"), None),
        P(("tu", "tv"), None, None),
        P(("tu", "tv"), None, None),
        P(("tu", "tv")),
        P(("tu", "tv")),
        P(("tu", "tv")),
    )
    return jax.shard_map(
        shards, mesh=mesh, in_specs=placed, out_specs=P(None, "tu", "tv"), check_vma=False
    )
```

```python
import functools
import math

import jax
import jax.numpy as jnp
import numpy as np
from jax import lax
from jax.experimental import pallas as pl
from jax.experimental.pallas import tpu as pltpu
from jax.sharding import PartitionSpec as P

TILE_U = 256
TILE_V = 512
QUAD = 4
UNROLL = 8
STEP = 2 * UNROLL
RING = 4
LEFT, RIGHT = 0, 1

def _fit(fn, degree):
    span = math.pi ** 2
    nodes = 0.5 * span * (1.0 - np.cos(np.pi * (np.arange(400) + 0.5) / 400))
    cheb = np.polynomial.chebyshev.Chebyshev.fit(nodes, fn(np.sqrt(nodes)), degree, domain=[0, span])
    return [float(c) for c in cheb.convert(kind=np.polynomial.Polynomial).coef]


COS_POLY = _fit(np.cos, 6)
SIN_POLY = _fit(lambda x: np.sin(x) / x, 5)


def horner(coefs, u):
    total = jnp.full_like(u, coefs[-1])
    for coef in coefs[-2::-1]:
        total = total * u + coef
    return total


def cos_sin(x):
    u = x * x
    return horner(COS_POLY, u), x * horner(SIN_POLY, u)


def around(block, axes):
    sizes = [lax.axis_size(axis) for axis in axes]
    route = []
    for place in np.ndindex(*sizes):
        target = [(i + 1) % n for i, n in zip(place, sizes)]
        route.append((int(np.ravel_multi_index(place, sizes)), int(np.ravel_multi_index(target, sizes))))
    return lax.ppermute(block, axes, route)


def past_first(axes, halo):
    real = functools.reduce(jnp.logical_and, [lax.axis_index(axis) > 0 for axis in axes])
    return jnp.where(real, halo.astype(jnp.float32), 0.0)


def in_hbm(array):
    return pltpu.with_memory_space_constraint(array, pltpu.HBM)


def in_vmem(array):
    return pltpu.with_memory_space_constraint(array, pltpu.VMEM)


def in_smem(array):
    return pltpu.with_memory_space_constraint(array, pltpu.SMEM)


def kernels_body(
    list_hbm, count_hbm, depth_hbm, amp_hbm, phase_hbm, out_ref,
    chosen_list, count, depth, amp, phase, table, screen, halves, made, small_sems, bulk_sems,
):
    screens, size, _ = amp.shape
    planes = depth.shape[0]
    kernel_size = out_ref.shape[1]
    small = [
        pltpu.make_async_copy(depth_hbm, depth, small_sems.at[0]),
        pltpu.make_async_copy(list_hbm, chosen_list, small_sems.at[1]),
        pltpu.make_async_copy(count_hbm, count, small_sems.at[2]),
    ]
    for copy in small:
        copy.start()

    def bulk(s):
        return [
            pltpu.make_async_copy(amp_hbm.at[s], amp.at[s], bulk_sems.at[0, s]),
            pltpu.make_async_copy(phase_hbm.at[s], phase.at[s], bulk_sems.at[1, s]),
        ]

    for copy in bulk(0):
        copy.start()

    frequency = lax.broadcasted_iota(jnp.int32, (kernel_size, size), 0) - kernel_size // 2
    cells = lax.broadcasted_iota(jnp.int32, (kernel_size, size), 1)
    turns = frequency.astype(jnp.float32) * cells.astype(jnp.float32) / size
    real_f, imag_f = cos_sin((2.0 * math.pi) * (turns - jnp.round(turns)))
    real_f = real_f.astype(jnp.bfloat16).astype(jnp.float32)
    imag_f = (-imag_f).astype(jnp.bfloat16).astype(jnp.float32)
    place = (lax.broadcasted_iota(jnp.int32, (1, size), 1).astype(jnp.float32) - size // 2) / size
    square = place * place
    for copy in small:
        copy.wait()
    for s in range(1, screens):
        for copy in bulk(s):
            copy.start()
    for p in range(planes):
        turns = depth[p] * square
        real_e, imag_e = cos_sin((2.0 * math.pi) * (turns - jnp.round(turns)))
        real_g = (real_f * real_e - imag_f * imag_e).astype(jnp.bfloat16)
        imag_g = (real_f * imag_e + imag_f * real_e).astype(jnp.bfloat16)
        top = slice(p * 2 * kernel_size, (p * 2 + 1) * kernel_size)
        low = slice((p * 2 + 1) * kernel_size, (p * 2 + 2) * kernel_size)
        table[top, :size] = real_g
        table[top, size:] = -imag_g
        table[low, :size] = imag_g
        table[low, size:] = real_g

    @pl.loop(0, screens)
    def _(s):
        for copy in bulk(s):
            copy.wait()
        magnitude = amp[s].astype(jnp.float32)
        real_e, imag_e = cos_sin(phase[s].astype(jnp.float32))
        screen[:size, :] = (magnitude * real_e).astype(jnp.bfloat16)
        screen[size:, :] = (magnitude * imag_e).astype(jnp.bfloat16)
        product = jnp.dot(table[...], screen[...], preferred_element_type=jnp.float32).astype(jnp.bfloat16)
        for p in range(planes):
            base = p * 2 * kernel_size
            halves[s, p, :, :size] = product[base : base + kernel_size]
            halves[s, p, :, size:] = product[base + kernel_size : base + 2 * kernel_size]

    for p in range(planes):
        second = lax.dot_general(
            jnp.concatenate([halves[s, p] for s in range(screens)], axis=0),
            table[p * 2 * kernel_size : (p + 1) * 2 * kernel_size, :],
            (((1,), (1,)), ((), ())),
            preferred_element_type=jnp.float32,
        )
        second = (second * (1.0 / size)).astype(jnp.bfloat16)
        for s in range(screens):
            made[s * planes + p] = second[s * kernel_size : (s + 1) * kernel_size]

    capacity, tiles = chosen_list.shape

    @pl.loop(0, tiles, unroll=8)
    def _(t):
        for c in range(capacity):
            chosen = made[chosen_list[c, t]]
            out_ref[t * capacity + c] = jnp.where(c < count[0, t], chosen, jnp.zeros_like(chosen))


def make_kernels(aperture_amp, aperture_phase, plane_depths, chosen_list, counts, kernel_size):
    screens, size, _ = aperture_amp.shape
    planes = plane_depths.shape[0]
    capacity, tiles = chosen_list.shape
    hbm = pl.BlockSpec(memory_space=pl.ANY)
    return pl.pallas_call(
        kernels_body,
        in_specs=[hbm] * 5,
        out_specs=pl.BlockSpec(memory_space=pltpu.VMEM),
        out_shape=pltpu.VMEM((tiles * capacity, kernel_size, 2 * kernel_size), jnp.bfloat16),
        scratch_shapes=[
            pltpu.SMEM((capacity, tiles), jnp.int32),
            pltpu.SMEM((1, tiles), jnp.int32),
            pltpu.SMEM((planes,), jnp.float32),
            pltpu.VMEM((screens, size, size), jnp.bfloat16),
            pltpu.VMEM((screens, size, size), jnp.bfloat16),
            pltpu.VMEM((planes * 2 * kernel_size, 2 * size), jnp.bfloat16),
            pltpu.VMEM((2 * size, size), jnp.bfloat16),
            pltpu.VMEM((screens, planes, kernel_size, 2 * size), jnp.bfloat16),
            pltpu.VMEM((screens * planes, kernel_size, 2 * kernel_size), jnp.bfloat16),
            pltpu.SemaphoreType.DMA((3,)),
            pltpu.SemaphoreType.DMA((2, screens)),
        ],
        compiler_params=pltpu.CompilerParams(vmem_limit_bytes=32 * 2**20),
        name="make_kernels",
    )(*map(in_hbm, (chosen_list, counts, plane_depths, aperture_amp, aperture_phase)))


class Layout:
    def __init__(self, blocks, anchors):
        self.parts = 2
        quads = (blocks + (QUAD - 1) * anchors) // QUAD + 1
        self.quads = (quads + STEP - 1) // STEP * STEP
        self.anchor = self.parts + 1
        self.slot = self.anchor + self.quads
        self.total = self.slot + (self.quads + UNROLL) * QUAD


def plan_body(
    pos_ref, slot_ref, count_ref, left_hbm, right_hbm, plan_ref, left_out, right_out,
    left_ref, right_ref, tally, cursor, sems, *, layout, row_slots, col_slots,
):
    anchors = row_slots * col_slots
    border = row_slots + col_slots - 1
    live = count_ref[0]

    def copies(block, place):
        return [
            pltpu.make_async_copy(left_hbm.at[block], left_ref.at[place], sems.at[0]),
            pltpu.make_async_copy(right_hbm.at[block], right_ref.at[place], sems.at[1]),
        ]

    def put(block, place, slot):
        plan_ref[layout.slot + place] = slot
        for copy in copies(block, place):
            copy.start()

    @pl.loop(0, anchors)
    def _(q):
        tally[q] = 0

    @pl.loop(0, live)
    def _(j):
        q = pos_ref[j]
        tally[q] = tally[q] + 1

    def lay(rank, quad):
        inner = rank - border
        q = jnp.where(
            rank < row_slots,
            rank * col_slots + col_slots - 1,
            jnp.where(
                rank < border,
                (row_slots - 1) * col_slots + rank - row_slots,
                (inner // (col_slots - 1)) * col_slots + lax.rem(inner, col_slots - 1),
            ),
        )
        number = tally[q]
        quads = (number + QUAD - 1) // QUAD
        cursor[q] = quad * QUAD

        @pl.loop(0, quads)
        def _(i):
            plan_ref[layout.anchor + quad + i] = q

        @pl.loop(quad * QUAD + number, (quad + quads) * QUAD)
        def _(i):
            put(0, i, -1)

        return quad + quads

    quad = 0
    begin = 0
    plan_ref[0] = 0
    for part, end in enumerate([border, anchors]):
        quad = lax.fori_loop(begin, end, lay, quad)
        begin = end
        plan_ref[part + 1] = ((quad + STEP - 1) // STEP) * STEP

    full = ((quad + STEP - 1) // STEP) * STEP

    @pl.loop(quad, full)
    def _(i):
        plan_ref[layout.anchor + i] = 0
        for e in range(QUAD):
            put(0, i * QUAD + e, -1)

    quad = full

    @pl.loop(quad * QUAD, (quad + UNROLL) * QUAD)
    def _(i):
        plan_ref[layout.slot + i] = -1

    @pl.loop(0, live)
    def _(j):
        q = pos_ref[j]
        at = cursor[q]
        cursor[q] = at + 1
        put(j, at, slot_ref[j])

    chunk = STEP * QUAD

    @pl.loop(0, quad // STEP)
    def _(i):
        rows = pl.ds(0, chunk)
        pltpu.make_async_copy(left_hbm.at[rows], left_ref.at[rows], sems.at[0]).wait()
        pltpu.make_async_copy(right_hbm.at[rows], right_ref.at[rows], sems.at[1]).wait()

    def writes(i):
        rows = pl.ds(i * chunk, chunk)
        return [
            pltpu.make_async_copy(left_ref.at[rows], left_out.at[rows], sems.at[2]),
            pltpu.make_async_copy(right_ref.at[rows], right_out.at[rows], sems.at[3]),
        ]

    @pl.loop(0, quad // STEP)
    def _(i):
        for copy in writes(i):
            copy.start()

    @pl.loop(0, quad // STEP)
    def _(i):
        for copy in writes(i):
            copy.wait()


def plan_blocks(block_pos, block_slot, block_count, vis_left, vis_right, layout):
    kernel_size = vis_right.shape[1]
    row_slots, col_slots = TILE_U // kernel_size, TILE_V // kernel_size
    smem = pl.BlockSpec(memory_space=pltpu.SMEM)
    hbm = pl.BlockSpec(memory_space=pl.ANY)
    places = layout.quads * QUAD
    return pl.pallas_call(
        functools.partial(plan_body, layout=layout, row_slots=row_slots, col_slots=col_slots),
        in_specs=[smem] * 3 + [hbm] * 2,
        out_specs=[smem, hbm, hbm],
        out_shape=[
            pltpu.SMEM((layout.total,), jnp.int32),
            pltpu.HBM((places,) + vis_left.shape[1:], vis_left.dtype),
            pltpu.HBM((places,) + vis_right.shape[1:], vis_right.dtype),
        ],
        scratch_shapes=[
            pltpu.VMEM((places,) + vis_left.shape[1:], vis_left.dtype),
            pltpu.VMEM((places,) + vis_right.shape[1:], vis_right.dtype),
            pltpu.SMEM((row_slots * col_slots,), jnp.int32),
            pltpu.SMEM((row_slots * col_slots,), jnp.int32),
            pltpu.SemaphoreType.DMA((4,)),
        ],
        compiler_params=pltpu.CompilerParams(vmem_limit_bytes=36 * 2**20),
        name="plan_blocks",
    )(block_pos, block_slot, block_count, in_hbm(vis_left), in_hbm(vis_right))


def strip(sums, row_slots, col_slots, kernel_size, plane, a, col):
    patch = sums.shape[1]
    lanes = slice(plane * patch, (plane + 1) * patch)
    total = None
    if a < row_slots:
        total = sums[a * col_slots + col, :kernel_size, lanes]
    if a > 0:
        above = sums[(a - 1) * col_slots + col, kernel_size:, lanes]
        total = above if total is None else total + above
    return total


def grid_body(
    plan_ref, kern_ref, left_hbm, right_hbm, *rest, part, first_part, layout, row_slots, col_slots
):
    if not first_part:
        rest = rest[4:]
    sums, left_ring, right_ring, ahead, *rest = rest
    if first_part:
        row_ref, col_ref, corner_ref, *rest = rest
    behind_ref, sems = rest
    mixed = (ahead, behind_ref)
    slots, kernel_size, _ = kern_ref.shape
    patch = left_hbm.shape[1]
    chunk = STEP * QUAD
    begin = plan_ref[part] // STEP
    end = plan_ref[part + 1] // STEP
    limit = jnp.minimum(plan_ref[layout.parts] // STEP, end + 2)

    def fetch(i):
        source = pl.ds(i * chunk, chunk)
        ring = lax.rem(i, RING)
        return [
            pltpu.make_async_copy(left_hbm.at[source], left_ring.at[ring], sems.at[0, ring]),
            pltpu.make_async_copy(right_hbm.at[source], right_ring.at[ring], sems.at[1, ring]),
        ]

    def start(i, which):
        @pl.when(i < limit)
        def _():
            fetch(i)[which].start()

    def wait(i, which):
        fresh = (i < limit) if first_part else ((i < limit) & (i > begin + 1))

        @pl.when(fresh)
        def _():
            fetch(i)[which].wait()

    if first_part:
        start(0, RIGHT)
        start(1, RIGHT)
        start(0, LEFT)

        @pl.loop(0, sums.shape[0])
        def _(q):
            sums[q] = jnp.zeros(sums.shape[1:], sums.dtype)

    zero = jnp.zeros((kernel_size, patch), jnp.bfloat16)

    def first(i, ring, at, ref, u):
        for e in range(QUAD):
            slot = plan_ref[layout.slot + (i * STEP + at) * QUAD + e]
            right = right_ring[ring, at * QUAD + e]
            kern = kern_ref[jnp.maximum(slot, 0)]
            kern = jnp.where(slot >= 0, kern, jnp.zeros_like(kern))
            spread = jnp.concatenate(
                [jnp.concatenate([right, zero], axis=1), jnp.concatenate([zero, right], axis=1)], axis=0
            )
            out = jnp.dot(kern, spread, preferred_element_type=jnp.float32).astype(jnp.bfloat16)
            top = slice(e * 2 * kernel_size, (e * 2 + 1) * kernel_size)
            low = slice((e * 2 + 1) * kernel_size, (e * 2 + 2) * kernel_size)
            ref[u, top, :] = out
            ref[u, low, :patch] = -out[:, patch:]
            ref[u, low, patch:] = out[:, :patch]

    def second(i, ring, at, ref, u):
        left = jnp.concatenate([left_ring[ring, at * QUAD + e] for e in range(QUAD)], axis=1)
        q = plan_ref[layout.anchor + i * STEP + at]
        sums[q] += jnp.dot(left, ref[u], preferred_element_type=jnp.float32)

    if first_part:
        wait(0, RIGHT)
        start(1, LEFT)
        for u in range(UNROLL):
            first(0, 0, u, mixed[0], u)
    start(begin + 2, RIGHT)
    start(begin + 2, LEFT)

    @pl.loop(begin, end)
    def _(i):
        here = lax.rem(i, RING)
        there = lax.rem(i + 1, RING)
        start(i + 3, RIGHT)
        start(i + 3, LEFT)
        wait(i, LEFT)
        wait(i + 1, RIGHT)
        for u in range(UNROLL):
            first(i, here, UNROLL + u, mixed[1], u)
            second(i, here, u, mixed[0], u)
        for u in range(UNROLL):
            first(i + 1, there, u, mixed[0], u)
            second(i, here, UNROLL + u, mixed[1], u)

    wait(end, LEFT)
    wait(end + 1, LEFT)
    wait(end + 1, RIGHT)
    if not first_part:
        return
    low = lax.broadcasted_iota(jnp.int32, (kernel_size, patch), 1) < kernel_size
    take = functools.partial(strip, sums, row_slots, col_slots, kernel_size)
    for a in range(row_slots + 1):
        real = pltpu.roll(take(0, a, col_slots - 1), kernel_size, 1)
        edge = jnp.where(low, real, take(1, a, col_slots - 1)).astype(col_ref.dtype)
        if a < row_slots:
            col_ref[a * kernel_size : (a + 1) * kernel_size, :] = edge
        else:
            corner_ref[...] = edge
    for plane in range(2):
        behind = 0.0
        for tile in range(col_slots // 2):
            odd = pltpu.roll(take(plane, row_slots, 2 * tile + 1), kernel_size, 1)
            value = take(plane, row_slots, 2 * tile) + jnp.where(low, behind, odd)
            row_ref[plane, :, tile * patch : (tile + 1) * patch] = value.astype(row_ref.dtype)
            behind = odd


def grid_part(plan, part, kernels, left, right, carried, layout):
    kernel_size = kernels.shape[1]
    patch = left.shape[1]
    row_slots, col_slots = TILE_U // kernel_size, TILE_V // kernel_size
    smem = pl.BlockSpec(memory_space=pltpu.SMEM)
    vmem = pl.BlockSpec(memory_space=pltpu.VMEM)
    hbm = pl.BlockSpec(memory_space=pl.ANY)
    first_part = carried is None
    carried = [] if first_part else [in_vmem(array) for array in carried]
    mixed_shape = (UNROLL, QUAD * 2 * kernel_size, 2 * patch)
    out_shape = [
        pltpu.VMEM((row_slots * col_slots, patch, 2 * patch), jnp.float32),
        pltpu.VMEM((RING, STEP * QUAD) + left.shape[1:], left.dtype),
        pltpu.VMEM((RING, STEP * QUAD) + right.shape[1:], right.dtype),
        pltpu.VMEM(mixed_shape, jnp.bfloat16),
    ]
    if first_part:
        out_shape += [
            pltpu.VMEM((2, kernel_size, TILE_V), jnp.bfloat16),
            pltpu.VMEM((TILE_U, 2 * kernel_size), jnp.bfloat16),
            pltpu.VMEM((kernel_size, 2 * kernel_size), jnp.bfloat16),
        ]
    out = pl.pallas_call(
        functools.partial(
            grid_body,
            part=part,
            first_part=first_part,
            layout=layout,
            row_slots=row_slots,
            col_slots=col_slots,
        ),
        in_specs=[smem, vmem, hbm, hbm] + [vmem] * len(carried),
        out_specs=[vmem] * len(out_shape),
        out_shape=out_shape,
        input_output_aliases={4 + i: i for i in range(len(carried))},
        scratch_shapes=[
            pltpu.VMEM(mixed_shape, jnp.bfloat16),
            pltpu.SemaphoreType.DMA((2, RING)),
        ],
        compiler_params=pltpu.CompilerParams(vmem_limit_bytes=12 * 2**20),
        name="grid_part",
    )(in_smem(plan), in_vmem(kernels), in_hbm(left), in_hbm(right), *carried)
    return out[:4], out[4:]


def merge_body(sums, row_ref, col_ref, corner_ref, out_hbm, out_ref, sems):
    kernel_size = row_ref.shape[1]
    patch = sums.shape[1]
    row_slots = out_ref.shape[1] // kernel_size
    col_slots = out_ref.shape[2] // kernel_size
    low = lax.broadcasted_iota(jnp.int32, (kernel_size, patch), 1) < kernel_size
    take = functools.partial(strip, sums, row_slots, col_slots, kernel_size)
    for a in range(row_slots):
        rows = slice(a * kernel_size, (a + 1) * kernel_size)
        edge = past_first(["tv"], col_ref[rows, :])
        if a == 0:
            edge = edge + past_first(["tu", "tv"], corner_ref[...])
        for plane in range(2):
            behind = edge if plane == 0 else pltpu.roll(edge, kernel_size, 1)
            for tile in range(col_slots // 2):
                lanes = slice(tile * patch, (tile + 1) * patch)
                odd = pltpu.roll(take(plane, a, 2 * tile + 1), kernel_size, 1)
                value = take(plane, a, 2 * tile) + jnp.where(low, behind, odd)
                if a == 0:
                    value = value + past_first(["tu"], row_ref[plane, :, lanes])
                out_ref[plane, rows, lanes] = value
                behind = odd
        pltpu.make_async_copy(out_ref.at[:, rows], out_hbm.at[:, rows], sems.at[a]).start()
    for a in range(row_slots):
        rows = slice(a * kernel_size, (a + 1) * kernel_size)
        pltpu.make_async_copy(out_ref.at[:, rows], out_hbm.at[:, rows], sems.at[a]).wait()


def merge_tile(sums, row, col, corner):
    vmem = pl.BlockSpec(memory_space=pltpu.VMEM)
    return pl.pallas_call(
        merge_body,
        in_specs=[vmem] * 4,
        out_specs=pl.BlockSpec(memory_space=pl.ANY),
        out_shape=jax.ShapeDtypeStruct((2, TILE_U, TILE_V), jnp.float32),
        scratch_shapes=[
            pltpu.VMEM((2, TILE_U, TILE_V), jnp.float32),
            pltpu.SemaphoreType.DMA((TILE_U // row.shape[1],)),
        ],
        compiler_params=pltpu.CompilerParams(vmem_limit_bytes=8 * 2**20),
        name="merge_tile",
    )(*map(in_vmem, (sums, row, col, corner)))


def shards(
    aperture_amp,
    aperture_phase,
    plane_depths,
    send_list,
    send_count,
    vis_left,
    vis_right,
    block_slot,
    block_pos,
    block_count,
):
    kernel_size = vis_right.shape[1]
    tiles, capacity = send_list.shape[1:]
    both = ("tu", "tv")
    outgoing = make_kernels(
        aperture_amp, aperture_phase, plane_depths, send_list[0].T, send_count, kernel_size
    )
    outgoing = outgoing.reshape((tiles, capacity) + outgoing.shape[1:])
    arrived = lax.all_to_all(outgoing, both, split_axis=0, concat_axis=0, tiled=True)
    received = arrived.reshape((-1,) + arrived.shape[2:])
    layout = Layout(block_pos.shape[0], (TILE_U // kernel_size) * (TILE_V // kernel_size))
    plan, left, right = plan_blocks(block_pos, block_slot, block_count, vis_left, vis_right, layout)
    carried, (row, col, corner) = grid_part(plan, 0, received, left, right, None, layout)
    row = around(row, ("tu",))
    col = around(col, ("tv",))
    corner = around(corner, ("tu", "tv"))
    carried, _ = grid_part(plan, 1, received, left, right, carried, layout)
    return merge_tile(carried[0], row, col, corner)


def solution(mesh):
    placed = (
        P(("tu", "tv"), None, None),
        P(("tu", "tv"), None, None),
        P(),
        P(("tu", "tv"), None, None),
        P(("tu", "tv"), None),
        P(("tu", "tv"), None, None),
        P(("tu", "tv"), None, None),
        P(("tu", "tv")),
        P(("tu", "tv")),
        P(("tu", "tv")),
    )
    return jax.shard_map(
        shards, mesh=mesh, in_specs=placed, out_specs=P(None, "tu", "tv"), check_vma=False
    )
```
